128 devices in a mesh: dp: 16 (over y, z_lo, core), row: 4 (over x), col: 2 (over z_hi).
Axes of the slice: x: 4, y: 4, z: 4 (z_hi: 2, z_lo: 2; z = z_hi * 2 + z_lo), core: 2. Of those that a mesh axis runs over, the one named last changes fastest.
Arguments:
- tokens: bfloat16 [20480, 2048], P(('dp', 'row', 'col')), may hold values from -6 to 6
- cotangent: bfloat16 [20480, 2048], P(('dp', 'row', 'col')), may hold values from -6 to 6
- gain_one: float32 [2048], replicated, may hold values from 0.5 to 1.5
- qkv_weight: bfloat16 [2048, 2560], P('col', 'row'), may hold values from -0.125 to 0.125
- out_weight: bfloat16 [2048, 2048], P(('row', 'col')), may hold values from -0.5 to 0.5
- gate_weight: bfloat16 [2048, 5632], P('col', 'row'), may hold values from -0.125 to 0.125
- up_weight: bfloat16 [2048, 5632], P('col', 'row'), may hold values from -0.125 to 0.125
- down_weight: bfloat16 [5632, 2048], P(('row', 'col')), may hold values from -0.15625 to 0.15625
- gain_two: float32 [2048], replicated, may hold values from 0.5 to 1.5
- seq_lengths: int32 [32], replicated, may hold values from 1 to 1280, as said below
- seq_replica: int32 [32], replicated, may hold values from 0 to 15, as said below
Outputs:
- layer_out: bfloat16 [20480, 2048], P(('dp', 'row', 'col'))
- input_grad: bfloat16 [20480, 2048], P(('dp', 'row', 'col'))
- grad_gain_one: float32 [2048], replicated
- grad_qkv: float32 [2048, 2560], P('col', 'row')
- grad_out: float32 [2048, 2048], P(('row', 'col'))
- grad_gate: float32 [2048, 5632], P('col', 'row')
- grad_up: float32 [2048, 5632], P('col', 'row')
- grad_down: float32 [5632, 2048], P(('row', 'col'))
- grad_gain_two: float32 [2048], replicated
The draws below stay inside these ranges and needn't reach their ends.
Inputs may be any that keep to these rules, and one draw needn't show every extreme that they name: `seq_lengths`: sequence i is dealt to replica seq_replica[i]; every replica receives sequences whose lengths sum to 1280 or less, one replica's exactly to 1280; the lowest-numbered sequence of each replica is longer than 1120, and a replica holds one or three sequences. `seq_replica`: each of the 32 sequences names its replica.
All inputs are finite; a program needn't handle non-finite values.
Results may differ from the reference program's by a relative error of at most 0.035.
Values may be sent and summed in bfloat16 or wider, within the bound.
No kernel may reach another device: no remote copies, remote signals or barrier semaphores. Data moves between devices by JAX's collectives and lax.ppermute only.
A program may use at most 192 MiB of HBM per device.

```python
import jax
import jax.numpy as jnp
from jax import lax

D = 2048
HEADS = 32
KV = 4
HD = 64
FF = 5632
CAP = 1280
TOKENS = 20480
QKVW = 2560
N_DP = 16


def deal(key):
    order = jax.random.permutation(jax.random.fold_in(key, 11), N_DP).astype(jnp.int32)
    extra_home = order[jnp.arange(N_DP, dtype=jnp.int32) // 2]
    replica = jnp.concatenate([order, extra_home]).astype(jnp.int32)
    extra_len = jax.random.randint(jax.random.fold_in(key, 12), (N_DP,), 1, CAP // 32 + 1, dtype=jnp.int32)
    padding = jax.random.randint(jax.random.fold_in(key, 13), (N_DP,), 0, CAP // 16, dtype=jnp.int32)
    replica_ids = jnp.arange(N_DP, dtype=jnp.int32)
    padding = jnp.where(replica_ids == order[N_DP - 1], 0, padding).astype(jnp.int32)
    extra_sum = jnp.sum(jnp.where(extra_home[None, :] == replica_ids[:, None], extra_len[None, :], 0), axis=1).astype(jnp.int32)
    main_len = (CAP - padding[order] - extra_sum[order]).astype(jnp.int32)
    lengths = jnp.concatenate([main_len, extra_len]).astype(jnp.int32)
    return (lengths, replica)


def draw_seq_lengths(key, part):
    return deal(key)[0]


def draw_seq_replica(key, part):
    return deal(key)[1]


def block_scale(own_key, shape, cuts, low, high):
    def one(dim, parts):
        draws = jax.random.uniform(jax.random.fold_in(jax.random.fold_in(own_key, 6), dim), (parts,), jnp.float32, low / len(cuts), high / len(cuts))
        return jnp.repeat(jnp.exp(draws), shape[dim] // parts).reshape((-1,) + (1,) * (len(shape) - dim - 1))

    level = one(*cuts[0])
    for cut in cuts[1:]:
        level = level * one(*cut)
    return level


def scatter_about(stream_key, extent, width, reach, shards=(), kind=jnp.bfloat16):
    values = width * jax.random.normal(stream_key, extent, jnp.float32)
    if shards:
        values = values * block_scale(stream_key, extent, shards, -0.22, 0.18)
    return jnp.clip(values, -reach, reach).astype(kind)


def setup_inputs(seed: int = 0) -> dict:
    arg_keys = jax.random.split(jax.random.key(seed), 12)
    tokens = scatter_about(arg_keys[0], (TOKENS, D), 1.0, 6.0, ((0, 128),))
    cotangent = scatter_about(arg_keys[1], (TOKENS, D), 1.0, 6.0, ((0, 128),))
    gain_one = jnp.clip(1.0 + 0.1 * jax.random.normal(arg_keys[2], (D,), jnp.float32), 0.5, 1.5)
    qkv_weight = scatter_about(arg_keys[3], (D, QKVW), D ** -0.5, 0.125, ((0, 2), (1, 4)))
    out_weight = scatter_about(arg_keys[4], (HEADS * HD, D), (HEADS * HD // 16) ** -0.5, 0.5, ((0, 8),))
    gate_weight = scatter_about(arg_keys[5], (D, FF), D ** -0.5, 0.125, ((0, 2), (1, 4)))
    up_weight = scatter_about(arg_keys[6], (D, FF), D ** -0.5, 0.125, ((0, 2), (1, 4)))
    down_weight = scatter_about(arg_keys[7], (FF, D), (FF // 4) ** -0.5, 0.15625, ((0, 8),))
    gain_two = jnp.clip(1.0 + 0.1 * jax.random.normal(arg_keys[8], (D,), jnp.float32), 0.5, 1.5)
    seq_lengths = draw_seq_lengths(jax.random.fold_in(arg_keys[11], 71), 0)
    seq_replica = draw_seq_replica(jax.random.fold_in(arg_keys[11], 71), 0)
    return {"tokens": tokens, "cotangent": cotangent, "gain_one": gain_one, "qkv_weight": qkv_weight, "out_weight": out_weight, "gate_weight": gate_weight, "up_weight": up_weight, "down_weight": down_weight, "gain_two": gain_two, "seq_lengths": seq_lengths, "seq_replica": seq_replica}


@jax.custom_vjp
def low(v):
    return lax.optimization_barrier(v.astype(jnp.bfloat16)).astype(jnp.float32)

@jax.custom_vjp
def low_back(v):
    return v

def low_keep(v):
    return (low(v), None)

def low_pass(kept, grad):
    return (grad,)

def back_keep(v):
    return (v, None)

def back_low(kept, grad):
    return (low(grad),)
low.defvjp(low_keep, low_pass)
low_back.defvjp(back_keep, back_low)
EPSILON = 1e-05
ROTARY_BASE = 10000.0
MASKED = -1e+30
HIGHEST = lax.Precision.HIGHEST

def product(left, right):
    return jnp.dot(left, right, precision=HIGHEST)

def normed(values, scale_gain):
    inverse_rms = lax.rsqrt(lax.optimization_barrier(jnp.mean(values * values, axis=-1, keepdims=True)) + EPSILON)
    return values * inverse_rms * scale_gain

def layout(lengths, replica, replica_id, capacity):
    is_own = replica == replica_id
    seq_sizes = jnp.where(is_own, lengths, 0).astype(jnp.int32)
    starts = (jnp.cumsum(seq_sizes) - seq_sizes).astype(jnp.int32)
    row_ids = jnp.arange(capacity, dtype=jnp.int32)
    inside = (row_ids[:, None] >= starts[None, :]) & (row_ids[:, None] < (starts + seq_sizes)[None, :])
    number = jnp.arange(1, lengths.shape[0] + 1, dtype=jnp.int32)
    segment = lax.optimization_barrier(jnp.sum(jnp.where(inside, number[None, :], 0), axis=1)).astype(jnp.int32)
    seq_begin = lax.optimization_barrier(jnp.sum(jnp.where(inside, starts[None, :], 0), axis=1)).astype(jnp.int32)
    filled = jnp.sum(seq_sizes).astype(jnp.int32)
    seq_begin = seq_begin + jnp.where(segment == 0, filled, 0).astype(jnp.int32)
    return (segment, (row_ids - seq_begin).astype(jnp.int32))

def rotary(position, head_size):
    half_size = head_size // 2
    frequency = ROTARY_BASE ** (-jnp.arange(half_size, dtype=jnp.float32) * (2.0 / head_size))
    angles = position.astype(jnp.float32)[:, None] * frequency[None, :]
    return (jnp.cos(angles)[:, None, :], jnp.sin(angles)[:, None, :])

def rotate(values, cosine, sine):
    half_size = values.shape[-1] // 2
    lower_half = values[..., :half_size]
    upper_half = values[..., half_size:]
    return jnp.concatenate([lower_half * cosine - upper_half * sine, upper_half * cosine + lower_half * sine], axis=-1)

def forward(params, inputs, segment, position):
    gain_one, qkv_weight, out_weight, gate_weight, up_weight, down_weight, gain_two = params
    seq_rows = inputs.shape[0]
    per_kv = HEADS // KV
    normed_one = low(normed(inputs, gain_one))
    mixed = low_back(product(normed_one, qkv_weight)).reshape(seq_rows, KV, (per_kv + 2) * HD)
    queries = mixed[:, :, :per_kv * HD].reshape(seq_rows, HEADS, HD)
    key_heads = mixed[:, :, per_kv * HD:(per_kv + 1) * HD]
    value_heads = mixed[:, :, (per_kv + 1) * HD:]
    cosine, sine = rotary(position, HD)
    queries = low(rotate(queries, cosine, sine))
    key_heads = jnp.repeat(low(rotate(key_heads, cosine, sine)), per_kv, axis=1)
    value_heads = jnp.repeat(low(value_heads), per_kv, axis=1)
    raw_scores = jnp.einsum('qhd,khd->hqk', queries, key_heads, precision=HIGHEST)
    scores = low_back(raw_scores * HD ** (-0.5))
    row_ids = jnp.arange(seq_rows, dtype=jnp.int32)
    allowed = (segment[:, None] == segment[None, :]) & (row_ids[:, None] >= row_ids[None, :])
    scores = jnp.where(allowed[None], scores, MASKED)
    row_max = lax.optimization_barrier(jnp.max(scores, axis=-1, keepdims=True))
    expvals = jnp.exp(scores - row_max)
    weights = low(expvals / lax.optimization_barrier(jnp.sum(expvals, axis=-1, keepdims=True)))
    attended = jnp.einsum('hqk,khd->qhd', weights, value_heads, precision=HIGHEST).reshape(seq_rows, HEADS * HD)
    attended = low_back(low(attended))
    after_attn = inputs + low_back(product(attended, out_weight))
    normed_two = low(normed(after_attn, gain_two))
    gate = low_back(product(normed_two, gate_weight))
    up_value = low_back(product(normed_two, up_weight))
    hidden = low(jax.nn.silu(gate) * up_value)
    return after_attn + low_back(product(hidden, down_weight))

def reference(tokens, cotangent, gain_one, qkv_weight, out_weight, gate_weight, up_weight, down_weight, gain_two, seq_lengths, seq_replica):
    params = tuple((item.astype(jnp.float32) for item in (gain_one, qkv_weight, out_weight, gate_weight, up_weight, down_weight, gain_two)))
    inputs_all = tokens.astype(jnp.float32).reshape(N_DP, CAP, D)
    cots_all = cotangent.astype(jnp.float32).reshape(N_DP, CAP, D)

    def replica_step(summed, scan_item):
        replica_id, inputs, cots = scan_item
        segment, position = layout(seq_lengths, seq_replica, replica_id, CAP)
        result, pullback = jax.vjp(lambda weights_in, rows_in: forward(weights_in, rows_in, segment, position), params, inputs)
        gradients, input_back = pullback(cots)
        summed = jax.tree.map(jnp.add, summed, gradients)
        return (summed, (result.astype(jnp.bfloat16), input_back.astype(jnp.bfloat16)))
    zero_grads = tuple((jnp.zeros_like(item) for item in params))
    summed, (outputs, input_grads) = lax.scan(replica_step, zero_grads, (jnp.arange(N_DP, dtype=jnp.int32), inputs_all, cots_all))
    grad_one, grad_qkv, grad_out, grad_gate, grad_up, grad_down, grad_two = summed
    return (outputs.reshape(TOKENS, D), input_grads.reshape(TOKENS, D), grad_one, grad_qkv, grad_out, grad_gate, grad_up, grad_down, grad_two)
```

```python
import jax
import jax.numpy as jnp
from jax import lax
from jax.experimental import pallas as pl
from jax.experimental.pallas import tpu as pltpu
from jax.sharding import Mesh
from jax.sharding import PartitionSpec as P

HEADS = 32
KV = 4
HD = 64
EPSILON = 1e-05
ROTARY_BASE = 10000.0
MASKED = -1e30

AXES = ("y", "zl", "core", "x", "zh")
SIZES = (4, 2, 2, 4, 2)
BLK = 160
HALF = BLK // 2
ROWS = 4 * BLK
CAP = 2 * ROWS
D = 2048
DH = D // 2
QW = 640
AW = 512
FF4 = 1408
TILE = 256
F32 = jnp.float32
BF16 = jnp.bfloat16
VLIM = 60 * 1024 * 1024


def spec(memory=pltpu.VMEM):
    return pl.BlockSpec(memory_space=memory)


def params(**kw):
    return pltpu.CompilerParams(vmem_limit_bytes=VLIM, **kw)


def cost(flops, nbytes):
    return pl.CostEstimate(flops=int(flops), bytes_accessed=int(nbytes), transcendentals=0)


def sds(shape, dtype=BF16):
    return jax.ShapeDtypeStruct(shape, dtype)


def dot(a, b):
    return jnp.dot(a, b, preferred_element_type=F32)


def dot_t(a, b):
    return lax.dot_general(a, b, (((1,), (1,)), ((), ())), preferred_element_type=F32)


def t_dot(a, b):
    return lax.dot_general(a, b, (((0,), (0,)), ((), ())), preferred_element_type=F32)


def shift(n, s):
    return [(i, (i + s) % n) for i in range(n)]


def gather_x(v):
    from_prev = lax.ppermute(v, "x", shift(4, 1))
    from_next = lax.ppermute(v, "x", shift(4, -1))
    opp_a = lax.ppermute(from_prev[:HALF], "x", shift(4, 1))
    opp_b = lax.ppermute(from_next[HALF:], "x", shift(4, -1))
    return v, from_next, opp_a, opp_b, from_prev


def scatter_x(parts):
    p0, p1, p2a, p2b, p3 = parts
    got_a = lax.ppermute(p2a, "x", shift(4, 1))
    got_b = lax.ppermute(p2b, "x", shift(4, -1))
    q1 = jnp.concatenate([(p1[:HALF].astype(F32) + got_a.astype(F32)).astype(BF16), p1[HALF:]], 0)
    q3 = jnp.concatenate([p3[:HALF], (p3[HALF:].astype(F32) + got_b.astype(F32)).astype(BF16)], 0)
    from_prev = lax.ppermute(q1, "x", shift(4, 1))
    from_next = lax.ppermute(q3, "x", shift(4, -1))
    return p0.astype(F32) + from_prev.astype(F32) + from_next.astype(F32)


PIECES = ((0, BLK), (1, BLK), (2, HALF), (2, HALF), (3, BLK))
PIECE_ROW = (0, BLK, 2 * BLK, 2 * BLK + HALF, 3 * BLK)


def part_shapes(width, dtype=BF16):
    return tuple(sds((n, width), dtype) for _, n in PIECES)


def low_lanes(shape):
    return lax.broadcasted_iota(jnp.int32, shape, 1) < HD


def swap_halves(v):
    lane = lax.broadcasted_iota(jnp.int32, v.shape, 1) % HD
    return jnp.where(lane < HD // 2, pltpu.roll(v, 128 - HD // 2, 1), pltpu.roll(v, HD // 2, 1))


def rows_at(block):
    return pl.ds(pl.multiple_of(block * BLK, 32), BLK)


def qkv_body(idx, n0, n1, n2a, n2b, n3, w_own, w_par, cosine, sine, q_ref, kv_ref):
    x = idx[0]
    lo = low_lanes((BLK, 128))
    for d in range(4):
        if d == 2:
            rows = jnp.concatenate([n2a[...], n2b[...]], 0)
        else:
            rows = (n0, n1, None, n3)[d][...]
        acc = dot(rows[:, :DH], w_own[...]) + dot(rows[:, DH:], w_par[...])
        at = rows_at((x + d) & 3)
        cs = cosine[at, :]
        sn = sine[at, :]
        for p in range(4):
            v = acc[:, p * 128 : (p + 1) * 128]
            v = v * cs + swap_halves(v) * sn
            q_ref[at, p * 128 : (p + 1) * 128] = (v * HD**-0.5).astype(BF16)
        v = acc[:, AW:]
        kv_ref[at, :] = jnp.where(lo, v * cs + swap_halves(v) * sn, v).astype(BF16)


def qkv_forward(idx, pieces, w_own, w_par, cosine, sine):
    return pl.pallas_call(
        qkv_body,
        out_shape=(sds((ROWS, AW)), sds((ROWS, 128))),
        in_specs=[spec(pltpu.SMEM)] + [spec()] * 9,
        out_specs=(spec(), spec()),
        compiler_params=params(),
        cost_estimate=cost(2 * ROWS * D * QW, 7e6),
        name="qkv_forward",
    )(idx, *pieces, w_own, w_par, cosine, sine)


def spread_keys(zh, kv_own, kv_par, kk, vv):
    lo = low_lanes((BLK, 128))
    for j in range(4):
        for src, off in ((kv_own, zh), (kv_par, 1 - zh)):
            v = src[j * BLK : (j + 1) * BLK, :].astype(F32)
            w = pltpu.roll(v, HD, 1)
            at = rows_at(2 * j + off)
            kk[at, :] = jnp.where(lo, v, w).astype(BF16)
            vv[at, :] = jnp.where(lo, w, v).astype(BF16)


def fill_bias(zh, j, n, first, bias):
    t = (2 * j + zh) * BLK + lax.broadcasted_iota(jnp.int32, (BLK, n), 0)
    u = lax.broadcasted_iota(jnp.int32, (BLK, n), 1)
    start = first[j * BLK : (j + 1) * BLK, :]
    value = jnp.where((u <= t) & (u >= start), 0.0, MASKED)
    bias[0:BLK, 0:n] = value
    bias[BLK : 2 * BLK, 0:n] = value


def two_heads(v):
    lo = low_lanes(v.shape)
    zero = jnp.zeros_like(v)
    return jnp.concatenate([jnp.where(lo, v, zero), jnp.where(lo, zero, v)], 0)


def attend_body(idx, q, kv_own, kv_par, first, att, lse_ref, kk, vv, bias):
    x, zh = idx[0], idx[1]
    spread_keys(zh, kv_own, kv_par, kk, vv)
    lo = low_lanes((BLK, 128))
    lane = lax.broadcasted_iota(jnp.int32, (BLK, 128), 1)
    for j in range(4):
        n = 2 * BLK * (j + 1)
        fill_bias(zh, j, n, first, bias)
        rel = (j - x) & 3

        def pair(p, lse):
            cols = pl.ds(pl.multiple_of(p * 128, 128), 128)
            q2 = two_heads(q[j * BLK : (j + 1) * BLK, cols])
            s = dot_t(q2, kk[0:n, :]) + bias[:, 0:n]
            top = jnp.max(s, axis=1, keepdims=True)
            e = jnp.exp(s - top)
            total = jnp.sum(e, axis=1, keepdims=True)
            o = dot(e.astype(BF16), vv[0:n, :]) / total
            att[rel, :, cols] = jnp.where(lo, o[:BLK], o[BLK:]).astype(BF16)
            ls = top + jnp.log(total)
            lse = jnp.where(lane == 2 * p, ls[:BLK], lse)
            return jnp.where(lane == 2 * p + 1, ls[BLK:], lse)

        lse_ref[j * BLK : (j + 1) * BLK, :] = lax.fori_loop(0, 4, pair, jnp.zeros((BLK, 128), F32))


def attend(idx, q, kv_own, kv_par, first):
    return pl.pallas_call(
        attend_body,
        out_shape=(sds((4, BLK, AW)), sds((ROWS, 128), F32)),
        in_specs=[spec(pltpu.SMEM)] + [spec()] * 4,
        out_specs=(spec(), spec()),
        scratch_shapes=[
            pltpu.VMEM((CAP, 128), BF16),
            pltpu.VMEM((CAP, 128), BF16),
            pltpu.VMEM((2 * BLK, CAP), F32),
        ],
        compiler_params=params(),
        cost_estimate=cost(1.2e10, 3e6),
        name="attend",
    )(idx, q, kv_own, kv_par, first)


def ordered(zh, own, par):
    own, par = own[...], par[...]
    return jnp.where(zh == 0, own, par), jnp.where(zh == 0, par, own)


def out_body(idx, att, w_own, w_par, o0, o1, o2a, o2b, o3):
    w_lo, w_hi = ordered(idx[1], w_own, w_par)
    for d, ref in ((2, None), (1, o1), (3, o3), (0, o0)):
        a = att[d]
        res = (dot(a[:, : AW // 2], w_lo) + dot(a[:, AW // 2 :], w_hi)).astype(BF16)
        if d == 2:
            o2a[...] = res[:HALF]
            o2b[...] = res[HALF:]
        else:
            ref[...] = res


def out_project(idx, att, w_own, w_par):
    return pl.pallas_call(
        out_body,
        out_shape=part_shapes(D),
        in_specs=[spec(pltpu.SMEM)] + [spec()] * 3,
        out_specs=(spec(),) * 5,
        compiler_params=params(),
        cost_estimate=cost(2 * ROWS * D * AW, 5.5e6),
        name="out_project",
    )(idx, att, w_own, w_par)


def attend_back_body(
    idx, q, kv_own, kv_par, first, lse_ref, att, b0, b1, b2a, b2b, b3, w_own, w_par,
    dq_ref, dkv_own, dkv_par, kk, vv, bias, dout, dkk, dvv,
):
    x, zh = idx[0], idx[1]
    spread_keys(zh, kv_own, kv_par, kk, vv)
    w_lo, w_hi = ordered(zh, w_own, w_par)
    for d in range(4):
        if d == 2:
            rows = jnp.concatenate([b2a[...], b2b[...]], 0)
        else:
            rows = (b0, b1, None, b3)[d][...]
        at = rows_at((x + d) & 3)
        dout[at, : AW // 2] = dot_t(rows, w_lo).astype(BF16)
        dout[at, AW // 2 :] = dot_t(rows, w_hi).astype(BF16)
    dkk[...] = jnp.zeros_like(dkk)
    dvv[...] = jnp.zeros_like(dvv)
    lo = low_lanes((BLK, 128))
    lane = lax.broadcasted_iota(jnp.int32, (BLK, 128), 1)
    for j in range(4):
        n = 2 * BLK * (j + 1)
        fill_bias(zh, j, n, first, bias)
        rel = (j - x) & 3
        lse_all = lse_ref[j * BLK : (j + 1) * BLK, :]

        def pair(p, carry):
            cols = pl.ds(pl.multiple_of(p * 128, 128), 128)
            q2 = two_heads(q[j * BLK : (j + 1) * BLK, cols])
            do = dout[j * BLK : (j + 1) * BLK, cols]
            do2 = two_heads(do)
            prod = two_heads(do.astype(F32) * att[rel, :, cols].astype(F32))
            delta = jnp.sum(prod, axis=1, keepdims=True)
            ls = jnp.concatenate(
                [
                    jnp.sum(jnp.where(lane == 2 * p, lse_all, 0.0), axis=1, keepdims=True),
                    jnp.sum(jnp.where(lane == 2 * p + 1, lse_all, 0.0), axis=1, keepdims=True),
                ],
                0,
            )
            s = dot_t(q2, kk[0:n, :]) + bias[:, 0:n]
            e = jnp.exp(s - ls)
            dp = dot_t(do2, vv[0:n, :])
            ds = (e * (dp - delta)).astype(BF16)
            dvv[0:n, :] += t_dot(e.astype(BF16), do2)
            dkk[0:n, :] += t_dot(ds, q2)
            dq = dot(ds, kk[0:n, :]) * HD**-0.5
            dq_ref[j * BLK : (j + 1) * BLK, cols] = jnp.where(lo, dq[:BLK], dq[BLK:])
            return carry

        lax.fori_loop(0, 4, pair, 0)
    for j in range(4):
        for dst, off in ((dkv_own, zh), (dkv_par, 1 - zh)):
            at = rows_at(2 * j + off)
            dk, dv = dkk[at, :], dvv[at, :]
            both = jnp.where(lo, dk + pltpu.roll(dk, HD, 1), dv + pltpu.roll(dv, HD, 1))
            dst[j * BLK : (j + 1) * BLK, :] = both.astype(dst.dtype)


def attend_back(idx, q, kv_own, kv_par, first, lse, att, branch, w_own, w_par):
    return pl.pallas_call(
        attend_back_body,
        out_shape=(sds((ROWS, AW), F32), sds((ROWS, 128), F32), sds((ROWS, 128))),
        in_specs=[spec(pltpu.SMEM)] + [spec()] * 13,
        out_specs=(spec(),) * 3,
        scratch_shapes=[
            pltpu.VMEM((CAP, 128), BF16),
            pltpu.VMEM((CAP, 128), BF16),
            pltpu.VMEM((2 * BLK, CAP), F32),
            pltpu.VMEM((ROWS, AW), BF16),
            pltpu.VMEM((CAP, 128), F32),
            pltpu.VMEM((CAP, 128), F32),
        ],
        compiler_params=params(),
        cost_estimate=cost(3e10, 8e6),
        name="attend_back",
    )(idx, q, kv_own, kv_par, first, lse, att, *branch, w_own, w_par)


def qkv_back_body(
    idx, dq, dkv_own, dkv_got, cosine, sine, w_own, w_par, dm_ref, o0, o1, o2a, o2b, o3
):
    x = idx[0]
    lo = low_lanes((BLK, 128))
    for d, ref in ((2, None), (1, o1), (3, o3), (0, o0)):
        at = rows_at((x + d) & 3)
        cs = cosine[at, :]
        sn = sine[at, :]
        mine = pl.ds(d * BLK, BLK)
        for p in range(4):
            v = dq[at, p * 128 : (p + 1) * 128]
            dm_ref[mine, p * 128 : (p + 1) * 128] = (v * cs - swap_halves(v) * sn).astype(BF16)
        v = dkv_own[at, :] + dkv_got[at, :].astype(F32)
        dm_ref[mine, AW:] = jnp.where(lo, v * cs - swap_halves(v) * sn, v).astype(BF16)
        rows = dm_ref[mine, :]
        r_own = dot_t(rows, w_own[...]).astype(BF16)
        r_par = dot_t(rows, w_par[...]).astype(BF16)
        if d == 2:
            o2a[:, :DH], o2b[:, :DH] = r_own[:HALF], r_own[HALF:]
            o2a[:, DH:], o2b[:, DH:] = r_par[:HALF], r_par[HALF:]
        else:
            ref[:, :DH], ref[:, DH:] = r_own, r_par


def qkv_back(idx, dq, dkv_own, dkv_got, cosine, sine, w_own, w_par):
    res = pl.pallas_call(
        qkv_back_body,
        out_shape=(sds((ROWS, QW)),) + part_shapes(D),
        in_specs=[spec(pltpu.SMEM)] + [spec()] * 7,
        out_specs=(spec(),) * 6,
        compiler_params=params(),
        cost_estimate=cost(2 * ROWS * D * QW, 8e6),
        name="qkv_back",
    )(idx, dq, dkv_own, dkv_got, cosine, sine, w_own, w_par)
    return res[0], res[1:]


def ffn_body(
    n0, n1, n2a, n2b, n3, c0, c1, c2a, c2b, c3, g_own, g_par, u_own, u_par, down,
    n_all, c_all, hid, dgate, dup,
):
    @pl.when(pl.program_id(0) == 0)
    def _():
        for refs, dst in (((n0, n1, n2a, n2b, n3), n_all), ((c0, c1, c2a, c2b, c3), c_all)):
            for ref, row, (_, n) in zip(refs, PIECE_ROW, PIECES):
                dst[row : row + n, :] = ref[...]

    gate = dot(n_all[:, :DH], g_own[...]) + dot(n_all[:, DH:], g_par[...])
    up = dot(n_all[:, :DH], u_own[...]) + dot(n_all[:, DH:], u_par[...])
    dh = dot_t(c_all[...], down[...])
    sig = 1.0 / (1.0 + jnp.exp(-gate))
    act = gate * sig
    hid[...] = (act * up).astype(BF16)
    dgate[...] = (dh * up * sig * (1.0 + gate * (1.0 - sig))).astype(BF16)
    dup[...] = (dh * act).astype(BF16)


def ffn(normed, cots, g_own, g_par, u_own, u_par, down):
    whole = lambda n, w: pl.BlockSpec((n, w), lambda i: (0, 0))
    pieces = [whole(n, D) for _, n in PIECES]
    column = pl.BlockSpec((DH, TILE), lambda i: (0, i))
    hidden = pl.BlockSpec((ROWS, TILE), lambda i: (0, i))
    return pl.pallas_call(
        ffn_body,
        grid=(pl.cdiv(FF4, TILE),),
        out_shape=(sds((ROWS, D)),) * 2 + (sds((ROWS, FF4)),) * 3,
        in_specs=pieces * 2 + [column] * 4 + [pl.BlockSpec((TILE, D), lambda i: (i, 0))],
        out_specs=[whole(ROWS, D)] * 2 + [hidden] * 3,
        compiler_params=params(),
        cost_estimate=cost(6 * ROWS * D * FF4, 3.4e7),
        name="ffn",
    )(*normed, *cots, g_own, g_par, u_own, u_par, down)


def store_parts(res, refs):
    for ref, row, (_, n) in zip(refs, PIECE_ROW, PIECES):
        ref[...] = res[row : row + n].astype(BF16)


def part_specs():
    return [pl.BlockSpec((n, TILE), lambda i: (0, i)) for _, n in PIECES]


def down_body(hid, down, *refs):
    store_parts(dot(hid[...], down[...]), refs)


def down_project(hid, down):
    return pl.pallas_call(
        down_body,
        grid=(D // TILE,),
        out_shape=part_shapes(D),
        in_specs=[
            pl.BlockSpec((ROWS, FF4), lambda i: (0, 0)),
            pl.BlockSpec((FF4, TILE), lambda i: (0, i)),
        ],
        out_specs=part_specs(),
        compiler_params=params(),
        cost_estimate=cost(2 * ROWS * D * FF4, 1.1e7),
        name="down_project",
    )(hid, down)


def ffn_back_body(dgate, dup, g_own, g_par, u_own, u_par, *refs):
    half = pl.num_programs(0) // 2

    @pl.when(pl.program_id(0) < half)
    def _():
        store_parts(dot_t(dgate[...], g_own[...]) + dot_t(dup[...], u_own[...]), refs)

    @pl.when(pl.program_id(0) >= half)
    def _():
        store_parts(dot_t(dgate[...], g_par[...]) + dot_t(dup[...], u_par[...]), refs)


def ffn_back(dgate, dup, g_own, g_par, u_own, u_par):
    half = DH // TILE
    all_rows = pl.BlockSpec((ROWS, FF4), lambda i: (0, 0))
    own = pl.BlockSpec((TILE, FF4), lambda i: (jnp.minimum(i, half - 1), 0))
    par = pl.BlockSpec((TILE, FF4), lambda i: (jnp.maximum(i - half, 0), 0))
    return pl.pallas_call(
        ffn_back_body,
        grid=(D // TILE,),
        out_shape=part_shapes(D),
        in_specs=[all_rows, all_rows, own, par, own, par],
        out_specs=part_specs(),
        compiler_params=params(),
        cost_estimate=cost(4 * ROWS * D * FF4, 1.8e7),
        name="ffn_back",
    )(dgate, dup, g_own, g_par, u_own, u_par)


def inverse_rms(v):
    return lax.rsqrt(jnp.mean(v * v, axis=-1, keepdims=True) + EPSILON)


def norm_back(v, r, gain, grad):
    pulled = grad * gain
    inner = jnp.mean(v * pulled, axis=-1, keepdims=True)
    return r * pulled - v * (r * r * r) * inner, jnp.sum(grad * v * r, axis=0)


def replica_layout(lengths, replica, replica_id):
    sizes = jnp.where(replica == replica_id, lengths, 0)
    starts = jnp.cumsum(sizes) - sizes
    row_ids = jnp.arange(CAP, dtype=jnp.int32)
    inside = (row_ids[:, None] >= starts[None, :]) & (row_ids[:, None] < (starts + sizes)[None, :])
    begin = jnp.sum(jnp.where(inside, starts[None, :], 0), axis=1)
    begin = begin + jnp.where(jnp.any(inside, axis=1), 0, jnp.sum(sizes))
    return begin, row_ids - begin


def on_device(
    tokens, cotangent, gain_one, qkv_weight, out_weight, gate_weight, up_weight, down_weight,
    gain_two, seq_lengths, seq_replica,
):
    x, zh, core = lax.axis_index("x"), lax.axis_index("zh"), lax.axis_index("core")
    eighth = lax.axis_index("y") * 2 + core
    idx = jnp.stack([x, zh, core]).astype(jnp.int32)

    def roll_features(v):
        return jnp.where(zh == 0, v, jnp.concatenate([v[..., DH:], v[..., :DH]], -1))

    def partner(w):
        rows = w.shape[0] // 8
        mine = lax.dynamic_slice_in_dim(w, eighth * rows, rows, 0)
        got = lax.ppermute(mine, "zh", shift(2, 1))
        return lax.all_gather(got, ("y", "core"), axis=0, tiled=True)

    def in_order(own, par):
        return jnp.where(
            zh == 0, jnp.concatenate([own, par], 0), jnp.concatenate([par, own], 0)
        )

    def reduce_grad(g):
        rows = g.shape[1]
        part = lax.psum_scatter(
            g.reshape(2 * 2 * 4 * 2, rows // 16 * 2, g.shape[2])[:, : rows // 16 * 2]
            .reshape(2, 8, rows // 8, g.shape[2]),
            ("y", "core"), scatter_dimension=1, tiled=True,
        )
        return part

    qkv_par = partner(qkv_weight)
    tok = tokens.astype(F32)
    s_one = inverse_rms(tok)
    normed_one = gather_x(roll_features((tok * s_one * gain_one).astype(BF16)))
    cots = gather_x(cotangent)

    begin, position = replica_layout(
        seq_lengths, seq_replica,
        (lax.axis_index("y") * 2 + lax.axis_index("zl")) * 2 + core,
    )
    half_rows = lambda v: lax.dynamic_index_in_dim(v.reshape(4, 2, BLK), zh, 1, False).reshape(ROWS, 1)
    first = half_rows(begin)
    lane = jnp.arange(128, dtype=jnp.int32)
    frequency = ROTARY_BASE ** (-(lane % 32).astype(F32) * (2.0 / HD))
    angles = half_rows(position).astype(F32) * frequency[None, :]
    cosine = jnp.cos(angles)
    sine = jnp.where((lane % HD) < HD // 2, -1.0, 1.0)[None, :] * jnp.sin(angles)

    q, kv_own = qkv_forward(idx, normed_one, qkv_weight, qkv_par, cosine, sine)
    kv_par = lax.ppermute(kv_own, "zh", shift(2, 1))
    att, lse = attend(idx, q, kv_own, kv_par, first)
    out_par = partner(out_weight)
    after_attn = tok + scatter_x(out_project(idx, att, out_weight, out_par))

    r_two = inverse_rms(after_attn)
    normed_two = gather_x(roll_features((after_attn * r_two * gain_two).astype(BF16)))
    gate_par, up_par = partner(gate_weight), partner(up_weight)
    down = in_order(down_weight, partner(down_weight))
    n_two, cot_all, hid, dgate, dup = ffn(
        normed_two, cots, gate_weight, gate_par, up_weight, up_par, down
    )
    d_two = roll_features(
        scatter_x(ffn_back(dgate, dup, gate_weight, gate_par, up_weight, up_par))
    )
    layer_out = after_attn + scatter_x(down_project(hid, down))
    back_two, gain_grad_two = norm_back(after_attn, r_two, gain_two, d_two)
    after_grad = cotangent.astype(F32) + back_two
    branch = gather_x(after_grad.astype(BF16))
    dq, dkv_own, dkv_par = attend_back(
        idx, q, kv_own, kv_par, first, lse, att, branch, out_weight, out_par
    )
    dkv_got = lax.ppermute(dkv_par, "zh", shift(2, 1))
    d_mixed, parts = qkv_back(idx, dq, dkv_own, dkv_got, cosine, sine, qkv_weight, qkv_par)
    d_one = roll_features(scatter_x(parts))
    back_one, gain_grad_one = norm_back(tok, s_one, gain_one, d_one)
    input_grad = (after_grad + back_one).astype(BF16)

    n_one = jnp.concatenate(normed_one, 0)
    branch_all = jnp.concatenate(branch, 0)

    def halves(g):
        return jnp.stack([g[: g.shape[0] // 2], g[g.shape[0] // 2 :]]).astype(BF16)

    def finish(g, rolled):
        g = g.astype(BF16)
        rows, columns = g.shape[0] // 2, g.shape[1]
        part = lax.psum_scatter(
            g.reshape(2, 8, rows // 8, columns).swapaxes(0, 1),
            ("y", "core"), scatter_dimension=0, tiled=True,
        ).reshape(2, rows // 8, columns)
        if rolled:
            own, other = part[0], part[1]
        else:
            own, other = jnp.where(zh == 0, part[0], part[1]), jnp.where(zh == 0, part[1], part[0])
        own = own.astype(F32) + lax.ppermute(other, "zh", shift(2, 1)).astype(F32)
        low = own.astype(BF16)
        own = low.astype(F32) + lax.ppermute(low, "zl", shift(2, 1)).astype(F32)
        return lax.all_gather(own.astype(BF16), ("y", "core"), axis=0, tiled=True).astype(F32)

    grad_down = finish(t_dot(hid, cot_all), False)
    grad_gate = finish(t_dot(n_two, dgate), True)
    grad_up = finish(t_dot(n_two, dup), True)
    grad_out = finish(t_dot(att.reshape(ROWS, AW), branch_all), False)
    grad_qkv = finish(t_dot(n_one, d_mixed), True)

    gains = jnp.stack([gain_grad_one, gain_grad_two])
    for axis, n in (("x", 4), ("zh", 2), ("zl", 2), ("y", 4), ("core", 2)):
        gains = gains + sum(lax.ppermute(gains, axis, shift(n, s)) for s in range(1, n))
    return (
        layer_out.astype(BF16), input_grad, gains[0], grad_qkv, grad_out, grad_gate, grad_up,
        grad_down, gains[1],
    )


def solution(mesh):
    grid = Mesh(mesh.devices.reshape(SIZES), AXES)
    rows = P(AXES, None)
    both = P(("x", "zh"), None)
    return jax.shard_map(
        on_device,
        mesh=grid,
        in_specs=(
            rows, rows, P(), P("zh", "x"), both, P("zh", "x"), P("zh", "x"), both, P(), P(), P(),
        ),
        out_specs=(
            rows, rows, P(), P("zh", "x"), both, P("zh", "x"), P("zh", "x"), both, P(),
        ),
        check_vma=False,
    )
```

```python
import jax
import jax.numpy as jnp
from jax import lax
from jax.experimental import pallas as pl
from jax.experimental.pallas import tpu as pltpu
from jax.sharding import Mesh
from jax.sharding import PartitionSpec as P

HEADS = 32
KV = 4
HD = 64
EPSILON = 1e-05
ROTARY_BASE = 10000.0
MASKED = -1e30

AXES = ("y", "zl", "core", "x", "zh")
SIZES = (4, 2, 2, 4, 2)
BLK = 160
HALF = BLK // 2
ROWS = 4 * BLK
CAP = 2 * ROWS
D = 2048
DH = D // 2
QW = 640
AW = 512
FF4 = 1408
TILE = 256
F32 = jnp.float32
BF16 = jnp.bfloat16
VLIM = 60 * 1024 * 1024


def spec(memory=pltpu.VMEM):
    return pl.BlockSpec(memory_space=memory)


def params(**kw):
    return pltpu.CompilerParams(vmem_limit_bytes=VLIM, **kw)


def cost(flops, nbytes):
    return pl.CostEstimate(flops=int(flops), bytes_accessed=int(nbytes), transcendentals=0)


def sds(shape, dtype=BF16):
    return jax.ShapeDtypeStruct(shape, dtype)


def dot(a, b):
    return jnp.dot(a, b, preferred_element_type=F32)


def dot_t(a, b):
    return lax.dot_general(a, b, (((1,), (1,)), ((), ())), preferred_element_type=F32)


def t_dot(a, b):
    return lax.dot_general(a, b, (((0,), (0,)), ((), ())), preferred_element_type=F32)


def tie(v, *deps):
    return lax.optimization_barrier((v,) + deps)[0]


def shift(n, s):
    return [(i, (i + s) % n) for i in range(n)]


def gather_x(v):
    from_prev = lax.ppermute(v, "x", shift(4, 1))
    from_next = lax.ppermute(v, "x", shift(4, -1))
    opp_a = lax.ppermute(from_prev[:HALF], "x", shift(4, 1))
    opp_b = lax.ppermute(from_next[HALF:], "x", shift(4, -1))
    return v, from_next, opp_a, opp_b, from_prev


def gather_direct(v):
    return v, *(lax.ppermute(v, "x", shift(4, -s)) for s in (1, 2, 3))


def scatter_direct(parts):
    got = [lax.ppermute(parts[s], "x", shift(4, s)) for s in (1, 2, 3)]
    return sum((g.astype(F32) for g in got), parts[0].astype(F32))


def scatter_x(parts):
    p0, p1, p2a, p2b, p3 = parts
    got_a = lax.ppermute(p2a, "x", shift(4, 1))
    got_b = lax.ppermute(p2b, "x", shift(4, -1))
    q1 = jnp.concatenate([(p1[:HALF].astype(F32) + got_a.astype(F32)).astype(BF16), p1[HALF:]], 0)
    q3 = jnp.concatenate([p3[:HALF], (p3[HALF:].astype(F32) + got_b.astype(F32)).astype(BF16)], 0)
    from_prev = lax.ppermute(q1, "x", shift(4, 1))
    from_next = lax.ppermute(q3, "x", shift(4, -1))
    return p0.astype(F32) + from_prev.astype(F32) + from_next.astype(F32)


PIECES = ((0, BLK), (1, BLK), (2, HALF), (2, HALF), (3, BLK))
PIECE_ROW = (0, BLK, 2 * BLK, 2 * BLK + HALF, 3 * BLK)


def part_shapes(width, dtype=BF16):
    return tuple(sds((n, width), dtype) for _, n in PIECES)


def low_lanes(shape):
    return lax.broadcasted_iota(jnp.int32, shape, 1) < HD


def swap_halves(v):
    lane = lax.broadcasted_iota(jnp.int32, v.shape, 1) % HD
    return jnp.where(lane < HD // 2, pltpu.roll(v, 128 - HD // 2, 1), pltpu.roll(v, HD // 2, 1))


def rows_at(block):
    return pl.ds(pl.multiple_of(block * BLK, 32), BLK)


def fetch_partner(w, core):
    half = w.shape[0] // 2
    got = lax.ppermute(lax.dynamic_slice_in_dim(w, core * half, half, 0), "zh", shift(2, 1))
    return w, got, lax.ppermute(got, "core", shift(2, 1))


def weight_rows(idx, rows):
    zh, core = idx[1], idx[2]
    far = (1 - zh) * rows
    half = rows // 2
    at = lambda first, n: pl.ds(pl.multiple_of(first, half), n)
    return at(zh * rows, rows), at(far + core * half, half), at(far + (1 - core) * half, half)


def qkv_body(idx, n0, n1, n2a, n2b, n3, w0, w1, w2, cosine, sine, q_ref, kv_ref, rows):
    x = idx[0]
    lo = low_lanes((BLK, 128))
    for ref, row, (_, n) in zip((n0, n1, n2a, n2b, n3), PIECE_ROW, PIECES):
        rows[row : row + n, :] = ref[...]
    s0, s1, s2 = weight_rows(idx, DH)
    acc = dot(rows[:, s0], w0[...]) + dot(rows[:, s1], w1[...]) + dot(rows[:, s2], w2[...])
    for d in range(4):
        at = rows_at((x + d) & 3)
        cs = cosine[at, :]
        sn = sine[at, :]
        for p in range(5):
            v = acc[d * BLK : (d + 1) * BLK, p * 128 : (p + 1) * 128]
            r = v * cs + swap_halves(v) * sn
            if p < 4:
                q_ref[at, p * 128 : (p + 1) * 128] = (r * HD**-0.5).astype(BF16)
            else:
                kv_ref[at, :] = jnp.where(lo, r, v).astype(BF16)


def qkv_forward(idx, pieces, weight, cosine, sine):
    return pl.pallas_call(
        qkv_body,
        out_shape=(sds((ROWS, AW)), sds((ROWS, 128))),
        in_specs=[spec(pltpu.SMEM)] + [spec()] * 10,
        out_specs=(spec(), spec()),
        scratch_shapes=[pltpu.VMEM((ROWS, D), BF16)],
        compiler_params=params(),
        cost_estimate=cost(2 * ROWS * D * QW, 7e6),
        name="qkv_forward",
    )(idx, *pieces, *weight, cosine, sine)


def spread_keys(zh, kv_own, kv_par, kk, vv):
    lo = low_lanes((BLK, 128))
    for j in range(4):
        for src, off in ((kv_own, zh), (kv_par, 1 - zh)):
            v = src[j * BLK : (j + 1) * BLK, :].astype(F32)
            w = pltpu.roll(v, HD, 1)
            at = rows_at(2 * j + off)
            kk[at, :] = jnp.where(lo, v, w).astype(BF16)
            vv[at, :] = jnp.where(lo, w, v).astype(BF16)


def fill_bias(zh, j, n, first, bias):
    t = (2 * j + zh) * BLK + lax.broadcasted_iota(jnp.int32, (BLK, n), 0)
    u = lax.broadcasted_iota(jnp.int32, (BLK, n), 1)
    start = first[j * BLK : (j + 1) * BLK, :]
    value = jnp.where((u <= t) & (u >= start), 0.0, MASKED)
    bias[0:BLK, 0:n] = value
    bias[BLK : 2 * BLK, 0:n] = value


def two_heads(v):
    lo = low_lanes(v.shape)
    zero = jnp.zeros_like(v)
    return jnp.concatenate([jnp.where(lo, v, zero), jnp.where(lo, zero, v)], 0)


def attend_body(idx, q, kv_own, kv_par, first, att, lse_ref, kk, vv, bias):
    x, zh = idx[0], idx[1]
    spread_keys(zh, kv_own, kv_par, kk, vv)
    lo = low_lanes((BLK, 128))
    lane = lax.broadcasted_iota(jnp.int32, (BLK, 128), 1)
    for j in range(4):
        n = 2 * BLK * (j + 1)
        fill_bias(zh, j, n, first, bias)
        rel = (j - x) & 3

        def pair(p, lse):
            cols = pl.ds(pl.multiple_of(p * 128, 128), 128)
            q2 = two_heads(q[j * BLK : (j + 1) * BLK, cols])
            s = dot_t(q2, kk[0:n, :]) + bias[:, 0:n]
            top = jnp.max(s, axis=1, keepdims=True)
            e = jnp.exp(s - top)
            total = jnp.sum(e, axis=1, keepdims=True)
            o = dot(e.astype(BF16), vv[0:n, :]) / total
            att[rel, :, cols] = jnp.where(lo, o[:BLK], o[BLK:]).astype(BF16)
            ls = top + jnp.log(total)
            lse = jnp.where(lane == 2 * p, ls[:BLK], lse)
            return jnp.where(lane == 2 * p + 1, ls[BLK:], lse)

        lse_ref[j * BLK : (j + 1) * BLK, :] = lax.fori_loop(0, 4, pair, jnp.zeros((BLK, 128), F32))


def attend(idx, q, kv_own, kv_par, first):
    return pl.pallas_call(
        attend_body,
        out_shape=(sds((4, BLK, AW)), sds((ROWS, 128), F32)),
        in_specs=[spec(pltpu.SMEM)] + [spec()] * 4,
        out_specs=(spec(), spec()),
        scratch_shapes=[
            pltpu.VMEM((CAP, 128), BF16),
            pltpu.VMEM((CAP, 128), BF16),
            pltpu.VMEM((2 * BLK, CAP), F32),
        ],
        compiler_params=params(),
        cost_estimate=cost(1.2e10, 3e6),
        name="attend",
    )(idx, q, kv_own, kv_par, first)


def out_body(idx, att, w0, w1, w2, o0, o1, o2a, o2b, o3):
    s0, s1, s2 = weight_rows(idx, AW // 2)
    for d, ref in ((2, None), (1, o1), (3, o3), (0, o0)):
        a = att.at[d]
        res = dot(a[:, s0], w0[...]) + dot(a[:, s1], w1[...]) + dot(a[:, s2], w2[...])
        res = res.astype(BF16)
        if d == 2:
            o2a[...] = res[:HALF]
            o2b[...] = res[HALF:]
        else:
            ref[...] = res


def out_project(idx, att, weight):
    return pl.pallas_call(
        out_body,
        out_shape=part_shapes(D),
        in_specs=[spec(pltpu.SMEM)] + [spec()] * 4,
        out_specs=(spec(),) * 5,
        compiler_params=params(),
        cost_estimate=cost(2 * ROWS * D * AW, 5.5e6),
        name="out_project",
    )(idx, att, *weight)


def attend_back_body(
    idx, q, kv_own, kv_par, first, lse_ref, att, b0, b1, b2a, b2b, b3, w0, w1, w2,
    dq_ref, dkv_own, dkv_par, kk, vv, bias, dout, dkk, dvv,
):
    x, zh = idx[0], idx[1]
    spread_keys(zh, kv_own, kv_par, kk, vv)
    s0, s1, s2 = weight_rows(idx, AW // 2)
    for d in range(4):
        if d == 2:
            rows = jnp.concatenate([b2a[...], b2b[...]], 0)
        else:
            rows = (b0, b1, None, b3)[d][...]
        at = rows_at((x + d) & 3)
        for s, w in ((s0, w0), (s1, w1), (s2, w2)):
            dout[at, s] = dot_t(rows, w[...]).astype(BF16)
    dkk[...] = jnp.zeros_like(dkk)
    dvv[...] = jnp.zeros_like(dvv)
    lo = low_lanes((BLK, 128))
    lane = lax.broadcasted_iota(jnp.int32, (BLK, 128), 1)
    for j in range(4):
        n = 2 * BLK * (j + 1)
        fill_bias(zh, j, n, first, bias)
        rel = (j - x) & 3
        lse_all = lse_ref[j * BLK : (j + 1) * BLK, :]

        def pair(p, carry):
            cols = pl.ds(pl.multiple_of(p * 128, 128), 128)
            q2 = two_heads(q[j * BLK : (j + 1) * BLK, cols])
            do = dout[j * BLK : (j + 1) * BLK, cols]
            do2 = two_heads(do)
            prod = two_heads(do.astype(F32) * att[rel, :, cols].astype(F32))
            delta = jnp.sum(prod, axis=1, keepdims=True)
            ls = jnp.concatenate(
                [
                    jnp.sum(jnp.where(lane == 2 * p, lse_all, 0.0), axis=1, keepdims=True),
                    jnp.sum(jnp.where(lane == 2 * p + 1, lse_all, 0.0), axis=1, keepdims=True),
                ],
                0,
            )
            s = dot_t(q2, kk[0:n, :]) + bias[:, 0:n]
            e = jnp.exp(s - ls)
            dp = dot_t(do2, vv[0:n, :])
            ds = (e * (dp - delta)).astype(BF16)
            dvv[0:n, :] += t_dot(e.astype(BF16), do2)
            dkk[0:n, :] += t_dot(ds, q2)
            dq = dot(ds, kk[0:n, :]) * HD**-0.5
            dq_ref[j * BLK : (j + 1) * BLK, cols] = jnp.where(lo, dq[:BLK], dq[BLK:])
            return carry

        lax.fori_loop(0, 4, pair, 0)
    for j in range(4):
        for dst, off in ((dkv_own, zh), (dkv_par, 1 - zh)):
            at = rows_at(2 * j + off)
            dk, dv = dkk[at, :], dvv[at, :]
            both = jnp.where(lo, dk + pltpu.roll(dk, HD, 1), dv + pltpu.roll(dv, HD, 1))
            dst[j * BLK : (j + 1) * BLK, :] = both.astype(dst.dtype)


def attend_back(idx, q, kv_own, kv_par, first, lse, att, branch, weight):
    return pl.pallas_call(
        attend_back_body,
        out_shape=(sds((ROWS, AW), F32), sds((ROWS, 128), F32), sds((ROWS, 128))),
        in_specs=[spec(pltpu.SMEM)] + [spec()] * 14,
        out_specs=(spec(),) * 3,
        scratch_shapes=[
            pltpu.VMEM((CAP, 128), BF16),
            pltpu.VMEM((CAP, 128), BF16),
            pltpu.VMEM((2 * BLK, CAP), F32),
            pltpu.VMEM((ROWS, AW), BF16),
            pltpu.VMEM((CAP, 128), F32),
            pltpu.VMEM((CAP, 128), F32),
        ],
        compiler_params=params(),
        cost_estimate=cost(3e10, 8e6),
        name="attend_back",
    )(idx, q, kv_own, kv_par, first, lse, att, *branch, *weight)


def qkv_back_body(
    idx, dq, dkv_own, dkv_got, cosine, sine, w0, w1, w2, n0, n1, n2a, n2b, n3, gain,
    dm_ref, n_all, gain_ref, o0, o1, o2a, o2b, o3, out,
):
    x = idx[0]
    lo = low_lanes((BLK, 128))
    for ref, row, (_, n) in zip((n0, n1, n2a, n2b, n3), PIECE_ROW, PIECES):
        n_all[row : row + n, :] = ref[...]
    slots = weight_rows(idx, DH)
    total = jnp.zeros((8, D), F32)
    for d, ref in ((2, None), (1, o1), (3, o3), (0, o0)):
        at = rows_at((x + d) & 3)
        cs = cosine[at, :]
        sn = sine[at, :]
        mine = pl.ds(d * BLK, BLK)
        for p in range(4):
            v = dq[at, p * 128 : (p + 1) * 128]
            dm_ref[mine, p * 128 : (p + 1) * 128] = (v * cs - swap_halves(v) * sn).astype(BF16)
        v = dkv_own[at, :] + dkv_got[at, :].astype(F32)
        dm_ref[mine, AW:] = jnp.where(lo, v * cs - swap_halves(v) * sn, v).astype(BF16)
        rows = dm_ref[mine, :]
        for s, w in zip(slots, (w0, w1, w2)):
            out[:, s] = dot_t(rows, w[...])
        res = out[...]
        total = total + jnp.sum((res * n_all[mine, :].astype(F32)).reshape(BLK // 8, 8, D), axis=0)
        res = res.astype(BF16)
        if d == 2:
            o2a[...], o2b[...] = res[:HALF], res[HALF:]
        else:
            ref[...] = res
    gain_ref[...] = jnp.sum(total, axis=0, keepdims=True) / gain[...]


def qkv_back(idx, dq, dkv_own, dkv_got, cosine, sine, weight, pieces, gain):
    res = pl.pallas_call(
        qkv_back_body,
        out_shape=(sds((ROWS, QW)), sds((ROWS, D)), sds((1, D), F32)) + part_shapes(D),
        in_specs=[spec(pltpu.SMEM)] + [spec()] * 14,
        out_specs=(spec(),) * 8,
        scratch_shapes=[pltpu.VMEM((BLK, D), F32)],
        compiler_params=params(),
        cost_estimate=cost(2 * ROWS * D * QW, 1.3e7),
        name="qkv_back",
    )(idx, dq, dkv_own, dkv_got, cosine, sine, *weight, *pieces, gain.reshape(1, D))
    return res[0], res[1], res[2], res[3:]


TILES = 6
FFP = TILES * TILE


def load_down(idx, refs, dst, sem):
    copies = []
    for k, (s, ref) in enumerate(zip(weight_rows(idx, FF4 // 2), refs)):
        copies.append(pltpu.make_async_copy(ref, dst.at[s], sem.at[k]))
    return copies


def ffn_body(
    idx, n0, n1, n2a, n2b, n3, c0, c1, c2, c3, gate_w, up_w, w0, w1, w2,
    n_all, c_all, hid, dgate, dup, down, sem,
):
    i = pl.program_id(0)

    @pl.when(i == 0)
    def _():
        copies = load_down(idx, (w0, w1, w2), down, sem)
        for c in copies:
            c.start()
        down[FF4:, :] = jnp.zeros((FFP - FF4, D), BF16)
        for ref, row, (_, n) in zip((n0, n1, n2a, n2b, n3), PIECE_ROW, PIECES):
            n_all[row : row + n, :] = ref[...]
        for d, ref in enumerate((c0, c1, c2, c3)):
            c_all[d * BLK : (d + 1) * BLK, :] = ref[...]
        for c in copies:
            c.wait()

    gate = dot(n_all[...], gate_w[...])
    up = dot(n_all[...], up_w[...])
    dh = dot_t(c_all[...], down[pl.ds(pl.multiple_of(i * TILE, TILE), TILE), :])
    sig = 1.0 / (1.0 + jnp.exp(-gate))
    act = gate * sig
    hid[...] = (act * up).astype(BF16)
    dgate[...] = (dh * up * sig * (1.0 + gate * (1.0 - sig))).astype(BF16)
    dup[...] = (dh * act).astype(BF16)


def whole(n, w):
    return pl.BlockSpec((n, w), lambda i: (0, 0))


def ffn(idx, normed, cots, gate_up, down):
    column = lambda first: pl.BlockSpec((D, TILE), lambda i: (0, i + first))
    hidden = pl.BlockSpec((ROWS, TILE), lambda i: (0, i))
    return pl.pallas_call(
        ffn_body,
        grid=(TILES,),
        out_shape=(sds((ROWS, D)),) * 2 + (sds((ROWS, FF4)),) + (sds((ROWS, FFP)),) * 2,
        in_specs=[spec(pltpu.SMEM)]
        + [whole(n, D) for _, n in PIECES]
        + [whole(BLK, D)] * 4
        + [column(0), column(TILES)]
        + [spec(pl.ANY)] * 3,
        out_specs=[whole(ROWS, D)] * 2 + [hidden] * 3,
        scratch_shapes=[pltpu.VMEM((FFP, D), BF16), pltpu.SemaphoreType.DMA((3,))],
        compiler_params=params(),
        cost_estimate=cost(6 * ROWS * D * FF4, 3.4e7),
        name="ffn",
    )(idx, *normed, *cots, gate_up, gate_up, *down)


def down_body(idx, hid, w0, w1, w2, o0, o1, o2, o3, down, sem):
    copies = load_down(idx, (w0, w1, w2), down, sem)
    for c in copies:
        c.start()
    for c in copies:
        c.wait()
    for n in range(D // 512):
        cols = slice(n * 512, (n + 1) * 512)
        res = dot(hid[...], down[:, cols]).astype(BF16)
        for d, ref in enumerate((o0, o1, o2, o3)):
            ref[:, cols] = res[d * BLK : (d + 1) * BLK]


def down_project(idx, hid, down):
    return pl.pallas_call(
        down_body,
        out_shape=(sds((BLK, D)),) * 4,
        in_specs=[spec(pltpu.SMEM), spec()] + [spec(pl.ANY)] * 3,
        out_specs=(spec(),) * 4,
        scratch_shapes=[pltpu.VMEM((FF4, D), BF16), pltpu.SemaphoreType.DMA((3,))],
        compiler_params=params(),
        cost_estimate=cost(2 * ROWS * D * FF4, 1.1e7),
        name="down_project",
    )(idx, hid, *down)


def ffn_back_body(dgate, dup, gate_up, *refs):
    res = dot_t(dgate[...], gate_up[:, :FFP]) + dot_t(dup[...], gate_up[:, FFP:])
    for ref, row, (_, n) in zip(refs, PIECE_ROW, PIECES):
        ref[...] = res[row : row + n].astype(BF16)


def ffn_back(dgate, dup, gate_up):
    return pl.pallas_call(
        ffn_back_body,
        grid=(D // TILE,),
        out_shape=part_shapes(D),
        in_specs=[whole(ROWS, FFP)] * 2 + [pl.BlockSpec((TILE, 2 * FFP), lambda i: (i, 0))],
        out_specs=[pl.BlockSpec((n, TILE), lambda i: (0, i)) for _, n in PIECES],
        compiler_params=params(),
        cost_estimate=cost(4 * ROWS * D * FF4, 1.8e7),
        name="ffn_back",
    )(dgate, dup, gate_up)


GU_ROWS = FF4 // 128 * 64
PIECE = 2 * GU_ROWS + FF4 // 2


def ffn_grads_body(na, nb, cot, hid, dgate, dup, out, hid_t):
    @pl.when(pl.program_id(0) == 0)
    def _():
        hid_t[...] = hid[...].T

    rows = jnp.concatenate([na[...], nb[...]], 1).T
    for k, ref in enumerate((dgate, dup)):
        g = dot(rows, ref[:, :FF4]).astype(BF16)
        for h in range(2):
            for q in range(2):
                r = g[(2 * h + q) * 64 : (2 * h + q + 1) * 64]
                for c in range(FF4 // 128):
                    first = k * GU_ROWS + c * 64
                    out[h, q, first : first + 64, :] = r[:, c * 128 : (c + 1) * 128]
    g = dot(hid_t[...], cot[...]).astype(BF16)
    for h in range(2):
        for q in range(2):
            out[h, q, 2 * GU_ROWS :, :] = g[
                h * (FF4 // 2) : (h + 1) * (FF4 // 2), q * 128 : (q + 1) * 128
            ]


def ffn_grads(n_all, c_all, hid, dgate, dup):
    return pl.pallas_call(
        ffn_grads_body,
        grid=(8,),
        out_shape=sds((2, 16, PIECE, 128)),
        in_specs=[
            pl.BlockSpec((ROWS, 128), lambda i: (0, i)),
            pl.BlockSpec((ROWS, 128), lambda i: (0, i + 8)),
            pl.BlockSpec((ROWS, 256), lambda i: (0, i)),
            whole(ROWS, FF4),
            whole(ROWS, FFP),
            whole(ROWS, FFP),
        ],
        out_specs=pl.BlockSpec((2, 2, PIECE, 128), lambda i: (0, i, 0, 0)),
        scratch_shapes=[pltpu.VMEM((FF4, ROWS), BF16)],
        compiler_params=params(),
        cost_estimate=cost(6 * ROWS * D * FF4, 3e7),
        name="ffn_grads",
    )(n_all, n_all, c_all, hid, dgate, dup)


def unpack_body(piece, gate, up, down):
    for k, ref in enumerate((gate, up)):
        for c in range(FF4 // 128):
            first = k * GU_ROWS + c * 64
            ref[:, c * 128 : (c + 1) * 128] = piece[0, first : first + 64, :].astype(F32)
    down[...] = piece[0, 2 * GU_ROWS :, :].astype(F32)


def unpack(pieces):
    return pl.pallas_call(
        unpack_body,
        grid=(16,),
        out_shape=(sds((DH, FF4), F32), sds((DH, FF4), F32), sds((FF4 // 2, D), F32)),
        in_specs=[pl.BlockSpec((1, PIECE, 128), lambda i: (i, 0, 0))],
        out_specs=[
            pl.BlockSpec((64, FF4), lambda i: (i, 0)),
            pl.BlockSpec((64, FF4), lambda i: (i, 0)),
            pl.BlockSpec((FF4 // 2, 128), lambda i: (0, i)),
        ],
        compiler_params=params(),
        cost_estimate=cost(1e6, 2.6e7),
        name="unpack",
    )(pieces)


QP = 5 * 128
OP = 2 * (AW // 2)
TAIL = QP + OP + 16


def attn_grads_body(n_all, dm, att, branch, gain_one, gain_two, out):
    rows = n_all[...].T
    g = dot(rows, dm[...]).astype(BF16)
    for h in range(2):
        for c in range(5):
            out[0, h, c * 128 : (c + 1) * 128, :] = g[h * 128 : (h + 1) * 128, c * 128 : (c + 1) * 128]
    g = dot(att[...].T, branch[...]).astype(BF16)
    gains = [r[:, c * 128 : (c + 1) * 128] for r in (gain_one, gain_two) for c in range(2)]
    gains = jnp.concatenate(gains + [jnp.zeros((12, 128), F32)], 0).astype(BF16)
    for h in range(2):
        for c in range(2):
            first = QP + c * (AW // 2)
            out[0, h, first : first + AW // 2, :] = g[
                h * (AW // 2) : (h + 1) * (AW // 2), c * 128 : (c + 1) * 128
            ]
        out[0, h, QP + OP :, :] = gains


def attn_grads_kernel(na, nb, dm, att, branch, gain_one, gain_two, out, rows):
    rows[:, :128] = na[...]
    rows[:, 128:] = nb[...]
    attn_grads_body(rows, dm, att, branch, gain_one, gain_two, out)


def attn_grads(n_all, dm, att, branch, gain_one, gain_two):
    return pl.pallas_call(
        attn_grads_kernel,
        grid=(8,),
        out_shape=sds((8, 2, TAIL, 128)),
        in_specs=[
            pl.BlockSpec((ROWS, 128), lambda i: (0, i)),
            pl.BlockSpec((ROWS, 128), lambda i: (0, i + 8)),
            whole(ROWS, QW),
            whole(ROWS, AW),
            pl.BlockSpec((ROWS, 256), lambda i: (0, i)),
            pl.BlockSpec((1, 256), lambda i: (0, i)),
            pl.BlockSpec((1, 256), lambda i: (0, i)),
        ],
        out_specs=pl.BlockSpec((1, 2, TAIL, 128), lambda i: (i, 0, 0, 0)),
        scratch_shapes=[pltpu.VMEM((ROWS, 256), BF16)],
        compiler_params=params(),
        cost_estimate=cost(2 * ROWS * D * (QW + AW), 1.5e7),
        name="attn_grads",
    )(n_all, n_all, dm, att, branch, gain_one, gain_two)


def unpack_tail_body(piece, qkv, out, gains):
    for c in range(5):
        qkv[:, c * 128 : (c + 1) * 128] = piece[0, c * 128 : (c + 1) * 128, :].astype(F32)
    for c in range(2):
        first = QP + c * (AW // 2)
        out[:, c * 128 : (c + 1) * 128] = piece[0, first : first + AW // 2, :].astype(F32)
    rows = piece[0, QP + OP :, :].astype(F32)
    for c in range(2):
        gains[0:1, c * 128 : (c + 1) * 128] = rows[c : c + 1]
        gains[1:2, c * 128 : (c + 1) * 128] = rows[2 + c : 3 + c]


def unpack_tail(pieces):
    return pl.pallas_call(
        unpack_tail_body,
        grid=(8,),
        out_shape=(sds((DH, QW), F32), sds((AW // 2, D), F32), sds((2, D), F32)),
        in_specs=[pl.BlockSpec((1, TAIL, 128), lambda i: (i, 0, 0))],
        out_specs=[
            pl.BlockSpec((128, QW), lambda i: (i, 0)),
            pl.BlockSpec((AW // 2, 256), lambda i: (0, i)),
            pl.BlockSpec((2, 256), lambda i: (0, i)),
        ],
        compiler_params=params(),
        cost_estimate=cost(1e6, 7e6),
        name="unpack_tail",
    )(pieces)


def bf_sum(*values):
    return sum((v.astype(F32) for v in values[1:]), values[0].astype(F32)).astype(BF16)


def sum_tail(g, y, zl, zh, core):
    g = g.reshape(4, 2, 2, TAIL, 128)
    pick = lambda v, i, axis: lax.dynamic_index_in_dim(v, i, axis, False)
    g = bf_sum(pick(g, core, 1), lax.ppermute(pick(g, 1 - core, 1), "core", shift(2, 1)))
    got = [lax.ppermute(pick(g, (y + s) % 4, 0), "y", shift(4, s)) for s in (1, 2, 3)]
    g = bf_sum(pick(g, y, 0), *got)
    own, other = pick(g, zh, 0), pick(g, 1 - zh, 0)
    cross = [(2 * a + b, 2 * (1 - a) + (1 - b)) for a in range(2) for b in range(2)]
    g = bf_sum(
        own,
        lax.ppermute(own, "zl", shift(2, 1)),
        lax.ppermute(other, "zh", shift(2, 1)),
        lax.ppermute(other, ("zl", "zh"), cross),
    )
    parts = jnp.stack([g] + [lax.ppermute(g, "y", shift(4, s)) for s in (1, 2, 3)])
    other = lax.ppermute(parts, "core", shift(2, 1))
    both = jnp.where(core == 0, jnp.stack([parts, other], 1), jnp.stack([other, parts], 1))
    both = jnp.take(both, (y - jnp.arange(4)) % 4, axis=0)
    return both.reshape(8, TAIL, 128)


def inverse_rms(v):
    return lax.rsqrt(jnp.mean(v * v, axis=-1, keepdims=True) + EPSILON)


def norm_back(v, r, gain, grad):
    pulled = grad * gain
    inner = jnp.mean(v * pulled, axis=-1, keepdims=True)
    return r * pulled - v * (r * r * r) * inner, jnp.sum(grad * v * r, axis=0)


def replica_layout(lengths, replica, replica_id):
    sizes = jnp.where(replica == replica_id, lengths, 0)
    starts = jnp.cumsum(sizes) - sizes
    row_ids = jnp.arange(CAP, dtype=jnp.int32)
    inside = (row_ids[:, None] >= starts[None, :]) & (row_ids[:, None] < (starts + sizes)[None, :])
    begin = jnp.sum(jnp.where(inside, starts[None, :], 0), axis=1)
    begin = begin + jnp.where(jnp.any(inside, axis=1), 0, jnp.sum(sizes))
    return begin, row_ids - begin


def on_device(
    tokens, cotangent, gain_one, qkv_weight, out_weight, gate_weight, up_weight, down_weight,
    gain_two, seq_lengths, seq_replica,
):
    x, zh, core = lax.axis_index("x"), lax.axis_index("zh"), lax.axis_index("core")
    y, zl = lax.axis_index("y"), lax.axis_index("zl")
    idx = jnp.stack([x, zh, core]).astype(jnp.int32)

    tok = tokens.astype(F32)
    s_one = inverse_rms(tok)
    normed_one = gather_x((tok * s_one * gain_one).astype(BF16))
    qkv_all = fetch_partner(qkv_weight, core)
    out_all = fetch_partner(tie(out_weight, qkv_all[1]), core)
    down_all = fetch_partner(tie(down_weight, out_all[1]), core)
    rows = DH // 8
    mine = lambda w: jnp.pad(
        lax.dynamic_slice_in_dim(w, (y * 2 + core) * rows, rows, 0), ((0, 0), (0, FFP - FF4))
    )
    gate_up = lax.all_gather(
        jnp.concatenate([mine(gate_weight), mine(up_weight)], 1), ("zh", "y", "core"), axis=0, tiled=True
    )
    cots = gather_direct(tie(cotangent, normed_one[2]))

    begin, position = replica_layout(seq_lengths, seq_replica, (y * 2 + zl) * 2 + core)
    half_rows = lambda v: lax.dynamic_index_in_dim(v.reshape(4, 2, BLK), zh, 1, False).reshape(ROWS, 1)
    first = half_rows(begin)
    lane = jnp.arange(128, dtype=jnp.int32)
    frequency = ROTARY_BASE ** (-(lane % 32).astype(F32) * (2.0 / HD))
    angles = half_rows(position).astype(F32) * frequency[None, :]
    cosine = jnp.cos(angles)
    sine = jnp.where((lane % HD) < HD // 2, -1.0, 1.0)[None, :] * jnp.sin(angles)

    q, kv_own = qkv_forward(idx, normed_one, qkv_all, cosine, sine)
    kv_par = lax.ppermute(kv_own, "zh", shift(2, 1))
    att, lse = attend(idx, q, kv_own, kv_par, first)
    att = tie(att, down_all[1], *cots)
    after_attn = tok + scatter_x(out_project(idx, att, out_all))

    r_two = inverse_rms(after_attn)
    normed_two = gather_x((after_attn * r_two * gain_two).astype(BF16))
    n_two, cot_all, hid, dgate, dup = ffn(idx, normed_two, cots, gate_up, down_all)
    grads = ffn_grads(n_two, cot_all, hid, dgate, dup)
    grads = lax.psum_scatter(
        grads.reshape(32, PIECE, 128), ("zh", "zl", "y", "core"), scatter_dimension=0, tiled=True
    )
    grads = lax.all_gather(grads, ("zl", "y", "core"), axis=0, tiled=True)
    grad_gate, grad_up, grad_down = unpack(grads)

    d_two = scatter_x(ffn_back(dgate, dup, gate_up))
    back_two, gain_grad_two = norm_back(after_attn, r_two, gain_two, d_two)
    after_grad = cotangent.astype(F32) + back_two
    branch = gather_x(after_grad.astype(BF16))
    layer_parts = down_project(idx, tie(hid, after_grad), down_all)
    layer_parts = [tie(p, branch[2], branch[3]) for p in layer_parts]
    layer_out = after_attn + scatter_direct(layer_parts)
    att = tie(att, *layer_parts)
    dq, dkv_own, dkv_par = attend_back(idx, q, kv_own, kv_par, first, lse, att, branch, out_all)
    dkv_got = lax.ppermute(dkv_par, "zh", shift(2, 1))
    layer_out = layer_out.astype(BF16)
    d_mixed, n_one, gain_grad_one, parts = qkv_back(
        idx, tie(dq, layer_out), dkv_own, dkv_got, cosine, sine, qkv_all, normed_one, gain_one
    )
    d_one = scatter_x(parts)
    back_one, _ = norm_back(tok, s_one, gain_one, d_one)
    input_grad = (after_grad + back_one).astype(BF16)

    over_x = lambda v: sum((lax.ppermute(v, "x", shift(4, s)) for s in (1, 2, 3)), v)
    tail = attn_grads(
        n_one, d_mixed, att.reshape(ROWS, AW), jnp.concatenate(branch, 0),
        gain_grad_one, gain_grad_two.reshape(1, D),
    )
    grad_qkv, grad_out, gains = unpack_tail(sum_tail(tail, y, zl, zh, core))
    gains = over_x(gains)
    return (
        layer_out, input_grad, gains[0], grad_qkv, grad_out, grad_gate, grad_up,
        grad_down, gains[1],
    )


def solution(mesh):
    grid = Mesh(mesh.devices.reshape(SIZES), AXES)
    rows = P(AXES, None)
    both = P(("x", "zh"), None)
    return jax.shard_map(
        on_device,
        mesh=grid,
        in_specs=(
            rows, rows, P(), P("zh", "x"), both, P("zh", "x"), P("zh", "x"), both, P(), P(), P(),
        ),
        out_specs=(
            rows, rows, P(), P("zh", "x"), both, P("zh", "x"), P("zh", "x"), both, P(),
        ),
        check_vma=False,
    )
```

```python
import jax
import jax.numpy as jnp
from jax import lax
from jax.experimental import pallas as pl
from jax.experimental.pallas import tpu as pltpu
from jax.sharding import Mesh
from jax.sharding import PartitionSpec as P

HEADS = 32
KV = 4
HD = 64
EPSILON = 1e-05
ROTARY_BASE = 10000.0
MASKED = -1e30

AXES = ("y", "zl", "core", "x", "zh")
SIZES = (4, 2, 2, 4, 2)
BLK = 160
HALF = BLK // 2
ROWS = 4 * BLK
CAP = 2 * ROWS
D = 2048
DH = D // 2
QW = 640
AW = 512
FF4 = 1408
TILE = 256
F32 = jnp.float32
BF16 = jnp.bfloat16
VLIM = 60 * 1024 * 1024


def spec(memory=pltpu.VMEM):
    return pl.BlockSpec(memory_space=memory)


def params(**kw):
    return pltpu.CompilerParams(vmem_limit_bytes=VLIM, **kw)


def cost(flops, nbytes):
    return pl.CostEstimate(flops=int(flops), bytes_accessed=int(nbytes), transcendentals=0)


def sds(shape, dtype=BF16):
    return jax.ShapeDtypeStruct(shape, dtype)


def dot(a, b):
    return jnp.dot(a, b, preferred_element_type=F32)


def dot_t(a, b):
    return lax.dot_general(a, b, (((1,), (1,)), ((), ())), preferred_element_type=F32)


def t_dot(a, b):
    return lax.dot_general(a, b, (((0,), (0,)), ((), ())), preferred_element_type=F32)


def tie(v, *deps):
    return lax.optimization_barrier((v,) + deps)[0]


def shift(n, s):
    return [(i, (i + s) % n) for i in range(n)]


def gather_x(v, *deps):
    from_prev = lax.ppermute(v, "x", shift(4, 1))
    from_next = lax.ppermute(v, "x", shift(4, -1))
    send_a, send_b = tie(from_prev[:HALF], *deps), tie(from_next[HALF:], *deps)
    opp_a = lax.ppermute(send_a, "x", shift(4, 1))
    opp_b = lax.ppermute(send_b, "x", shift(4, -1))
    return (v, from_next, opp_a, opp_b, from_prev), (send_a, send_b)


def gather_direct(v):
    return v, *(lax.ppermute(v, "x", shift(4, -s)) for s in (1, 2, 3))


def scatter_direct(parts):
    got = [lax.ppermute(parts[s], "x", shift(4, s)) for s in (1, 2, 3)]
    return sum((g.astype(F32) for g in got), parts[0].astype(F32))


def scatter_x(parts):
    p0, p1, p2a, p2b, p3 = parts
    got_a = lax.ppermute(p2a, "x", shift(4, 1))
    got_b = lax.ppermute(p2b, "x", shift(4, -1))
    q1 = jnp.concatenate([(p1[:HALF].astype(F32) + got_a.astype(F32)).astype(BF16), p1[HALF:]], 0)
    q3 = jnp.concatenate([p3[:HALF], (p3[HALF:].astype(F32) + got_b.astype(F32)).astype(BF16)], 0)
    from_prev = lax.ppermute(q1, "x", shift(4, 1))
    from_next = lax.ppermute(q3, "x", shift(4, -1))
    return p0.astype(F32) + from_prev.astype(F32) + from_next.astype(F32)


PIECES = ((0, BLK), (1, BLK), (2, HALF), (2, HALF), (3, BLK))
PIECE_ROW = (0, BLK, 2 * BLK, 2 * BLK + HALF, 3 * BLK)


def part_shapes(width, dtype=BF16):
    return tuple(sds((n, width), dtype) for _, n in PIECES)


def low_lanes(shape):
    return lax.broadcasted_iota(jnp.int32, shape, 1) < HD


def swap_halves(v):
    lane = lax.broadcasted_iota(jnp.int32, v.shape, 1) % HD
    return jnp.where(lane < HD // 2, pltpu.roll(v, 128 - HD // 2, 1), pltpu.roll(v, HD // 2, 1))


def rows_at(block):
    return pl.ds(pl.multiple_of(block * BLK, 32), BLK)


def fetch_half(w, core):
    half = w.shape[0] // 2
    return lax.ppermute(lax.dynamic_slice_in_dim(w, core * half, half, 0), "zh", shift(2, 1))


def fetch_partner(w, core, *deps):
    got = fetch_half(tie(w, *deps), core)
    return w, got, lax.ppermute(got, "core", shift(2, 1))


def weight_rows(idx, rows):
    zh, core = idx[1], idx[3]
    far = (1 - zh) * rows
    half = rows // 2
    at = lambda first, n: pl.ds(pl.multiple_of(first, half), n)
    return at(zh * rows, rows), at(far + core * half, half), at(far + (1 - core) * half, half)


def qkv_body(idx, n0, n1, n2a, n2b, n3, w0, w1, w2, cosine, sine, q_ref, kv_ref, rows):
    x = idx[0]
    lo = low_lanes((BLK, 128))
    for ref, row, (_, n) in zip((n0, n1, n2a, n2b, n3), PIECE_ROW, PIECES):
        rows[row : row + n, :] = ref[...]
    s0, s1, s2 = weight_rows(idx, DH)
    acc = dot(rows[:, s0], w0[...]) + dot(rows[:, s1], w1[...]) + dot(rows[:, s2], w2[...])
    for d in range(4):
        at = rows_at((x + d) & 3)
        cs = cosine[at, :]
        sn = sine[at, :]
        for p in range(5):
            v = acc[d * BLK : (d + 1) * BLK, p * 128 : (p + 1) * 128]
            r = v * cs + swap_halves(v) * sn
            if p < 4:
                q_ref[at, p * 128 : (p + 1) * 128] = (r * HD**-0.5).astype(BF16)
            else:
                kv_ref[at, :] = jnp.where(lo, r, v).astype(BF16)


def qkv_forward(idx, pieces, weight, cosine, sine):
    return pl.pallas_call(
        qkv_body,
        out_shape=(sds((ROWS, AW)), sds((ROWS, 128))),
        in_specs=[spec(pltpu.SMEM)] + [spec()] * 10,
        out_specs=(spec(), spec()),
        scratch_shapes=[pltpu.VMEM((ROWS, D), BF16)],
        compiler_params=params(),
        cost_estimate=cost(2 * ROWS * D * QW, 7e6),
        name="qkv_forward",
    )(idx, *pieces, *weight, cosine, sine)


def spread_keys(zh, kv_own, kv_par, kk, vv):
    lo = low_lanes((BLK, 128))
    for j in range(4):
        for src, off in ((kv_own, zh), (kv_par, 1 - zh)):
            v = src[j * BLK : (j + 1) * BLK, :].astype(F32)
            w = pltpu.roll(v, HD, 1)
            at = rows_at(2 * j + off)
            kk[at, :] = jnp.where(lo, v, w).astype(BF16)
            vv[at, :] = jnp.where(lo, w, v).astype(BF16)


def fill_bias(zh, j, n, first, bias):
    t = (2 * j + zh) * BLK + lax.broadcasted_iota(jnp.int32, (BLK, n), 0)
    u = lax.broadcasted_iota(jnp.int32, (BLK, n), 1)
    start = first[j * BLK : (j + 1) * BLK, :]
    value = jnp.where((u <= t) & (u >= start), 0.0, MASKED)
    bias[0:BLK, 0:n] = value
    bias[BLK : 2 * BLK, 0:n] = value


def two_heads(v):
    lo = low_lanes(v.shape)
    zero = jnp.zeros_like(v)
    return jnp.concatenate([jnp.where(lo, v, zero), jnp.where(lo, zero, v)], 0)


def attend_body(idx, q, kv_own, kv_par, first, att, lse_ref, kk, vv, bias):
    x, zh = idx[0], idx[1]
    spread_keys(zh, kv_own, kv_par, kk, vv)
    lo = low_lanes((BLK, 128))
    lane = lax.broadcasted_iota(jnp.int32, (BLK, 128), 1)
    for j in range(4):
        n = 2 * BLK * (j + 1)
        fill_bias(zh, j, n, first, bias)
        rel = (j - x) & 3

        def pair(p, lse):
            cols = pl.ds(pl.multiple_of(p * 128, 128), 128)
            q2 = two_heads(q[j * BLK : (j + 1) * BLK, cols])
            s = dot_t(q2, kk[0:n, :]) + bias[:, 0:n]
            top = jnp.max(s, axis=1, keepdims=True)
            e = jnp.exp(s - top)
            total = jnp.sum(e, axis=1, keepdims=True)
            o = dot(e.astype(BF16), vv[0:n, :]) / total
            att[rel, :, cols] = jnp.where(lo, o[:BLK], o[BLK:]).astype(BF16)
            ls = top + jnp.log(total)
            lse = jnp.where(lane == 2 * p, ls[:BLK], lse)
            return jnp.where(lane == 2 * p + 1, ls[BLK:], lse)

        lse_ref[j * BLK : (j + 1) * BLK, :] = lax.fori_loop(0, 4, pair, jnp.zeros((BLK, 128), F32))


def attend(idx, q, kv_own, kv_par, first):
    return pl.pallas_call(
        attend_body,
        out_shape=(sds((4, BLK, AW)), sds((ROWS, 128), F32)),
        in_specs=[spec(pltpu.SMEM)] + [spec()] * 4,
        out_specs=(spec(), spec()),
        scratch_shapes=[
            pltpu.VMEM((CAP, 128), BF16),
            pltpu.VMEM((CAP, 128), BF16),
            pltpu.VMEM((2 * BLK, CAP), F32),
        ],
        compiler_params=params(),
        cost_estimate=cost(1.2e10, 3e6),
        name="attend",
    )(idx, q, kv_own, kv_par, first)


def out_body(idx, att, w0, w1, w2, o0, o1, o2a, o2b, o3):
    s0, s1, s2 = weight_rows(idx, AW // 2)
    for d, ref in ((2, None), (1, o1), (3, o3), (0, o0)):
        a = att.at[d]
        res = dot(a[:, s0], w0[...]) + dot(a[:, s1], w1[...]) + dot(a[:, s2], w2[...])
        res = res.astype(BF16)
        if d == 2:
            o2a[...] = res[:HALF]
            o2b[...] = res[HALF:]
        else:
            ref[...] = res


def out_project(idx, att, weight):
    return pl.pallas_call(
        out_body,
        out_shape=part_shapes(D),
        in_specs=[spec(pltpu.SMEM)] + [spec()] * 4,
        out_specs=(spec(),) * 5,
        compiler_params=params(),
        cost_estimate=cost(2 * ROWS * D * AW, 5.5e6),
        name="out_project",
    )(idx, att, *weight)


def attend_back_body(
    idx, q, kv_own, kv_par, first, lse_ref, att, cosine, sine, b0, b1, b2a, b2b, b3, w0, w1, w2,
    dq_ref, dkv_own, dkv_par, kk, vv, bias, dout, dkk, dvv,
):
    x, zh = idx[0], idx[1]
    spread_keys(zh, kv_own, kv_par, kk, vv)
    s0, s1, s2 = weight_rows(idx, AW // 2)
    for d in range(4):
        if d == 2:
            rows = jnp.concatenate([b2a[...], b2b[...]], 0)
        else:
            rows = (b0, b1, None, b3)[d][...]
        at = rows_at((x + d) & 3)
        for s, w in ((s0, w0), (s1, w1), (s2, w2)):
            dout[at, s] = dot_t(rows, w[...]).astype(BF16)
    dkk[...] = jnp.zeros_like(dkk)
    dvv[...] = jnp.zeros_like(dvv)
    lo = low_lanes((BLK, 128))
    lane = lax.broadcasted_iota(jnp.int32, (BLK, 128), 1)
    for j in range(4):
        n = 2 * BLK * (j + 1)
        fill_bias(zh, j, n, first, bias)
        rel = (j - x) & 3
        lse_all = lse_ref[j * BLK : (j + 1) * BLK, :]

        def pair(p, carry):
            cols = pl.ds(pl.multiple_of(p * 128, 128), 128)
            q2 = two_heads(q[j * BLK : (j + 1) * BLK, cols])
            do = dout[j * BLK : (j + 1) * BLK, cols]
            do2 = two_heads(do)
            prod = two_heads(do.astype(F32) * att[rel, :, cols].astype(F32))
            delta = jnp.sum(prod, axis=1, keepdims=True)
            ls = jnp.concatenate(
                [
                    jnp.sum(jnp.where(lane == 2 * p, lse_all, 0.0), axis=1, keepdims=True),
                    jnp.sum(jnp.where(lane == 2 * p + 1, lse_all, 0.0), axis=1, keepdims=True),
                ],
                0,
            )
            s = dot_t(q2, kk[0:n, :]) + bias[:, 0:n]
            e = jnp.exp(s - ls)
            dp = dot_t(do2, vv[0:n, :])
            ds = (e * (dp - delta)).astype(BF16)
            dvv[0:n, :] += t_dot(e.astype(BF16), do2)
            dkk[0:n, :] += t_dot(ds, q2)
            dq = dot(ds, kk[0:n, :]) * HD**-0.5
            v = jnp.where(lo, dq[:BLK], dq[BLK:])
            here = slice(j * BLK, (j + 1) * BLK)
            dq_ref[rel, :, cols] = (v * cosine[here, :] - swap_halves(v) * sine[here, :]).astype(BF16)
            return carry

        lax.fori_loop(0, 4, pair, 0)
    for j in range(4):
        for dst, off in ((dkv_own, zh), (dkv_par, 1 - zh)):
            at = rows_at(2 * j + off)
            dk, dv = dkk[at, :], dvv[at, :]
            both = jnp.where(lo, dk + pltpu.roll(dk, HD, 1), dv + pltpu.roll(dv, HD, 1))
            dst[j * BLK : (j + 1) * BLK, :] = both.astype(dst.dtype)


def attend_back(idx, q, kv_own, kv_par, first, lse, att, cosine, sine, branch, weight):
    return pl.pallas_call(
        attend_back_body,
        out_shape=(sds((4, BLK, AW)), sds((ROWS, 128), F32), sds((ROWS, 128))),
        in_specs=[spec(pltpu.SMEM)] + [spec()] * 16,
        out_specs=(spec(),) * 3,
        scratch_shapes=[
            pltpu.VMEM((CAP, 128), BF16),
            pltpu.VMEM((CAP, 128), BF16),
            pltpu.VMEM((2 * BLK, CAP), F32),
            pltpu.VMEM((ROWS, AW), BF16),
            pltpu.VMEM((CAP, 128), F32),
            pltpu.VMEM((CAP, 128), F32),
        ],
        compiler_params=params(),
        cost_estimate=cost(3e10, 8e6),
        name="attend_back",
    )(idx, q, kv_own, kv_par, first, lse, att, cosine, sine, *branch, *weight)


def qkv_back_body(
    idx, dqm, dkv_own, dkv_got, cosine, sine, w0, w1, w2, n0, n1, n2a, n2b, n3, gain_one, gain_grad_two,
    mine, theirs, o0, o1, o2a, o2b, o3, n_all, dkv, out, grad, gains,
):
    x, y, core = idx[0], idx[2], idx[3]
    lo = low_lanes((BLK, 128))
    for ref, row, (_, n) in zip((n0, n1, n2a, n2b, n3), PIECE_ROW, PIECES):
        n_all[row : row + n, :] = ref[...]
    slots = weight_rows(idx, DH)
    total = jnp.zeros((8, D), F32)
    for d, ref in ((2, None), (1, o1), (3, o3), (0, o0)):
        at = rows_at((x + d) & 3)
        v = dkv_own[at, :] + dkv_got[at, :].astype(F32)
        v = jnp.where(lo, v * cosine[at, :] - swap_halves(v) * sine[at, :], v).astype(BF16)
        here = slice(d * BLK, (d + 1) * BLK)
        dkv[here, :] = v
        rows = jnp.concatenate([dqm[d], v], 1)
        for s, w in zip(slots, (w0, w1, w2)):
            out[:, s] = dot_t(rows, w[...])
        res = out[...]
        total = total + jnp.sum((res * n_all[here, :].astype(F32)).reshape(BLK // 8, 8, D), axis=0)
        res = res.astype(BF16)
        if d == 2:
            o2a[...], o2b[...] = res[:HALF], res[HALF:]
        else:
            ref[...] = res
    grad[...] = dot(dkv[...].T, n_all[...]).astype(BF16)
    gains[0:1, :] = jnp.sum(total, axis=0, keepdims=True) / gain_one[...]
    gains[1:2, :] = gain_grad_two[...]
    for s in range(4):
        for k, ref in enumerate((mine, theirs)):
            p = ((y + s) & 3) * 2 + (core if k == 0 else 1 - core)
            both = gains[:, pl.ds(pl.multiple_of(p * 256, 256), 256)]
            both = jnp.concatenate([both[:, :128], both[:, 128:], jnp.zeros((12, 128), F32)], 0)
            for h in range(2):
                ref[s, h, :128, :] = grad[:, pl.ds(pl.multiple_of(h * DH + p * 128, 128), 128)]
                ref[s, h, 128:, :] = both.astype(BF16)


def qkv_back(idx, dqm, dkv_own, dkv_got, cosine, sine, weight, pieces, gain_one, gain_grad_two):
    res = pl.pallas_call(
        qkv_back_body,
        out_shape=(sds((4, 2, KVP, 128)),) * 2 + part_shapes(D),
        in_specs=[spec(pltpu.SMEM)] + [spec()] * 15,
        out_specs=(spec(),) * 7,
        scratch_shapes=[
            pltpu.VMEM((ROWS, D), BF16),
            pltpu.VMEM((ROWS, 128), BF16),
            pltpu.VMEM((BLK, D), F32),
            pltpu.VMEM((128, D), BF16),
            pltpu.VMEM((2, D), F32),
        ],
        compiler_params=params(),
        cost_estimate=cost(2 * ROWS * D * QW, 1.3e7),
        name="qkv_back",
    )(
        idx, dqm, dkv_own, dkv_got, cosine, sine, *weight, *pieces,
        gain_one.reshape(1, D), gain_grad_two.reshape(1, D),
    )
    return res[0], res[1], res[2:]


TILES = 6
GAP = TILES * TILE


def load_down(idx, refs, dst, sem):
    copies = []
    for k, (s, ref) in enumerate(zip(weight_rows(idx, FF4 // 2), refs)):
        copies.append(pltpu.make_async_copy(ref, dst.at[s], sem.at[k]))
    return copies


def ffn_body(
    idx, n0, n1, n2a, n2b, n3, c0, c1, c2, c3, gate_own, up_own, gate_par, up_par, w0, w1, w2,
    hid, dgate, dup, n_all, c_all, down, sem,
):
    i = pl.program_id(0)
    zh = idx[1]

    @pl.when(i == 0)
    def _():
        copies = load_down(idx, (w0, w1, w2), down, sem)
        for c in copies:
            c.start()
        for ref, row, (_, n) in zip((n0, n1, n2a, n2b, n3), PIECE_ROW, PIECES):
            n_all[row : row + n, :] = ref[...]
        for d, ref in enumerate((c0, c1, c2, c3)):
            c_all[d * BLK : (d + 1) * BLK, :] = ref[...]
        for c in copies:
            c.wait()

    own = n_all[:, pl.ds(pl.multiple_of(zh * DH, DH), DH)]
    par = n_all[:, pl.ds(pl.multiple_of((1 - zh) * DH, DH), DH)]
    gate = dot(own, gate_own[...]) + dot(par, gate_par[...])
    up = dot(own, up_own[...]) + dot(par, up_par[...])
    dh = dot_t(c_all[...], down[pl.ds(pl.multiple_of(i * TILE, TILE), TILE), :])
    sig = 1.0 / (1.0 + jnp.exp(-gate))
    act = gate * sig
    hid[...] = (act * up).astype(BF16)
    dgate[...] = (dh * up * sig * (1.0 + gate * (1.0 - sig))).astype(BF16)
    dup[...] = (dh * act).astype(BF16)


def whole(n, w):
    return pl.BlockSpec((n, w), lambda i: (0, 0))


def ffn(idx, normed, cots, gate, up, gate_up, down):
    column = lambda first: pl.BlockSpec((DH, TILE), lambda i: (0, i + first))
    hidden = pl.BlockSpec((ROWS, TILE), lambda i: (0, i))
    return pl.pallas_call(
        ffn_body,
        grid=(TILES,),
        out_shape=(sds((ROWS, FF4)),) * 3,
        in_specs=[spec(pltpu.SMEM)]
        + [whole(n, D) for _, n in PIECES]
        + [whole(BLK, D)] * 4
        + [column(0), column(0), column(0), column(TILES)]
        + [spec(pl.ANY)] * 3,
        out_specs=[hidden] * 3,
        scratch_shapes=[
            pltpu.VMEM((ROWS, D), BF16),
            pltpu.VMEM((ROWS, D), BF16),
            pltpu.VMEM((GAP, D), BF16),
            pltpu.SemaphoreType.DMA((3,)),
        ],
        compiler_params=params(),
        cost_estimate=cost(6 * ROWS * D * FF4, 3.4e7),
        name="ffn",
    )(idx, *normed, *cots, gate, up, gate_up, gate_up, *down)


def down_body(idx, hid, w0, w1, w2, o0, o1, o2, o3, down, sem):
    copies = load_down(idx, (w0, w1, w2), down, sem)
    for c in copies:
        c.start()
    for c in copies:
        c.wait()
    for n in range(D // 512):
        cols = slice(n * 512, (n + 1) * 512)
        res = dot(hid[...], down[:, cols]).astype(BF16)
        for d, ref in enumerate((o0, o1, o2, o3)):
            ref[:, cols] = res[d * BLK : (d + 1) * BLK]


def down_project(idx, hid, down):
    return pl.pallas_call(
        down_body,
        out_shape=(sds((BLK, D)),) * 4,
        in_specs=[spec(pltpu.SMEM), spec()] + [spec(pl.ANY)] * 3,
        out_specs=(spec(),) * 4,
        scratch_shapes=[pltpu.VMEM((FF4, D), BF16), pltpu.SemaphoreType.DMA((3,))],
        compiler_params=params(),
        cost_estimate=cost(2 * ROWS * D * FF4, 1.1e7),
        name="down_project",
    )(idx, hid, *down)


def ffn_back_body(idx, dgate, dup, gate_own, up_own, par, *refs):
    half = pl.num_programs(0) // 2

    def store(res):
        for ref, row, (_, n) in zip(refs, PIECE_ROW, PIECES):
            ref[...] = res[row : row + n].astype(BF16)

    @pl.when(pl.program_id(0) < half)
    def _():
        store(dot_t(dgate[...], gate_own[...]) + dot_t(dup[...], up_own[...]))

    @pl.when(pl.program_id(0) >= half)
    def _():
        store(dot_t(dgate[...], par[:, :FF4]) + dot_t(dup[...], par[:, GAP:]))


def ffn_back(idx, dgate, dup, gate, up, gate_up):
    half = DH // TILE
    rows = pl.BlockSpec((ROWS, FF4), lambda i, idx: (0, 0))
    own = pl.BlockSpec((TILE, FF4), lambda i, idx: (jnp.minimum(i, half - 1), 0))
    par = pl.BlockSpec((TILE, GAP + FF4), lambda i, idx: (jnp.maximum(i - half, 0), 0))
    place = lambda i, idx: (0, i ^ (idx[1] * half))
    return pl.pallas_call(
        ffn_back_body,
        grid_spec=pltpu.PrefetchScalarGridSpec(
            num_scalar_prefetch=1,
            grid=(D // TILE,),
            in_specs=[rows, rows, own, own, par],
            out_specs=[pl.BlockSpec((n, TILE), place) for _, n in PIECES],
        ),
        out_shape=part_shapes(D),
        compiler_params=params(),
        cost_estimate=cost(4 * ROWS * D * FF4, 1.8e7),
        name="ffn_back",
    )(idx, dgate, dup, gate, up, gate_up)


GU_ROWS = FF4 // 128 * 64
PIECE = 2 * GU_ROWS + FF4 // 2


def ffn_grads_body(*refs):
    na, nb, cots = refs[0:5], refs[5:10], refs[10:14]
    hid, dgate, dup, out, hid_t = refs[14:]

    @pl.when(pl.program_id(0) == 0)
    def _():
        hid_t[...] = hid[...].T

    stack = lambda parts: jnp.concatenate([r[...] for r in parts], 0)
    rows = jnp.concatenate([stack(na), stack(nb)], 1).T
    for k, ref in enumerate((dgate, dup)):
        g = dot(rows, ref[...]).astype(BF16)
        for h in range(2):
            for q in range(2):
                r = g[(2 * h + q) * 64 : (2 * h + q + 1) * 64]
                for c in range(FF4 // 128):
                    first = k * GU_ROWS + c * 64
                    out[h, q, first : first + 64, :] = r[:, c * 128 : (c + 1) * 128]
    g = dot(hid_t[...], stack(cots)).astype(BF16)
    for h in range(2):
        for q in range(2):
            out[h, q, 2 * GU_ROWS :, :] = g[
                h * (FF4 // 2) : (h + 1) * (FF4 // 2), q * 128 : (q + 1) * 128
            ]


def ffn_grads(normed, cots, hid, dgate, dup):
    return pl.pallas_call(
        ffn_grads_body,
        grid=(8,),
        out_shape=sds((2, 16, PIECE, 128)),
        in_specs=[pl.BlockSpec((n, 128), lambda i: (0, i)) for _, n in PIECES]
        + [pl.BlockSpec((n, 128), lambda i: (0, i + 8)) for _, n in PIECES]
        + [pl.BlockSpec((BLK, 256), lambda i: (0, i))] * 4
        + [whole(ROWS, FF4)] * 3,
        out_specs=pl.BlockSpec((2, 2, PIECE, 128), lambda i: (0, i, 0, 0)),
        scratch_shapes=[pltpu.VMEM((FF4, ROWS), BF16)],
        compiler_params=params(),
        cost_estimate=cost(6 * ROWS * D * FF4, 3e7),
        name="ffn_grads",
    )(*normed, *normed, *cots, hid, dgate, dup)


def unpack_body(piece, gate, up, down):
    for k, ref in enumerate((gate, up)):
        for c in range(FF4 // 128):
            first = k * GU_ROWS + c * 64
            ref[:, c * 128 : (c + 1) * 128] = piece[0, first : first + 64, :].astype(F32)
    down[...] = piece[0, 2 * GU_ROWS :, :].astype(F32)


def unpack(pieces):
    return pl.pallas_call(
        unpack_body,
        grid=(16,),
        out_shape=(sds((DH, FF4), F32), sds((DH, FF4), F32), sds((FF4 // 2, D), F32)),
        in_specs=[pl.BlockSpec((1, PIECE, 128), lambda i: (i, 0, 0))],
        out_specs=[
            pl.BlockSpec((64, FF4), lambda i: (i, 0)),
            pl.BlockSpec((64, FF4), lambda i: (i, 0)),
            pl.BlockSpec((FF4 // 2, 128), lambda i: (0, i)),
        ],
        compiler_params=params(),
        cost_estimate=cost(1e6, 2.6e7),
        name="unpack",
    )(pieces)


QP = 4 * 128
OP = 2 * (AW // 2)
QOP = QP + OP
KVP = 128 + 16
TAIL = QOP + KVP


def attn_grads_body(idx, *refs):
    na, nb, branch = refs[0:5], refs[5:10], refs[10:15]
    dqm, att, mine, theirs, att_t = refs[15:]
    core = idx[3]

    @pl.when(pl.program_id(0) == 0)
    def _():
        att_t[...] = att[...].T

    stack = lambda parts: jnp.concatenate([r[...] for r in parts], 0)

    def store(h, first, n, zero, one):
        mine[0, h, first : first + n, :] = jnp.where(core == 0, zero, one)
        theirs[0, h, first : first + n, :] = jnp.where(core == 0, one, zero)

    for h, cols in enumerate((na, nb)):
        g = dot(stack(cols).T, dqm[...]).astype(BF16)
        for c in range(4):
            lanes = slice(c * 128, (c + 1) * 128)
            store(h, c * 128, 128, g[:128, lanes], g[128:, lanes])
    g = dot(att_t[...], stack(branch)).astype(BF16)
    for h in range(2):
        r = g[h * (AW // 2) : (h + 1) * (AW // 2)]
        for c in range(2):
            lanes = lambda k: slice(k * 256 + c * 128, k * 256 + (c + 1) * 128)
            store(h, QP + c * (AW // 2), AW // 2, r[:, lanes(0)], r[:, lanes(1)])


def attn_grads(idx, normed, branch, dqm, att):
    turn = lambda s, idx: (s + idx[2]) & 3
    piece = pl.BlockSpec((1, 2, QOP, 128), lambda s, idx: (s, 0, 0, 0))
    fixed = pl.BlockSpec((ROWS, AW), lambda s, idx: (0, 0))
    return pl.pallas_call(
        attn_grads_body,
        grid_spec=pltpu.PrefetchScalarGridSpec(
            num_scalar_prefetch=1,
            grid=(4,),
            in_specs=[pl.BlockSpec((n, 256), lambda s, idx: (0, turn(s, idx))) for _, n in PIECES]
            + [pl.BlockSpec((n, 256), lambda s, idx: (0, turn(s, idx) + 4)) for _, n in PIECES]
            + [pl.BlockSpec((n, 512), lambda s, idx: (0, turn(s, idx))) for _, n in PIECES]
            + [fixed, fixed],
            out_specs=[piece, piece],
            scratch_shapes=[pltpu.VMEM((AW, ROWS), BF16)],
        ),
        out_shape=(sds((4, 2, QOP, 128)),) * 2,
        compiler_params=params(),
        cost_estimate=cost(4 * ROWS * D * AW, 1e7),
        name="attn_grads",
    )(idx, *normed, *normed, *branch, dqm, att)


def small_call(body, out_shape, *args, name):
    return pl.pallas_call(
        body,
        out_shape=out_shape,
        in_specs=[spec(pltpu.SMEM)] + [spec()] * (len(args) - 1),
        out_specs=jax.tree.map(lambda _: spec(), out_shape),
        compiler_params=params(),
        cost_estimate=cost(1e6, 4e6),
        name=name,
    )(*args)


def add(*values):
    return sum((v.astype(F32) for v in values[1:]), values[0].astype(F32)).astype(BF16)


def sum_core_body(idx, a, b, c, d, *outs):
    for s, out in enumerate(outs):
        out[:, :QOP, :] = add(a[s], b[s])
        out[:, QOP:, :] = add(c[s], d[s])


def sum_y_body(idx, a, b, c, d, own, other):
    zh = idx[1]
    own[...] = add(a[zh], b[zh], c[zh], d[zh])
    far = 1 - zh
    other[...] = add(a[far], b[far], c[far], d[far])


def sum_z_body(idx, a, b, c, d, out):
    out[...] = add(a[...], b[...], c[...], d[...])


def unpack_tail_body(idx, *refs):
    y, core = idx[2], idx[3]
    qkv, out, gains = refs[8:]
    for k in range(8):
        piece = refs[k]
        p = ((y - k % 4) & 3) * 2 + (core if k < 4 else 1 - core)
        rows = pl.ds(pl.multiple_of(p * 128, 128), 128)
        for c in range(4):
            qkv[rows, c * 128 : (c + 1) * 128] = piece[c * 128 : (c + 1) * 128, :].astype(F32)
        qkv[rows, AW:] = piece[QOP : QOP + 128, :].astype(F32).T
        g = piece[QOP + 128 :, :].astype(F32)
        for c in range(2):
            first = QP + c * (AW // 2)
            cols = pl.ds(pl.multiple_of(p * 256 + c * 128, 128), 128)
            out[:, cols] = piece[first : first + AW // 2, :].astype(F32)
            gains[:, cols] = g[2 * c : 2 * c + 2]


def sum_tail(idx, first, second):
    got_a = lax.ppermute(first[1], "core", shift(2, 1))
    got_b = lax.ppermute(second[1], "core", shift(2, 1))
    part = sds((2, TAIL, 128))
    g = small_call(sum_core_body, (part,) * 4, idx, first[0], got_a, second[0], got_b, name="sum_core")
    got = [lax.ppermute(g[s], "y", shift(4, s)) for s in (2, 1, 3)]
    part = sds((TAIL, 128))
    own, other = small_call(sum_y_body, (part,) * 2, idx, g[0], *got, name="sum_y")
    cross = [(2 * a + b, 2 * (1 - a) + (1 - b)) for a in range(2) for b in range(2)]
    g = small_call(
        sum_z_body,
        part,
        idx,
        own,
        lax.ppermute(own, "zl", shift(2, 1)),
        lax.ppermute(other, "zh", shift(2, 1)),
        lax.ppermute(other, ("zl", "zh"), cross),
        name="sum_z",
    )
    mine = [g] + [lax.ppermute(g, "y", shift(4, s)) for s in (1, 2, 3)]
    theirs = [lax.ppermute(v, "core", shift(2, 1)) for v in mine]
    shapes = (sds((DH, QW), F32), sds((AW // 2, D), F32), sds((2, D), F32))
    return small_call(unpack_tail_body, shapes, idx, *mine, *theirs, name="unpack_tail")


def inverse_rms(v):
    return lax.rsqrt(jnp.mean(v * v, axis=-1, keepdims=True) + EPSILON)


def norm_back(v, r, gain, grad):
    pulled = grad * gain
    inner = jnp.mean(v * pulled, axis=-1, keepdims=True)
    return r * pulled - v * (r * r * r) * inner, jnp.sum(grad * v * r, axis=0)


def replica_layout(lengths, replica, replica_id):
    sizes = jnp.where(replica == replica_id, lengths, 0)
    starts = jnp.cumsum(sizes) - sizes
    row_ids = jnp.arange(CAP, dtype=jnp.int32)
    inside = (row_ids[:, None] >= starts[None, :]) & (row_ids[:, None] < (starts + sizes)[None, :])
    begin = jnp.sum(jnp.where(inside, starts[None, :], 0), axis=1)
    begin = begin + jnp.where(jnp.any(inside, axis=1), 0, jnp.sum(sizes))
    return begin, row_ids - begin


def on_device(
    tokens, cotangent, gain_one, qkv_weight, out_weight, gate_weight, up_weight, down_weight,
    gain_two, seq_lengths, seq_replica,
):
    x, zh, core = lax.axis_index("x"), lax.axis_index("zh"), lax.axis_index("core")
    y, zl = lax.axis_index("y"), lax.axis_index("zl")
    idx = jnp.stack([x, zh, y, core]).astype(jnp.int32)

    tok = tokens.astype(F32)
    s_one = inverse_rms(tok)
    qkv_got = fetch_half(qkv_weight, core)
    normed_one, sent = gather_x((tok * s_one * gain_one).astype(BF16), qkv_got)
    qkv_all = qkv_weight, qkv_got, lax.ppermute(tie(qkv_got, *sent), "core", shift(2, 1))
    rows = DH // 8
    mine = lambda w: lax.dynamic_slice_in_dim(w, (y * 2 + core) * rows, rows, 0)
    cross = [(2 * a + b, 2 * (1 - a) + (1 - b)) for a in range(2) for b in range(2)]
    gate_up = lax.ppermute(
        jnp.concatenate(
            [
                tie(mine(gate_weight), normed_one[2]),
                jnp.zeros((rows, GAP - FF4), BF16),
                mine(up_weight),
            ],
            1,
        ),
        ("zl", "zh"),
        cross,
    )
    out_all = fetch_partner(out_weight, core, *sent)
    gate_up = lax.all_gather(gate_up, ("y", "core"), axis=0, tiled=True)
    cots = gather_direct(tie(cotangent, normed_one[2]))

    begin, position = replica_layout(seq_lengths, seq_replica, (y * 2 + zl) * 2 + core)
    half_rows = lambda v: lax.dynamic_index_in_dim(v.reshape(4, 2, BLK), zh, 1, False).reshape(ROWS, 1)
    first = half_rows(begin)
    lane = jnp.arange(128, dtype=jnp.int32)
    frequency = ROTARY_BASE ** (-(lane % 32).astype(F32) * (2.0 / HD))
    angles = half_rows(position).astype(F32) * frequency[None, :]
    cosine = jnp.cos(angles)
    sine = jnp.where((lane % HD) < HD // 2, -1.0, 1.0)[None, :] * jnp.sin(angles)

    q, kv_own = qkv_forward(idx, normed_one, qkv_all, cosine, sine)
    kv_par = lax.ppermute(kv_own, "zh", shift(2, 1))
    down_all = fetch_partner(down_weight, core, kv_par)
    att, lse = attend(idx, q, kv_own, kv_par, first)
    att = tie(att, *cots)
    after_attn = tok + scatter_x(out_project(idx, att, out_all))

    r_two = inverse_rms(after_attn)
    normed_two, _ = gather_x((after_attn * r_two * gain_two).astype(BF16))
    hid, dgate, dup = ffn(idx, normed_two, cots, gate_weight, up_weight, gate_up, down_all)
    own_grads = ffn_grads(normed_two, cots, hid, dgate, dup)
    grads = lax.psum_scatter(
        own_grads.reshape(32, PIECE, 128), ("zh", "zl", "y", "core"), scatter_dimension=0, tiled=True
    )
    d_two = scatter_x(ffn_back(idx, tie(dgate, own_grads), dup, gate_weight, up_weight, gate_up))
    back_two, gain_grad_two = norm_back(after_attn, r_two, gain_two, d_two)
    after_grad = cotangent.astype(F32) + back_two
    branch, _ = gather_x(after_grad.astype(BF16))
    layer_parts = down_project(idx, tie(hid, after_grad), down_all)
    layer_parts = [tie(p, branch[2], branch[3]) for p in layer_parts]
    layer_out = after_attn + scatter_direct(layer_parts)
    att = tie(att, *layer_parts)
    dqm, dkv_own, dkv_par = attend_back(
        idx, q, kv_own, kv_par, first, lse, att, cosine, sine, branch, out_all
    )
    dkv_got = lax.ppermute(dkv_par, "zh", shift(2, 1))
    tail = attn_grads(idx, normed_one, branch, dqm.reshape(ROWS, AW), att.reshape(ROWS, AW))
    layer_out = layer_out.astype(BF16)
    *tail_kv, parts = qkv_back(
        idx, dqm, tie(dkv_own, layer_out), dkv_got, cosine, sine, qkv_all, normed_one, gain_one,
        gain_grad_two,
    )
    grads = lax.all_gather(tie(grads, dkv_got), ("zl", "y", "core"), axis=0, tiled=True)
    grad_gate, grad_up, grad_down = unpack(grads)
    d_one = scatter_x(parts)
    back_one, _ = norm_back(tok, s_one, gain_one, d_one)
    input_grad = (after_grad + back_one).astype(BF16)

    over_x = lambda v: sum((lax.ppermute(v, "x", shift(4, s)) for s in (1, 2, 3)), v)
    grad_qkv, grad_out, gains = sum_tail(idx, tail, tail_kv)
    gains = over_x(gains)
    return (
        layer_out, input_grad, gains[0], grad_qkv, grad_out, grad_gate, grad_up,
        grad_down, gains[1],
    )


def solution(mesh):
    grid = Mesh(mesh.devices.reshape(SIZES), AXES)
    rows = P(AXES, None)
    both = P(("x", "zh"), None)
    return jax.shard_map(
        on_device,
        mesh=grid,
        in_specs=(
            rows, rows, P(), P("zh", "x"), both, P("zh", "x"), P("zh", "x"), both, P(), P(), P(),
        ),
        out_specs=(
            rows, rows, P(), P("zh", "x"), both, P("zh", "x"), P("zh", "x"), both, P(),
        ),
        check_vma=False,
    )
```

```python
import jax
import jax.numpy as jnp
from jax import lax
from jax.experimental import pallas as pl
from jax.experimental.pallas import tpu as pltpu
from jax.sharding import Mesh
from jax.sharding import PartitionSpec as P

HEADS = 32
KV = 4
HD = 64
EPSILON = 1e-05
ROTARY_BASE = 10000.0
MASKED = -1e30

AXES = ("y", "zl", "core", "x", "zh")
SIZES = (4, 2, 2, 4, 2)
BLK = 160
HALF = BLK // 2
ROWS = 4 * BLK
CAP = 2 * ROWS
D = 2048
DH = D // 2
QW = 640
AW = 512
FF4 = 1408
TILE = 256
F32 = jnp.float32
BF16 = jnp.bfloat16
VLIM = 60 * 1024 * 1024


def spec(memory=pltpu.VMEM):
    return pl.BlockSpec(memory_space=memory)


def params(**kw):
    return pltpu.CompilerParams(vmem_limit_bytes=VLIM, **kw)


def cost(flops, nbytes):
    return pl.CostEstimate(flops=int(flops), bytes_accessed=int(nbytes), transcendentals=0)


def sds(shape, dtype=BF16):
    return jax.ShapeDtypeStruct(shape, dtype)


def dot(a, b):
    return jnp.dot(a, b, preferred_element_type=F32)


def dot_t(a, b):
    return lax.dot_general(a, b, (((1,), (1,)), ((), ())), preferred_element_type=F32)


def t_dot(a, b):
    return lax.dot_general(a, b, (((0,), (0,)), ((), ())), preferred_element_type=F32)


def tie(v, *deps):
    return lax.optimization_barrier((v,) + deps)[0]


def shift(n, s):
    return [(i, (i + s) % n) for i in range(n)]


def gather_x(v, *deps):
    from_prev = lax.ppermute(v, "x", shift(4, 1))
    from_next = lax.ppermute(v, "x", shift(4, -1))
    send_a = tie(from_prev[:HALF], from_next, *deps)
    send_b = tie(from_next[HALF:], from_prev, *deps)
    opp_a = lax.ppermute(send_a, "x", shift(4, 1))
    opp_b = lax.ppermute(send_b, "x", shift(4, -1))
    return (v, from_next, opp_a, opp_b, from_prev), (send_a, send_b)


def gather_direct(v):
    return v, *(lax.ppermute(v, "x", shift(4, -s)) for s in (1, 2, 3))


def scatter_direct(parts):
    got = [lax.ppermute(parts[s], "x", shift(4, s)) for s in (1, 2, 3)]
    return sum((g.astype(F32) for g in got), parts[0].astype(F32))


def scatter_x(parts):
    p0, p1, p2a, p2b, p3 = parts
    got_a = lax.ppermute(p2a, "x", shift(4, 1))
    got_b = lax.ppermute(p2b, "x", shift(4, -1))
    q1 = jnp.concatenate([(p1[:HALF].astype(F32) + got_a.astype(F32)).astype(BF16), p1[HALF:]], 0)
    q3 = jnp.concatenate([p3[:HALF], (p3[HALF:].astype(F32) + got_b.astype(F32)).astype(BF16)], 0)
    from_prev = lax.ppermute(q1, "x", shift(4, 1))
    from_next = lax.ppermute(q3, "x", shift(4, -1))
    return p0.astype(F32) + from_prev.astype(F32) + from_next.astype(F32)


PIECES = ((0, BLK), (1, BLK), (2, HALF), (2, HALF), (3, BLK))
PIECE_ROW = (0, BLK, 2 * BLK, 2 * BLK + HALF, 3 * BLK)


def part_shapes(width, dtype=BF16):
    return tuple(sds((n, width), dtype) for _, n in PIECES)


def low_lanes(shape):
    return lax.broadcasted_iota(jnp.int32, shape, 1) < HD


def swap_halves(v):
    lane = lax.broadcasted_iota(jnp.int32, v.shape, 1) % HD
    return jnp.where(lane < HD // 2, pltpu.roll(v, 128 - HD // 2, 1), pltpu.roll(v, HD // 2, 1))


def rows_at(block):
    return pl.ds(pl.multiple_of(block * BLK, 32), BLK)


def fetch_half(w, core):
    half = w.shape[0] // 2
    return lax.ppermute(lax.dynamic_slice_in_dim(w, core * half, half, 0), "zh", shift(2, 1))


def fetch_partner(w, core, *deps):
    got = fetch_half(tie(w, *deps), core)
    return w, got, lax.ppermute(got, "core", shift(2, 1))


def weight_rows(idx, rows):
    zh, core = idx[1], idx[3]
    far = (1 - zh) * rows
    half = rows // 2
    at = lambda first, n: pl.ds(pl.multiple_of(first, half), n)
    return at(zh * rows, rows), at(far + core * half, half), at(far + (1 - core) * half, half)


def qkv_body(idx, n0, n1, n2a, n2b, n3, w0, w1, w2, cosine, sine, q_ref, kv_ref, rows):
    x = idx[0]
    lo = low_lanes((BLK, 128))
    for ref, row, (_, n) in zip((n0, n1, n2a, n2b, n3), PIECE_ROW, PIECES):
        rows[row : row + n, :] = ref[...]
    s0, s1, s2 = weight_rows(idx, DH)
    acc = dot(rows[:, s0], w0[...]) + dot(rows[:, s1], w1[...]) + dot(rows[:, s2], w2[...])
    for d in range(4):
        at = rows_at((x + d) & 3)
        cs = cosine[at, :]
        sn = sine[at, :]
        for p in range(5):
            v = acc[d * BLK : (d + 1) * BLK, p * 128 : (p + 1) * 128]
            r = v * cs + swap_halves(v) * sn
            if p < 4:
                r = r * (HD**-0.5 * LOG2E)
                a = (x + d) & 3
                for k, w in enumerate((r, pltpu.roll(r, HD, 1))):
                    head = slice((2 * p + k) * BLK, (2 * p + k + 1) * BLK)
                    q_ref[a, head, :] = jnp.where(lo, w, 0.0).astype(BF16)
            else:
                kv_ref[at, :] = jnp.where(lo, r, v).astype(BF16)


def qkv_forward(idx, pieces, weight, cosine, sine):
    return pl.pallas_call(
        qkv_body,
        out_shape=(sds((4, QALL, 128)), sds((ROWS, 128))),
        in_specs=[spec(pltpu.SMEM)] + [spec()] * 10,
        out_specs=(spec(), spec()),
        scratch_shapes=[pltpu.VMEM((ROWS, D), BF16)],
        compiler_params=params(),
        cost_estimate=cost(2 * ROWS * D * QW, 7e6),
        name="qkv_forward",
    )(idx, *pieces, *weight, cosine, sine)


QALL = 8 * BLK
PAIR = 2 * BLK
LOG2E = 1.4426950408889634
LN2 = 0.6931471805599453


def split3(v):
    a = v.astype(BF16).astype(F32)
    b = (v - a).astype(BF16).astype(F32)
    return a, b, v - a - b


def with_lanes(v, parts):
    lane = lax.broadcasted_iota(jnp.int32, v.shape, 1)
    out = jnp.where(lane < HD, v, 0.0)
    for k, part in enumerate(parts):
        out = jnp.where(lane == HD + k, part, out)
    return out


def spread_keys(zh, kv_own, kv_par, kk, vv, fill):
    shape = (BLK, 128)
    lo = low_lanes(shape)
    rest = fill(lax.broadcasted_iota(jnp.int32, shape, 1) - HD)
    for j in range(4):
        for src, off in ((kv_own, zh), (kv_par, 1 - zh)):
            v = src[j * BLK : (j + 1) * BLK, :].astype(F32)
            at = rows_at(2 * j + off)
            kk[at, :] = jnp.where(lo, v, rest).astype(BF16)
            vv[at, :] = jnp.where(lo, pltpu.roll(v, HD, 1), rest).astype(BF16)


def masked(s, zh, j, kb, first):
    if j < 3 and kb < j:
        return s
    u = kb * PAIR + lax.broadcasted_iota(jnp.int32, (PAIR, QALL), 0)
    allowed = None
    if kb == j:
        t = (2 * j + zh) * BLK + lax.broadcasted_iota(jnp.int32, (1, QALL), 1) % BLK
        allowed = u <= t
    if j == 3:
        later = u >= first[...]
        allowed = later if allowed is None else allowed & later
    return jnp.where(allowed, s, MASKED)


def attend_body(idx, q, kv_own, kv_par, first, att, qx, kk, vv, vt, s_ref, e_ref):
    x, zh = idx[0], idx[1]
    spread_keys(zh, kv_own, kv_par, kk, vv, lambda lane: 1.0)
    vt[...] = vv[...].T
    lo = low_lanes((BLK, 128))
    for j in range(4):
        n = PAIR * (j + 1)
        qj = q[j]
        top = jnp.full((1, QALL), MASKED, F32)
        for kb in range(j + 1):
            rows = slice(kb * PAIR, (kb + 1) * PAIR)
            s = masked(dot_t(kk[rows, :], qj), zh, j, kb, first)
            s_ref[rows, :] = s
            top = jnp.maximum(top, jnp.max(s, axis=0, keepdims=True))
        for k in range(n // 64):
            rows = slice(k * 64, (k + 1) * 64)
            e_ref[rows, :] = jnp.exp2(s_ref[rows, :] - top).astype(BF16)
        o = dot(vt[:, :n], e_ref[:n, :])
        lse = split3(top + jnp.log(o[HD : HD + 1, :]) * LOG2E)
        row = lax.broadcasted_iota(jnp.int32, (128, QALL), 0)
        extra = jnp.zeros((128, QALL), F32)
        for k, part in enumerate(lse):
            extra = jnp.where(row == HD + k, part, extra)
        qx[j] = (qj.astype(F32) + extra.T).astype(BF16)
        o = o.T
        r = pltpu.roll(o, HD, 1)
        rel = (j - x) & 3
        for p in range(4):
            even, odd = slice(2 * p * BLK, (2 * p + 1) * BLK), slice((2 * p + 1) * BLK, (2 * p + 2) * BLK)
            num = jnp.where(lo, o[even], r[odd])
            den = jnp.where(lo, r[even], o[odd])
            att[rel, :, p * 128 : (p + 1) * 128] = (num / den).astype(BF16)


def attend(idx, q, kv_own, kv_par, first):
    return pl.pallas_call(
        attend_body,
        out_shape=(sds((4, BLK, AW)), sds((4, QALL, 128))),
        in_specs=[spec(pltpu.SMEM)] + [spec()] * 4,
        out_specs=(spec(), spec()),
        scratch_shapes=[
            pltpu.VMEM((CAP, 128), BF16),
            pltpu.VMEM((CAP, 128), BF16),
            pltpu.VMEM((128, CAP), BF16),
            pltpu.VMEM((CAP, QALL), F32),
            pltpu.VMEM((CAP, QALL), BF16),
        ],
        compiler_params=params(),
        cost_estimate=cost(1.2e10, 3e6),
        name="attend",
    )(idx, q, kv_own, kv_par, first)


def out_body(idx, att, w0, w1, w2, o0, o1, o2a, o2b, o3):
    s0, s1, s2 = weight_rows(idx, AW // 2)
    for d, ref in ((2, None), (1, o1), (3, o3), (0, o0)):
        a = att.at[d]
        res = dot(a[:, s0], w0[...]) + dot(a[:, s1], w1[...]) + dot(a[:, s2], w2[...])
        res = res.astype(BF16)
        if d == 2:
            o2a[...] = res[:HALF]
            o2b[...] = res[HALF:]
        else:
            ref[...] = res


def out_project(idx, att, weight):
    return pl.pallas_call(
        out_body,
        out_shape=part_shapes(D),
        in_specs=[spec(pltpu.SMEM)] + [spec()] * 4,
        out_specs=(spec(),) * 5,
        compiler_params=params(),
        cost_estimate=cost(2 * ROWS * D * AW, 5.5e6),
        name="out_project",
    )(idx, att, *weight)


def stack_heads(v):
    return v, pltpu.roll(v, HD, 1)


def attend_back_body(
    idx, qx, kv_own, kv_par, first, att, cosine, sine, b0, b1, b2a, b2b, b3, w0, w1, w2,
    dq_ref, dkv_own, dkv_par, kk, vv, dout, do_all, dkk, dvv, e_ref, ds_ref, dq_acc,
):
    x, zh = idx[0], idx[1]
    spread_keys(zh, kv_own, kv_par, kk, vv, lambda lane: jnp.where(lane < 3, -1.0, 0.0))
    s0, s1, s2 = weight_rows(idx, AW // 2)
    for d in range(4):
        if d == 2:
            rows = jnp.concatenate([b2a[...], b2b[...]], 0)
        else:
            rows = (b0, b1, None, b3)[d][...]
        at = rows_at((x + d) & 3)
        for s, w in ((s0, w0), (s1, w1), (s2, w2)):
            dout[at, s] = dot_t(rows, w[...]).astype(BF16)
    lo = low_lanes((BLK, 128))
    for j in range(4):
        rel = (j - x) & 3
        here = slice(j * BLK, (j + 1) * BLK)
        for p in range(4):
            cols = slice(p * 128, (p + 1) * 128)
            do = dout[here, cols].astype(F32)
            prod = do * att[rel, :, cols].astype(F32)
            for k, (v, w) in enumerate(zip(stack_heads(do), stack_heads(prod))):
                delta = jnp.sum(jnp.where(lo, w, 0.0), axis=1, keepdims=True)
                head = slice((2 * p + k) * BLK, (2 * p + k + 1) * BLK)
                do_all[head, :] = with_lanes(v, split3(delta)).astype(BF16)
        for kb in range(j + 1):
            rows = slice(kb * PAIR, (kb + 1) * PAIR)
            e = jnp.exp2(masked(dot_t(kk[rows, :], qx[j]), zh, j, kb, first))
            e_ref[...] = e.astype(BF16)
            ds_ref[...] = (e * dot_t(vv[rows, :], do_all[...])).astype(BF16)
            dv = dot(e_ref[...], do_all[...])
            dk = dot(ds_ref[...], qx[j])
            dq = t_dot(ds_ref[...], kk[rows, :])
            if kb == j:
                dvv[rows, :], dkk[rows, :] = dv, dk
            else:
                dvv[rows, :] += dv
                dkk[rows, :] += dk
            if kb == 0:
                dq_acc[...] = dq
            else:
                dq_acc[...] += dq
        for p in range(4):
            even, odd = slice(2 * p * BLK, (2 * p + 1) * BLK), slice((2 * p + 1) * BLK, (2 * p + 2) * BLK)
            v = jnp.where(lo, dq_acc[even, :], pltpu.roll(dq_acc[odd, :], HD, 1)) * HD**-0.5
            v = v * cosine[here, :] - swap_halves(v) * sine[here, :]
            dq_ref[rel, :, p * 128 : (p + 1) * 128] = v.astype(BF16)
    for j in range(4):
        for dst, off in ((dkv_own, zh), (dkv_par, 1 - zh)):
            at = rows_at(2 * j + off)
            both = jnp.where(lo, dkk[at, :] * LN2, pltpu.roll(dvv[at, :], HD, 1))
            dst[j * BLK : (j + 1) * BLK, :] = both.astype(dst.dtype)


def attend_back(idx, qx, kv_own, kv_par, first, att, cosine, sine, branch, weight):
    return pl.pallas_call(
        attend_back_body,
        out_shape=(sds((4, BLK, AW)), sds((ROWS, 128), F32), sds((ROWS, 128))),
        in_specs=[spec(pltpu.SMEM)] + [spec()] * 15,
        out_specs=(spec(),) * 3,
        scratch_shapes=[
            pltpu.VMEM((CAP, 128), BF16),
            pltpu.VMEM((CAP, 128), BF16),
            pltpu.VMEM((ROWS, AW), BF16),
            pltpu.VMEM((QALL, 128), BF16),
            pltpu.VMEM((CAP, 128), F32),
            pltpu.VMEM((CAP, 128), F32),
            pltpu.VMEM((PAIR, QALL), BF16),
            pltpu.VMEM((PAIR, QALL), BF16),
            pltpu.VMEM((QALL, 128), F32),
        ],
        compiler_params=params(),
        cost_estimate=cost(3e10, 8e6),
        name="attend_back",
    )(idx, qx, kv_own, kv_par, first, att, cosine, sine, *branch, *weight)


def qkv_back_body(
    idx, dqm, dkv_own, dkv_got, cosine, sine, w0, w1, w2, n0, n1, n2a, n2b, n3, gain_one, gain_grad_two,
    mine, theirs, o0, o1, o2a, o2b, o3, n_all, dkv, out, grad, gains,
):
    x, y, core = idx[0], idx[2], idx[3]
    lo = low_lanes((BLK, 128))
    for ref, row, (_, n) in zip((n0, n1, n2a, n2b, n3), PIECE_ROW, PIECES):
        n_all[row : row + n, :] = ref[...]
    slots = weight_rows(idx, DH)
    total = jnp.zeros((8, D), F32)
    for d, ref in ((2, None), (1, o1), (3, o3), (0, o0)):
        at = rows_at((x + d) & 3)
        v = dkv_own[at, :] + dkv_got[at, :].astype(F32)
        v = jnp.where(lo, v * cosine[at, :] - swap_halves(v) * sine[at, :], v).astype(BF16)
        here = slice(d * BLK, (d + 1) * BLK)
        dkv[here, :] = v
        rows = jnp.concatenate([dqm[d], v], 1)
        for s, w in zip(slots, (w0, w1, w2)):
            out[:, s] = dot_t(rows, w[...])
        res = out[...]
        total = total + jnp.sum((res * n_all[here, :].astype(F32)).reshape(BLK // 8, 8, D), axis=0)
        res = res.astype(BF16)
        if d == 2:
            o2a[...], o2b[...] = res[:HALF], res[HALF:]
        else:
            ref[...] = res
    grad[...] = dot(dkv[...].T, n_all[...]).astype(BF16)
    gains[0:1, :] = jnp.sum(total, axis=0, keepdims=True) / gain_one[...]
    gains[1:2, :] = gain_grad_two[...]
    for s in range(4):
        for k, ref in enumerate((mine, theirs)):
            p = ((y + s) & 3) * 2 + (core if k == 0 else 1 - core)
            both = gains[:, pl.ds(pl.multiple_of(p * 256, 256), 256)]
            both = jnp.concatenate([both[:, :128], both[:, 128:], jnp.zeros((12, 128), F32)], 0)
            for h in range(2):
                ref[s, h, :128, :] = grad[:, pl.ds(pl.multiple_of(h * DH + p * 128, 128), 128)]
                ref[s, h, 128:, :] = both.astype(BF16)


def qkv_back(idx, dqm, dkv_own, dkv_got, cosine, sine, weight, pieces, gain_one, gain_grad_two):
    res = pl.pallas_call(
        qkv_back_body,
        out_shape=(sds((4, 2, KVP, 128)),) * 2 + part_shapes(D),
        in_specs=[spec(pltpu.SMEM)] + [spec()] * 15,
        out_specs=(spec(),) * 7,
        scratch_shapes=[
            pltpu.VMEM((ROWS, D), BF16),
            pltpu.VMEM((ROWS, 128), BF16),
            pltpu.VMEM((BLK, D), F32),
            pltpu.VMEM((128, D), BF16),
            pltpu.VMEM((2, D), F32),
        ],
        compiler_params=params(),
        cost_estimate=cost(2 * ROWS * D * QW, 1.3e7),
        name="qkv_back",
    )(
        idx, dqm, dkv_own, dkv_got, cosine, sine, *weight, *pieces,
        gain_one.reshape(1, D), gain_grad_two.reshape(1, D),
    )
    return res[0], res[1], res[2:]


TILES = 6
GAP = TILES * TILE


def load_down(idx, refs, dst, sem):
    copies = []
    for k, (s, ref) in enumerate(zip(weight_rows(idx, FF4 // 2), refs)):
        copies.append(pltpu.make_async_copy(ref, dst.at[s], sem.at[k]))
    return copies


def ffn_body(
    idx, n0, n1, n2a, n2b, n3, c0, c1, c2, c3, gate_own, up_own, gate_par, up_par, w0, w1, w2,
    hid, dgate, dup, n_all, c_all, down, sem,
):
    i = pl.program_id(0)
    zh = idx[1]

    @pl.when(i == 0)
    def _():
        copies = load_down(idx, (w0, w1, w2), down, sem)
        for c in copies:
            c.start()
        for ref, row, (_, n) in zip((n0, n1, n2a, n2b, n3), PIECE_ROW, PIECES):
            n_all[row : row + n, :] = ref[...]
        for d, ref in enumerate((c0, c1, c2, c3)):
            c_all[d * BLK : (d + 1) * BLK, :] = ref[...]
        for c in copies:
            c.wait()

    own = n_all[:, pl.ds(pl.multiple_of(zh * DH, DH), DH)]
    par = n_all[:, pl.ds(pl.multiple_of((1 - zh) * DH, DH), DH)]
    gate = dot(own, gate_own[...]) + dot(par, gate_par[...])
    up = dot(own, up_own[...]) + dot(par, up_par[...])
    dh = dot_t(c_all[...], down[pl.ds(pl.multiple_of(i * TILE, TILE), TILE), :])
    sig = 1.0 / (1.0 + jnp.exp(-gate))
    act = gate * sig
    hid[...] = (act * up).astype(BF16)
    dgate[...] = (dh * up * sig * (1.0 + gate * (1.0 - sig))).astype(BF16)
    dup[...] = (dh * act).astype(BF16)


def whole(n, w):
    return pl.BlockSpec((n, w), lambda i: (0, 0))


def ffn(idx, normed, cots, gate, up, gate_up, down):
    column = lambda first: pl.BlockSpec((DH, TILE), lambda i: (0, i + first))
    hidden = pl.BlockSpec((ROWS, TILE), lambda i: (0, i))
    return pl.pallas_call(
        ffn_body,
        grid=(TILES,),
        out_shape=(sds((ROWS, FF4)),) * 3,
        in_specs=[spec(pltpu.SMEM)]
        + [whole(n, D) for _, n in PIECES]
        + [whole(BLK, D)] * 4
        + [column(0), column(0), column(0), column(TILES)]
        + [spec(pl.ANY)] * 3,
        out_specs=[hidden] * 3,
        scratch_shapes=[
            pltpu.VMEM((ROWS, D), BF16),
            pltpu.VMEM((ROWS, D), BF16),
            pltpu.VMEM((GAP, D), BF16),
            pltpu.SemaphoreType.DMA((3,)),
        ],
        compiler_params=params(),
        cost_estimate=cost(6 * ROWS * D * FF4, 3.4e7),
        name="ffn",
    )(idx, *normed, *cots, gate, up, gate_up, gate_up, *down)


def down_body(idx, hid, w0, w1, w2, o0, o1, o2, o3, down, sem):
    copies = load_down(idx, (w0, w1, w2), down, sem)
    for c in copies:
        c.start()
    for c in copies:
        c.wait()
    for n in range(D // 512):
        cols = slice(n * 512, (n + 1) * 512)
        res = dot(hid[...], down[:, cols]).astype(BF16)
        for d, ref in enumerate((o0, o1, o2, o3)):
            ref[:, cols] = res[d * BLK : (d + 1) * BLK]


def down_project(idx, hid, down):
    return pl.pallas_call(
        down_body,
        out_shape=(sds((BLK, D)),) * 4,
        in_specs=[spec(pltpu.SMEM), spec()] + [spec(pl.ANY)] * 3,
        out_specs=(spec(),) * 4,
        scratch_shapes=[pltpu.VMEM((FF4, D), BF16), pltpu.SemaphoreType.DMA((3,))],
        compiler_params=params(),
        cost_estimate=cost(2 * ROWS * D * FF4, 1.1e7),
        name="down_project",
    )(idx, hid, *down)


def ffn_back_body(idx, dgate, dup, gate_own, up_own, par, *refs):
    half = pl.num_programs(0) // 2

    def store(res):
        for ref, row, (_, n) in zip(refs, PIECE_ROW, PIECES):
            ref[...] = res[row : row + n].astype(BF16)

    @pl.when(pl.program_id(0) < half)
    def _():
        store(dot_t(dgate[...], gate_own[...]) + dot_t(dup[...], up_own[...]))

    @pl.when(pl.program_id(0) >= half)
    def _():
        store(dot_t(dgate[...], par[:, :FF4]) + dot_t(dup[...], par[:, GAP:]))


def ffn_back(idx, dgate, dup, gate, up, gate_up):
    half = DH // TILE
    rows = pl.BlockSpec((ROWS, FF4), lambda i, idx: (0, 0))
    own = pl.BlockSpec((TILE, FF4), lambda i, idx: (jnp.minimum(i, half - 1), 0))
    par = pl.BlockSpec((TILE, GAP + FF4), lambda i, idx: (jnp.maximum(i - half, 0), 0))
    place = lambda i, idx: (0, i ^ (idx[1] * half))
    return pl.pallas_call(
        ffn_back_body,
        grid_spec=pltpu.PrefetchScalarGridSpec(
            num_scalar_prefetch=1,
            grid=(D // TILE,),
            in_specs=[rows, rows, own, own, par],
            out_specs=[pl.BlockSpec((n, TILE), place) for _, n in PIECES],
        ),
        out_shape=part_shapes(D),
        compiler_params=params(),
        cost_estimate=cost(4 * ROWS * D * FF4, 1.8e7),
        name="ffn_back",
    )(idx, dgate, dup, gate, up, gate_up)


GU_ROWS = FF4 // 128 * 64
PIECE = 2 * GU_ROWS + FF4 // 2


def ffn_grads_body(*refs):
    na, nb, cots = refs[0:5], refs[5:10], refs[10:14]
    hid, dgate, dup, out, hid_t = refs[14:]

    @pl.when(pl.program_id(0) == 0)
    def _():
        hid_t[...] = hid[...].T

    stack = lambda parts: jnp.concatenate([r[...] for r in parts], 0)
    rows = jnp.concatenate([stack(na), stack(nb)], 1).T
    for k, ref in enumerate((dgate, dup)):
        g = dot(rows, ref[...]).astype(BF16)
        for h in range(2):
            for q in range(2):
                r = g[(2 * h + q) * 64 : (2 * h + q + 1) * 64]
                for c in range(FF4 // 128):
                    first = k * GU_ROWS + c * 64
                    out[h, q, first : first + 64, :] = r[:, c * 128 : (c + 1) * 128]
    g = dot(hid_t[...], stack(cots)).astype(BF16)
    for h in range(2):
        for q in range(2):
            out[h, q, 2 * GU_ROWS :, :] = g[
                h * (FF4 // 2) : (h + 1) * (FF4 // 2), q * 128 : (q + 1) * 128
            ]


def ffn_grads(normed, cots, hid, dgate, dup):
    return pl.pallas_call(
        ffn_grads_body,
        grid=(8,),
        out_shape=sds((2, 16, PIECE, 128)),
        in_specs=[pl.BlockSpec((n, 128), lambda i: (0, i)) for _, n in PIECES]
        + [pl.BlockSpec((n, 128), lambda i: (0, i + 8)) for _, n in PIECES]
        + [pl.BlockSpec((BLK, 256), lambda i: (0, i))] * 4
        + [whole(ROWS, FF4)] * 3,
        out_specs=pl.BlockSpec((2, 2, PIECE, 128), lambda i: (0, i, 0, 0)),
        scratch_shapes=[pltpu.VMEM((FF4, ROWS), BF16)],
        compiler_params=params(),
        cost_estimate=cost(6 * ROWS * D * FF4, 3e7),
        name="ffn_grads",
    )(*normed, *normed, *cots, hid, dgate, dup)


def unpack_body(piece, gate, up, down):
    for k, ref in enumerate((gate, up)):
        for c in range(FF4 // 128):
            first = k * GU_ROWS + c * 64
            ref[:, c * 128 : (c + 1) * 128] = piece[0, first : first + 64, :].astype(F32)
    down[...] = piece[0, 2 * GU_ROWS :, :].astype(F32)


def unpack(pieces):
    return pl.pallas_call(
        unpack_body,
        grid=(16,),
        out_shape=(sds((DH, FF4), F32), sds((DH, FF4), F32), sds((FF4 // 2, D), F32)),
        in_specs=[pl.BlockSpec((1, PIECE, 128), lambda i: (i, 0, 0))],
        out_specs=[
            pl.BlockSpec((64, FF4), lambda i: (i, 0)),
            pl.BlockSpec((64, FF4), lambda i: (i, 0)),
            pl.BlockSpec((FF4 // 2, 128), lambda i: (0, i)),
        ],
        compiler_params=params(),
        cost_estimate=cost(1e6, 2.6e7),
        name="unpack",
    )(pieces)


QP = 4 * 128
OP = 2 * (AW // 2)
QOP = QP + OP
KVP = 128 + 16
TAIL = QOP + KVP


def attn_grads_body(idx, *refs):
    na, nb, branch = refs[0:5], refs[5:10], refs[10:15]
    dqm, att, mine, theirs, att_t = refs[15:]
    core = idx[3]

    @pl.when(pl.program_id(0) == 0)
    def _():
        att_t[...] = att[...].T

    stack = lambda parts: jnp.concatenate([r[...] for r in parts], 0)

    def store(h, first, n, zero, one):
        mine[0, h, first : first + n, :] = jnp.where(core == 0, zero, one)
        theirs[0, h, first : first + n, :] = jnp.where(core == 0, one, zero)

    for h, cols in enumerate((na, nb)):
        g = dot(stack(cols).T, dqm[...]).astype(BF16)
        for c in range(4):
            lanes = slice(c * 128, (c + 1) * 128)
            store(h, c * 128, 128, g[:128, lanes], g[128:, lanes])
    g = dot(att_t[...], stack(branch)).astype(BF16)
    for h in range(2):
        r = g[h * (AW // 2) : (h + 1) * (AW // 2)]
        for c in range(2):
            lanes = lambda k: slice(k * 256 + c * 128, k * 256 + (c + 1) * 128)
            store(h, QP + c * (AW // 2), AW // 2, r[:, lanes(0)], r[:, lanes(1)])


def attn_grads(idx, normed, branch, dqm, att):
    turn = lambda s, idx: (s + idx[2]) & 3
    piece = pl.BlockSpec((1, 2, QOP, 128), lambda s, idx: (s, 0, 0, 0))
    fixed = pl.BlockSpec((ROWS, AW), lambda s, idx: (0, 0))
    return pl.pallas_call(
        attn_grads_body,
        grid_spec=pltpu.PrefetchScalarGridSpec(
            num_scalar_prefetch=1,
            grid=(4,),
            in_specs=[pl.BlockSpec((n, 256), lambda s, idx: (0, turn(s, idx))) for _, n in PIECES]
            + [pl.BlockSpec((n, 256), lambda s, idx: (0, turn(s, idx) + 4)) for _, n in PIECES]
            + [pl.BlockSpec((n, 512), lambda s, idx: (0, turn(s, idx))) for _, n in PIECES]
            + [fixed, fixed],
            out_specs=[piece, piece],
            scratch_shapes=[pltpu.VMEM((AW, ROWS), BF16)],
        ),
        out_shape=(sds((4, 2, QOP, 128)),) * 2,
        compiler_params=params(),
        cost_estimate=cost(4 * ROWS * D * AW, 1e7),
        name="attn_grads",
    )(idx, *normed, *normed, *branch, dqm, att)


def small_call(body, out_shape, *args, name):
    return pl.pallas_call(
        body,
        out_shape=out_shape,
        in_specs=[spec(pltpu.SMEM)] + [spec()] * (len(args) - 1),
        out_specs=jax.tree.map(lambda _: spec(), out_shape),
        compiler_params=params(),
        cost_estimate=cost(1e6, 4e6),
        name=name,
    )(*args)


def add(*values):
    return sum((v.astype(F32) for v in values[1:]), values[0].astype(F32)).astype(BF16)


def sum_core_body(idx, a, b, c, d, *outs):
    for s, out in enumerate(outs):
        out[:, :QOP, :] = add(a[s], b[s])
        out[:, QOP:, :] = add(c[s], d[s])


def sum_y_body(idx, a, b, c, d, own, other):
    zh = idx[1]
    own[...] = add(a[zh], b[zh], c[zh], d[zh])
    far = 1 - zh
    other[...] = add(a[far], b[far], c[far], d[far])


def sum_z_body(idx, a, b, c, d, out):
    out[...] = add(a[...], b[...], c[...], d[...])


def unpack_tail_body(idx, *refs):
    y, core = idx[2], idx[3]
    qkv, out, gains = refs[8:]
    for k in range(8):
        piece = refs[k]
        p = ((y - k % 4) & 3) * 2 + (core if k < 4 else 1 - core)
        rows = pl.ds(pl.multiple_of(p * 128, 128), 128)
        for c in range(4):
            qkv[rows, c * 128 : (c + 1) * 128] = piece[c * 128 : (c + 1) * 128, :].astype(F32)
        qkv[rows, AW:] = piece[QOP : QOP + 128, :].astype(F32).T
        g = piece[QOP + 128 :, :].astype(F32)
        for c in range(2):
            first = QP + c * (AW // 2)
            cols = pl.ds(pl.multiple_of(p * 256 + c * 128, 128), 128)
            out[:, cols] = piece[first : first + AW // 2, :].astype(F32)
            gains[:, cols] = g[2 * c : 2 * c + 2]


def sum_tail(idx, first, second):
    got_a = lax.ppermute(first[1], "core", shift(2, 1))
    got_b = lax.ppermute(second[1], "core", shift(2, 1))
    part = sds((2, TAIL, 128))
    g = small_call(sum_core_body, (part,) * 4, idx, first[0], got_a, second[0], got_b, name="sum_core")
    got = [lax.ppermute(g[s], "y", shift(4, s)) for s in (2, 1, 3)]
    part = sds((TAIL, 128))
    own, other = small_call(sum_y_body, (part,) * 2, idx, g[0], *got, name="sum_y")
    cross = [(2 * a + b, 2 * (1 - a) + (1 - b)) for a in range(2) for b in range(2)]
    g = small_call(
        sum_z_body,
        part,
        idx,
        own,
        lax.ppermute(own, "zl", shift(2, 1)),
        lax.ppermute(other, "zh", shift(2, 1)),
        lax.ppermute(other, ("zl", "zh"), cross),
        name="sum_z",
    )
    mine = [g] + [lax.ppermute(g, "y", shift(4, s)) for s in (1, 2, 3)]
    theirs = [lax.ppermute(v, "core", shift(2, 1)) for v in mine]
    shapes = (sds((DH, QW), F32), sds((AW // 2, D), F32), sds((2, D), F32))
    return small_call(unpack_tail_body, shapes, idx, *mine, *theirs, name="unpack_tail")


def inverse_rms(v):
    return lax.rsqrt(jnp.mean(v * v, axis=-1, keepdims=True) + EPSILON)


def norm_back(v, r, gain, grad):
    pulled = grad * gain
    inner = jnp.mean(v * pulled, axis=-1, keepdims=True)
    return r * pulled - v * (r * r * r) * inner, jnp.sum(grad * v * r, axis=0)


def replica_layout(lengths, replica, replica_id):
    sizes = jnp.where(replica == replica_id, lengths, 0)
    starts = jnp.cumsum(sizes) - sizes
    row_ids = jnp.arange(CAP, dtype=jnp.int32)
    inside = (row_ids[:, None] >= starts[None, :]) & (row_ids[:, None] < (starts + sizes)[None, :])
    begin = jnp.sum(jnp.where(inside, starts[None, :], 0), axis=1)
    begin = begin + jnp.where(jnp.any(inside, axis=1), 0, jnp.sum(sizes))
    return begin, row_ids - begin


def on_device(
    tokens, cotangent, gain_one, qkv_weight, out_weight, gate_weight, up_weight, down_weight,
    gain_two, seq_lengths, seq_replica,
):
    x, zh, core = lax.axis_index("x"), lax.axis_index("zh"), lax.axis_index("core")
    y, zl = lax.axis_index("y"), lax.axis_index("zl")
    idx = jnp.stack([x, zh, y, core]).astype(jnp.int32)

    tok = tokens.astype(F32)
    s_one = inverse_rms(tok)
    qkv_got = fetch_half(qkv_weight, core)
    normed_one, sent = gather_x((tok * s_one * gain_one).astype(BF16), qkv_got)
    qkv_all = qkv_weight, qkv_got, lax.ppermute(tie(qkv_got, *sent), "core", shift(2, 1))
    out_all = fetch_partner(out_weight, core, *sent)
    rows = DH // 8
    mine = lambda w: lax.dynamic_slice_in_dim(w, (y * 2 + core) * rows, rows, 0)
    cross = [(2 * a + b, 2 * (1 - a) + (1 - b)) for a in range(2) for b in range(2)]
    gate_up = lax.ppermute(
        jnp.concatenate(
            [
                tie(mine(gate_weight), out_all[1], normed_one[2], normed_one[3]),
                jnp.zeros((rows, GAP - FF4), BF16),
                mine(up_weight),
            ],
            1,
        ),
        ("zl", "zh"),
        cross,
    )
    cots = gather_direct(tie(cotangent, normed_one[2]))

    begin, position = replica_layout(seq_lengths, seq_replica, (y * 2 + zl) * 2 + core)
    half_rows = lambda v: lax.dynamic_index_in_dim(v.reshape(4, 2, BLK), zh, 1, False).reshape(ROWS, 1)
    first = jnp.tile(half_rows(begin)[3 * BLK :, 0], 8).reshape(1, QALL)
    lane = jnp.arange(128, dtype=jnp.int32)
    frequency = ROTARY_BASE ** (-(lane % 32).astype(F32) * (2.0 / HD))
    angles = half_rows(position).astype(F32) * frequency[None, :]
    cosine = jnp.cos(angles)
    sine = jnp.where((lane % HD) < HD // 2, -1.0, 1.0)[None, :] * jnp.sin(angles)

    q, kv_own = qkv_forward(idx, normed_one, qkv_all, cosine, sine)
    kv_par = lax.ppermute(kv_own, "zh", shift(2, 1))
    gate_up = lax.all_gather(tie(gate_up, kv_par), ("y", "core"), axis=0, tiled=True)
    down_all = fetch_partner(down_weight, core, kv_par)
    att, qx = attend(idx, q, kv_own, kv_par, first)
    parts = [tie(p, *cots) for p in out_project(idx, att, out_all)]
    after_attn = tok + scatter_x(parts)

    r_two = inverse_rms(after_attn)
    normed_two, _ = gather_x((after_attn * r_two * gain_two).astype(BF16))
    hid, dgate, dup = ffn(idx, normed_two, cots, gate_weight, up_weight, gate_up, down_all)
    own_grads = ffn_grads(normed_two, cots, hid, dgate, dup)
    grads = lax.psum_scatter(
        own_grads.reshape(32, PIECE, 128), ("zh", "zl", "y", "core"), scatter_dimension=0, tiled=True
    )
    d_two = scatter_x(ffn_back(idx, tie(dgate, own_grads), dup, gate_weight, up_weight, gate_up))
    back_two, gain_grad_two = norm_back(after_attn, r_two, gain_two, d_two)
    after_grad = cotangent.astype(F32) + back_two
    branch, _ = gather_x(after_grad.astype(BF16))
    layer_parts = down_project(idx, tie(hid, after_grad), down_all)
    att = tie(att, *layer_parts)
    dqm, dkv_own, dkv_par = attend_back(
        idx, qx, kv_own, kv_par, first, att, cosine, sine, branch, out_all
    )
    dkv_got = lax.ppermute(dkv_par, "zh", shift(2, 1))
    tail = attn_grads(idx, normed_one, branch, dqm.reshape(ROWS, AW), att.reshape(ROWS, AW))
    dkv_got = tie(dkv_got, tail[0])
    *tail_kv, parts = qkv_back(
        idx, dqm, dkv_own, dkv_got, cosine, sine, qkv_all, normed_one, gain_one,
        gain_grad_two,
    )
    grads = lax.all_gather(tie(grads, dkv_got), ("zl", "y", "core"), axis=0, tiled=True)
    grad_gate, grad_up, grad_down = unpack(grads)
    d_one = scatter_x(parts)
    layer_parts = [tie(p, d_one) for p in layer_parts]
    layer_out = (after_attn + scatter_direct(layer_parts)).astype(BF16)
    back_one, _ = norm_back(tok, s_one, gain_one, d_one)
    input_grad = (after_grad + back_one).astype(BF16)

    over_x = lambda v: sum((lax.ppermute(v, "x", shift(4, s)) for s in (1, 2, 3)), v)
    grad_qkv, grad_out, gains = sum_tail(idx, tail, tail_kv)
    gains = over_x(gains)
    return (
        layer_out, input_grad, gains[0], grad_qkv, grad_out, grad_gate, grad_up,
        grad_down, gains[1],
    )


def solution(mesh):
    grid = Mesh(mesh.devices.reshape(SIZES), AXES)
    rows = P(AXES, None)
    both = P(("x", "zh"), None)
    return jax.shard_map(
        on_device,
        mesh=grid,
        in_specs=(
            rows, rows, P(), P("zh", "x"), both, P("zh", "x"), P("zh", "x"), both, P(), P(), P(),
        ),
        out_specs=(
            rows, rows, P(), P("zh", "x"), both, P("zh", "x"), P("zh", "x"), both, P(),
        ),
        check_vma=False,
    )
```

```python
import jax
import jax.numpy as jnp
from jax import lax
from jax.experimental import pallas as pl
from jax.experimental.pallas import tpu as pltpu
from jax.sharding import Mesh
from jax.sharding import PartitionSpec as P

HEADS = 32
KV = 4
HD = 64
EPSILON = 1e-05
ROTARY_BASE = 10000.0
MASKED = -1e30

AXES = ("y", "zl", "core", "x", "zh")
SIZES = (4, 2, 2, 4, 2)
BLK = 160
HALF = BLK // 2
ROWS = 4 * BLK
CAP = 2 * ROWS
D = 2048
DH = D // 2
QW = 640
AW = 512
FF4 = 1408
TILE = 256
F32 = jnp.float32
BF16 = jnp.bfloat16
VLIM = 60 * 1024 * 1024


def spec(memory=pltpu.VMEM):
    return pl.BlockSpec(memory_space=memory)


def params(**kw):
    return pltpu.CompilerParams(vmem_limit_bytes=VLIM, **kw)


def cost(flops, nbytes):
    return pl.CostEstimate(flops=int(flops), bytes_accessed=int(nbytes), transcendentals=0)


def sds(shape, dtype=BF16):
    return jax.ShapeDtypeStruct(shape, dtype)


def dot(a, b):
    return jnp.dot(a, b, preferred_element_type=F32)


def dot_t(a, b):
    return lax.dot_general(a, b, (((1,), (1,)), ((), ())), preferred_element_type=F32)


def t_dot(a, b):
    return lax.dot_general(a, b, (((0,), (0,)), ((), ())), preferred_element_type=F32)


def tie(v, *deps):
    return lax.optimization_barrier((v,) + deps)[0]


def shift(n, s):
    return [(i, (i + s) % n) for i in range(n)]


def gather_x(v):
    from_prev = lax.ppermute(v, "x", shift(4, 1))
    from_next = lax.ppermute(v, "x", shift(4, -1))
    send_a = tie(from_prev[:HALF], from_next)
    send_b = tie(from_next[HALF:], from_prev)
    opp_a = lax.ppermute(send_a, "x", shift(4, 1))
    opp_b = lax.ppermute(send_b, "x", shift(4, -1))
    return v, from_next, opp_a, opp_b, from_prev


def scatter_x(parts):
    p0, p1, p2a, p2b, p3 = parts
    got_a = lax.ppermute(p2a, "x", shift(4, 1))
    got_b = lax.ppermute(p2b, "x", shift(4, -1))
    q1 = jnp.concatenate([(p1[:HALF].astype(F32) + got_a.astype(F32)).astype(BF16), p1[HALF:]], 0)
    q3 = jnp.concatenate([p3[:HALF], (p3[HALF:].astype(F32) + got_b.astype(F32)).astype(BF16)], 0)
    from_prev = lax.ppermute(q1, "x", shift(4, 1))
    from_next = lax.ppermute(q3, "x", shift(4, -1))
    return p0.astype(F32) + from_prev.astype(F32) + from_next.astype(F32), (got_a, got_b)


PIECES = ((0, BLK), (1, BLK), (2, HALF), (2, HALF), (3, BLK))
PIECE_ROW = (0, BLK, 2 * BLK, 2 * BLK + HALF, 3 * BLK)


def part_shapes(width, dtype=BF16):
    return tuple(sds((n, width), dtype) for _, n in PIECES)


def low_lanes(shape):
    return lax.broadcasted_iota(jnp.int32, shape, 1) < HD


def swap_halves(v):
    lane = lax.broadcasted_iota(jnp.int32, v.shape, 1) % HD
    return jnp.where(lane < HD // 2, pltpu.roll(v, 128 - HD // 2, 1), pltpu.roll(v, HD // 2, 1))


def rows_at(block):
    return pl.ds(pl.multiple_of(block * BLK, 32), BLK)


def fetch_half(w, core):
    half = w.shape[0] // 2
    return lax.ppermute(lax.dynamic_slice_in_dim(w, core * half, half, 0), "zh", shift(2, 1))


def fetch_partner(w, core, *deps):
    got = fetch_half(tie(w, *deps), core)
    return w, got, lax.ppermute(got, "core", shift(2, 1))


def weight_rows(idx, rows):
    zh, core = idx[1], idx[3]
    far = (1 - zh) * rows
    half = rows // 2
    at = lambda first, n: pl.ds(pl.multiple_of(first, half), n)
    return at(zh * rows, rows), at(far + core * half, half), at(far + (1 - core) * half, half)


def qkv_body(idx, n0, n1, n2a, n2b, n3, w0, w1, w2, cosine, sine, q_ref, kv_ref, rows):
    x = idx[0]
    lo = low_lanes((BLK, 128))
    for ref, row, (_, n) in zip((n0, n1, n2a, n2b, n3), PIECE_ROW, PIECES):
        rows[row : row + n, :] = ref[...]
    s0, s1, s2 = weight_rows(idx, DH)
    acc = dot(rows[:, s0], w0[...]) + dot(rows[:, s1], w1[...]) + dot(rows[:, s2], w2[...])
    for d in range(4):
        at = rows_at((x + d) & 3)
        cs = cosine[at, :]
        sn = sine[at, :]
        for p in range(5):
            v = acc[d * BLK : (d + 1) * BLK, p * 128 : (p + 1) * 128]
            r = v * cs + swap_halves(v) * sn
            if p < 4:
                r = r * (HD**-0.5 * LOG2E)
                a = (x + d) & 3
                for k, w in enumerate((r, pltpu.roll(r, HD, 1))):
                    head = slice((2 * p + k) * BLK, (2 * p + k + 1) * BLK)
                    q_ref[a, head, :] = jnp.where(lo, w, 0.0).astype(BF16)
            else:
                kv_ref[at, :] = jnp.where(lo, r, v).astype(BF16)


def qkv_forward(idx, pieces, weight, cosine, sine):
    return pl.pallas_call(
        qkv_body,
        out_shape=(sds((4, QALL, 128)), sds((ROWS, 128))),
        in_specs=[spec(pltpu.SMEM)] + [spec()] * 10,
        out_specs=(spec(), spec()),
        scratch_shapes=[pltpu.VMEM((ROWS, D), BF16)],
        compiler_params=params(),
        cost_estimate=cost(2 * ROWS * D * QW, 7e6),
        name="qkv_forward",
    )(idx, *pieces, *weight, cosine, sine)


QALL = 8 * BLK
PAIR = 2 * BLK
LOG2E = 1.4426950408889634
LN2 = 0.6931471805599453


def split3(v):
    a = v.astype(BF16).astype(F32)
    b = (v - a).astype(BF16).astype(F32)
    return a, b, v - a - b


def with_lanes(v, parts):
    lane = lax.broadcasted_iota(jnp.int32, v.shape, 1)
    out = jnp.where(lane < HD, v, 0.0)
    for k, part in enumerate(parts):
        out = jnp.where(lane == HD + k, part, out)
    return out


def spread_keys(zh, kv_own, kv_par, kk, vv, fill):
    shape = (BLK, 128)
    lo = low_lanes(shape)
    rest = fill(lax.broadcasted_iota(jnp.int32, shape, 1) - HD)
    for j in range(4):
        for src, off in ((kv_own, zh), (kv_par, 1 - zh)):
            v = src[j * BLK : (j + 1) * BLK, :].astype(F32)
            at = rows_at(2 * j + off)
            kk[at, :] = jnp.where(lo, v, rest).astype(BF16)
            vv[at, :] = jnp.where(lo, pltpu.roll(v, HD, 1), rest).astype(BF16)


def masked(s, zh, j, kb, first):
    if j < 3 and kb < j:
        return s
    u = kb * PAIR + lax.broadcasted_iota(jnp.int32, (PAIR, QALL), 0)
    allowed = None
    if kb == j:
        t = (2 * j + zh) * BLK + lax.broadcasted_iota(jnp.int32, (1, QALL), 1) % BLK
        allowed = u <= t
    if j == 3:
        later = u >= first[...]
        allowed = later if allowed is None else allowed & later
    return jnp.where(allowed, s, MASKED)


def attend_body(idx, q, kv_own, kv_par, first, att, qx, kk, vv, vt, s_ref, e_ref):
    x, zh = idx[0], idx[1]
    spread_keys(zh, kv_own, kv_par, kk, vv, lambda lane: 1.0)
    vt[...] = vv[...].T
    lo = low_lanes((BLK, 128))
    for j in range(4):
        n = PAIR * (j + 1)
        qj = q[j]
        top = jnp.full((1, QALL), MASKED, F32)
        for kb in range(j + 1):
            rows = slice(kb * PAIR, (kb + 1) * PAIR)
            s = masked(dot_t(kk[rows, :], qj), zh, j, kb, first)
            s_ref[rows, :] = s
            top = jnp.maximum(top, jnp.max(s, axis=0, keepdims=True))
        for k in range(n // 64):
            rows = slice(k * 64, (k + 1) * 64)
            e_ref[rows, :] = jnp.exp2(s_ref[rows, :] - top).astype(BF16)
        o = dot(vt[:, :n], e_ref[:n, :])
        lse = split3(top + jnp.log(o[HD : HD + 1, :]) * LOG2E)
        row = lax.broadcasted_iota(jnp.int32, (128, QALL), 0)
        extra = jnp.zeros((128, QALL), F32)
        for k, part in enumerate(lse):
            extra = jnp.where(row == HD + k, part, extra)
        qx[j] = (qj.astype(F32) + extra.T).astype(BF16)
        o = o.T
        r = pltpu.roll(o, HD, 1)
        rel = (j - x) & 3
        for p in range(4):
            even, odd = slice(2 * p * BLK, (2 * p + 1) * BLK), slice((2 * p + 1) * BLK, (2 * p + 2) * BLK)
            num = jnp.where(lo, o[even], r[odd])
            den = jnp.where(lo, r[even], o[odd])
            att[rel, :, p * 128 : (p + 1) * 128] = (num / den).astype(BF16)


def attend(idx, q, kv_own, kv_par, first):
    return pl.pallas_call(
        attend_body,
        out_shape=(sds((4, BLK, AW)), sds((4, QALL, 128))),
        in_specs=[spec(pltpu.SMEM)] + [spec()] * 4,
        out_specs=(spec(), spec()),
        scratch_shapes=[
            pltpu.VMEM((CAP, 128), BF16),
            pltpu.VMEM((CAP, 128), BF16),
            pltpu.VMEM((128, CAP), BF16),
            pltpu.VMEM((CAP, QALL), F32),
            pltpu.VMEM((CAP, QALL), BF16),
        ],
        compiler_params=params(),
        cost_estimate=cost(1.2e10, 3e6),
        name="attend",
    )(idx, q, kv_own, kv_par, first)


def store_parts(res, refs):
    for ref, row, (_, n) in zip(refs, PIECE_ROW, PIECES):
        ref[...] = res[row : row + n].astype(BF16)


def out_body(idx, att, w0, w1, w2, o0, o1, o2a, o2b, o3):
    s0, s1, s2 = weight_rows(idx, AW // 2)
    for d, ref in ((2, None), (1, o1), (3, o3), (0, o0)):
        a = att.at[d]
        res = dot(a[:, s0], w0[...]) + dot(a[:, s1], w1[...]) + dot(a[:, s2], w2[...])
        res = res.astype(BF16)
        if d == 2:
            o2a[...] = res[:HALF]
            o2b[...] = res[HALF:]
        else:
            ref[...] = res


def out_project(idx, att, weight):
    return pl.pallas_call(
        out_body,
        out_shape=part_shapes(D),
        in_specs=[spec(pltpu.SMEM)] + [spec()] * 4,
        out_specs=(spec(),) * 5,
        compiler_params=params(),
        cost_estimate=cost(2 * ROWS * D * AW, 5.5e6),
        name="out_project",
    )(idx, att, *weight)


def stack_heads(v):
    return v, pltpu.roll(v, HD, 1)


def attend_back_body(
    idx, qx, kv_own, kv_par, first, att, cosine, sine, b0, b1, b2a, b2b, b3, w0, w1, w2,
    dq_ref, dkv_own, dkv_par, kk, vv, dout, do_all, dkk, dvv, e_ref, ds_ref, dq_acc,
):
    x, zh = idx[0], idx[1]
    spread_keys(zh, kv_own, kv_par, kk, vv, lambda lane: jnp.where(lane < 3, -1.0, 0.0))
    s0, s1, s2 = weight_rows(idx, AW // 2)
    for d in range(4):
        if d == 2:
            rows = jnp.concatenate([b2a[...], b2b[...]], 0)
        else:
            rows = (b0, b1, None, b3)[d][...]
        at = rows_at((x + d) & 3)
        for s, w in ((s0, w0), (s1, w1), (s2, w2)):
            dout[at, s] = dot_t(rows, w[...]).astype(BF16)
    lo = low_lanes((BLK, 128))
    for j in range(4):
        rel = (j - x) & 3
        here = slice(j * BLK, (j + 1) * BLK)
        for p in range(4):
            cols = slice(p * 128, (p + 1) * 128)
            do = dout[here, cols].astype(F32)
            prod = do * att[rel, :, cols].astype(F32)
            for k, (v, w) in enumerate(zip(stack_heads(do), stack_heads(prod))):
                delta = jnp.sum(jnp.where(lo, w, 0.0), axis=1, keepdims=True)
                head = slice((2 * p + k) * BLK, (2 * p + k + 1) * BLK)
                do_all[head, :] = with_lanes(v, split3(delta)).astype(BF16)
        for kb in range(j + 1):
            rows = slice(kb * PAIR, (kb + 1) * PAIR)
            e = jnp.exp2(masked(dot_t(kk[rows, :], qx[j]), zh, j, kb, first))
            e_ref[...] = e.astype(BF16)
            ds_ref[...] = (e * dot_t(vv[rows, :], do_all[...])).astype(BF16)
            dv = dot(e_ref[...], do_all[...])
            dk = dot(ds_ref[...], qx[j])
            dq = t_dot(ds_ref[...], kk[rows, :])
            if kb == j:
                dvv[rows, :], dkk[rows, :] = dv, dk
            else:
                dvv[rows, :] += dv
                dkk[rows, :] += dk
            if kb == 0:
                dq_acc[...] = dq
            else:
                dq_acc[...] += dq
        for p in range(4):
            even, odd = slice(2 * p * BLK, (2 * p + 1) * BLK), slice((2 * p + 1) * BLK, (2 * p + 2) * BLK)
            v = jnp.where(lo, dq_acc[even, :], pltpu.roll(dq_acc[odd, :], HD, 1)) * HD**-0.5
            v = v * cosine[here, :] - swap_halves(v) * sine[here, :]
            dq_ref[rel, :, p * 128 : (p + 1) * 128] = v.astype(BF16)
    for j in range(4):
        for dst, off in ((dkv_own, zh), (dkv_par, 1 - zh)):
            at = rows_at(2 * j + off)
            both = jnp.where(lo, dkk[at, :] * LN2, pltpu.roll(dvv[at, :], HD, 1))
            dst[j * BLK : (j + 1) * BLK, :] = both.astype(dst.dtype)


def attend_back(idx, qx, kv_own, kv_par, first, att, cosine, sine, branch, weight):
    return pl.pallas_call(
        attend_back_body,
        out_shape=(sds((4, BLK, AW)), sds((ROWS, 128), F32), sds((ROWS, 128))),
        in_specs=[spec(pltpu.SMEM)] + [spec()] * 15,
        out_specs=(spec(),) * 3,
        scratch_shapes=[
            pltpu.VMEM((CAP, 128), BF16),
            pltpu.VMEM((CAP, 128), BF16),
            pltpu.VMEM((ROWS, AW), BF16),
            pltpu.VMEM((QALL, 128), BF16),
            pltpu.VMEM((CAP, 128), F32),
            pltpu.VMEM((CAP, 128), F32),
            pltpu.VMEM((PAIR, QALL), BF16),
            pltpu.VMEM((PAIR, QALL), BF16),
            pltpu.VMEM((QALL, 128), F32),
        ],
        compiler_params=params(),
        cost_estimate=cost(3e10, 8e6),
        name="attend_back",
    )(idx, qx, kv_own, kv_par, first, att, cosine, sine, *branch, *weight)


def qkv_back_body(
    idx, dqm, dkv_own, dkv_got, cosine, sine, w0, w1, w2, n0, n1, n2a, n2b, n3, gain_one,
    gain_grad_two,
    mine, theirs, o0, o1, o2a, o2b, o3, n_all, dkv, grad, gains,
):
    x, y, core = idx[0], idx[2], idx[3]
    lo = low_lanes((BLK, 128))
    for ref, row, (_, n) in zip((n0, n1, n2a, n2b, n3), PIECE_ROW, PIECES):
        n_all[row : row + n, :] = ref[...]
    for d in range(4):
        at = rows_at((x + d) & 3)
        v = dkv_own[at, :] + dkv_got[at, :].astype(F32)
        v = jnp.where(lo, v * cosine[at, :] - swap_halves(v) * sine[at, :], v).astype(BF16)
        dkv[d * BLK : (d + 1) * BLK, :] = v
    rows = jnp.concatenate([dqm[...], dkv[...]], 1)
    for s, w in zip(weight_rows(idx, DH), (w0, w1, w2)):
        for c in range(w.shape[0] // 512):
            cols = pl.ds(pl.multiple_of(s.start + c * 512, 512), 512)
            res = dot_t(rows, w[c * 512 : (c + 1) * 512, :])
            part = (res * n_all[:, cols].astype(F32)).reshape(ROWS // 8, 8, 512)
            gains[0:1, cols] = jnp.sum(jnp.sum(part, axis=0), axis=0, keepdims=True) / gain_one[:, cols]
            store_parts(res, [r.at[:, cols] for r in (o0, o1, o2a, o2b, o3)])
    grad[...] = dot(dkv[...].T, n_all[...]).astype(BF16)
    gains[1:2, :] = gain_grad_two[...]
    for s in range(4):
        for k, ref in enumerate((mine, theirs)):
            p = ((y + s) & 3) * 2 + (core if k == 0 else 1 - core)
            both = gains[:, pl.ds(pl.multiple_of(p * 256, 256), 256)]
            both = jnp.concatenate([both[:, :128], both[:, 128:], jnp.zeros((12, 128), F32)], 0)
            for h in range(2):
                ref[s, h, :128, :] = grad[:, pl.ds(pl.multiple_of(h * DH + p * 128, 128), 128)]
                ref[s, h, 128:, :] = both.astype(BF16)


def qkv_back(idx, dqm, dkv_own, dkv_got, cosine, sine, weight, pieces, gain_one, gain_grad_two):
    res = pl.pallas_call(
        qkv_back_body,
        out_shape=(sds((4, 2, KVP, 128)),) * 2 + part_shapes(D),
        in_specs=[spec(pltpu.SMEM)] + [spec()] * 15,
        out_specs=(spec(),) * 7,
        scratch_shapes=[
            pltpu.VMEM((ROWS, D), BF16),
            pltpu.VMEM((ROWS, 128), BF16),
            pltpu.VMEM((128, D), BF16),
            pltpu.VMEM((2, D), F32),
        ],
        compiler_params=params(),
        cost_estimate=cost(2 * ROWS * D * QW, 1.3e7),
        name="qkv_back",
    )(
        idx, dqm, dkv_own, dkv_got, cosine, sine, *weight, *pieces,
        gain_one.reshape(1, D), gain_grad_two.reshape(1, D),
    )
    return res[0], res[1], res[2:]


TILES = 6
GAP = TILES * TILE


def load_down(idx, refs, dst, sem):
    copies = []
    for k, (s, ref) in enumerate(zip(weight_rows(idx, FF4 // 2), refs)):
        copies.append(pltpu.make_async_copy(ref, dst.at[s], sem.at[k]))
    return copies


def ffn_body(
    idx, n0, n1, n2a, n2b, n3, c0, c1, c2a, c2b, c3, gate_own, up_own, gate_par, up_par, w0, w1, w2,
    hid, dgate, dup, n_all, c_all, down, sem,
):
    i = pl.program_id(0)
    zh = idx[1]

    @pl.when(i == 0)
    def _():
        copies = load_down(idx, (w0, w1, w2), down, sem)
        for c in copies:
            c.start()
        for refs, dst in (((n0, n1, n2a, n2b, n3), n_all), ((c0, c1, c2a, c2b, c3), c_all)):
            for ref, row, (_, n) in zip(refs, PIECE_ROW, PIECES):
                dst[row : row + n, :] = ref[...]
        for c in copies:
            c.wait()

    own = n_all[:, pl.ds(pl.multiple_of(zh * DH, DH), DH)]
    par = n_all[:, pl.ds(pl.multiple_of((1 - zh) * DH, DH), DH)]
    gate = dot(own, gate_own[...]) + dot(par, gate_par[...])
    up = dot(own, up_own[...]) + dot(par, up_par[...])
    dh = dot_t(c_all[...], down[pl.ds(pl.multiple_of(i * TILE, TILE), TILE), :])
    sig = 1.0 / (1.0 + jnp.exp(-gate))
    act = gate * sig
    hid[...] = (act * up).astype(BF16)
    dgate[...] = (dh * up * sig * (1.0 + gate * (1.0 - sig))).astype(BF16)
    dup[...] = (dh * act).astype(BF16)


def whole(n, w):
    return pl.BlockSpec((n, w), lambda i: (0, 0))


def ffn(idx, normed, cots, gate, up, gate_up, down):
    column = lambda first: pl.BlockSpec((DH, TILE), lambda i: (0, i + first))
    hidden = pl.BlockSpec((ROWS, TILE), lambda i: (0, i))
    return pl.pallas_call(
        ffn_body,
        grid=(TILES,),
        out_shape=(sds((ROWS, FF4)),) * 3,
        in_specs=[spec(pltpu.SMEM)]
        + [whole(n, D) for _, n in PIECES] * 2
        + [column(0), column(0), column(0), column(TILES)]
        + [spec(pl.ANY)] * 3,
        out_specs=[hidden] * 3,
        scratch_shapes=[
            pltpu.VMEM((ROWS, D), BF16),
            pltpu.VMEM((ROWS, D), BF16),
            pltpu.VMEM((GAP, D), BF16),
            pltpu.SemaphoreType.DMA((3,)),
        ],
        compiler_params=params(),
        cost_estimate=cost(6 * ROWS * D * FF4, 3.4e7),
        name="ffn",
    )(idx, *normed, *cots, gate, up, gate_up, gate_up, *down)


def down_body(idx, hid, w0, w1, w2, o0, o1, o2, o3, down, sem):
    copies = load_down(idx, (w0, w1, w2), down, sem)
    for c in copies:
        c.start()
    for c in copies:
        c.wait()
    for n in range(D // 512):
        cols = slice(n * 512, (n + 1) * 512)
        res = dot(hid[...], down[:, cols]).astype(BF16)
        for d, ref in enumerate((o0, o1, o2, o3)):
            ref[:, cols] = res[d * BLK : (d + 1) * BLK]


def down_project(idx, hid, down):
    return pl.pallas_call(
        down_body,
        out_shape=(sds((BLK, D)),) * 4,
        in_specs=[spec(pltpu.SMEM), spec()] + [spec(pl.ANY)] * 3,
        out_specs=(spec(),) * 4,
        scratch_shapes=[pltpu.VMEM((FF4, D), BF16), pltpu.SemaphoreType.DMA((3,))],
        compiler_params=params(),
        cost_estimate=cost(2 * ROWS * D * FF4, 1.1e7),
        name="down_project",
    )(idx, hid, *down)


def ffn_back_body(idx, dgate, dup, gate_own, up_own, par, *refs):
    half = pl.num_programs(0) // 2

    @pl.when(pl.program_id(0) < half)
    def _():
        store_parts(dot_t(dgate[...], gate_own[...]) + dot_t(dup[...], up_own[...]), refs)

    @pl.when(pl.program_id(0) >= half)
    def _():
        store_parts(dot_t(dgate[...], par[:, :FF4]) + dot_t(dup[...], par[:, GAP:]), refs)


def ffn_back(idx, dgate, dup, gate, up, gate_up):
    half = DH // TILE
    rows = pl.BlockSpec((ROWS, FF4), lambda i, idx: (0, 0))
    own = pl.BlockSpec((TILE, FF4), lambda i, idx: (jnp.minimum(i, half - 1), 0))
    par = pl.BlockSpec((TILE, GAP + FF4), lambda i, idx: (jnp.maximum(i - half, 0), 0))
    place = lambda i, idx: (0, i ^ (idx[1] * half))
    return pl.pallas_call(
        ffn_back_body,
        grid_spec=pltpu.PrefetchScalarGridSpec(
            num_scalar_prefetch=1,
            grid=(D // TILE,),
            in_specs=[rows, rows, own, own, par],
            out_specs=[pl.BlockSpec((n, TILE), place) for _, n in PIECES],
        ),
        out_shape=part_shapes(D),
        compiler_params=params(),
        cost_estimate=cost(4 * ROWS * D * FF4, 1.8e7),
        name="ffn_back",
    )(idx, dgate, dup, gate, up, gate_up)


GU_ROWS = FF4 // 128 * 64
PIECE = 2 * GU_ROWS + FF4 // 2
QS = 4


def ffn_grads_body(*refs):
    na, nb, cots = refs[0:5], refs[5:10], refs[10:15]
    hid, dgate, dup, out, hid_t = refs[15:]

    @pl.when(pl.program_id(0) == 0)
    def _():
        hid_t[...] = hid[...].T

    stack = lambda parts: jnp.concatenate([r[...] for r in parts], 0)
    rows = jnp.concatenate([stack(na), stack(nb)], 1).T
    for k, ref in enumerate((dgate, dup)):
        g = dot(rows, ref[...]).astype(BF16)
        for h in range(2):
            for q in range(QS):
                r = g[(QS * h + q) * 64 : (QS * h + q + 1) * 64]
                for c in range(FF4 // 128):
                    first = k * GU_ROWS + c * 64
                    out[h, q, first : first + 64, :] = r[:, c * 128 : (c + 1) * 128]
    g = dot(hid_t[...], stack(cots)).astype(BF16)
    for h in range(2):
        for q in range(QS):
            out[h, q, 2 * GU_ROWS :, :] = g[
                h * (FF4 // 2) : (h + 1) * (FF4 // 2), q * 128 : (q + 1) * 128
            ]


def ffn_grads(normed, cots, hid, dgate, dup):
    return pl.pallas_call(
        ffn_grads_body,
        grid=(16 // QS,),
        out_shape=sds((2, 16, PIECE, 128)),
        in_specs=[pl.BlockSpec((n, 64 * QS), lambda i: (0, i)) for _, n in PIECES]
        + [pl.BlockSpec((n, 64 * QS), lambda i: (0, i + 16 // QS)) for _, n in PIECES]
        + [pl.BlockSpec((n, 128 * QS), lambda i: (0, i)) for _, n in PIECES]
        + [whole(ROWS, FF4)] * 3,
        out_specs=pl.BlockSpec((2, QS, PIECE, 128), lambda i: (0, i, 0, 0)),
        scratch_shapes=[pltpu.VMEM((FF4, ROWS), BF16)],
        compiler_params=params(),
        cost_estimate=cost(6 * ROWS * D * FF4, 3e7),
        name="ffn_grads",
    )(*normed, *normed, *cots, hid, dgate, dup)


def unpack_body(piece, gate, up, down):
    for q in range(QS):
        rows = slice(q * 64, (q + 1) * 64)
        for k, ref in enumerate((gate, up)):
            for c in range(FF4 // 128):
                first = k * GU_ROWS + c * 64
                ref[rows, c * 128 : (c + 1) * 128] = piece[q, first : first + 64, :].astype(F32)
        down[:, q * 128 : (q + 1) * 128] = piece[q, 2 * GU_ROWS :, :].astype(F32)


def unpack(pieces):
    return pl.pallas_call(
        unpack_body,
        grid=(16 // QS,),
        out_shape=(sds((DH, FF4), F32), sds((DH, FF4), F32), sds((FF4 // 2, D), F32)),
        in_specs=[pl.BlockSpec((QS, PIECE, 128), lambda i: (i, 0, 0))],
        out_specs=[
            pl.BlockSpec((64 * QS, FF4), lambda i: (i, 0)),
            pl.BlockSpec((64 * QS, FF4), lambda i: (i, 0)),
            pl.BlockSpec((FF4 // 2, 128 * QS), lambda i: (0, i)),
        ],
        compiler_params=params(),
        cost_estimate=cost(1e6, 2.6e7),
        name="unpack",
    )(pieces)


QP = 4 * 128
OP = 2 * (AW // 2)
QOP = QP + OP
KVP = 128 + 16
TAIL = QOP + KVP


def attn_grads_body(idx, *refs):
    na, nb, branch = refs[0:5], refs[5:10], refs[10:15]
    dqm, att, mine, theirs, att_t = refs[15:]
    core = idx[3]

    @pl.when(pl.program_id(0) == 0)
    def _():
        att_t[...] = att[...].T

    stack = lambda parts: jnp.concatenate([r[...] for r in parts], 0)

    def store(h, first, n, zero, one):
        mine[0, h, first : first + n, :] = jnp.where(core == 0, zero, one)
        theirs[0, h, first : first + n, :] = jnp.where(core == 0, one, zero)

    for h, cols in enumerate((na, nb)):
        g = dot(stack(cols).T, dqm[...]).astype(BF16)
        for c in range(4):
            lanes = slice(c * 128, (c + 1) * 128)
            store(h, c * 128, 128, g[:128, lanes], g[128:, lanes])
    g = dot(att_t[...], stack(branch)).astype(BF16)
    for h in range(2):
        r = g[h * (AW // 2) : (h + 1) * (AW // 2)]
        for c in range(2):
            lanes = lambda k: slice(k * 256 + c * 128, k * 256 + (c + 1) * 128)
            store(h, QP + c * (AW // 2), AW // 2, r[:, lanes(0)], r[:, lanes(1)])


def attn_grads(idx, normed, branch, dqm, att):
    turn = lambda s, idx: (s + idx[2]) & 3
    piece = pl.BlockSpec((1, 2, QOP, 128), lambda s, idx: (s, 0, 0, 0))
    fixed = pl.BlockSpec((ROWS, AW), lambda s, idx: (0, 0))
    return pl.pallas_call(
        attn_grads_body,
        grid_spec=pltpu.PrefetchScalarGridSpec(
            num_scalar_prefetch=1,
            grid=(4,),
            in_specs=[pl.BlockSpec((n, 256), lambda s, idx: (0, turn(s, idx))) for _, n in PIECES]
            + [pl.BlockSpec((n, 256), lambda s, idx: (0, turn(s, idx) + 4)) for _, n in PIECES]
            + [pl.BlockSpec((n, 512), lambda s, idx: (0, turn(s, idx))) for _, n in PIECES]
            + [fixed, fixed],
            out_specs=[piece, piece],
            scratch_shapes=[pltpu.VMEM((AW, ROWS), BF16)],
        ),
        out_shape=(sds((4, 2, QOP, 128)),) * 2,
        compiler_params=params(),
        cost_estimate=cost(4 * ROWS * D * AW, 1e7),
        name="attn_grads",
    )(idx, *normed, *normed, *branch, dqm, att)


def small_call(body, out_shape, *args, name):
    return pl.pallas_call(
        body,
        out_shape=out_shape,
        in_specs=[spec(pltpu.SMEM)] + [spec()] * (len(args) - 1),
        out_specs=jax.tree.map(lambda _: spec(), out_shape),
        compiler_params=params(),
        cost_estimate=cost(1e6, 4e6),
        name=name,
    )(*args)


def add(*values):
    return sum((v.astype(F32) for v in values[1:]), values[0].astype(F32)).astype(BF16)


def sum_core_body(idx, a, b, c, d, *outs):
    for s, out in enumerate(outs):
        out[:, :QOP, :] = add(a[s], b[s])
        out[:, QOP:, :] = add(c[s], d[s])


def sum_y_body(idx, a, b, c, d, own, other):
    zh = idx[1]
    own[...] = add(a[zh], b[zh], c[zh], d[zh])
    far = 1 - zh
    other[...] = add(a[far], b[far], c[far], d[far])


def sum_z_body(idx, a, b, c, d, out):
    out[...] = add(a[...], b[...], c[...], d[...])


def unpack_tail_body(idx, *refs):
    y, core = idx[2], idx[3]
    qkv, out, gains = refs[8:]
    for k in range(8):
        piece = refs[k]
        p = ((y - k % 4) & 3) * 2 + (core if k < 4 else 1 - core)
        rows = pl.ds(pl.multiple_of(p * 128, 128), 128)
        for c in range(4):
            qkv[rows, c * 128 : (c + 1) * 128] = piece[c * 128 : (c + 1) * 128, :].astype(F32)
        qkv[rows, AW:] = piece[QOP : QOP + 128, :].astype(F32).T
        g = piece[QOP + 128 :, :].astype(F32)
        for c in range(2):
            first = QP + c * (AW // 2)
            cols = pl.ds(pl.multiple_of(p * 256 + c * 128, 128), 128)
            out[:, cols] = piece[first : first + AW // 2, :].astype(F32)
            gains[:, cols] = g[2 * c : 2 * c + 2]


def sum_tail(idx, first, second, before):
    got_a = lax.ppermute(first[1], "core", shift(2, 1))
    got_b = lax.ppermute(second[1], "core", shift(2, 1))
    part = sds((2, TAIL, 128))
    g = small_call(sum_core_body, (part,) * 4, idx, first[0], got_a, second[0], got_b, name="sum_core")
    summed = g[0]
    got = [tie(lax.ppermute(g[s], "y", shift(4, s)), before) for s in (2, 1, 3)]
    part = sds((TAIL, 128))
    own, other = small_call(sum_y_body, (part,) * 2, idx, g[0], *got, name="sum_y")
    cross = [(2 * a + b, 2 * (1 - a) + (1 - b)) for a in range(2) for b in range(2)]
    g = small_call(
        sum_z_body,
        part,
        idx,
        own,
        lax.ppermute(own, "zl", shift(2, 1)),
        lax.ppermute(other, "zh", shift(2, 1)),
        lax.ppermute(other, ("zl", "zh"), cross),
        name="sum_z",
    )
    mine = [g] + [lax.ppermute(g, "y", shift(4, s)) for s in (1, 2, 3)]
    theirs = [lax.ppermute(v, "core", shift(2, 1)) for v in mine]
    shapes = (sds((DH, QW), F32), sds((AW // 2, D), F32), sds((2, D), F32))
    return summed, small_call(unpack_tail_body, shapes, idx, *mine, *theirs, name="unpack_tail")


def inverse_rms(v):
    return lax.rsqrt(jnp.mean(v * v, axis=-1, keepdims=True) + EPSILON)


def norm_back(v, r, gain, grad):
    pulled = grad * gain
    inner = jnp.mean(v * pulled, axis=-1, keepdims=True)
    return r * pulled - v * (r * r * r) * inner, jnp.sum(grad * v * r, axis=0)


def replica_layout(lengths, replica, replica_id):
    sizes = jnp.where(replica == replica_id, lengths, 0)
    starts = jnp.cumsum(sizes) - sizes
    row_ids = jnp.arange(CAP, dtype=jnp.int32)
    inside = (row_ids[:, None] >= starts[None, :]) & (row_ids[:, None] < (starts + sizes)[None, :])
    begin = jnp.sum(jnp.where(inside, starts[None, :], 0), axis=1)
    begin = begin + jnp.where(jnp.any(inside, axis=1), 0, jnp.sum(sizes))
    return begin, row_ids - begin


def on_device(
    tokens, cotangent, gain_one, qkv_weight, out_weight, gate_weight, up_weight, down_weight,
    gain_two, seq_lengths, seq_replica,
):
    x, zh, core = lax.axis_index("x"), lax.axis_index("zh"), lax.axis_index("core")
    y, zl = lax.axis_index("y"), lax.axis_index("zl")
    idx = jnp.stack([x, zh, y, core]).astype(jnp.int32)

    tok = tokens.astype(F32)
    s_one = inverse_rms(tok)
    qkv_all = fetch_partner(qkv_weight, core)
    normed_one = gather_x((tok * s_one * gain_one).astype(BF16))
    out_all = fetch_partner(out_weight, core, normed_one[2])
    cots = gather_x(tie(cotangent, normed_one[2]))

    begin, position = replica_layout(seq_lengths, seq_replica, (y * 2 + zl) * 2 + core)
    half_rows = lambda v: lax.dynamic_index_in_dim(v.reshape(4, 2, BLK), zh, 1, False).reshape(ROWS, 1)
    first = jnp.tile(half_rows(begin)[3 * BLK :, 0], 8).reshape(1, QALL)
    lane = jnp.arange(128, dtype=jnp.int32)
    frequency = ROTARY_BASE ** (-(lane % 32).astype(F32) * (2.0 / HD))
    angles = half_rows(position).astype(F32) * frequency[None, :]
    cosine = jnp.cos(angles)
    sine = jnp.where((lane % HD) < HD // 2, -1.0, 1.0)[None, :] * jnp.sin(angles)

    q, kv_own = qkv_forward(idx, normed_one, qkv_all, cosine, sine)
    kv_par = lax.ppermute(kv_own, "zh", shift(2, 1))
    rows = DH // 8
    mine = lambda w: lax.dynamic_slice_in_dim(w, (y * 2 + core) * rows, rows, 0)
    cross = [(2 * a + b, 2 * (1 - a) + (1 - b)) for a in range(2) for b in range(2)]
    gate_up = lax.ppermute(
        jnp.concatenate(
            [
                tie(mine(gate_weight), kv_par),
                jnp.zeros((rows, GAP - FF4), BF16),
                mine(up_weight),
            ],
            1,
        ),
        ("zl", "zh"),
        cross,
    )
    down_got = fetch_half(tie(down_weight, kv_par), core)
    q = tie(q, cots[1], cots[4], out_all[1])
    att, qx = attend(idx, q, kv_own, kv_par, first)
    gate_up = lax.all_gather(tie(gate_up, qx), ("y", "core"), axis=0, tiled=True)
    parts = [tie(p, cots[2], cots[3]) for p in out_project(idx, att, out_all)]
    after_attn = tok + scatter_x(parts)[0]

    r_two = inverse_rms(after_attn)
    normed_two = gather_x((after_attn * r_two * gain_two).astype(BF16))
    down_all = down_weight, down_got, lax.ppermute(tie(down_got, normed_two[1], normed_two[4]), "core", shift(2, 1))
    hid, dgate, dup = ffn(idx, normed_two, cots, gate_weight, up_weight, gate_up, down_all)
    own_grads = ffn_grads(normed_two, cots, hid, dgate, dup)
    grads = lax.psum_scatter(
        own_grads.reshape(32, PIECE, 128), ("zh", "zl", "y", "core"), scatter_dimension=0, tiled=True
    )
    d_two, _ = scatter_x(
        ffn_back(idx, tie(dgate, own_grads), dup, gate_weight, up_weight, gate_up)
    )
    back_two, gain_grad_two = norm_back(after_attn, r_two, gain_two, d_two)
    after_grad = cotangent.astype(F32) + back_two
    branch = gather_x(after_grad.astype(BF16))
    layer_parts = down_project(idx, tie(hid, after_grad), down_all)
    att = tie(att, *layer_parts)
    layer = [layer_parts[0]] + [
        lax.ppermute(tie(layer_parts[k], branch[2], branch[3]), "x", shift(4, k)) for k in (1, 3)
    ]
    dqm, dkv_own, dkv_par = attend_back(
        idx, qx, kv_own, kv_par, first, att, cosine, sine, branch, out_all
    )
    dkv_got = lax.ppermute(dkv_par, "zh", shift(2, 1))
    tail = attn_grads(
        idx, normed_one, branch, dqm.reshape(ROWS, AW), tie(att, *layer).reshape(ROWS, AW)
    )
    *tail_kv, parts = qkv_back(
        idx, dqm.reshape(ROWS, AW), dkv_own, dkv_got, cosine, sine, qkv_all, normed_one, gain_one,
        gain_grad_two,
    )
    d_one, first_step = scatter_x(parts)
    layer.append(lax.ppermute(tie(layer_parts[2], d_one), "x", shift(4, 2)))
    layer_out = sum((v.astype(F32) for v in layer), after_attn).astype(BF16)
    back_one, _ = norm_back(tok, s_one, gain_one, d_one)
    input_grad = (after_grad + back_one).astype(BF16)

    over_x = lambda v: sum((lax.ppermute(v, "x", shift(4, s)) for s in (1, 2, 3)), v)
    tail = tie(tail[0], *first_step), tie(tail[1], dkv_got)
    summed, (grad_qkv, grad_out, gains) = sum_tail(idx, tail, tail_kv, d_one)
    grads = lax.all_gather(tie(grads, summed), ("zl", "y", "core"), axis=0, tiled=True)
    grad_gate, grad_up, grad_down = unpack(grads)
    gains = over_x(gains)
    return (
        layer_out, input_grad, gains[0], grad_qkv, grad_out, grad_gate, grad_up,
        grad_down, gains[1],
    )


def solution(mesh):
    grid = Mesh(mesh.devices.reshape(SIZES), AXES)
    rows = P(AXES, None)
    both = P(("x", "zh"), None)
    return jax.shard_map(
        on_device,
        mesh=grid,
        in_specs=(
            rows, rows, P(), P("zh", "x"), both, P("zh", "x"), P("zh", "x"), both, P(), P(), P(),
        ),
        out_specs=(
            rows, rows, P(), P("zh", "x"), both, P("zh", "x"), P("zh", "x"), both, P(),
        ),
        check_vma=False,
    )
```

```python
import jax
import jax.numpy as jnp
from jax import lax
from jax.experimental import pallas as pl
from jax.experimental.pallas import tpu as pltpu
from jax.sharding import Mesh
from jax.sharding import PartitionSpec as P

HEADS = 32
KV = 4
HD = 64
EPSILON = 1e-05
ROTARY_BASE = 10000.0
MASKED = -1e30

AXES = ("y", "zl", "core", "x", "zh")
SIZES = (4, 2, 2, 4, 2)
BLK = 160
HALF = BLK // 2
ROWS = 4 * BLK
CAP = 2 * ROWS
D = 2048
DH = D // 2
QW = 640
AW = 512
FF4 = 1408
TILE = 256
F32 = jnp.float32
BF16 = jnp.bfloat16
VLIM = 60 * 1024 * 1024


def spec(memory=pltpu.VMEM):
    return pl.BlockSpec(memory_space=memory)


def params(**kw):
    return pltpu.CompilerParams(vmem_limit_bytes=VLIM, **kw)


def cost(flops, nbytes):
    return pl.CostEstimate(flops=int(flops), bytes_accessed=int(nbytes), transcendentals=0)


def sds(shape, dtype=BF16):
    return jax.ShapeDtypeStruct(shape, dtype)


def dot(a, b):
    return jnp.dot(a, b, preferred_element_type=F32)


def dot_t(a, b):
    return lax.dot_general(a, b, (((1,), (1,)), ((), ())), preferred_element_type=F32)


def t_dot(a, b):
    return lax.dot_general(a, b, (((0,), (0,)), ((), ())), preferred_element_type=F32)


def tie(v, *deps):
    return lax.optimization_barrier((v,) + deps)[0]


def shift(n, s):
    return [(i, (i + s) % n) for i in range(n)]


def gather_x(v):
    from_prev = lax.ppermute(v, "x", shift(4, 1))
    from_next = lax.ppermute(v, "x", shift(4, -1))
    send_a = tie(from_prev[:HALF], from_next)
    send_b = tie(from_next[HALF:], from_prev)
    opp_a = lax.ppermute(send_a, "x", shift(4, 1))
    opp_b = lax.ppermute(send_b, "x", shift(4, -1))
    return v, from_next, opp_a, opp_b, from_prev


def scatter_x(parts, *deps):
    p0, p1, p2a, p2b, p3 = parts
    got_a = lax.ppermute(p2a, "x", shift(4, 1))
    got_b = tie(lax.ppermute(p2b, "x", shift(4, -1)), *deps)
    q1 = jnp.concatenate([(p1[:HALF].astype(F32) + got_a.astype(F32)).astype(BF16), p1[HALF:]], 0)
    q3 = jnp.concatenate([p3[:HALF], (p3[HALF:].astype(F32) + got_b.astype(F32)).astype(BF16)], 0)
    from_prev = lax.ppermute(q1, "x", shift(4, 1))
    from_next = lax.ppermute(q3, "x", shift(4, -1))
    return p0.astype(F32) + from_prev.astype(F32) + from_next.astype(F32), (got_a, got_b)


PIECES = ((0, BLK), (1, BLK), (2, HALF), (2, HALF), (3, BLK))
PIECE_ROW = (0, BLK, 2 * BLK, 2 * BLK + HALF, 3 * BLK)


def part_shapes(width, dtype=BF16):
    return tuple(sds((n, width), dtype) for _, n in PIECES)


def low_lanes(shape):
    return lax.broadcasted_iota(jnp.int32, shape, 1) < HD


def swap_halves(v):
    lane = lax.broadcasted_iota(jnp.int32, v.shape, 1) % HD
    return jnp.where(lane < HD // 2, pltpu.roll(v, 128 - HD // 2, 1), pltpu.roll(v, HD // 2, 1))


def rows_at(block):
    return pl.ds(pl.multiple_of(block * BLK, 32), BLK)


def fetch_half(w, core):
    half = w.shape[0] // 2
    return lax.ppermute(lax.dynamic_slice_in_dim(w, core * half, half, 0), "zh", shift(2, 1))


def fetch_partner(w, core, *deps):
    got = fetch_half(tie(w, *deps), core)
    return w, got, lax.ppermute(got, "core", shift(2, 1))


def weight_rows(idx, rows):
    zh, core = idx[1], idx[3]
    far = (1 - zh) * rows
    half = rows // 2
    at = lambda first, n: pl.ds(pl.multiple_of(first, half), n)
    return at(zh * rows, rows), at(far + core * half, half), at(far + (1 - core) * half, half)


def qkv_body(idx, n0, n1, n2a, n2b, n3, w0, w1, w2, cosine, sine, q_ref, kv_ref, rows):
    x = idx[0]
    lo = low_lanes((BLK, 128))
    for ref, row, (_, n) in zip((n0, n1, n2a, n2b, n3), PIECE_ROW, PIECES):
        rows[row : row + n, :] = ref[...]
    s0, s1, s2 = weight_rows(idx, DH)
    acc = dot(rows[:, s0], w0[...]) + dot(rows[:, s1], w1[...]) + dot(rows[:, s2], w2[...])
    for d in range(4):
        at = rows_at((x + d) & 3)
        cs = cosine[at, :]
        sn = sine[at, :]
        for p in range(5):
            v = acc[d * BLK : (d + 1) * BLK, p * 128 : (p + 1) * 128]
            r = v * cs + swap_halves(v) * sn
            if p < 4:
                r = r * (HD**-0.5 * LOG2E)
                a = (x + d) & 3
                for k, w in enumerate((r, pltpu.roll(r, HD, 1))):
                    head = slice((2 * p + k) * BLK, (2 * p + k + 1) * BLK)
                    q_ref[a, head, :] = jnp.where(lo, w, 0.0).astype(BF16)
            else:
                kv_ref[at, :] = jnp.where(lo, r, v).astype(BF16)


def qkv_forward(idx, pieces, weight, cosine, sine):
    return pl.pallas_call(
        qkv_body,
        out_shape=(sds((4, QALL, 128)), sds((ROWS, 128))),
        in_specs=[spec(pltpu.SMEM)] + [spec()] * 10,
        out_specs=(spec(), spec()),
        scratch_shapes=[pltpu.VMEM((ROWS, D), BF16)],
        compiler_params=params(),
        cost_estimate=cost(2 * ROWS * D * QW, 7e6),
        name="qkv_forward",
    )(idx, *pieces, *weight, cosine, sine)


QALL = 8 * BLK
PAIR = 2 * BLK
LOG2E = 1.4426950408889634
LN2 = 0.6931471805599453


def split3(v):
    a = v.astype(BF16).astype(F32)
    b = (v - a).astype(BF16).astype(F32)
    return a, b, v - a - b


def with_lanes(v, parts):
    lane = lax.broadcasted_iota(jnp.int32, v.shape, 1)
    out = jnp.where(lane < HD, v, 0.0)
    for k, part in enumerate(parts):
        out = jnp.where(lane == HD + k, part, out)
    return out


def spread_keys(zh, kv_own, kv_par, kk, vv, fill):
    shape = (BLK, 128)
    lo = low_lanes(shape)
    rest = fill(lax.broadcasted_iota(jnp.int32, shape, 1) - HD)
    for j in range(4):
        for src, off in ((kv_own, zh), (kv_par, 1 - zh)):
            v = src[j * BLK : (j + 1) * BLK, :].astype(F32)
            at = rows_at(2 * j + off)
            kk[at, :] = jnp.where(lo, v, rest).astype(BF16)
            vv[at, :] = jnp.where(lo, pltpu.roll(v, HD, 1), rest).astype(BF16)


def masked(s, zh, j, kb, first):
    if j < 3 and kb < j:
        return s
    u = kb * PAIR + lax.broadcasted_iota(jnp.int32, (PAIR, QALL), 0)
    allowed = None
    if kb == j:
        t = (2 * j + zh) * BLK + lax.broadcasted_iota(jnp.int32, (1, QALL), 1) % BLK
        allowed = u <= t
    if j == 3:
        later = u >= first[...]
        allowed = later if allowed is None else allowed & later
    return jnp.where(allowed, s, MASKED)


def attend_body(idx, q, kv_own, kv_par, first, att, qx, kk, vv, vt, s_ref, e_ref):
    x, zh = idx[0], idx[1]
    spread_keys(zh, kv_own, kv_par, kk, vv, lambda lane: 1.0)
    vt[...] = vv[...].T
    lo = low_lanes((BLK, 128))
    for j in range(4):
        n = PAIR * (j + 1)
        qj = q[j]
        top = jnp.full((1, QALL), MASKED, F32)
        for kb in range(j + 1):
            rows = slice(kb * PAIR, (kb + 1) * PAIR)
            s = masked(dot_t(kk[rows, :], qj), zh, j, kb, first)
            s_ref[rows, :] = s
            top = jnp.maximum(top, jnp.max(s, axis=0, keepdims=True))
        for k in range(n // 64):
            rows = slice(k * 64, (k + 1) * 64)
            e_ref[rows, :] = jnp.exp2(s_ref[rows, :] - top).astype(BF16)
        o = dot(vt[:, :n], e_ref[:n, :])
        lse = split3(top + jnp.log(o[HD : HD + 1, :]) * LOG2E)
        row = lax.broadcasted_iota(jnp.int32, (128, QALL), 0)
        extra = jnp.zeros((128, QALL), F32)
        for k, part in enumerate(lse):
            extra = jnp.where(row == HD + k, part, extra)
        qx[j] = (qj.astype(F32) + extra.T).astype(BF16)
        o = o.T
        r = pltpu.roll(o, HD, 1)
        rel = (j - x) & 3
        for p in range(4):
            even, odd = slice(2 * p * BLK, (2 * p + 1) * BLK), slice((2 * p + 1) * BLK, (2 * p + 2) * BLK)
            num = jnp.where(lo, o[even], r[odd])
            den = jnp.where(lo, r[even], o[odd])
            att[rel, :, p * 128 : (p + 1) * 128] = (num / den).astype(BF16)


def attend(idx, q, kv_own, kv_par, first):
    return pl.pallas_call(
        attend_body,
        out_shape=(sds((4, BLK, AW)), sds((4, QALL, 128))),
        in_specs=[spec(pltpu.SMEM)] + [spec()] * 4,
        out_specs=(spec(), spec()),
        scratch_shapes=[
            pltpu.VMEM((CAP, 128), BF16),
            pltpu.VMEM((CAP, 128), BF16),
            pltpu.VMEM((128, CAP), BF16),
            pltpu.VMEM((CAP, QALL), F32),
            pltpu.VMEM((CAP, QALL), BF16),
        ],
        compiler_params=params(),
        cost_estimate=cost(1.2e10, 3e6),
        name="attend",
    )(idx, q, kv_own, kv_par, first)


def store_parts(res, refs):
    for ref, row, (_, n) in zip(refs, PIECE_ROW, PIECES):
        ref[...] = res[row : row + n].astype(BF16)


def out_body(idx, att, w0, w1, w2, o0, o1, o2a, o2b, o3):
    s0, s1, s2 = weight_rows(idx, AW // 2)
    for d, ref in ((2, None), (1, o1), (3, o3), (0, o0)):
        a = att.at[d]
        res = dot(a[:, s0], w0[...]) + dot(a[:, s1], w1[...]) + dot(a[:, s2], w2[...])
        res = res.astype(BF16)
        if d == 2:
            o2a[...] = res[:HALF]
            o2b[...] = res[HALF:]
        else:
            ref[...] = res


def out_project(idx, att, weight):
    return pl.pallas_call(
        out_body,
        out_shape=part_shapes(D),
        in_specs=[spec(pltpu.SMEM)] + [spec()] * 4,
        out_specs=(spec(),) * 5,
        compiler_params=params(),
        cost_estimate=cost(2 * ROWS * D * AW, 5.5e6),
        name="out_project",
    )(idx, att, *weight)


def stack_heads(v):
    return v, pltpu.roll(v, HD, 1)


def attend_back_body(
    idx, qx, kv_own, kv_par, first, att, cosine, sine, b0, b1, b2a, b2b, b3, w0, w1, w2,
    dq_ref, dkv_own, dkv_par, kk, vv, dout, do_all, dkk, dvv, e_ref, ds_ref, dq_acc,
):
    x, zh = idx[0], idx[1]
    spread_keys(zh, kv_own, kv_par, kk, vv, lambda lane: jnp.where(lane < 3, -1.0, 0.0))
    s0, s1, s2 = weight_rows(idx, AW // 2)
    for d in range(4):
        if d == 2:
            rows = jnp.concatenate([b2a[...], b2b[...]], 0)
        else:
            rows = (b0, b1, None, b3)[d][...]
        at = rows_at((x + d) & 3)
        for s, w in ((s0, w0), (s1, w1), (s2, w2)):
            dout[at, s] = dot_t(rows, w[...]).astype(BF16)
    lo = low_lanes((BLK, 128))
    for j in range(4):
        rel = (j - x) & 3
        here = slice(j * BLK, (j + 1) * BLK)
        for p in range(4):
            cols = slice(p * 128, (p + 1) * 128)
            do = dout[here, cols].astype(F32)
            prod = do * att[rel, :, cols].astype(F32)
            for k, (v, w) in enumerate(zip(stack_heads(do), stack_heads(prod))):
                delta = jnp.sum(jnp.where(lo, w, 0.0), axis=1, keepdims=True)
                head = slice((2 * p + k) * BLK, (2 * p + k + 1) * BLK)
                do_all[head, :] = with_lanes(v, split3(delta)).astype(BF16)
        for kb in range(j + 1):
            rows = slice(kb * PAIR, (kb + 1) * PAIR)
            e = jnp.exp2(masked(dot_t(kk[rows, :], qx[j]), zh, j, kb, first))
            e_ref[...] = e.astype(BF16)
            ds_ref[...] = (e * dot_t(vv[rows, :], do_all[...])).astype(BF16)
            dv = dot(e_ref[...], do_all[...])
            dk = dot(ds_ref[...], qx[j])
            dq = t_dot(ds_ref[...], kk[rows, :])
            if kb == j:
                dvv[rows, :], dkk[rows, :] = dv, dk
            else:
                dvv[rows, :] += dv
                dkk[rows, :] += dk
            if kb == 0:
                dq_acc[...] = dq
            else:
                dq_acc[...] += dq
        for p in range(4):
            even, odd = slice(2 * p * BLK, (2 * p + 1) * BLK), slice((2 * p + 1) * BLK, (2 * p + 2) * BLK)
            v = jnp.where(lo, dq_acc[even, :], pltpu.roll(dq_acc[odd, :], HD, 1)) * HD**-0.5
            v = v * cosine[here, :] - swap_halves(v) * sine[here, :]
            dq_ref[rel, :, p * 128 : (p + 1) * 128] = v.astype(BF16)
    for j in range(4):
        for dst, off in ((dkv_own, zh), (dkv_par, 1 - zh)):
            at = rows_at(2 * j + off)
            both = jnp.where(lo, dkk[at, :] * LN2, pltpu.roll(dvv[at, :], HD, 1))
            dst[j * BLK : (j + 1) * BLK, :] = both.astype(dst.dtype)


def attend_back(idx, qx, kv_own, kv_par, first, att, cosine, sine, branch, weight):
    return pl.pallas_call(
        attend_back_body,
        out_shape=(sds((4, BLK, AW)), sds((ROWS, 128), F32), sds((ROWS, 128))),
        in_specs=[spec(pltpu.SMEM)] + [spec()] * 15,
        out_specs=(spec(),) * 3,
        scratch_shapes=[
            pltpu.VMEM((CAP, 128), BF16),
            pltpu.VMEM((CAP, 128), BF16),
            pltpu.VMEM((ROWS, AW), BF16),
            pltpu.VMEM((QALL, 128), BF16),
            pltpu.VMEM((CAP, 128), F32),
            pltpu.VMEM((CAP, 128), F32),
            pltpu.VMEM((PAIR, QALL), BF16),
            pltpu.VMEM((PAIR, QALL), BF16),
            pltpu.VMEM((QALL, 128), F32),
        ],
        compiler_params=params(),
        cost_estimate=cost(3e10, 8e6),
        name="attend_back",
    )(idx, qx, kv_own, kv_par, first, att, cosine, sine, *branch, *weight)


def qkv_back_body(
    idx, dqm, dkv_own, dkv_got, cosine, sine, w0, w1, w2, n0, n1, n2a, n2b, n3, gain_one,
    gain_grad_two,
    mine, theirs, o0, o1, o2a, o2b, o3, n_all, dkv, grad, gains,
):
    x, y, core = idx[0], idx[2], idx[3]
    lo = low_lanes((BLK, 128))
    for ref, row, (_, n) in zip((n0, n1, n2a, n2b, n3), PIECE_ROW, PIECES):
        n_all[row : row + n, :] = ref[...]
    for d in range(4):
        at = rows_at((x + d) & 3)
        v = dkv_own[at, :] + dkv_got[at, :].astype(F32)
        v = jnp.where(lo, v * cosine[at, :] - swap_halves(v) * sine[at, :], v).astype(BF16)
        dkv[d * BLK : (d + 1) * BLK, :] = v
    rows = jnp.concatenate([dqm[...], dkv[...]], 1)
    for s, w in zip(weight_rows(idx, DH), (w0, w1, w2)):
        for c in range(w.shape[0] // 512):
            cols = pl.ds(pl.multiple_of(s.start + c * 512, 512), 512)
            res = dot_t(rows, w[c * 512 : (c + 1) * 512, :])
            part = (res * n_all[:, cols].astype(F32)).reshape(ROWS // 8, 8, 512)
            gains[0:1, cols] = jnp.sum(jnp.sum(part, axis=0), axis=0, keepdims=True) / gain_one[:, cols]
            store_parts(res, [r.at[:, cols] for r in (o0, o1, o2a, o2b, o3)])
    grad[...] = dot(dkv[...].T, n_all[...]).astype(BF16)
    gains[1:2, :] = gain_grad_two[...]
    for s in range(4):
        for k, ref in enumerate((mine, theirs)):
            p = ((y + s) & 3) * 2 + (core if k == 0 else 1 - core)
            both = gains[:, pl.ds(pl.multiple_of(p * 256, 256), 256)]
            both = jnp.concatenate([both[:, :128], both[:, 128:], jnp.zeros((12, 128), F32)], 0)
            for h in range(2):
                ref[s, h, :128, :] = grad[:, pl.ds(pl.multiple_of(h * DH + p * 128, 128), 128)]
                ref[s, h, 128:, :] = both.astype(BF16)


def qkv_back(idx, dqm, dkv_own, dkv_got, cosine, sine, weight, pieces, gain_one, gain_grad_two):
    res = pl.pallas_call(
        qkv_back_body,
        out_shape=(sds((4, 2, KVP, 128)),) * 2 + part_shapes(D),
        in_specs=[spec(pltpu.SMEM)] + [spec()] * 15,
        out_specs=(spec(),) * 7,
        scratch_shapes=[
            pltpu.VMEM((ROWS, D), BF16),
            pltpu.VMEM((ROWS, 128), BF16),
            pltpu.VMEM((128, D), BF16),
            pltpu.VMEM((2, D), F32),
        ],
        compiler_params=params(),
        cost_estimate=cost(2 * ROWS * D * QW, 1.3e7),
        name="qkv_back",
    )(
        idx, dqm, dkv_own, dkv_got, cosine, sine, *weight, *pieces,
        gain_one.reshape(1, D), gain_grad_two.reshape(1, D),
    )
    return res[0], res[1], res[2:]


TILES = 6
GAP = TILES * TILE


def load_down(idx, refs, dst, sem):
    copies = []
    for k, (s, ref) in enumerate(zip(weight_rows(idx, FF4 // 2), refs)):
        copies.append(pltpu.make_async_copy(ref, dst.at[s], sem.at[k]))
    return copies


def ffn_body(
    idx, n0, n1, n2a, n2b, n3, c0, c1, c2a, c2b, c3, gate_own, up_own, gate_par, up_par, w0, w1, w2,
    hid, dgate, dup, n_all, c_all, down, sem,
):
    i = pl.program_id(0)
    zh = idx[1]

    @pl.when(i == 0)
    def _():
        copies = load_down(idx, (w0, w1, w2), down, sem)
        for c in copies:
            c.start()
        for refs, dst in (((n0, n1, n2a, n2b, n3), n_all), ((c0, c1, c2a, c2b, c3), c_all)):
            for ref, row, (_, n) in zip(refs, PIECE_ROW, PIECES):
                dst[row : row + n, :] = ref[...]
        for c in copies:
            c.wait()

    own = n_all[:, pl.ds(pl.multiple_of(zh * DH, DH), DH)]
    par = n_all[:, pl.ds(pl.multiple_of((1 - zh) * DH, DH), DH)]
    gate = dot(own, gate_own[...]) + dot(par, gate_par[...])
    up = dot(own, up_own[...]) + dot(par, up_par[...])
    dh = dot_t(c_all[...], down[pl.ds(pl.multiple_of(i * TILE, TILE), TILE), :])
    sig = 1.0 / (1.0 + jnp.exp(-gate))
    act = gate * sig
    hid[...] = (act * up).astype(BF16)
    dgate[...] = (dh * up * sig * (1.0 + gate * (1.0 - sig))).astype(BF16)
    dup[...] = (dh * act).astype(BF16)


def whole(n, w):
    return pl.BlockSpec((n, w), lambda i: (0, 0))


def ffn(idx, normed, cots, gate, up, gate_up, down):
    column = lambda first: pl.BlockSpec((DH, TILE), lambda i: (0, i + first))
    hidden = pl.BlockSpec((ROWS, TILE), lambda i: (0, i))
    return pl.pallas_call(
        ffn_body,
        grid=(TILES,),
        out_shape=(sds((ROWS, FF4)),) * 3,
        in_specs=[spec(pltpu.SMEM)]
        + [whole(n, D) for _, n in PIECES] * 2
        + [column(0), column(0), column(0), column(TILES)]
        + [spec(pl.ANY)] * 3,
        out_specs=[hidden] * 3,
        scratch_shapes=[
            pltpu.VMEM((ROWS, D), BF16),
            pltpu.VMEM((ROWS, D), BF16),
            pltpu.VMEM((GAP, D), BF16),
            pltpu.SemaphoreType.DMA((3,)),
        ],
        compiler_params=params(),
        cost_estimate=cost(6 * ROWS * D * FF4, 3.4e7),
        name="ffn",
    )(idx, *normed, *cots, gate, up, gate_up, gate_up, *down)


def down_body(idx, hid, w0, w1, w2, o0, o1, o2, o3, down, sem):
    copies = load_down(idx, (w0, w1, w2), down, sem)
    for c in copies:
        c.start()
    for c in copies:
        c.wait()
    for n in range(D // 512):
        cols = slice(n * 512, (n + 1) * 512)
        res = dot(hid[...], down[:, cols]).astype(BF16)
        for d, ref in enumerate((o0, o1, o2, o3)):
            ref[:, cols] = res[d * BLK : (d + 1) * BLK]


def down_project(idx, hid, down):
    return pl.pallas_call(
        down_body,
        out_shape=(sds((BLK, D)),) * 4,
        in_specs=[spec(pltpu.SMEM), spec()] + [spec(pl.ANY)] * 3,
        out_specs=(spec(),) * 4,
        scratch_shapes=[pltpu.VMEM((FF4, D), BF16), pltpu.SemaphoreType.DMA((3,))],
        compiler_params=params(),
        cost_estimate=cost(2 * ROWS * D * FF4, 1.1e7),
        name="down_project",
    )(idx, hid, *down)


def ffn_back_body(idx, dgate, dup, gate_own, up_own, par, *refs):
    half = pl.num_programs(0) // 2

    @pl.when(pl.program_id(0) < half)
    def _():
        store_parts(dot_t(dgate[...], gate_own[...]) + dot_t(dup[...], up_own[...]), refs)

    @pl.when(pl.program_id(0) >= half)
    def _():
        store_parts(dot_t(dgate[...], par[:, :FF4]) + dot_t(dup[...], par[:, GAP:]), refs)


def ffn_back(idx, dgate, dup, gate, up, gate_up):
    half = DH // TILE
    rows = pl.BlockSpec((ROWS, FF4), lambda i, idx: (0, 0))
    own = pl.BlockSpec((TILE, FF4), lambda i, idx: (jnp.minimum(i, half - 1), 0))
    par = pl.BlockSpec((TILE, GAP + FF4), lambda i, idx: (jnp.maximum(i - half, 0), 0))
    place = lambda i, idx: (0, i ^ (idx[1] * half))
    return pl.pallas_call(
        ffn_back_body,
        grid_spec=pltpu.PrefetchScalarGridSpec(
            num_scalar_prefetch=1,
            grid=(D // TILE,),
            in_specs=[rows, rows, own, own, par],
            out_specs=[pl.BlockSpec((n, TILE), place) for _, n in PIECES],
        ),
        out_shape=part_shapes(D),
        compiler_params=params(),
        cost_estimate=cost(4 * ROWS * D * FF4, 1.8e7),
        name="ffn_back",
    )(idx, dgate, dup, gate, up, gate_up)


GU_ROWS = FF4 // 128 * 64
PIECE = 2 * GU_ROWS + FF4 // 2
QS = 4


def ffn_grads_body(*refs):
    na, nb, cots = refs[0:5], refs[5:10], refs[10:15]
    hid, dgate, dup, out, hid_t = refs[15:]

    @pl.when(pl.program_id(0) == 0)
    def _():
        hid_t[...] = hid[...].T

    stack = lambda parts: jnp.concatenate([r[...] for r in parts], 0)
    rows = jnp.concatenate([stack(na), stack(nb)], 1).T
    for k, ref in enumerate((dgate, dup)):
        g = dot(rows, ref[...]).astype(BF16)
        for h in range(2):
            for q in range(QS):
                r = g[(QS * h + q) * 64 : (QS * h + q + 1) * 64]
                for c in range(FF4 // 128):
                    first = k * GU_ROWS + c * 64
                    out[h, q, first : first + 64, :] = r[:, c * 128 : (c + 1) * 128]
    g = dot(hid_t[...], stack(cots)).astype(BF16)
    for h in range(2):
        for q in range(QS):
            out[h, q, 2 * GU_ROWS :, :] = g[
                h * (FF4 // 2) : (h + 1) * (FF4 // 2), q * 128 : (q + 1) * 128
            ]


def ffn_grads(normed, cots, hid, dgate, dup):
    return pl.pallas_call(
        ffn_grads_body,
        grid=(16 // QS,),
        out_shape=sds((2, 16, PIECE, 128)),
        in_specs=[pl.BlockSpec((n, 64 * QS), lambda i: (0, i)) for _, n in PIECES]
        + [pl.BlockSpec((n, 64 * QS), lambda i: (0, i + 16 // QS)) for _, n in PIECES]
        + [pl.BlockSpec((n, 128 * QS), lambda i: (0, i)) for _, n in PIECES]
        + [whole(ROWS, FF4)] * 3,
        out_specs=pl.BlockSpec((2, QS, PIECE, 128), lambda i: (0, i, 0, 0)),
        scratch_shapes=[pltpu.VMEM((FF4, ROWS), BF16)],
        compiler_params=params(),
        cost_estimate=cost(6 * ROWS * D * FF4, 3e7),
        name="ffn_grads",
    )(*normed, *normed, *cots, hid, dgate, dup)


def unpack_body(piece, gate, up, down):
    for q in range(QS):
        rows = slice(q * 64, (q + 1) * 64)
        for k, ref in enumerate((gate, up)):
            for c in range(FF4 // 128):
                first = k * GU_ROWS + c * 64
                ref[rows, c * 128 : (c + 1) * 128] = piece[q, first : first + 64, :].astype(F32)
        down[:, q * 128 : (q + 1) * 128] = piece[q, 2 * GU_ROWS :, :].astype(F32)


def unpack(pieces):
    return pl.pallas_call(
        unpack_body,
        grid=(16 // QS,),
        out_shape=(sds((DH, FF4), F32), sds((DH, FF4), F32), sds((FF4 // 2, D), F32)),
        in_specs=[pl.BlockSpec((QS, PIECE, 128), lambda i: (i, 0, 0))],
        out_specs=[
            pl.BlockSpec((64 * QS, FF4), lambda i: (i, 0)),
            pl.BlockSpec((64 * QS, FF4), lambda i: (i, 0)),
            pl.BlockSpec((FF4 // 2, 128 * QS), lambda i: (0, i)),
        ],
        compiler_params=params(),
        cost_estimate=cost(1e6, 2.6e7),
        name="unpack",
    )(pieces)


QP = 4 * 128
OP = 2 * (AW // 2)
QOP = QP + OP
KVP = 128 + 16
TAIL = QOP + KVP


def attn_grads_body(idx, *refs):
    na, nb, branch = refs[0:5], refs[5:10], refs[10:15]
    dqm, att, mine, theirs, att_t = refs[15:]
    core = idx[3]

    @pl.when(pl.program_id(0) == 0)
    def _():
        att_t[...] = att[...].T

    stack = lambda parts: jnp.concatenate([r[...] for r in parts], 0)

    def store(h, first, n, zero, one):
        mine[0, h, first : first + n, :] = jnp.where(core == 0, zero, one)
        theirs[0, h, first : first + n, :] = jnp.where(core == 0, one, zero)

    for h, cols in enumerate((na, nb)):
        g = dot(stack(cols).T, dqm[...]).astype(BF16)
        for c in range(4):
            lanes = slice(c * 128, (c + 1) * 128)
            store(h, c * 128, 128, g[:128, lanes], g[128:, lanes])
    g = dot(att_t[...], stack(branch)).astype(BF16)
    for h in range(2):
        r = g[h * (AW // 2) : (h + 1) * (AW // 2)]
        for c in range(2):
            lanes = lambda k: slice(k * 256 + c * 128, k * 256 + (c + 1) * 128)
            store(h, QP + c * (AW // 2), AW // 2, r[:, lanes(0)], r[:, lanes(1)])


def attn_grads(idx, normed, branch, dqm, att):
    turn = lambda s, idx: (s + idx[2]) & 3
    piece = pl.BlockSpec((1, 2, QOP, 128), lambda s, idx: (s, 0, 0, 0))
    fixed = pl.BlockSpec((ROWS, AW), lambda s, idx: (0, 0))
    return pl.pallas_call(
        attn_grads_body,
        grid_spec=pltpu.PrefetchScalarGridSpec(
            num_scalar_prefetch=1,
            grid=(4,),
            in_specs=[pl.BlockSpec((n, 256), lambda s, idx: (0, turn(s, idx))) for _, n in PIECES]
            + [pl.BlockSpec((n, 256), lambda s, idx: (0, turn(s, idx) + 4)) for _, n in PIECES]
            + [pl.BlockSpec((n, 512), lambda s, idx: (0, turn(s, idx))) for _, n in PIECES]
            + [fixed, fixed],
            out_specs=[piece, piece],
            scratch_shapes=[pltpu.VMEM((AW, ROWS), BF16)],
        ),
        out_shape=(sds((4, 2, QOP, 128)),) * 2,
        compiler_params=params(),
        cost_estimate=cost(4 * ROWS * D * AW, 1e7),
        name="attn_grads",
    )(idx, *normed, *normed, *branch, dqm, att)


def small_call(body, out_shape, *args, name):
    return pl.pallas_call(
        body,
        out_shape=out_shape,
        in_specs=[spec(pltpu.SMEM)] + [spec()] * (len(args) - 1),
        out_specs=jax.tree.map(lambda _: spec(), out_shape),
        compiler_params=params(),
        cost_estimate=cost(1e6, 4e6),
        name=name,
    )(*args)


def add(*values):
    return sum((v.astype(F32) for v in values[1:]), values[0].astype(F32)).astype(BF16)


def sum_core_body(idx, a, b, c, d, *outs):
    for s, out in enumerate(outs):
        out[:, :QOP, :] = add(a[s], b[s])
        out[:, QOP:, :] = add(c[s], d[s])


def sum_y_body(idx, a, b, c, d, own, other):
    zh = idx[1]
    own[...] = add(a[zh], b[zh], c[zh], d[zh])
    far = 1 - zh
    other[...] = add(a[far], b[far], c[far], d[far])


def sum_z_body(idx, a, b, c, d, out):
    out[...] = add(a[...], b[...], c[...], d[...])


def unpack_tail_body(idx, *refs):
    y, core = idx[2], idx[3]
    qkv, out, gains = refs[8:]
    for k in range(8):
        piece = refs[k]
        p = ((y - k % 4) & 3) * 2 + (core if k < 4 else 1 - core)
        rows = pl.ds(pl.multiple_of(p * 128, 128), 128)
        for c in range(4):
            qkv[rows, c * 128 : (c + 1) * 128] = piece[c * 128 : (c + 1) * 128, :].astype(F32)
        qkv[rows, AW:] = piece[QOP : QOP + 128, :].astype(F32).T
        g = piece[QOP + 128 :, :].astype(F32)
        for c in range(2):
            first = QP + c * (AW // 2)
            cols = pl.ds(pl.multiple_of(p * 256 + c * 128, 128), 128)
            out[:, cols] = piece[first : first + AW // 2, :].astype(F32)
            gains[:, cols] = g[2 * c : 2 * c + 2]


def sum_tail(idx, first, second, before):
    got_a = lax.ppermute(first[1], "core", shift(2, 1))
    got_b = lax.ppermute(second[1], "core", shift(2, 1))
    part = sds((2, TAIL, 128))
    g = small_call(sum_core_body, (part,) * 4, idx, first[0], got_a, second[0], got_b, name="sum_core")
    got = [tie(lax.ppermute(g[s], "y", shift(4, s)), before) for s in (2, 1, 3)]
    part = sds((TAIL, 128))
    own, other = small_call(sum_y_body, (part,) * 2, idx, g[0], *got, name="sum_y")
    cross = [(2 * a + b, 2 * (1 - a) + (1 - b)) for a in range(2) for b in range(2)]
    g = small_call(
        sum_z_body,
        part,
        idx,
        own,
        lax.ppermute(own, "zl", shift(2, 1)),
        lax.ppermute(other, "zh", shift(2, 1)),
        lax.ppermute(other, ("zl", "zh"), cross),
        name="sum_z",
    )
    mine = [g] + [lax.ppermute(g, "y", shift(4, s)) for s in (1, 2, 3)]
    theirs = [lax.ppermute(v, "core", shift(2, 1)) for v in mine]
    shapes = (sds((DH, QW), F32), sds((AW // 2, D), F32), sds((2, D), F32))
    return own, small_call(unpack_tail_body, shapes, idx, *mine, *theirs, name="unpack_tail")


def inverse_rms(v):
    return lax.rsqrt(jnp.mean(v * v, axis=-1, keepdims=True) + EPSILON)


def norm_back(v, r, gain, grad):
    pulled = grad * gain
    inner = jnp.mean(v * pulled, axis=-1, keepdims=True)
    return r * pulled - v * (r * r * r) * inner, jnp.sum(grad * v * r, axis=0)


def replica_layout(lengths, replica, replica_id):
    sizes = jnp.where(replica == replica_id, lengths, 0)
    starts = jnp.cumsum(sizes) - sizes
    row_ids = jnp.arange(CAP, dtype=jnp.int32)
    inside = (row_ids[:, None] >= starts[None, :]) & (row_ids[:, None] < (starts + sizes)[None, :])
    begin = jnp.sum(jnp.where(inside, starts[None, :], 0), axis=1)
    begin = begin + jnp.where(jnp.any(inside, axis=1), 0, jnp.sum(sizes))
    return begin, row_ids - begin


def on_device(
    tokens, cotangent, gain_one, qkv_weight, out_weight, gate_weight, up_weight, down_weight,
    gain_two, seq_lengths, seq_replica,
):
    x, zh, core = lax.axis_index("x"), lax.axis_index("zh"), lax.axis_index("core")
    y, zl = lax.axis_index("y"), lax.axis_index("zl")
    idx = jnp.stack([x, zh, y, core]).astype(jnp.int32)

    tok = tokens.astype(F32)
    s_one = inverse_rms(tok)
    qkv_all = fetch_partner(qkv_weight, core)
    normed_one = gather_x((tok * s_one * gain_one).astype(BF16))
    out_all = fetch_partner(out_weight, core, qkv_all[1], normed_one[1], normed_one[4])
    rows = DH // 8
    mine = lambda w: lax.dynamic_slice_in_dim(w, (y * 2 + core) * rows, rows, 0)
    cross = [(2 * a + b, 2 * (1 - a) + (1 - b)) for a in range(2) for b in range(2)]
    gate_up = lax.ppermute(
        jnp.concatenate(
            [
                tie(mine(gate_weight), out_all[1], normed_one[2], normed_one[3]),
                jnp.zeros((rows, GAP - FF4), BF16),
                mine(up_weight),
            ],
            1,
        ),
        ("zl", "zh"),
        cross,
    )
    cots = gather_x(tie(cotangent, normed_one[2]))

    begin, position = replica_layout(seq_lengths, seq_replica, (y * 2 + zl) * 2 + core)
    half_rows = lambda v: lax.dynamic_index_in_dim(v.reshape(4, 2, BLK), zh, 1, False).reshape(ROWS, 1)
    first = jnp.tile(half_rows(begin)[3 * BLK :, 0], 8).reshape(1, QALL)
    lane = jnp.arange(128, dtype=jnp.int32)
    frequency = ROTARY_BASE ** (-(lane % 32).astype(F32) * (2.0 / HD))
    angles = half_rows(position).astype(F32) * frequency[None, :]
    cosine = jnp.cos(angles)
    sine = jnp.where((lane % HD) < HD // 2, -1.0, 1.0)[None, :] * jnp.sin(angles)

    q, kv_own = qkv_forward(idx, normed_one, qkv_all, tie(cosine, out_all[1]), sine)
    kv_par = lax.ppermute(tie(kv_own, cots[1], cots[4]), "zh", shift(2, 1))
    down_got = fetch_half(tie(down_weight, gate_up), core)
    q = tie(q, cots[1], cots[4], gate_up)
    att, qx = attend(idx, q, kv_own, kv_par, first)
    gate_up = lax.all_gather(tie(gate_up, kv_par), ("y", "core"), axis=0, tiled=True)
    parts = out_project(idx, tie(att, cots[2], cots[3]), out_all)
    after_attn = tok + scatter_x(parts, down_got)[0]

    r_two = inverse_rms(after_attn)
    normed_two = gather_x((after_attn * r_two * gain_two).astype(BF16))
    down_all = down_weight, down_got, lax.ppermute(tie(down_got, normed_two[1], normed_two[4]), "core", shift(2, 1))
    hid, dgate, dup = ffn(idx, normed_two, cots, gate_weight, up_weight, gate_up, down_all)
    own_grads = ffn_grads(normed_two, cots, hid, dgate, dup)
    grads = lax.psum_scatter(
        own_grads.reshape(32, PIECE, 128), ("zh", "zl", "y", "core"), scatter_dimension=0, tiled=True
    )
    d_two, _ = scatter_x(
        ffn_back(idx, tie(dgate, own_grads), dup, gate_weight, up_weight, gate_up)
    )
    back_two, gain_grad_two = norm_back(after_attn, r_two, gain_two, d_two)
    after_grad = cotangent.astype(F32) + back_two
    branch = gather_x(after_grad.astype(BF16))
    layer_parts = down_project(idx, tie(hid, after_grad), down_all)
    att = tie(att, *layer_parts)
    layer = [layer_parts[0]] + [
        lax.ppermute(tie(layer_parts[k], branch[2], branch[3]), "x", shift(4, k)) for k in (1, 3)
    ]
    dqm, dkv_own, dkv_par = attend_back(
        idx, qx, kv_own, kv_par, first, att, cosine, sine, branch, out_all
    )
    dkv_got = lax.ppermute(dkv_par, "zh", shift(2, 1))
    tail = attn_grads(
        idx, normed_one, branch, dqm.reshape(ROWS, AW), tie(att, *layer).reshape(ROWS, AW)
    )
    dkv_got = tie(dkv_got, tail[0])
    *tail_kv, parts = qkv_back(
        idx, dqm.reshape(ROWS, AW), dkv_own, dkv_got, cosine, sine, qkv_all, normed_one, gain_one,
        gain_grad_two,
    )
    d_one, first_step = scatter_x(parts)
    layer.append(lax.ppermute(tie(layer_parts[2], d_one), "x", shift(4, 2)))
    layer_out = sum((v.astype(F32) for v in layer), after_attn).astype(BF16)
    back_one, _ = norm_back(tok, s_one, gain_one, d_one)
    input_grad = (after_grad + back_one).astype(BF16)

    over_x = lambda v: sum((lax.ppermute(v, "x", shift(4, s)) for s in (1, 2, 3)), v)
    tail = tie(tail[0], *first_step), tie(tail[1], dkv_got)
    summed, (grad_qkv, grad_out, gains) = sum_tail(idx, tail, tail_kv, d_one)
    grads = lax.all_gather(tie(grads, summed), ("zl", "y", "core"), axis=0, tiled=True)
    grad_gate, grad_up, grad_down = unpack(grads)
    gains = over_x(gains)
    return (
        layer_out, input_grad, gains[0], grad_qkv, grad_out, grad_gate, grad_up,
        grad_down, gains[1],
    )


def solution(mesh):
    grid = Mesh(mesh.devices.reshape(SIZES), AXES)
    rows = P(AXES, None)
    both = P(("x", "zh"), None)
    return jax.shard_map(
        on_device,
        mesh=grid,
        in_specs=(
            rows, rows, P(), P("zh", "x"), both, P("zh", "x"), P("zh", "x"), both, P(), P(), P(),
        ),
        out_specs=(
            rows, rows, P(), P("zh", "x"), both, P("zh", "x"), P("zh", "x"), both, P(),
        ),
        check_vma=False,
    )
```

```python
import jax
import jax.numpy as jnp
from jax import lax
from jax.experimental import pallas as pl
from jax.experimental.pallas import tpu as pltpu
from jax.sharding import Mesh
from jax.sharding import PartitionSpec as P

HEADS = 32
KV = 4
HD = 64
EPSILON = 1e-05
ROTARY_BASE = 10000.0
MASKED = -1e30

AXES = ("y", "zl", "core", "x", "zh")
SIZES = (4, 2, 2, 4, 2)
BLK = 160
HALF = BLK // 2
ROWS = 4 * BLK
CAP = 2 * ROWS
D = 2048
DH = D // 2
QW = 640
AW = 512
FF4 = 1408
TILE = 256
F32 = jnp.float32
BF16 = jnp.bfloat16
VLIM = 60 * 1024 * 1024


def spec(memory=pltpu.VMEM):
    return pl.BlockSpec(memory_space=memory)


def params(**kw):
    return pltpu.CompilerParams(vmem_limit_bytes=VLIM, **kw)


def cost(flops, nbytes):
    return pl.CostEstimate(flops=int(flops), bytes_accessed=int(nbytes), transcendentals=0)


def sds(shape, dtype=BF16):
    return jax.ShapeDtypeStruct(shape, dtype)


def dot(a, b):
    return jnp.dot(a, b, preferred_element_type=F32)


def dot_t(a, b):
    return lax.dot_general(a, b, (((1,), (1,)), ((), ())), preferred_element_type=F32)


def t_dot(a, b):
    return lax.dot_general(a, b, (((0,), (0,)), ((), ())), preferred_element_type=F32)


def tie(v, *deps):
    return lax.optimization_barrier((v,) + deps)[0]


def shift(n, s):
    return [(i, (i + s) % n) for i in range(n)]


def gather_x(v, wait=()):
    from_prev = lax.ppermute(v, "x", shift(4, 1))
    from_next = lax.ppermute(v, "x", shift(4, -1))
    send_a = tie(from_prev[:HALF], from_next, *wait)
    send_b = tie(from_next[HALF:], from_prev, *wait)
    opp_a = lax.ppermute(send_a, "x", shift(4, 1))
    opp_b = lax.ppermute(send_b, "x", shift(4, -1))
    return v, from_next, opp_a, opp_b, from_prev


def relay_body(p1, got_a, p3, got_b, q1, q3):
    q1[:HALF, :] = (p1[:HALF, :].astype(F32) + got_a[...].astype(F32)).astype(BF16)
    q1[HALF:, :] = p1[HALF:, :]
    q3[:HALF, :] = p3[:HALF, :]
    q3[HALF:, :] = (p3[HALF:, :].astype(F32) + got_b[...].astype(F32)).astype(BF16)


def scatter_x(parts):
    p0, p1, p2a, p2b, p3 = parts
    got_a = lax.ppermute(p2a, "x", shift(4, 1))
    got_b = lax.ppermute(p2b, "x", shift(4, -1))
    q1, q3 = pl.pallas_call(
        relay_body,
        out_shape=(sds((BLK, D)),) * 2,
        in_specs=[spec()] * 4,
        out_specs=(spec(),) * 2,
        compiler_params=params(),
        cost_estimate=cost(1e6, 3e6),
        name="relay",
    )(p1, got_a, p3, got_b)
    from_prev = lax.ppermute(q1, "x", shift(4, 1))
    from_next = lax.ppermute(q3, "x", shift(4, -1))
    return p0.astype(F32) + from_prev.astype(F32) + from_next.astype(F32), (got_a, got_b)


PIECES = ((0, BLK), (1, BLK), (2, HALF), (2, HALF), (3, BLK))
PIECE_ROW = (0, BLK, 2 * BLK, 2 * BLK + HALF, 3 * BLK)


def part_shapes(width, dtype=BF16):
    return tuple(sds((n, width), dtype) for _, n in PIECES)


def low_lanes(shape):
    return lax.broadcasted_iota(jnp.int32, shape, 1) < HD


def swap_halves(v):
    lane = lax.broadcasted_iota(jnp.int32, v.shape, 1) % HD
    return jnp.where(lane < HD // 2, pltpu.roll(v, 128 - HD // 2, 1), pltpu.roll(v, HD // 2, 1))


def rows_at(block):
    return pl.ds(pl.multiple_of(block * BLK, 32), BLK)


def fetch_half(w, core):
    half = w.shape[0] // 2
    return lax.ppermute(lax.dynamic_slice_in_dim(w, core * half, half, 0), "zh", shift(2, 1))


def fetch_partner(w, core, *deps):
    got = fetch_half(tie(w, *deps), core)
    return w, got, lax.ppermute(got, "core", shift(2, 1))


def weight_rows(idx, rows):
    zh, core = idx[1], idx[3]
    far = (1 - zh) * rows
    half = rows // 2
    at = lambda first, n: pl.ds(pl.multiple_of(first, half), n)
    return at(zh * rows, rows), at(far + core * half, half), at(far + (1 - core) * half, half)


def qkv_body(idx, n0, n1, n2a, n2b, n3, w0, w1, w2, cosine, sine, q_ref, kv_ref, rows):
    x = idx[0]
    lo = low_lanes((BLK, 128))
    for ref, row, (_, n) in zip((n0, n1, n2a, n2b, n3), PIECE_ROW, PIECES):
        rows[row : row + n, :] = ref[...]
    s0, s1, s2 = weight_rows(idx, DH)
    acc = dot(rows[:, s0], w0[...]) + dot(rows[:, s1], w1[...]) + dot(rows[:, s2], w2[...])
    for d in range(4):
        at = rows_at((x + d) & 3)
        cs = cosine[at, :]
        sn = sine[at, :]
        for p in range(5):
            v = acc[d * BLK : (d + 1) * BLK, p * 128 : (p + 1) * 128]
            r = v * cs + swap_halves(v) * sn
            if p < 4:
                r = r * (HD**-0.5 * LOG2E)
                a = (x + d) & 3
                for k, w in enumerate((r, pltpu.roll(r, HD, 1))):
                    head = slice((2 * p + k) * BLK, (2 * p + k + 1) * BLK)
                    q_ref[a, head, :] = jnp.where(lo, w, 0.0).astype(BF16)
            else:
                kv_ref[at, :] = jnp.where(lo, r, v).astype(BF16)


def qkv_forward(idx, pieces, weight, cosine, sine):
    return pl.pallas_call(
        qkv_body,
        out_shape=(sds((4, QALL, 128)), sds((ROWS, 128))),
        in_specs=[spec(pltpu.SMEM)] + [spec()] * 10,
        out_specs=(spec(), spec()),
        scratch_shapes=[pltpu.VMEM((ROWS, D), BF16)],
        compiler_params=params(),
        cost_estimate=cost(2 * ROWS * D * QW, 7e6),
        name="qkv_forward",
    )(idx, *pieces, *weight, cosine, sine)


QALL = 8 * BLK
PAIR = 2 * BLK
LOG2E = 1.4426950408889634
LN2 = 0.6931471805599453


def split3(v):
    a = v.astype(BF16).astype(F32)
    b = (v - a).astype(BF16).astype(F32)
    return a, b, v - a - b


def with_lanes(v, parts):
    lane = lax.broadcasted_iota(jnp.int32, v.shape, 1)
    out = jnp.where(lane < HD, v, 0.0)
    for k, part in enumerate(parts):
        out = jnp.where(lane == HD + k, part, out)
    return out


def spread_keys(zh, kv_own, kv_par, kk, vv, fill):
    shape = (BLK, 128)
    lo = low_lanes(shape)
    rest = fill(lax.broadcasted_iota(jnp.int32, shape, 1) - HD)
    for j in range(4):
        for src, off in ((kv_own, zh), (kv_par, 1 - zh)):
            v = src[j * BLK : (j + 1) * BLK, :].astype(F32)
            at = rows_at(2 * j + off)
            kk[at, :] = jnp.where(lo, v, rest).astype(BF16)
            vv[at, :] = jnp.where(lo, pltpu.roll(v, HD, 1), rest).astype(BF16)


def masked(s, zh, j, kb, first):
    if j < 3 and kb < j:
        return s
    u = kb * PAIR + lax.broadcasted_iota(jnp.int32, (PAIR, QALL), 0)
    allowed = None
    if kb == j:
        t = (2 * j + zh) * BLK + lax.broadcasted_iota(jnp.int32, (1, QALL), 1) % BLK
        allowed = u <= t
    if j == 3:
        later = u >= first[...]
        allowed = later if allowed is None else allowed & later
    return jnp.where(allowed, s, MASKED)


def attend_body(idx, q, kv_own, kv_par, first, att, qx, kk, vv, vt, s_ref, e_ref):
    x, zh = idx[0], idx[1]
    spread_keys(zh, kv_own, kv_par, kk, vv, lambda lane: 1.0)
    vt[...] = vv[...].T
    lo = low_lanes((BLK, 128))
    for j in range(4):
        n = PAIR * (j + 1)
        qj = q[j]
        top = jnp.full((1, QALL), MASKED, F32)
        for kb in range(j + 1):
            rows = slice(kb * PAIR, (kb + 1) * PAIR)
            s = masked(dot_t(kk[rows, :], qj), zh, j, kb, first)
            s_ref[rows, :] = s
            top = jnp.maximum(top, jnp.max(s, axis=0, keepdims=True))
        for k in range(n // 64):
            rows = slice(k * 64, (k + 1) * 64)
            e_ref[rows, :] = jnp.exp2(s_ref[rows, :] - top).astype(BF16)
        o = dot(vt[:, :n], e_ref[:n, :])
        lse = split3(top + jnp.log(o[HD : HD + 1, :]) * LOG2E)
        row = lax.broadcasted_iota(jnp.int32, (128, QALL), 0)
        extra = jnp.zeros((128, QALL), F32)
        for k, part in enumerate(lse):
            extra = jnp.where(row == HD + k, part, extra)
        qx[j] = (qj.astype(F32) + extra.T).astype(BF16)
        o = o.T
        r = pltpu.roll(o, HD, 1)
        rel = (j - x) & 3
        for p in range(4):
            even, odd = slice(2 * p * BLK, (2 * p + 1) * BLK), slice((2 * p + 1) * BLK, (2 * p + 2) * BLK)
            num = jnp.where(lo, o[even], r[odd])
            den = jnp.where(lo, r[even], o[odd])
            att[rel, :, p * 128 : (p + 1) * 128] = (num / den).astype(BF16)


def attend(idx, q, kv_own, kv_par, first):
    return pl.pallas_call(
        attend_body,
        out_shape=(sds((4, BLK, AW)), sds((4, QALL, 128))),
        in_specs=[spec(pltpu.SMEM)] + [spec()] * 4,
        out_specs=(spec(), spec()),
        scratch_shapes=[
            pltpu.VMEM((CAP, 128), BF16),
            pltpu.VMEM((CAP, 128), BF16),
            pltpu.VMEM((128, CAP), BF16),
            pltpu.VMEM((CAP, QALL), F32),
            pltpu.VMEM((CAP, QALL), BF16),
        ],
        compiler_params=params(),
        cost_estimate=cost(1.2e10, 3e6),
        name="attend",
    )(idx, q, kv_own, kv_par, first)


def store_parts(res, refs):
    for ref, row, (_, n) in zip(refs, PIECE_ROW, PIECES):
        ref[...] = res[row : row + n].astype(BF16)


def out_body(idx, att, w0, w1, w2, o0, o1, o2a, o2b, o3):
    s0, s1, s2 = weight_rows(idx, AW // 2)
    for d, ref in ((2, None), (1, o1), (3, o3), (0, o0)):
        a = att.at[d]
        res = dot(a[:, s0], w0[...]) + dot(a[:, s1], w1[...]) + dot(a[:, s2], w2[...])
        res = res.astype(BF16)
        if d == 2:
            o2a[...] = res[:HALF]
            o2b[...] = res[HALF:]
        else:
            ref[...] = res


def out_project(idx, att, weight):
    return pl.pallas_call(
        out_body,
        out_shape=part_shapes(D),
        in_specs=[spec(pltpu.SMEM)] + [spec()] * 4,
        out_specs=(spec(),) * 5,
        compiler_params=params(),
        cost_estimate=cost(2 * ROWS * D * AW, 5.5e6),
        name="out_project",
    )(idx, att, *weight)


def stack_heads(v):
    return v, pltpu.roll(v, HD, 1)


def attend_back_body(
    idx, qx, kv_own, kv_par, first, att, cosine, sine, b0, b1, b2a, b2b, b3, w0, w1, w2,
    dq_ref, dkv_own, dkv_par, kk, vv, dout, do_all, dkk, dvv, e_ref, ds_ref, dq_acc,
):
    x, zh = idx[0], idx[1]
    spread_keys(zh, kv_own, kv_par, kk, vv, lambda lane: jnp.where(lane < 3, -1.0, 0.0))
    s0, s1, s2 = weight_rows(idx, AW // 2)
    for d in range(4):
        if d == 2:
            rows = jnp.concatenate([b2a[...], b2b[...]], 0)
        else:
            rows = (b0, b1, None, b3)[d][...]
        at = rows_at((x + d) & 3)
        for s, w in ((s0, w0), (s1, w1), (s2, w2)):
            dout[at, s] = dot_t(rows, w[...]).astype(BF16)
    lo = low_lanes((BLK, 128))
    for j in range(4):
        rel = (j - x) & 3
        here = slice(j * BLK, (j + 1) * BLK)
        for p in range(4):
            cols = slice(p * 128, (p + 1) * 128)
            do = dout[here, cols].astype(F32)
            prod = do * att[rel, :, cols].astype(F32)
            for k, (v, w) in enumerate(zip(stack_heads(do), stack_heads(prod))):
                delta = jnp.sum(jnp.where(lo, w, 0.0), axis=1, keepdims=True)
                head = slice((2 * p + k) * BLK, (2 * p + k + 1) * BLK)
                do_all[head, :] = with_lanes(v, split3(delta)).astype(BF16)
        for kb in range(j + 1):
            rows = slice(kb * PAIR, (kb + 1) * PAIR)
            e = jnp.exp2(masked(dot_t(kk[rows, :], qx[j]), zh, j, kb, first))
            e_ref[...] = e.astype(BF16)
            ds_ref[...] = (e * dot_t(vv[rows, :], do_all[...])).astype(BF16)
            dv = dot(e_ref[...], do_all[...])
            dk = dot(ds_ref[...], qx[j])
            dq = t_dot(ds_ref[...], kk[rows, :])
            if kb == j:
                dvv[rows, :], dkk[rows, :] = dv, dk
            else:
                dvv[rows, :] += dv
                dkk[rows, :] += dk
            if kb == 0:
                dq_acc[...] = dq
            else:
                dq_acc[...] += dq
        for p in range(4):
            even, odd = slice(2 * p * BLK, (2 * p + 1) * BLK), slice((2 * p + 1) * BLK, (2 * p + 2) * BLK)
            v = jnp.where(lo, dq_acc[even, :], pltpu.roll(dq_acc[odd, :], HD, 1)) * HD**-0.5
            v = v * cosine[here, :] - swap_halves(v) * sine[here, :]
            dq_ref[rel, :, p * 128 : (p + 1) * 128] = v.astype(BF16)
    for j in range(4):
        for dst, off in ((dkv_own, zh), (dkv_par, 1 - zh)):
            at = rows_at(2 * j + off)
            both = jnp.where(lo, dkk[at, :] * LN2, pltpu.roll(dvv[at, :], HD, 1))
            dst[j * BLK : (j + 1) * BLK, :] = both.astype(dst.dtype)


def attend_back(idx, qx, kv_own, kv_par, first, att, cosine, sine, branch, weight):
    return pl.pallas_call(
        attend_back_body,
        out_shape=(sds((4, BLK, AW)), sds((ROWS, 128), F32), sds((ROWS, 128))),
        in_specs=[spec(pltpu.SMEM)] + [spec()] * 15,
        out_specs=(spec(),) * 3,
        scratch_shapes=[
            pltpu.VMEM((CAP, 128), BF16),
            pltpu.VMEM((CAP, 128), BF16),
            pltpu.VMEM((ROWS, AW), BF16),
            pltpu.VMEM((QALL, 128), BF16),
            pltpu.VMEM((CAP, 128), F32),
            pltpu.VMEM((CAP, 128), F32),
            pltpu.VMEM((PAIR, QALL), BF16),
            pltpu.VMEM((PAIR, QALL), BF16),
            pltpu.VMEM((QALL, 128), F32),
        ],
        compiler_params=params(),
        cost_estimate=cost(3e10, 8e6),
        name="attend_back",
    )(idx, qx, kv_own, kv_par, first, att, cosine, sine, *branch, *weight)


def qkv_back_body(
    idx, dqm, dkv_own, dkv_got, cosine, sine, w0, w1, w2, n0, n1, n2a, n2b, n3, gain_one,
    gain_grad_two,
    mine, theirs, o0, o1, o2a, o2b, o3, n_all, dkv, grad, gains,
):
    x, y, core = idx[0], idx[2], idx[3]
    lo = low_lanes((BLK, 128))
    for ref, row, (_, n) in zip((n0, n1, n2a, n2b, n3), PIECE_ROW, PIECES):
        n_all[row : row + n, :] = ref[...]
    for d in range(4):
        at = rows_at((x + d) & 3)
        v = dkv_own[at, :] + dkv_got[at, :].astype(F32)
        v = jnp.where(lo, v * cosine[at, :] - swap_halves(v) * sine[at, :], v).astype(BF16)
        dkv[d * BLK : (d + 1) * BLK, :] = v
    rows = jnp.concatenate([dqm[...], dkv[...]], 1)
    for s, w in zip(weight_rows(idx, DH), (w0, w1, w2)):
        for c in range(w.shape[0] // 512):
            cols = pl.ds(pl.multiple_of(s.start + c * 512, 512), 512)
            res = dot_t(rows, w[c * 512 : (c + 1) * 512, :])
            part = (res * n_all[:, cols].astype(F32)).reshape(ROWS // 8, 8, 512)
            gains[0:1, cols] = jnp.sum(jnp.sum(part, axis=0), axis=0, keepdims=True) / gain_one[:, cols]
            store_parts(res, [r.at[:, cols] for r in (o0, o1, o2a, o2b, o3)])
    grad[...] = dot(dkv[...].T, n_all[...]).astype(BF16)
    gains[1:2, :] = gain_grad_two[...]
    for s in range(4):
        for k, ref in enumerate((mine, theirs)):
            p = ((y + s) & 3) * 2 + (core if k == 0 else 1 - core)
            both = gains[:, pl.ds(pl.multiple_of(p * 256, 256), 256)]
            both = jnp.concatenate([both[:, :128], both[:, 128:], jnp.zeros((12, 128), F32)], 0)
            for h in range(2):
                ref[s, h, :128, :] = grad[:, pl.ds(pl.multiple_of(h * DH + p * 128, 128), 128)]
                ref[s, h, 128:, :] = both.astype(BF16)


def qkv_back(idx, dqm, dkv_own, dkv_got, cosine, sine, weight, pieces, gain_one, gain_grad_two):
    res = pl.pallas_call(
        qkv_back_body,
        out_shape=(sds((4, 2, KVP, 128)),) * 2 + part_shapes(D),
        in_specs=[spec(pltpu.SMEM)] + [spec()] * 15,
        out_specs=(spec(),) * 7,
        scratch_shapes=[
            pltpu.VMEM((ROWS, D), BF16),
            pltpu.VMEM((ROWS, 128), BF16),
            pltpu.VMEM((128, D), BF16),
            pltpu.VMEM((2, D), F32),
        ],
        compiler_params=params(),
        cost_estimate=cost(2 * ROWS * D * QW, 1.3e7),
        name="qkv_back",
    )(
        idx, dqm, dkv_own, dkv_got, cosine, sine, *weight, *pieces,
        gain_one.reshape(1, D), gain_grad_two.reshape(1, D),
    )
    return res[0], res[1], res[2:]


TILES = 6
GAP = TILES * TILE


def load_down(idx, refs, dst, sem):
    copies = []
    for k, (s, ref) in enumerate(zip(weight_rows(idx, FF4 // 2), refs)):
        copies.append(pltpu.make_async_copy(ref, dst.at[s], sem.at[k]))
    return copies


def ffn_body(
    idx, n0, n1, n2a, n2b, n3, c0, c1, c2a, c2b, c3, gate_own, up_own, gate_par, up_par, w0, w1, w2,
    hid, dgate, dup, n_all, c_all, down, sem,
):
    i = pl.program_id(0)
    zh = idx[1]

    @pl.when(i == 0)
    def _():
        copies = load_down(idx, (w0, w1, w2), down, sem)
        for c in copies:
            c.start()
        for refs, dst in (((n0, n1, n2a, n2b, n3), n_all), ((c0, c1, c2a, c2b, c3), c_all)):
            for ref, row, (_, n) in zip(refs, PIECE_ROW, PIECES):
                dst[row : row + n, :] = ref[...]
        for c in copies:
            c.wait()

    own = n_all[:, pl.ds(pl.multiple_of(zh * DH, DH), DH)]
    par = n_all[:, pl.ds(pl.multiple_of((1 - zh) * DH, DH), DH)]
    gate = dot(own, gate_own[...]) + dot(par, gate_par[...])
    up = dot(own, up_own[...]) + dot(par, up_par[...])
    dh = dot_t(c_all[...], down[pl.ds(pl.multiple_of(i * TILE, TILE), TILE), :])
    sig = 1.0 / (1.0 + jnp.exp(-gate))
    act = gate * sig
    hid[...] = (act * up).astype(BF16)
    dgate[...] = (dh * up * sig * (1.0 + gate * (1.0 - sig))).astype(BF16)
    dup[...] = (dh * act).astype(BF16)


def whole(n, w):
    return pl.BlockSpec((n, w), lambda i: (0, 0))


def ffn(idx, normed, cots, gate, up, gate_up, down):
    column = lambda first: pl.BlockSpec((DH, TILE), lambda i: (0, i + first))
    hidden = pl.BlockSpec((ROWS, TILE), lambda i: (0, i))
    return pl.pallas_call(
        ffn_body,
        grid=(TILES,),
        out_shape=(sds((ROWS, FF4)),) * 3,
        in_specs=[spec(pltpu.SMEM)]
        + [whole(n, D) for _, n in PIECES] * 2
        + [column(0), column(0), column(0), column(TILES)]
        + [spec(pl.ANY)] * 3,
        out_specs=[hidden] * 3,
        scratch_shapes=[
            pltpu.VMEM((ROWS, D), BF16),
            pltpu.VMEM((ROWS, D), BF16),
            pltpu.VMEM((GAP, D), BF16),
            pltpu.SemaphoreType.DMA((3,)),
        ],
        compiler_params=params(),
        cost_estimate=cost(6 * ROWS * D * FF4, 3.4e7),
        name="ffn",
    )(idx, *normed, *cots, gate, up, gate_up, gate_up, *down)


def down_body(idx, hid, w0, w1, w2, o0, o1, o2, o3, down, sem):
    copies = load_down(idx, (w0, w1, w2), down, sem)
    for c in copies:
        c.start()
    for c in copies:
        c.wait()
    for n in range(D // 512):
        cols = slice(n * 512, (n + 1) * 512)
        res = dot(hid[...], down[:, cols]).astype(BF16)
        for d, ref in enumerate((o0, o1, o2, o3)):
            ref[:, cols] = res[d * BLK : (d + 1) * BLK]


def down_project(idx, hid, down):
    return pl.pallas_call(
        down_body,
        out_shape=(sds((BLK, D)),) * 4,
        in_specs=[spec(pltpu.SMEM), spec()] + [spec(pl.ANY)] * 3,
        out_specs=(spec(),) * 4,
        scratch_shapes=[pltpu.VMEM((FF4, D), BF16), pltpu.SemaphoreType.DMA((3,))],
        compiler_params=params(),
        cost_estimate=cost(2 * ROWS * D * FF4, 1.1e7),
        name="down_project",
    )(idx, hid, *down)


def ffn_back_body(idx, dgate, dup, gate_own, up_own, par, *refs):
    half = pl.num_programs(0) // 2

    @pl.when(pl.program_id(0) < half)
    def _():
        store_parts(dot_t(dgate[...], gate_own[...]) + dot_t(dup[...], up_own[...]), refs)

    @pl.when(pl.program_id(0) >= half)
    def _():
        store_parts(dot_t(dgate[...], par[:, :FF4]) + dot_t(dup[...], par[:, GAP:]), refs)


def ffn_back(idx, dgate, dup, gate, up, gate_up):
    half = DH // TILE
    rows = pl.BlockSpec((ROWS, FF4), lambda i, idx: (0, 0))
    own = pl.BlockSpec((TILE, FF4), lambda i, idx: (jnp.minimum(i, half - 1), 0))
    par = pl.BlockSpec((TILE, GAP + FF4), lambda i, idx: (jnp.maximum(i - half, 0), 0))
    place = lambda i, idx: (0, i ^ (idx[1] * half))
    return pl.pallas_call(
        ffn_back_body,
        grid_spec=pltpu.PrefetchScalarGridSpec(
            num_scalar_prefetch=1,
            grid=(D // TILE,),
            in_specs=[rows, rows, own, own, par],
            out_specs=[pl.BlockSpec((n, TILE), place) for _, n in PIECES],
        ),
        out_shape=part_shapes(D),
        compiler_params=params(),
        cost_estimate=cost(4 * ROWS * D * FF4, 1.8e7),
        name="ffn_back",
    )(idx, dgate, dup, gate, up, gate_up)


GU_ROWS = FF4 // 128 * 64
PIECE = 2 * GU_ROWS + FF4 // 2
QS = 4


def ffn_grads_body(*refs):
    na, nb, cots = refs[0:5], refs[5:10], refs[10:15]
    hid, dgate, dup, out, hid_t = refs[15:]

    @pl.when(pl.program_id(0) == 0)
    def _():
        hid_t[...] = hid[...].T

    stack = lambda parts: jnp.concatenate([r[...] for r in parts], 0)
    rows = jnp.concatenate([stack(na), stack(nb)], 1).T
    for k, ref in enumerate((dgate, dup)):
        g = dot(rows, ref[...]).astype(BF16)
        for h in range(2):
            for q in range(QS):
                r = g[(QS * h + q) * 64 : (QS * h + q + 1) * 64]
                for c in range(FF4 // 128):
                    first = k * GU_ROWS + c * 64
                    out[h, q, first : first + 64, :] = r[:, c * 128 : (c + 1) * 128]
    g = dot(hid_t[...], stack(cots)).astype(BF16)
    for h in range(2):
        for q in range(QS):
            out[h, q, 2 * GU_ROWS :, :] = g[
                h * (FF4 // 2) : (h + 1) * (FF4 // 2), q * 128 : (q + 1) * 128
            ]


def ffn_grads(normed, cots, hid, dgate, dup):
    return pl.pallas_call(
        ffn_grads_body,
        grid=(16 // QS,),
        out_shape=sds((2, 16, PIECE, 128)),
        in_specs=[pl.BlockSpec((n, 64 * QS), lambda i: (0, i)) for _, n in PIECES]
        + [pl.BlockSpec((n, 64 * QS), lambda i: (0, i + 16 // QS)) for _, n in PIECES]
        + [pl.BlockSpec((n, 128 * QS), lambda i: (0, i)) for _, n in PIECES]
        + [whole(ROWS, FF4)] * 3,
        out_specs=pl.BlockSpec((2, QS, PIECE, 128), lambda i: (0, i, 0, 0)),
        scratch_shapes=[pltpu.VMEM((FF4, ROWS), BF16)],
        compiler_params=params(),
        cost_estimate=cost(6 * ROWS * D * FF4, 3e7),
        name="ffn_grads",
    )(*normed, *normed, *cots, hid, dgate, dup)


def unpack_body(piece, gate, up, down):
    for q in range(QS):
        rows = slice(q * 64, (q + 1) * 64)
        for k, ref in enumerate((gate, up)):
            for c in range(FF4 // 128):
                first = k * GU_ROWS + c * 64
                ref[rows, c * 128 : (c + 1) * 128] = piece[q, first : first + 64, :].astype(F32)
        down[:, q * 128 : (q + 1) * 128] = piece[q, 2 * GU_ROWS :, :].astype(F32)


def unpack(pieces):
    return pl.pallas_call(
        unpack_body,
        grid=(16 // QS,),
        out_shape=(sds((DH, FF4), F32), sds((DH, FF4), F32), sds((FF4 // 2, D), F32)),
        in_specs=[pl.BlockSpec((QS, PIECE, 128), lambda i: (i, 0, 0))],
        out_specs=[
            pl.BlockSpec((64 * QS, FF4), lambda i: (i, 0)),
            pl.BlockSpec((64 * QS, FF4), lambda i: (i, 0)),
            pl.BlockSpec((FF4 // 2, 128 * QS), lambda i: (0, i)),
        ],
        compiler_params=params(),
        cost_estimate=cost(1e6, 2.6e7),
        name="unpack",
    )(pieces)


QP = 4 * 128
OP = 2 * (AW // 2)
QOP = QP + OP
KVP = 128 + 16
TAIL = QOP + KVP


def attn_grads_body(idx, *refs):
    na, nb, branch = refs[0:5], refs[5:10], refs[10:15]
    dqm, att, mine, theirs, att_t = refs[15:]
    core = idx[3]

    @pl.when(pl.program_id(0) == 0)
    def _():
        att_t[...] = att[...].T

    stack = lambda parts: jnp.concatenate([r[...] for r in parts], 0)

    def store(h, first, n, zero, one):
        mine[0, h, first : first + n, :] = jnp.where(core == 0, zero, one)
        theirs[0, h, first : first + n, :] = jnp.where(core == 0, one, zero)

    for h, cols in enumerate((na, nb)):
        g = dot(stack(cols).T, dqm[...]).astype(BF16)
        for c in range(4):
            lanes = slice(c * 128, (c + 1) * 128)
            store(h, c * 128, 128, g[:128, lanes], g[128:, lanes])
    g = dot(att_t[...], stack(branch)).astype(BF16)
    for h in range(2):
        r = g[h * (AW // 2) : (h + 1) * (AW // 2)]
        for c in range(2):
            lanes = lambda k: slice(k * 256 + c * 128, k * 256 + (c + 1) * 128)
            store(h, QP + c * (AW // 2), AW // 2, r[:, lanes(0)], r[:, lanes(1)])


def attn_grads(idx, normed, branch, dqm, att):
    turn = lambda s, idx: (s + idx[2]) & 3
    piece = pl.BlockSpec((1, 2, QOP, 128), lambda s, idx: (s, 0, 0, 0))
    fixed = pl.BlockSpec((ROWS, AW), lambda s, idx: (0, 0))
    return pl.pallas_call(
        attn_grads_body,
        grid_spec=pltpu.PrefetchScalarGridSpec(
            num_scalar_prefetch=1,
            grid=(4,),
            in_specs=[pl.BlockSpec((n, 256), lambda s, idx: (0, turn(s, idx))) for _, n in PIECES]
            + [pl.BlockSpec((n, 256), lambda s, idx: (0, turn(s, idx) + 4)) for _, n in PIECES]
            + [pl.BlockSpec((n, 512), lambda s, idx: (0, turn(s, idx))) for _, n in PIECES]
            + [fixed, fixed],
            out_specs=[piece, piece],
            scratch_shapes=[pltpu.VMEM((AW, ROWS), BF16)],
        ),
        out_shape=(sds((4, 2, QOP, 128)),) * 2,
        compiler_params=params(),
        cost_estimate=cost(4 * ROWS * D * AW, 1e7),
        name="attn_grads",
    )(idx, *normed, *normed, *branch, dqm, att)


def small_call(body, out_shape, *args, name):
    return pl.pallas_call(
        body,
        out_shape=out_shape,
        in_specs=[spec(pltpu.SMEM)] + [spec()] * (len(args) - 1),
        out_specs=jax.tree.map(lambda _: spec(), out_shape),
        compiler_params=params(),
        cost_estimate=cost(1e6, 4e6),
        name=name,
    )(*args)


def add(*values):
    return sum((v.astype(F32) for v in values[1:]), values[0].astype(F32)).astype(BF16)


def sum_core_body(idx, a, b, c, d, *outs):
    for s, out in enumerate(outs):
        out[:, :QOP, :] = add(a[s], b[s])
        out[:, QOP:, :] = add(c[s], d[s])


def sum_y_body(idx, a, b, c, d, own, other):
    zh = idx[1]
    own[...] = add(a[zh], b[zh], c[zh], d[zh])
    far = 1 - zh
    other[...] = add(a[far], b[far], c[far], d[far])


def sum_z_body(idx, a, b, c, d, out):
    out[...] = add(a[...], b[...], c[...], d[...])


def unpack_tail_body(idx, *refs):
    y, core = idx[2], idx[3]
    qkv, out, gains = refs[8:]
    for k in range(8):
        piece = refs[k]
        p = ((y - k % 4) & 3) * 2 + (core if k < 4 else 1 - core)
        rows = pl.ds(pl.multiple_of(p * 128, 128), 128)
        for c in range(4):
            qkv[rows, c * 128 : (c + 1) * 128] = piece[c * 128 : (c + 1) * 128, :].astype(F32)
        qkv[rows, AW:] = piece[QOP : QOP + 128, :].astype(F32).T
        g = piece[QOP + 128 :, :].astype(F32)
        for c in range(2):
            first = QP + c * (AW // 2)
            cols = pl.ds(pl.multiple_of(p * 256 + c * 128, 128), 128)
            out[:, cols] = piece[first : first + AW // 2, :].astype(F32)
            gains[:, cols] = g[2 * c : 2 * c + 2]


def sum_tail(idx, first, second, before):
    got_a = lax.ppermute(first[1], "core", shift(2, 1))
    got_b = lax.ppermute(second[1], "core", shift(2, 1))
    part = sds((2, TAIL, 128))
    g = small_call(sum_core_body, (part,) * 4, idx, first[0], got_a, second[0], got_b, name="sum_core")
    got = [tie(lax.ppermute(g[s], "y", shift(4, s)), before) for s in (2, 1, 3)]
    part = sds((TAIL, 128))
    own, other = small_call(sum_y_body, (part,) * 2, idx, g[0], *got, name="sum_y")
    cross = [(2 * a + b, 2 * (1 - a) + (1 - b)) for a in range(2) for b in range(2)]
    g = small_call(
        sum_z_body,
        part,
        idx,
        own,
        lax.ppermute(own, "zl", shift(2, 1)),
        lax.ppermute(other, "zh", shift(2, 1)),
        lax.ppermute(other, ("zl", "zh"), cross),
        name="sum_z",
    )
    mine = [g] + [lax.ppermute(g, "y", shift(4, s)) for s in (1, 2, 3)]
    theirs = [lax.ppermute(v, "core", shift(2, 1)) for v in mine]
    shapes = (sds((DH, QW), F32), sds((AW // 2, D), F32), sds((2, D), F32))
    return own, small_call(unpack_tail_body, shapes, idx, *mine, *theirs, name="unpack_tail")


def inverse_rms(v):
    return lax.rsqrt(jnp.mean(v * v, axis=-1, keepdims=True) + EPSILON)


def norm_back(v, r, gain, grad):
    pulled = grad * gain
    inner = jnp.mean(v * pulled, axis=-1, keepdims=True)
    return r * pulled - v * (r * r * r) * inner, jnp.sum(grad * v * r, axis=0)


def replica_layout(lengths, replica, replica_id):
    sizes = jnp.where(replica == replica_id, lengths, 0)
    starts = jnp.cumsum(sizes) - sizes
    row_ids = jnp.arange(CAP, dtype=jnp.int32)
    inside = (row_ids[:, None] >= starts[None, :]) & (row_ids[:, None] < (starts + sizes)[None, :])
    begin = jnp.sum(jnp.where(inside, starts[None, :], 0), axis=1)
    begin = begin + jnp.where(jnp.any(inside, axis=1), 0, jnp.sum(sizes))
    return begin, row_ids - begin


def on_device(
    tokens, cotangent, gain_one, qkv_weight, out_weight, gate_weight, up_weight, down_weight,
    gain_two, seq_lengths, seq_replica,
):
    x, zh, core = lax.axis_index("x"), lax.axis_index("zh"), lax.axis_index("core")
    y, zl = lax.axis_index("y"), lax.axis_index("zl")
    idx = jnp.stack([x, zh, y, core]).astype(jnp.int32)

    tok = tokens.astype(F32)
    s_one = inverse_rms(tok)
    qkv_got = fetch_half(qkv_weight, core)
    normed_one = gather_x((tok * s_one * gain_one).astype(BF16))
    qkv_all = qkv_weight, qkv_got, lax.ppermute(tie(qkv_got, normed_one[2], normed_one[3]), "core", shift(2, 1))
    out_all = fetch_partner(out_weight, core, qkv_got, normed_one[2], normed_one[3])

    begin, position = replica_layout(seq_lengths, seq_replica, (y * 2 + zl) * 2 + core)
    half_rows = lambda v: lax.dynamic_index_in_dim(v.reshape(4, 2, BLK), zh, 1, False).reshape(ROWS, 1)
    first = jnp.tile(half_rows(begin)[3 * BLK :, 0], 8).reshape(1, QALL)
    lane = jnp.arange(128, dtype=jnp.int32)
    frequency = ROTARY_BASE ** (-(lane % 32).astype(F32) * (2.0 / HD))
    angles = half_rows(position).astype(F32) * frequency[None, :]
    cosine = jnp.cos(angles)
    sine = jnp.where((lane % HD) < HD // 2, -1.0, 1.0)[None, :] * jnp.sin(angles)

    q, kv_own = qkv_forward(idx, normed_one, qkv_all, cosine, sine)
    cots = gather_x(tie(cotangent, normed_one[2], normed_one[3]), (kv_own,))
    rows = DH // 8
    mine = lambda w: lax.dynamic_slice_in_dim(w, (y * 2 + core) * rows, rows, 0)
    cross = [(2 * a + b, 2 * (1 - a) + (1 - b)) for a in range(2) for b in range(2)]
    gate_up = lax.ppermute(
        jnp.concatenate(
            [
                tie(mine(gate_weight), out_all[1], kv_own),
                jnp.zeros((rows, GAP - FF4), BF16),
                mine(up_weight),
            ],
            1,
        ),
        ("zl", "zh"),
        cross,
    )
    kv_par = lax.ppermute(tie(kv_own, cots[1], cots[4]), "zh", shift(2, 1))
    down_got = fetch_half(tie(down_weight, gate_up), core)
    att, qx = attend(idx, tie(q, cots[2], cots[3]), kv_own, kv_par, first)
    gate_up = lax.all_gather(tie(gate_up, qx), ("y", "core"), axis=0, tiled=True)
    parts = out_project(idx, att, out_all)
    after_attn = tie(tok, down_got) + scatter_x(parts)[0]

    r_two = inverse_rms(after_attn)
    normed_two = gather_x((after_attn * r_two * gain_two).astype(BF16))
    down_all = down_weight, down_got, lax.ppermute(tie(down_got, normed_two[1], normed_two[4]), "core", shift(2, 1))
    hid, dgate, dup = ffn(idx, normed_two, cots, gate_weight, up_weight, gate_up, down_all)
    own_grads = ffn_grads(normed_two, cots, hid, dgate, dup)
    grads = lax.psum_scatter(
        own_grads.reshape(32, PIECE, 128), ("zh", "zl", "y", "core"), scatter_dimension=0, tiled=True
    )
    d_two, _ = scatter_x(
        ffn_back(idx, tie(dgate, own_grads), dup, gate_weight, up_weight, gate_up)
    )
    back_two, gain_grad_two = norm_back(after_attn, r_two, gain_two, d_two)
    after_grad = cotangent.astype(F32) + back_two
    branch = gather_x(after_grad.astype(BF16))
    layer_parts = down_project(idx, tie(hid, after_grad), down_all)
    att = tie(att, *layer_parts)
    layer = [layer_parts[0]] + [
        lax.ppermute(tie(layer_parts[k], branch[2], branch[3]), "x", shift(4, k)) for k in (1, 3)
    ]
    dqm, dkv_own, dkv_par = attend_back(
        idx, qx, kv_own, kv_par, first, att, cosine, sine, branch, out_all
    )
    dkv_got = lax.ppermute(dkv_par, "zh", shift(2, 1))
    tail = attn_grads(
        idx, normed_one, branch, dqm.reshape(ROWS, AW), tie(att, *layer).reshape(ROWS, AW)
    )
    dkv_got = tie(dkv_got, tail[0])
    *tail_kv, parts = qkv_back(
        idx, dqm.reshape(ROWS, AW), dkv_own, dkv_got, cosine, sine, qkv_all, normed_one, gain_one,
        gain_grad_two,
    )
    d_one, first_step = scatter_x(parts)
    layer.append(lax.ppermute(tie(layer_parts[2], d_one), "x", shift(4, 2)))
    layer_out = sum((v.astype(F32) for v in layer), after_attn).astype(BF16)
    back_one, _ = norm_back(tok, s_one, gain_one, d_one)
    input_grad = (after_grad + back_one).astype(BF16)

    over_x = lambda v: sum((lax.ppermute(v, "x", shift(4, s)) for s in (1, 2, 3)), v)
    tail = tie(tail[0], *first_step), tie(tail[1], dkv_got)
    summed, (grad_qkv, grad_out, gains) = sum_tail(idx, tail, tail_kv, d_one)
    grads = lax.all_gather(tie(grads, summed), ("zl", "y", "core"), axis=0, tiled=True)
    grad_gate, grad_up, grad_down = unpack(grads)
    gains = over_x(gains)
    return (
        layer_out, input_grad, gains[0], grad_qkv, grad_out, grad_gate, grad_up,
        grad_down, gains[1],
    )


def solution(mesh):
    grid = Mesh(mesh.devices.reshape(SIZES), AXES)
    rows = P(AXES, None)
    both = P(("x", "zh"), None)
    return jax.shard_map(
        on_device,
        mesh=grid,
        in_specs=(
            rows, rows, P(), P("zh", "x"), both, P("zh", "x"), P("zh", "x"), both, P(), P(), P(),
        ),
        out_specs=(
            rows, rows, P(), P("zh", "x"), both, P("zh", "x"), P("zh", "x"), both, P(),
        ),
        check_vma=False,
    )
```

```python
import jax
import jax.numpy as jnp
from jax import lax
from jax.experimental import pallas as pl
from jax.experimental.pallas import tpu as pltpu
from jax.sharding import Mesh
from jax.sharding import PartitionSpec as P

HEADS = 32
KV = 4
HD = 64
EPSILON = 1e-05
ROTARY_BASE = 10000.0
MASKED = -1e30

AXES = ("y", "zl", "core", "x", "zh")
SIZES = (4, 2, 2, 4, 2)
BLK = 160
HALF = BLK // 2
ROWS = 4 * BLK
CAP = 2 * ROWS
D = 2048
DH = D // 2
QW = 640
AW = 512
FF4 = 1408
TILE = 256
F32 = jnp.float32
BF16 = jnp.bfloat16
VLIM = 60 * 1024 * 1024


def spec(memory=pltpu.VMEM):
    return pl.BlockSpec(memory_space=memory)


def params(**kw):
    return pltpu.CompilerParams(vmem_limit_bytes=VLIM, **kw)


def cost(flops, nbytes):
    return pl.CostEstimate(flops=int(flops), bytes_accessed=int(nbytes), transcendentals=0)


def sds(shape, dtype=BF16):
    return jax.ShapeDtypeStruct(shape, dtype)


def dot(a, b):
    return jnp.dot(a, b, preferred_element_type=F32)


def dot_t(a, b):
    return lax.dot_general(a, b, (((1,), (1,)), ((), ())), preferred_element_type=F32)


def t_dot(a, b):
    return lax.dot_general(a, b, (((0,), (0,)), ((), ())), preferred_element_type=F32)


def tie(v, *deps):
    return lax.optimization_barrier((v,) + deps)[0]


def shift(n, s):
    return [(i, (i + s) % n) for i in range(n)]


def gather_x(v, wait=()):
    from_prev = lax.ppermute(v, "x", shift(4, 1))
    from_next = lax.ppermute(v, "x", shift(4, -1))
    send_a = tie(from_prev[:HALF], from_next, *wait)
    send_b = tie(from_next[HALF:], from_prev, *wait)
    opp_a = lax.ppermute(send_a, "x", shift(4, 1))
    opp_b = lax.ppermute(send_b, "x", shift(4, -1))
    return v, from_next, opp_a, opp_b, from_prev


def relay_body(p1, got_a, p3, got_b, q1, q3):
    q1[:HALF, :] = (p1[:HALF, :].astype(F32) + got_a[...].astype(F32)).astype(BF16)
    q1[HALF:, :] = p1[HALF:, :]
    q3[:HALF, :] = p3[:HALF, :]
    q3[HALF:, :] = (p3[HALF:, :].astype(F32) + got_b[...].astype(F32)).astype(BF16)


def relay(parts):
    p0, p1, p2a, p2b, p3 = parts
    got_a = lax.ppermute(p2a, "x", shift(4, 1))
    got_b = lax.ppermute(p2b, "x", shift(4, -1))
    q1, q3 = pl.pallas_call(
        relay_body,
        out_shape=(sds((BLK, D)),) * 2,
        in_specs=[spec()] * 4,
        out_specs=(spec(),) * 2,
        compiler_params=params(),
        cost_estimate=cost(1e6, 3e6),
        name="relay",
    )(p1, got_a, p3, got_b)
    return p0, q1, q3


def scatter_x(parts):
    p0, q1, q3 = relay(parts)
    from_prev = lax.ppermute(q1, "x", shift(4, 1))
    from_next = lax.ppermute(q3, "x", shift(4, -1))
    return p0.astype(F32) + from_prev.astype(F32) + from_next.astype(F32), (q1, q3)


PIECES = ((0, BLK), (1, BLK), (2, HALF), (2, HALF), (3, BLK))
PIECE_ROW = (0, BLK, 2 * BLK, 2 * BLK + HALF, 3 * BLK)


def part_shapes(width, dtype=BF16):
    return tuple(sds((n, width), dtype) for _, n in PIECES)


def low_lanes(shape):
    return lax.broadcasted_iota(jnp.int32, shape, 1) < HD


def swap_halves(v):
    lane = lax.broadcasted_iota(jnp.int32, v.shape, 1) % HD
    return jnp.where(lane < HD // 2, pltpu.roll(v, 128 - HD // 2, 1), pltpu.roll(v, HD // 2, 1))


def rows_at(block):
    return pl.ds(pl.multiple_of(block * BLK, 32), BLK)


def fetch_half(w, core):
    half = w.shape[0] // 2
    return lax.ppermute(lax.dynamic_slice_in_dim(w, core * half, half, 0), "zh", shift(2, 1))


def fetch_partner(w, core, *deps):
    got = fetch_half(tie(w, *deps), core)
    return w, got, lax.ppermute(got, "core", shift(2, 1))


def weight_rows(idx, rows):
    zh, core = idx[1], idx[3]
    far = (1 - zh) * rows
    half = rows // 2
    at = lambda first, n: pl.ds(pl.multiple_of(first, half), n)
    return at(zh * rows, rows), at(far + core * half, half), at(far + (1 - core) * half, half)


def qkv_body(idx, n0, n1, n2a, n2b, n3, w0, w1, w2, cosine, sine, q_ref, kv_ref, rows):
    x = idx[0]
    lo = low_lanes((BLK, 128))
    for ref, row, (_, n) in zip((n0, n1, n2a, n2b, n3), PIECE_ROW, PIECES):
        rows[row : row + n, :] = ref[...]
    s0, s1, s2 = weight_rows(idx, DH)
    acc = dot(rows[:, s0], w0[...]) + dot(rows[:, s1], w1[...]) + dot(rows[:, s2], w2[...])
    for d in range(4):
        at = rows_at((x + d) & 3)
        cs = cosine[at, :]
        sn = sine[at, :]
        for p in range(5):
            v = acc[d * BLK : (d + 1) * BLK, p * 128 : (p + 1) * 128]
            r = v * cs + swap_halves(v) * sn
            if p < 4:
                r = r * (HD**-0.5 * LOG2E)
                a = (x + d) & 3
                for k, w in enumerate((r, pltpu.roll(r, HD, 1))):
                    head = slice((2 * p + k) * BLK, (2 * p + k + 1) * BLK)
                    q_ref[a, head, :] = jnp.where(lo, w, 0.0).astype(BF16)
            else:
                kv_ref[at, :] = jnp.where(lo, r, v).astype(BF16)


def qkv_forward(idx, pieces, weight, cosine, sine):
    return pl.pallas_call(
        qkv_body,
        out_shape=(sds((4, QALL, 128)), sds((ROWS, 128))),
        in_specs=[spec(pltpu.SMEM)] + [spec()] * 10,
        out_specs=(spec(), spec()),
        scratch_shapes=[pltpu.VMEM((ROWS, D), BF16)],
        compiler_params=params(),
        cost_estimate=cost(2 * ROWS * D * QW, 7e6),
        name="qkv_forward",
    )(idx, *pieces, *weight, cosine, sine)


QALL = 8 * BLK
PAIR = 2 * BLK
LOG2E = 1.4426950408889634
LN2 = 0.6931471805599453


def split3(v):
    a = v.astype(BF16).astype(F32)
    b = (v - a).astype(BF16).astype(F32)
    return a, b, v - a - b


def with_lanes(v, parts):
    lane = lax.broadcasted_iota(jnp.int32, v.shape, 1)
    out = jnp.where(lane < HD, v, 0.0)
    for k, part in enumerate(parts):
        out = jnp.where(lane == HD + k, part, out)
    return out


def spread_keys(zh, kv_own, kv_par, kk, vv, fill):
    shape = (BLK, 128)
    lo = low_lanes(shape)
    rest = fill(lax.broadcasted_iota(jnp.int32, shape, 1) - HD)
    for j in range(4):
        for src, off in ((kv_own, zh), (kv_par, 1 - zh)):
            v = src[j * BLK : (j + 1) * BLK, :].astype(F32)
            at = rows_at(2 * j + off)
            kk[at, :] = jnp.where(lo, v, rest).astype(BF16)
            vv[at, :] = jnp.where(lo, pltpu.roll(v, HD, 1), rest).astype(BF16)


def masked(s, zh, j, kb, first):
    if j < 3 and kb < j:
        return s
    u = kb * PAIR + lax.broadcasted_iota(jnp.int32, (PAIR, QALL), 0)
    allowed = None
    if kb == j:
        t = (2 * j + zh) * BLK + lax.broadcasted_iota(jnp.int32, (1, QALL), 1) % BLK
        allowed = u <= t
    if j == 3:
        later = u >= first[...]
        allowed = later if allowed is None else allowed & later
    return jnp.where(allowed, s, MASKED)


def attend_body(idx, q, kv_own, kv_par, first, att, qx, kk, vv, vt, s_ref, e_ref):
    x, zh = idx[0], idx[1]
    spread_keys(zh, kv_own, kv_par, kk, vv, lambda lane: 1.0)
    vt[...] = vv[...].T
    lo = low_lanes((BLK, 128))
    for j in range(4):
        n = PAIR * (j + 1)
        qj = q[j]
        top = jnp.full((1, QALL), MASKED, F32)
        for kb in range(j + 1):
            rows = slice(kb * PAIR, (kb + 1) * PAIR)
            s = masked(dot_t(kk[rows, :], qj), zh, j, kb, first)
            s_ref[rows, :] = s
            top = jnp.maximum(top, jnp.max(s, axis=0, keepdims=True))
        for k in range(n // 64):
            rows = slice(k * 64, (k + 1) * 64)
            e_ref[rows, :] = jnp.exp2(s_ref[rows, :] - top).astype(BF16)
        o = dot(vt[:, :n], e_ref[:n, :])
        lse = split3(top + jnp.log(o[HD : HD + 1, :]) * LOG2E)
        row = lax.broadcasted_iota(jnp.int32, (128, QALL), 0)
        extra = jnp.zeros((128, QALL), F32)
        for k, part in enumerate(lse):
            extra = jnp.where(row == HD + k, part, extra)
        qx[j] = (qj.astype(F32) + extra.T).astype(BF16)
        o = o.T
        r = pltpu.roll(o, HD, 1)
        rel = (j - x) & 3
        for p in range(4):
            even, odd = slice(2 * p * BLK, (2 * p + 1) * BLK), slice((2 * p + 1) * BLK, (2 * p + 2) * BLK)
            num = jnp.where(lo, o[even], r[odd])
            den = jnp.where(lo, r[even], o[odd])
            att[rel, :, p * 128 : (p + 1) * 128] = (num / den).astype(BF16)


def attend(idx, q, kv_own, kv_par, first):
    return pl.pallas_call(
        attend_body,
        out_shape=(sds((4, BLK, AW)), sds((4, QALL, 128))),
        in_specs=[spec(pltpu.SMEM)] + [spec()] * 4,
        out_specs=(spec(), spec()),
        scratch_shapes=[
            pltpu.VMEM((CAP, 128), BF16),
            pltpu.VMEM((CAP, 128), BF16),
            pltpu.VMEM((128, CAP), BF16),
            pltpu.VMEM((CAP, QALL), F32),
            pltpu.VMEM((CAP, QALL), BF16),
        ],
        compiler_params=params(),
        cost_estimate=cost(1.2e10, 3e6),
        name="attend",
    )(idx, q, kv_own, kv_par, first)


def store_parts(res, refs):
    for ref, row, (_, n) in zip(refs, PIECE_ROW, PIECES):
        ref[...] = res[row : row + n].astype(BF16)


def out_body(idx, att, w0, w1, w2, o0, o1, o2a, o2b, o3):
    s0, s1, s2 = weight_rows(idx, AW // 2)
    for d, ref in ((2, None), (1, o1), (3, o3), (0, o0)):
        a = att.at[d]
        res = dot(a[:, s0], w0[...]) + dot(a[:, s1], w1[...]) + dot(a[:, s2], w2[...])
        res = res.astype(BF16)
        if d == 2:
            o2a[...] = res[:HALF]
            o2b[...] = res[HALF:]
        else:
            ref[...] = res


def out_project(idx, att, weight):
    return pl.pallas_call(
        out_body,
        out_shape=part_shapes(D),
        in_specs=[spec(pltpu.SMEM)] + [spec()] * 4,
        out_specs=(spec(),) * 5,
        compiler_params=params(),
        cost_estimate=cost(2 * ROWS * D * AW, 5.5e6),
        name="out_project",
    )(idx, att, *weight)


def stack_heads(v):
    return v, pltpu.roll(v, HD, 1)


def attend_back_body(
    idx, qx, kv_own, kv_par, first, att, cosine, sine, b0, b1, b2a, b2b, b3, w0, w1, w2,
    dq_ref, dkv_own, dkv_par, kk, vv, dout, do_all, dkk, dvv, e_ref, ds_ref, dq_acc,
):
    x, zh = idx[0], idx[1]
    spread_keys(zh, kv_own, kv_par, kk, vv, lambda lane: jnp.where(lane < 3, -1.0, 0.0))
    s0, s1, s2 = weight_rows(idx, AW // 2)
    for d in range(4):
        if d == 2:
            rows = jnp.concatenate([b2a[...], b2b[...]], 0)
        else:
            rows = (b0, b1, None, b3)[d][...]
        at = rows_at((x + d) & 3)
        for s, w in ((s0, w0), (s1, w1), (s2, w2)):
            dout[at, s] = dot_t(rows, w[...]).astype(BF16)
    lo = low_lanes((BLK, 128))
    for j in range(4):
        rel = (j - x) & 3
        here = slice(j * BLK, (j + 1) * BLK)
        for p in range(4):
            cols = slice(p * 128, (p + 1) * 128)
            do = dout[here, cols].astype(F32)
            prod = do * att[rel, :, cols].astype(F32)
            for k, (v, w) in enumerate(zip(stack_heads(do), stack_heads(prod))):
                delta = jnp.sum(jnp.where(lo, w, 0.0), axis=1, keepdims=True)
                head = slice((2 * p + k) * BLK, (2 * p + k + 1) * BLK)
                do_all[head, :] = with_lanes(v, split3(delta)).astype(BF16)
        for kb in range(j + 1):
            rows = slice(kb * PAIR, (kb + 1) * PAIR)
            e = jnp.exp2(masked(dot_t(kk[rows, :], qx[j]), zh, j, kb, first))
            e_ref[...] = e.astype(BF16)
            ds_ref[...] = (e * dot_t(vv[rows, :], do_all[...])).astype(BF16)
            dv = dot(e_ref[...], do_all[...])
            dk = dot(ds_ref[...], qx[j])
            dq = t_dot(ds_ref[...], kk[rows, :])
            if kb == j:
                dvv[rows, :], dkk[rows, :] = dv, dk
            else:
                dvv[rows, :] += dv
                dkk[rows, :] += dk
            if kb == 0:
                dq_acc[...] = dq
            else:
                dq_acc[...] += dq
        for p in range(4):
            even, odd = slice(2 * p * BLK, (2 * p + 1) * BLK), slice((2 * p + 1) * BLK, (2 * p + 2) * BLK)
            v = jnp.where(lo, dq_acc[even, :], pltpu.roll(dq_acc[odd, :], HD, 1)) * HD**-0.5
            v = v * cosine[here, :] - swap_halves(v) * sine[here, :]
            dq_ref[rel, :, p * 128 : (p + 1) * 128] = v.astype(BF16)
    for j in range(4):
        for dst, off in ((dkv_own, zh), (dkv_par, 1 - zh)):
            at = rows_at(2 * j + off)
            both = jnp.where(lo, dkk[at, :] * LN2, pltpu.roll(dvv[at, :], HD, 1))
            dst[j * BLK : (j + 1) * BLK, :] = both.astype(dst.dtype)


def attend_back(idx, qx, kv_own, kv_par, first, att, cosine, sine, branch, weight):
    return pl.pallas_call(
        attend_back_body,
        out_shape=(sds((4, BLK, AW)), sds((ROWS, 128), F32), sds((ROWS, 128))),
        in_specs=[spec(pltpu.SMEM)] + [spec()] * 15,
        out_specs=(spec(),) * 3,
        scratch_shapes=[
            pltpu.VMEM((CAP, 128), BF16),
            pltpu.VMEM((CAP, 128), BF16),
            pltpu.VMEM((ROWS, AW), BF16),
            pltpu.VMEM((QALL, 128), BF16),
            pltpu.VMEM((CAP, 128), F32),
            pltpu.VMEM((CAP, 128), F32),
            pltpu.VMEM((PAIR, QALL), BF16),
            pltpu.VMEM((PAIR, QALL), BF16),
            pltpu.VMEM((QALL, 128), F32),
        ],
        compiler_params=params(),
        cost_estimate=cost(3e10, 8e6),
        name="attend_back",
    )(idx, qx, kv_own, kv_par, first, att, cosine, sine, *branch, *weight)


def qkv_back_body(
    idx, dqm, dkv_own, dkv_got, cosine, sine, w0, w1, w2, n0, n1, n2a, n2b, n3, gain_one,
    gain_grad_two,
    mine, theirs, o0, o1, o2a, o2b, o3, n_all, dkv, grad, gains,
):
    x, y, core = idx[0], idx[2], idx[3]
    lo = low_lanes((BLK, 128))
    for ref, row, (_, n) in zip((n0, n1, n2a, n2b, n3), PIECE_ROW, PIECES):
        n_all[row : row + n, :] = ref[...]
    for d in range(4):
        at = rows_at((x + d) & 3)
        v = dkv_own[at, :] + dkv_got[at, :].astype(F32)
        v = jnp.where(lo, v * cosine[at, :] - swap_halves(v) * sine[at, :], v).astype(BF16)
        dkv[d * BLK : (d + 1) * BLK, :] = v
    rows = jnp.concatenate([dqm[...], dkv[...]], 1)
    for s, w in zip(weight_rows(idx, DH), (w0, w1, w2)):
        for c in range(w.shape[0] // 512):
            cols = pl.ds(pl.multiple_of(s.start + c * 512, 512), 512)
            res = dot_t(rows, w[c * 512 : (c + 1) * 512, :])
            part = (res * n_all[:, cols].astype(F32)).reshape(ROWS // 8, 8, 512)
            gains[0:1, cols] = jnp.sum(jnp.sum(part, axis=0), axis=0, keepdims=True) / gain_one[:, cols]
            store_parts(res, [r.at[:, cols] for r in (o0, o1, o2a, o2b, o3)])
    grad[...] = dot(dkv[...].T, n_all[...]).astype(BF16)
    gains[1:2, :] = gain_grad_two[...]
    for s in range(4):
        for k, ref in enumerate((mine, theirs)):
            p = ((y + s) & 3) * 2 + (core if k == 0 else 1 - core)
            both = gains[:, pl.ds(pl.multiple_of(p * 256, 256), 256)]
            both = jnp.concatenate([both[:, :128], both[:, 128:], jnp.zeros((12, 128), F32)], 0)
            for h in range(2):
                ref[s, h, :128, :] = grad[:, pl.ds(pl.multiple_of(h * DH + p * 128, 128), 128)]
                ref[s, h, 128:, :] = both.astype(BF16)


def qkv_back(idx, dqm, dkv_own, dkv_got, cosine, sine, weight, pieces, gain_one, gain_grad_two):
    res = pl.pallas_call(
        qkv_back_body,
        out_shape=(sds((4, 2, KVP, 128)),) * 2 + part_shapes(D),
        in_specs=[spec(pltpu.SMEM)] + [spec()] * 15,
        out_specs=(spec(),) * 7,
        scratch_shapes=[
            pltpu.VMEM((ROWS, D), BF16),
            pltpu.VMEM((ROWS, 128), BF16),
            pltpu.VMEM((128, D), BF16),
            pltpu.VMEM((2, D), F32),
        ],
        compiler_params=params(),
        cost_estimate=cost(2 * ROWS * D * QW, 1.3e7),
        name="qkv_back",
    )(
        idx, dqm, dkv_own, dkv_got, cosine, sine, *weight, *pieces,
        gain_one.reshape(1, D), gain_grad_two.reshape(1, D),
    )
    return res[0], res[1], res[2:]


TILES = 6
GAP = TILES * TILE


def load_down(idx, refs, dst, sem):
    copies = []
    for k, (s, ref) in enumerate(zip(weight_rows(idx, FF4 // 2), refs)):
        copies.append(pltpu.make_async_copy(ref, dst.at[s], sem.at[k]))
    return copies


def ffn_body(
    idx, n0, n1, n2a, n2b, n3, c0, c1, c2a, c2b, c3, gate_own, up_own, gate_par, up_par, w0, w1, w2,
    hid, dgate, dup, n_all, c_all, down, sem,
):
    i = pl.program_id(0)
    zh = idx[1]

    @pl.when(i == 0)
    def _():
        copies = load_down(idx, (w0, w1, w2), down, sem)
        for c in copies:
            c.start()
        for refs, dst in (((n0, n1, n2a, n2b, n3), n_all), ((c0, c1, c2a, c2b, c3), c_all)):
            for ref, row, (_, n) in zip(refs, PIECE_ROW, PIECES):
                dst[row : row + n, :] = ref[...]
        for c in copies:
            c.wait()

    own = n_all[:, pl.ds(pl.multiple_of(zh * DH, DH), DH)]
    par = n_all[:, pl.ds(pl.multiple_of((1 - zh) * DH, DH), DH)]
    gate = dot(own, gate_own[...]) + dot(par, gate_par[...])
    up = dot(own, up_own[...]) + dot(par, up_par[...])
    dh = dot_t(c_all[...], down[pl.ds(pl.multiple_of(i * TILE, TILE), TILE), :])
    sig = 1.0 / (1.0 + jnp.exp(-gate))
    act = gate * sig
    hid[...] = (act * up).astype(BF16)
    dgate[...] = (dh * up * sig * (1.0 + gate * (1.0 - sig))).astype(BF16)
    dup[...] = (dh * act).astype(BF16)


def whole(n, w):
    return pl.BlockSpec((n, w), lambda i: (0, 0))


def ffn(idx, normed, cots, gate, up, gate_up, down):
    column = lambda first: pl.BlockSpec((DH, TILE), lambda i: (0, i + first))
    hidden = pl.BlockSpec((ROWS, TILE), lambda i: (0, i))
    return pl.pallas_call(
        ffn_body,
        grid=(TILES,),
        out_shape=(sds((ROWS, FF4)),) * 3,
        in_specs=[spec(pltpu.SMEM)]
        + [whole(n, D) for _, n in PIECES] * 2
        + [column(0), column(0), column(0), column(TILES)]
        + [spec(pl.ANY)] * 3,
        out_specs=[hidden] * 3,
        scratch_shapes=[
            pltpu.VMEM((ROWS, D), BF16),
            pltpu.VMEM((ROWS, D), BF16),
            pltpu.VMEM((GAP, D), BF16),
            pltpu.SemaphoreType.DMA((3,)),
        ],
        compiler_params=params(),
        cost_estimate=cost(6 * ROWS * D * FF4, 3.4e7),
        name="ffn",
    )(idx, *normed, *cots, gate, up, gate_up, gate_up, *down)


def down_body(idx, hid, w0, w1, w2, o0, o1, o2, o3, down, sem):
    copies = load_down(idx, (w0, w1, w2), down, sem)
    for c in copies:
        c.start()
    for c in copies:
        c.wait()
    for n in range(D // 512):
        cols = slice(n * 512, (n + 1) * 512)
        res = dot(hid[...], down[:, cols]).astype(BF16)
        for d, ref in enumerate((o0, o1, o2, o3)):
            ref[:, cols] = res[d * BLK : (d + 1) * BLK]


def down_project(idx, hid, down):
    return pl.pallas_call(
        down_body,
        out_shape=(sds((BLK, D)),) * 4,
        in_specs=[spec(pltpu.SMEM), spec()] + [spec(pl.ANY)] * 3,
        out_specs=(spec(),) * 4,
        scratch_shapes=[pltpu.VMEM((FF4, D), BF16), pltpu.SemaphoreType.DMA((3,))],
        compiler_params=params(),
        cost_estimate=cost(2 * ROWS * D * FF4, 1.1e7),
        name="down_project",
    )(idx, hid, *down)


def ffn_back_body(idx, dgate, dup, gate_own, up_own, par, *refs):
    half = pl.num_programs(0) // 2

    @pl.when(pl.program_id(0) < half)
    def _():
        store_parts(dot_t(dgate[...], gate_own[...]) + dot_t(dup[...], up_own[...]), refs)

    @pl.when(pl.program_id(0) >= half)
    def _():
        store_parts(dot_t(dgate[...], par[:, :FF4]) + dot_t(dup[...], par[:, GAP:]), refs)


def ffn_back(idx, dgate, dup, gate, up, gate_up):
    half = DH // TILE
    rows = pl.BlockSpec((ROWS, FF4), lambda i, idx: (0, 0))
    own = pl.BlockSpec((TILE, FF4), lambda i, idx: (jnp.minimum(i, half - 1), 0))
    par = pl.BlockSpec((TILE, GAP + FF4), lambda i, idx: (jnp.maximum(i - half, 0), 0))
    place = lambda i, idx: (0, i ^ (idx[1] * half))
    return pl.pallas_call(
        ffn_back_body,
        grid_spec=pltpu.PrefetchScalarGridSpec(
            num_scalar_prefetch=1,
            grid=(D // TILE,),
            in_specs=[rows, rows, own, own, par],
            out_specs=[pl.BlockSpec((n, TILE), place) for _, n in PIECES],
        ),
        out_shape=part_shapes(D),
        compiler_params=params(),
        cost_estimate=cost(4 * ROWS * D * FF4, 1.8e7),
        name="ffn_back",
    )(idx, dgate, dup, gate, up, gate_up)


GU_ROWS = FF4 // 128 * 64
PIECE = 2 * GU_ROWS + FF4 // 2
QS = 4


def gate_up_grads_body(*refs):
    na, nb = refs[0:5], refs[5:10]
    dgate, dup, _, out = refs[10:]
    stack = lambda parts: jnp.concatenate([r[...] for r in parts], 0)
    rows = jnp.concatenate([stack(na), stack(nb)], 1).T
    for k, ref in enumerate((dgate, dup)):
        g = dot(rows, ref[...]).astype(BF16)
        for h in range(2):
            for q in range(QS):
                r = g[(QS * h + q) * 64 : (QS * h + q + 1) * 64]
                for c in range(FF4 // 128):
                    first = k * GU_ROWS + c * 64
                    out[h, q, first : first + 64, :] = r[:, c * 128 : (c + 1) * 128]


def gate_up_grads(normed, dgate, dup, pieces):
    return pl.pallas_call(
        gate_up_grads_body,
        grid=(16 // QS,),
        out_shape=sds((2, 16, PIECE, 128)),
        in_specs=[pl.BlockSpec((n, 64 * QS), lambda i: (0, i)) for _, n in PIECES]
        + [pl.BlockSpec((n, 64 * QS), lambda i: (0, i + 16 // QS)) for _, n in PIECES]
        + [whole(ROWS, FF4)] * 2
        + [spec(pl.ANY)],
        out_specs=pl.BlockSpec((2, QS, 2 * GU_ROWS, 128), lambda i: (0, i, 0, 0)),
        input_output_aliases={12: 0},
        compiler_params=params(),
        cost_estimate=cost(4 * ROWS * D * FF4, 2e7),
        name="gate_up_grads",
    )(*normed, *normed, dgate, dup, pieces)


def down_grads_body(*refs):
    cots = refs[0:5]
    hid, out, hid_t = refs[5:]

    @pl.when(pl.program_id(0) == 0)
    def _():
        hid_t[...] = hid[...].T

    g = dot(hid_t[...], jnp.concatenate([r[...] for r in cots], 0)).astype(BF16)
    for h in range(2):
        for q in range(QS):
            out[h, q, :, :] = g[h * (FF4 // 2) : (h + 1) * (FF4 // 2), q * 128 : (q + 1) * 128]


def down_grads(cots, hid):
    return pl.pallas_call(
        down_grads_body,
        grid=(16 // QS,),
        out_shape=sds((2, 16, PIECE, 128)),
        in_specs=[pl.BlockSpec((n, 128 * QS), lambda i: (0, i)) for _, n in PIECES]
        + [whole(ROWS, FF4)],
        out_specs=pl.BlockSpec((2, QS, FF4 // 2, 128), lambda i: (0, i, 2, 0)),
        scratch_shapes=[pltpu.VMEM((FF4, ROWS), BF16)],
        compiler_params=params(),
        cost_estimate=cost(2 * ROWS * D * FF4, 1e7),
        name="down_grads",
    )(*cots, hid)


def unpack_body(piece, gate, up, down):
    for q in range(QS):
        rows = slice(q * 64, (q + 1) * 64)
        for k, ref in enumerate((gate, up)):
            for c in range(FF4 // 128):
                first = k * GU_ROWS + c * 64
                ref[rows, c * 128 : (c + 1) * 128] = piece[q, first : first + 64, :].astype(F32)
        down[:, q * 128 : (q + 1) * 128] = piece[q, 2 * GU_ROWS :, :].astype(F32)


def unpack(pieces):
    return pl.pallas_call(
        unpack_body,
        grid=(16 // QS,),
        out_shape=(sds((DH, FF4), F32), sds((DH, FF4), F32), sds((FF4 // 2, D), F32)),
        in_specs=[pl.BlockSpec((QS, PIECE, 128), lambda i: (i, 0, 0))],
        out_specs=[
            pl.BlockSpec((64 * QS, FF4), lambda i: (i, 0)),
            pl.BlockSpec((64 * QS, FF4), lambda i: (i, 0)),
            pl.BlockSpec((FF4 // 2, 128 * QS), lambda i: (0, i)),
        ],
        compiler_params=params(),
        cost_estimate=cost(1e6, 2.6e7),
        name="unpack",
    )(pieces)


QP = 4 * 128
OP = 2 * (AW // 2)
QOP = QP + OP
KVP = 128 + 16
TAIL = QOP + KVP


def attn_grads_body(idx, *refs):
    na, nb, branch = refs[0:5], refs[5:10], refs[10:15]
    dqm, att, mine, theirs, att_t = refs[15:]
    core = idx[3]

    @pl.when(pl.program_id(0) == 0)
    def _():
        att_t[...] = att[...].T

    stack = lambda parts: jnp.concatenate([r[...] for r in parts], 0)

    def store(h, first, n, zero, one):
        mine[0, h, first : first + n, :] = jnp.where(core == 0, zero, one)
        theirs[0, h, first : first + n, :] = jnp.where(core == 0, one, zero)

    for h, cols in enumerate((na, nb)):
        g = dot(stack(cols).T, dqm[...]).astype(BF16)
        for c in range(4):
            lanes = slice(c * 128, (c + 1) * 128)
            store(h, c * 128, 128, g[:128, lanes], g[128:, lanes])
    g = dot(att_t[...], stack(branch)).astype(BF16)
    for h in range(2):
        r = g[h * (AW // 2) : (h + 1) * (AW // 2)]
        for c in range(2):
            lanes = lambda k: slice(k * 256 + c * 128, k * 256 + (c + 1) * 128)
            store(h, QP + c * (AW // 2), AW // 2, r[:, lanes(0)], r[:, lanes(1)])


def attn_grads(idx, normed, branch, dqm, att):
    turn = lambda s, idx: (s + idx[2]) & 3
    piece = pl.BlockSpec((1, 2, QOP, 128), lambda s, idx: (s, 0, 0, 0))
    fixed = pl.BlockSpec((ROWS, AW), lambda s, idx: (0, 0))
    return pl.pallas_call(
        attn_grads_body,
        grid_spec=pltpu.PrefetchScalarGridSpec(
            num_scalar_prefetch=1,
            grid=(4,),
            in_specs=[pl.BlockSpec((n, 256), lambda s, idx: (0, turn(s, idx))) for _, n in PIECES]
            + [pl.BlockSpec((n, 256), lambda s, idx: (0, turn(s, idx) + 4)) for _, n in PIECES]
            + [pl.BlockSpec((n, 512), lambda s, idx: (0, turn(s, idx))) for _, n in PIECES]
            + [fixed, fixed],
            out_specs=[piece, piece],
            scratch_shapes=[pltpu.VMEM((AW, ROWS), BF16)],
        ),
        out_shape=(sds((4, 2, QOP, 128)),) * 2,
        compiler_params=params(),
        cost_estimate=cost(4 * ROWS * D * AW, 1e7),
        name="attn_grads",
    )(idx, *normed, *normed, *branch, dqm, att)


def small_call(body, out_shape, *args, name):
    return pl.pallas_call(
        body,
        out_shape=out_shape,
        in_specs=[spec(pltpu.SMEM)] + [spec()] * (len(args) - 1),
        out_specs=jax.tree.map(lambda _: spec(), out_shape),
        compiler_params=params(),
        cost_estimate=cost(1e6, 4e6),
        name=name,
    )(*args)


def add(*values):
    return sum((v.astype(F32) for v in values[1:]), values[0].astype(F32)).astype(BF16)


def sum_core_body(idx, a, b, c, d, *outs):
    for s, out in enumerate(outs):
        out[:, :QOP, :] = add(a[s], b[s])
        out[:, QOP:, :] = add(c[s], d[s])


def sum_y_body(idx, a, b, c, d, own, other):
    zh = idx[1]
    own[...] = add(a[zh], b[zh], c[zh], d[zh])
    far = 1 - zh
    other[...] = add(a[far], b[far], c[far], d[far])


def sum_z_body(idx, a, b, c, d, out):
    out[...] = add(a[...], b[...], c[...], d[...])


def unpack_tail_body(idx, *refs):
    y, core = idx[2], idx[3]
    qkv, out, gains = refs[8:]
    for k in range(8):
        piece = refs[k]
        p = ((y - k % 4) & 3) * 2 + (core if k < 4 else 1 - core)
        rows = pl.ds(pl.multiple_of(p * 128, 128), 128)
        for c in range(4):
            qkv[rows, c * 128 : (c + 1) * 128] = piece[c * 128 : (c + 1) * 128, :].astype(F32)
        qkv[rows, AW:] = piece[QOP : QOP + 128, :].astype(F32).T
        g = piece[QOP + 128 :, :].astype(F32)
        for c in range(2):
            first = QP + c * (AW // 2)
            cols = pl.ds(pl.multiple_of(p * 256 + c * 128, 128), 128)
            out[:, cols] = piece[first : first + AW // 2, :].astype(F32)
            gains[:, cols] = g[2 * c : 2 * c + 2]


def sum_tail(idx, first, second, before):
    got_a = lax.ppermute(first[1], "core", shift(2, 1))
    got_b = lax.ppermute(second[1], "core", shift(2, 1))
    part = sds((2, TAIL, 128))
    g = small_call(sum_core_body, (part,) * 4, idx, first[0], got_a, second[0], got_b, name="sum_core")
    got = [tie(lax.ppermute(g[s], "y", shift(4, s)), before) for s in (2, 1, 3)]
    part = sds((TAIL, 128))
    own, other = small_call(sum_y_body, (part,) * 2, idx, g[0], *got, name="sum_y")
    cross = [(2 * a + b, 2 * (1 - a) + (1 - b)) for a in range(2) for b in range(2)]
    g = small_call(
        sum_z_body,
        part,
        idx,
        own,
        lax.ppermute(own, "zl", shift(2, 1)),
        lax.ppermute(other, "zh", shift(2, 1)),
        lax.ppermute(other, ("zl", "zh"), cross),
        name="sum_z",
    )
    mine = [g] + [lax.ppermute(g, "y", shift(4, s)) for s in (1, 2, 3)]
    theirs = [lax.ppermute(v, "core", shift(2, 1)) for v in mine]
    shapes = (sds((DH, QW), F32), sds((AW // 2, D), F32), sds((2, D), F32))
    return own, small_call(unpack_tail_body, shapes, idx, *mine, *theirs, name="unpack_tail")


def inverse_rms(v):
    return lax.rsqrt(jnp.mean(v * v, axis=-1, keepdims=True) + EPSILON)


def norm_back(v, r, gain, grad):
    pulled = grad * gain
    inner = jnp.mean(v * pulled, axis=-1, keepdims=True)
    return r * pulled - v * (r * r * r) * inner, jnp.sum(grad * v * r, axis=0)


def replica_layout(lengths, replica, replica_id):
    sizes = jnp.where(replica == replica_id, lengths, 0)
    starts = jnp.cumsum(sizes) - sizes
    row_ids = jnp.arange(CAP, dtype=jnp.int32)
    inside = (row_ids[:, None] >= starts[None, :]) & (row_ids[:, None] < (starts + sizes)[None, :])
    begin = jnp.sum(jnp.where(inside, starts[None, :], 0), axis=1)
    begin = begin + jnp.where(jnp.any(inside, axis=1), 0, jnp.sum(sizes))
    return begin, row_ids - begin


def on_device(
    tokens, cotangent, gain_one, qkv_weight, out_weight, gate_weight, up_weight, down_weight,
    gain_two, seq_lengths, seq_replica,
):
    x, zh, core = lax.axis_index("x"), lax.axis_index("zh"), lax.axis_index("core")
    y, zl = lax.axis_index("y"), lax.axis_index("zl")
    idx = jnp.stack([x, zh, y, core]).astype(jnp.int32)

    tok = tokens.astype(F32)
    s_one = inverse_rms(tok)
    qkv_got = fetch_half(qkv_weight, core)
    normed_one = gather_x((tok * s_one * gain_one).astype(BF16))
    qkv_all = qkv_weight, qkv_got, lax.ppermute(tie(qkv_got, normed_one[2], normed_one[3]), "core", shift(2, 1))
    out_all = fetch_partner(out_weight, core, qkv_got, normed_one[2], normed_one[3])

    begin, position = replica_layout(seq_lengths, seq_replica, (y * 2 + zl) * 2 + core)
    half_rows = lambda v: lax.dynamic_index_in_dim(v.reshape(4, 2, BLK), zh, 1, False).reshape(ROWS, 1)
    first = jnp.tile(half_rows(begin)[3 * BLK :, 0], 8).reshape(1, QALL)
    lane = jnp.arange(128, dtype=jnp.int32)
    frequency = ROTARY_BASE ** (-(lane % 32).astype(F32) * (2.0 / HD))
    angles = half_rows(position).astype(F32) * frequency[None, :]
    cosine = jnp.cos(angles)
    sine = jnp.where((lane % HD) < HD // 2, -1.0, 1.0)[None, :] * jnp.sin(angles)

    q, kv_own = qkv_forward(idx, normed_one, qkv_all, cosine, sine)
    cots = gather_x(tie(cotangent, normed_one[2], normed_one[3]), (kv_own,))
    rows = DH // 8
    mine = lambda w: lax.dynamic_slice_in_dim(w, (y * 2 + core) * rows, rows, 0)
    cross = [(2 * a + b, 2 * (1 - a) + (1 - b)) for a in range(2) for b in range(2)]
    gate_up = lax.ppermute(
        jnp.concatenate(
            [
                tie(mine(gate_weight), out_all[1], kv_own),
                jnp.zeros((rows, GAP - FF4), BF16),
                mine(up_weight),
            ],
            1,
        ),
        ("zl", "zh"),
        cross,
    )
    kv_par = lax.ppermute(tie(kv_own, cots[1], cots[4]), "zh", shift(2, 1))
    down_got = fetch_half(tie(down_weight, gate_up), core)
    att, qx = attend(idx, tie(q, cots[2], cots[3]), kv_own, kv_par, first)
    gate_up = lax.all_gather(tie(gate_up, qx), ("y", "core"), axis=0, tiled=True)
    parts = out_project(idx, att, out_all)
    after_attn = tie(tok, down_got) + scatter_x(parts)[0]

    r_two = inverse_rms(after_attn)
    normed_two = gather_x((after_attn * r_two * gain_two).astype(BF16))
    down_all = down_weight, down_got, lax.ppermute(tie(down_got, normed_two[1], normed_two[4]), "core", shift(2, 1))
    hid, dgate, dup = ffn(idx, normed_two, cots, gate_weight, up_weight, gate_up, down_all)
    d_parts = ffn_back(idx, dgate, dup, gate_weight, up_weight, gate_up)
    own_grads = down_grads(cots, tie(hid, d_parts[2]))
    d_own, q1, q3 = relay(d_parts)
    own_grads = gate_up_grads(normed_two, tie(dgate, q1, q3), dup, own_grads)
    from_prev = lax.ppermute(q1, "x", shift(4, 1))
    from_next = lax.ppermute(q3, "x", shift(4, -1))
    grads = lax.psum_scatter(
        tie(own_grads, from_prev, from_next).reshape(32, PIECE, 128),
        ("zh", "zl", "y", "core"), scatter_dimension=0, tiled=True,
    )
    d_two = d_own.astype(F32) + from_prev.astype(F32) + from_next.astype(F32)
    back_two, gain_grad_two = norm_back(after_attn, r_two, gain_two, d_two)
    after_grad = cotangent.astype(F32) + back_two
    branch = gather_x(after_grad.astype(BF16))
    layer_parts = down_project(idx, tie(hid, after_grad), down_all)
    att = tie(att, *layer_parts)
    layer = [layer_parts[0]] + [
        lax.ppermute(tie(layer_parts[k], branch[2], branch[3]), "x", shift(4, k)) for k in (1, 3)
    ]
    dqm, dkv_own, dkv_par = attend_back(
        idx, qx, kv_own, kv_par, first, att, cosine, sine, branch, out_all
    )
    dkv_got = lax.ppermute(dkv_par, "zh", shift(2, 1))
    tail = attn_grads(
        idx, normed_one, branch, dqm.reshape(ROWS, AW), tie(att, *layer).reshape(ROWS, AW)
    )
    dkv_got = tie(dkv_got, tail[0])
    *tail_kv, parts = qkv_back(
        idx, dqm.reshape(ROWS, AW), dkv_own, dkv_got, cosine, sine, qkv_all, normed_one, gain_one,
        gain_grad_two,
    )
    d_one, first_step = scatter_x(parts)
    layer.append(lax.ppermute(tie(layer_parts[2], d_one), "x", shift(4, 2)))
    layer_out = sum((v.astype(F32) for v in layer), after_attn).astype(BF16)
    back_one, _ = norm_back(tok, s_one, gain_one, d_one)
    input_grad = (after_grad + back_one).astype(BF16)

    over_x = lambda v: sum((lax.ppermute(v, "x", shift(4, s)) for s in (1, 2, 3)), v)
    tail = tie(tail[0], *first_step), tie(tail[1], dkv_got)
    summed, (grad_qkv, grad_out, gains) = sum_tail(idx, tail, tail_kv, d_one)
    grads = lax.all_gather(tie(grads, summed), ("zl", "y", "core"), axis=0, tiled=True)
    grad_gate, grad_up, grad_down = unpack(grads)
    gains = over_x(gains)
    return (
        layer_out, input_grad, gains[0], grad_qkv, grad_out, grad_gate, grad_up,
        grad_down, gains[1],
    )


def solution(mesh):
    grid = Mesh(mesh.devices.reshape(SIZES), AXES)
    rows = P(AXES, None)
    both = P(("x", "zh"), None)
    return jax.shard_map(
        on_device,
        mesh=grid,
        in_specs=(
            rows, rows, P(), P("zh", "x"), both, P("zh", "x"), P("zh", "x"), both, P(), P(), P(),
        ),
        out_specs=(
            rows, rows, P(), P("zh", "x"), both, P("zh", "x"), P("zh", "x"), both, P(),
        ),
        check_vma=False,
    )
```

```python
import jax
import jax.numpy as jnp
from jax import lax
from jax.experimental import pallas as pl
from jax.experimental.pallas import tpu as pltpu
from jax.sharding import Mesh
from jax.sharding import PartitionSpec as P

HEADS = 32
KV = 4
HD = 64
EPSILON = 1e-05
ROTARY_BASE = 10000.0
MASKED = -1e30

AXES = ("y", "zl", "core", "x", "zh")
SIZES = (4, 2, 2, 4, 2)
BLK = 160
HALF = BLK // 2
ROWS = 4 * BLK
CAP = 2 * ROWS
D = 2048
DH = D // 2
QW = 640
AW = 512
FF4 = 1408
TILE = 256
F32 = jnp.float32
BF16 = jnp.bfloat16
VLIM = 60 * 1024 * 1024


def spec(memory=pltpu.VMEM):
    return pl.BlockSpec(memory_space=memory)


def params(**kw):
    return pltpu.CompilerParams(vmem_limit_bytes=VLIM, **kw)


def cost(flops, nbytes):
    return pl.CostEstimate(flops=int(flops), bytes_accessed=int(nbytes), transcendentals=0)


def sds(shape, dtype=BF16):
    return jax.ShapeDtypeStruct(shape, dtype)


def dot(a, b):
    return jnp.dot(a, b, preferred_element_type=F32)


def dot_t(a, b):
    return lax.dot_general(a, b, (((1,), (1,)), ((), ())), preferred_element_type=F32)


def t_dot(a, b):
    return lax.dot_general(a, b, (((0,), (0,)), ((), ())), preferred_element_type=F32)


def tie(v, *deps):
    return lax.optimization_barrier((v,) + deps)[0]


def shift(n, s):
    return [(i, (i + s) % n) for i in range(n)]


def gather_x(v, wait=()):
    from_prev = lax.ppermute(v, "x", shift(4, 1))
    from_next = lax.ppermute(v, "x", shift(4, -1))
    send_a = tie(from_prev[:HALF], from_next, *wait)
    send_b = tie(from_next[HALF:], from_prev, *wait)
    opp_a = lax.ppermute(send_a, "x", shift(4, 1))
    opp_b = lax.ppermute(send_b, "x", shift(4, -1))
    return v, from_next, opp_a, opp_b, from_prev


def relay_body(p1, got_a, p3, got_b, q1, q3):
    q1[...] = (p1[...].astype(F32) + got_a[...].astype(F32)).astype(BF16)
    q3[...] = (p3[...].astype(F32) + got_b[...].astype(F32)).astype(BF16)


def relay(parts):
    p0, p1, p2a, p2b, p3 = parts
    got_a = lax.ppermute(p2a, "x", shift(4, 1))
    got_b = lax.ppermute(p2b, "x", shift(4, -1))
    half = lambda k: pl.BlockSpec((HALF, D), lambda i: (k, 0))
    q1, q3 = pl.pallas_call(
        relay_body,
        grid=(1,),
        out_shape=(sds((BLK, D)),) * 2,
        in_specs=[half(0), half(0), half(1), half(0)],
        out_specs=(half(0), half(1)),
        input_output_aliases={0: 0, 2: 1},
        compiler_params=params(),
        cost_estimate=cost(1e6, 2e6),
        name="relay",
    )(p1, got_a, p3, got_b)
    return p0, q1, q3


def scatter_x(parts):
    return last_step(*relay(parts))


def last_step(p0, q1, q3):
    return p0, lax.ppermute(q1, "x", shift(4, 1)), lax.ppermute(q3, "x", shift(4, -1))


PIECES = ((0, BLK), (1, BLK), (2, HALF), (2, HALF), (3, BLK))
PIECE_ROW = (0, BLK, 2 * BLK, 2 * BLK + HALF, 3 * BLK)


def part_shapes(width, dtype=BF16):
    return tuple(sds((n, width), dtype) for _, n in PIECES)


def low_lanes(shape):
    return lax.broadcasted_iota(jnp.int32, shape, 1) < HD


def swap_halves(v):
    lane = lax.broadcasted_iota(jnp.int32, v.shape, 1) % HD
    return jnp.where(lane < HD // 2, pltpu.roll(v, 128 - HD // 2, 1), pltpu.roll(v, HD // 2, 1))


def rows_at(block):
    return pl.ds(pl.multiple_of(block * BLK, 32), BLK)


def fetch_half(w, core):
    half = w.shape[0] // 2
    return lax.ppermute(lax.dynamic_slice_in_dim(w, core * half, half, 0), "zh", shift(2, 1))


def fetch_partner(w, core, *deps):
    got = fetch_half(tie(w, *deps), core)
    return w, got, lax.ppermute(got, "core", shift(2, 1))


def weight_rows(idx, rows):
    zh, core = idx[1], idx[3]
    far = (1 - zh) * rows
    half = rows // 2
    at = lambda first, n: pl.ds(pl.multiple_of(first, half), n)
    return at(zh * rows, rows), at(far + core * half, half), at(far + (1 - core) * half, half)


def qkv_body(idx, n0, n1, n2a, n2b, n3, w0, w1, w2, cosine, sine, q_ref, kv_ref, rows):
    x = idx[0]
    lo = low_lanes((BLK, 128))
    for ref, row, (_, n) in zip((n0, n1, n2a, n2b, n3), PIECE_ROW, PIECES):
        rows[row : row + n, :] = ref[...]
    s0, s1, s2 = weight_rows(idx, DH)
    acc = dot(rows[:, s0], w0[...]) + dot(rows[:, s1], w1[...]) + dot(rows[:, s2], w2[...])
    for d in range(4):
        at = rows_at((x + d) & 3)
        cs = cosine[at, :]
        sn = sine[at, :]
        for p in range(5):
            v = acc[d * BLK : (d + 1) * BLK, p * 128 : (p + 1) * 128]
            r = v * cs + swap_halves(v) * sn
            if p < 4:
                r = r * (HD**-0.5 * LOG2E)
                a = (x + d) & 3
                for k, w in enumerate((r, pltpu.roll(r, HD, 1))):
                    head = slice((2 * p + k) * BLK, (2 * p + k + 1) * BLK)
                    q_ref[a, head, :] = jnp.where(lo, w, 0.0).astype(BF16)
            else:
                kv_ref[at, :] = jnp.where(lo, r, v).astype(BF16)


def qkv_forward(idx, pieces, weight, cosine, sine):
    return pl.pallas_call(
        qkv_body,
        out_shape=(sds((4, QALL, 128)), sds((ROWS, 128))),
        in_specs=[spec(pltpu.SMEM)] + [spec()] * 10,
        out_specs=(spec(), spec()),
        scratch_shapes=[pltpu.VMEM((ROWS, D), BF16)],
        compiler_params=params(),
        cost_estimate=cost(2 * ROWS * D * QW, 7e6),
        name="qkv_forward",
    )(idx, *pieces, *weight, cosine, sine)


QALL = 8 * BLK
PAIR = 2 * BLK
LOG2E = 1.4426950408889634
LN2 = 0.6931471805599453


def split3(v):
    a = v.astype(BF16).astype(F32)
    b = (v - a).astype(BF16).astype(F32)
    return a, b, v - a - b


def with_lanes(v, parts):
    lane = lax.broadcasted_iota(jnp.int32, v.shape, 1)
    out = jnp.where(lane < HD, v, 0.0)
    for k, part in enumerate(parts):
        out = jnp.where(lane == HD + k, part, out)
    return out


def spread_keys(zh, kv_own, kv_par, kk, vv, fill):
    shape = (BLK, 128)
    lo = low_lanes(shape)
    rest = fill(lax.broadcasted_iota(jnp.int32, shape, 1) - HD)
    for j in range(4):
        for src, off in ((kv_own, zh), (kv_par, 1 - zh)):
            v = src[j * BLK : (j + 1) * BLK, :].astype(F32)
            at = rows_at(2 * j + off)
            kk[at, :] = jnp.where(lo, v, rest).astype(BF16)
            vv[at, :] = jnp.where(lo, pltpu.roll(v, HD, 1), rest).astype(BF16)


def masked(s, zh, j, kb, first):
    if j < 3 and kb < j:
        return s
    u = kb * PAIR + lax.broadcasted_iota(jnp.int32, (PAIR, QALL), 0)
    allowed = None
    if kb == j:
        t = (2 * j + zh) * BLK + lax.broadcasted_iota(jnp.int32, (1, QALL), 1) % BLK
        allowed = u <= t
    if j == 3:
        later = u >= first[...]
        allowed = later if allowed is None else allowed & later
    return jnp.where(allowed, s, MASKED)


def attend_body(idx, q, kv_own, kv_par, first, att, qx, kk, vv, vt, s_ref, e_ref):
    x, zh = idx[0], idx[1]
    spread_keys(zh, kv_own, kv_par, kk, vv, lambda lane: 1.0)
    vt[...] = vv[...].T
    lo = low_lanes((BLK, 128))
    for j in range(4):
        n = PAIR * (j + 1)
        qj = q[j]
        top = jnp.full((1, QALL), MASKED, F32)
        for kb in range(j + 1):
            rows = slice(kb * PAIR, (kb + 1) * PAIR)
            s = masked(dot_t(kk[rows, :], qj), zh, j, kb, first)
            s_ref[rows, :] = s
            top = jnp.maximum(top, jnp.max(s, axis=0, keepdims=True))
        for k in range(n // 64):
            rows = slice(k * 64, (k + 1) * 64)
            e_ref[rows, :] = jnp.exp2(s_ref[rows, :] - top).astype(BF16)
        o = dot(vt[:, :n], e_ref[:n, :])
        lse = split3(top + jnp.log(o[HD : HD + 1, :]) * LOG2E)
        row = lax.broadcasted_iota(jnp.int32, (128, QALL), 0)
        extra = jnp.zeros((128, QALL), F32)
        for k, part in enumerate(lse):
            extra = jnp.where(row == HD + k, part, extra)
        qx[j] = (qj.astype(F32) + extra.T).astype(BF16)
        o = o.T
        r = pltpu.roll(o, HD, 1)
        rel = (j - x) & 3
        for p in range(4):
            even, odd = slice(2 * p * BLK, (2 * p + 1) * BLK), slice((2 * p + 1) * BLK, (2 * p + 2) * BLK)
            num = jnp.where(lo, o[even], r[odd])
            den = jnp.where(lo, r[even], o[odd])
            att[rel, :, p * 128 : (p + 1) * 128] = (num / den).astype(BF16)


def attend(idx, q, kv_own, kv_par, first):
    return pl.pallas_call(
        attend_body,
        out_shape=(sds((4, BLK, AW)), sds((4, QALL, 128))),
        in_specs=[spec(pltpu.SMEM)] + [spec()] * 4,
        out_specs=(spec(), spec()),
        scratch_shapes=[
            pltpu.VMEM((CAP, 128), BF16),
            pltpu.VMEM((CAP, 128), BF16),
            pltpu.VMEM((128, CAP), BF16),
            pltpu.VMEM((CAP, QALL), F32),
            pltpu.VMEM((CAP, QALL), BF16),
        ],
        compiler_params=params(),
        cost_estimate=cost(1.2e10, 3e6),
        name="attend",
    )(idx, q, kv_own, kv_par, first)


def store_parts(res, refs):
    for ref, row, (_, n) in zip(refs, PIECE_ROW, PIECES):
        ref[...] = res[row : row + n].astype(BF16)


def out_body(idx, att, w0, w1, w2, o0, o1, o2a, o2b, o3):
    s0, s1, s2 = weight_rows(idx, AW // 2)
    for d, ref in ((2, None), (1, o1), (3, o3), (0, o0)):
        a = att.at[d]
        res = dot(a[:, s0], w0[...]) + dot(a[:, s1], w1[...]) + dot(a[:, s2], w2[...])
        res = res.astype(BF16)
        if d == 2:
            o2a[...] = res[:HALF]
            o2b[...] = res[HALF:]
        else:
            ref[...] = res


def out_project(idx, att, weight):
    return pl.pallas_call(
        out_body,
        out_shape=part_shapes(D),
        in_specs=[spec(pltpu.SMEM)] + [spec()] * 4,
        out_specs=(spec(),) * 5,
        compiler_params=params(),
        cost_estimate=cost(2 * ROWS * D * AW, 5.5e6),
        name="out_project",
    )(idx, att, *weight)


def stack_heads(v):
    return v, pltpu.roll(v, HD, 1)


def attend_back_body(
    idx, qx, kv_own, kv_par, first, att, cosine, sine, b0, b1, b2a, b2b, b3, w0, w1, w2,
    dq_ref, dkv_own, dkv_par, kk, vv, dout, do_all, dkk, dvv, e_ref, ds_ref, dq_acc,
):
    x, zh = idx[0], idx[1]
    spread_keys(zh, kv_own, kv_par, kk, vv, lambda lane: jnp.where(lane < 3, -1.0, 0.0))
    s0, s1, s2 = weight_rows(idx, AW // 2)
    for d in range(4):
        if d == 2:
            rows = jnp.concatenate([b2a[...], b2b[...]], 0)
        else:
            rows = (b0, b1, None, b3)[d][...]
        at = rows_at((x + d) & 3)
        for s, w in ((s0, w0), (s1, w1), (s2, w2)):
            dout[at, s] = dot_t(rows, w[...]).astype(BF16)
    lo = low_lanes((BLK, 128))
    for j in range(4):
        rel = (j - x) & 3
        here = slice(j * BLK, (j + 1) * BLK)
        for p in range(4):
            cols = slice(p * 128, (p + 1) * 128)
            do = dout[here, cols].astype(F32)
            prod = do * att[rel, :, cols].astype(F32)
            for k, (v, w) in enumerate(zip(stack_heads(do), stack_heads(prod))):
                delta = jnp.sum(jnp.where(lo, w, 0.0), axis=1, keepdims=True)
                head = slice((2 * p + k) * BLK, (2 * p + k + 1) * BLK)
                do_all[head, :] = with_lanes(v, split3(delta)).astype(BF16)
        for kb in range(j + 1):
            rows = slice(kb * PAIR, (kb + 1) * PAIR)
            e = jnp.exp2(masked(dot_t(kk[rows, :], qx[j]), zh, j, kb, first))
            e_ref[...] = e.astype(BF16)
            ds_ref[...] = (e * dot_t(vv[rows, :], do_all[...])).astype(BF16)
            dv = dot(e_ref[...], do_all[...])
            dk = dot(ds_ref[...], qx[j])
            dq = t_dot(ds_ref[...], kk[rows, :])
            if kb == j:
                dvv[rows, :], dkk[rows, :] = dv, dk
            else:
                dvv[rows, :] += dv
                dkk[rows, :] += dk
            if kb == 0:
                dq_acc[...] = dq
            else:
                dq_acc[...] += dq
        for p in range(4):
            even, odd = slice(2 * p * BLK, (2 * p + 1) * BLK), slice((2 * p + 1) * BLK, (2 * p + 2) * BLK)
            v = jnp.where(lo, dq_acc[even, :], pltpu.roll(dq_acc[odd, :], HD, 1)) * HD**-0.5
            v = v * cosine[here, :] - swap_halves(v) * sine[here, :]
            dq_ref[rel, :, p * 128 : (p + 1) * 128] = v.astype(BF16)
    for j in range(4):
        for dst, off in ((dkv_own, zh), (dkv_par, 1 - zh)):
            at = rows_at(2 * j + off)
            both = jnp.where(lo, dkk[at, :] * LN2, pltpu.roll(dvv[at, :], HD, 1))
            dst[j * BLK : (j + 1) * BLK, :] = both.astype(dst.dtype)


def attend_back(idx, qx, kv_own, kv_par, first, att, cosine, sine, branch, weight):
    return pl.pallas_call(
        attend_back_body,
        out_shape=(sds((4, BLK, AW)), sds((ROWS, 128), F32), sds((ROWS, 128))),
        in_specs=[spec(pltpu.SMEM)] + [spec()] * 15,
        out_specs=(spec(),) * 3,
        scratch_shapes=[
            pltpu.VMEM((CAP, 128), BF16),
            pltpu.VMEM((CAP, 128), BF16),
            pltpu.VMEM((ROWS, AW), BF16),
            pltpu.VMEM((QALL, 128), BF16),
            pltpu.VMEM((CAP, 128), F32),
            pltpu.VMEM((CAP, 128), F32),
            pltpu.VMEM((PAIR, QALL), BF16),
            pltpu.VMEM((PAIR, QALL), BF16),
            pltpu.VMEM((QALL, 128), F32),
        ],
        compiler_params=params(),
        cost_estimate=cost(3e10, 8e6),
        name="attend_back",
    )(idx, qx, kv_own, kv_par, first, att, cosine, sine, *branch, *weight)


def qkv_back_body(
    idx, dqm, dkv_own, dkv_got, cosine, sine, w0, w1, w2, n0, n1, n2a, n2b, n3, gain_one,
    gain_grad_two,
    mine, theirs, o0, o1, o2a, o2b, o3, n_all, dkv, grad, gains,
):
    x, y, core = idx[0], idx[2], idx[3]
    lo = low_lanes((BLK, 128))
    for ref, row, (_, n) in zip((n0, n1, n2a, n2b, n3), PIECE_ROW, PIECES):
        n_all[row : row + n, :] = ref[...]
    for d in range(4):
        at = rows_at((x + d) & 3)
        v = dkv_own[at, :] + dkv_got[at, :].astype(F32)
        v = jnp.where(lo, v * cosine[at, :] - swap_halves(v) * sine[at, :], v).astype(BF16)
        dkv[d * BLK : (d + 1) * BLK, :] = v
    rows = jnp.concatenate([dqm[...], dkv[...]], 1)
    for s, w in zip(weight_rows(idx, DH), (w0, w1, w2)):
        for c in range(w.shape[0] // 512):
            cols = pl.ds(pl.multiple_of(s.start + c * 512, 512), 512)
            res = dot_t(rows, w[c * 512 : (c + 1) * 512, :])
            part = (res * n_all[:, cols].astype(F32)).reshape(ROWS // 8, 8, 512)
            gains[0:1, cols] = jnp.sum(jnp.sum(part, axis=0), axis=0, keepdims=True) / gain_one[:, cols]
            store_parts(res, [r.at[:, cols] for r in (o0, o1, o2a, o2b, o3)])
    grad[...] = dot(dkv[...].T, n_all[...]).astype(BF16)
    gains[1:2, :] = gain_grad_two[...]
    for s in range(4):
        for k, ref in enumerate((mine, theirs)):
            p = ((y + s) & 3) * 2 + (core if k == 0 else 1 - core)
            both = gains[:, pl.ds(pl.multiple_of(p * 256, 256), 256)]
            both = jnp.concatenate([both[:, :128], both[:, 128:], jnp.zeros((12, 128), F32)], 0)
            for h in range(2):
                ref[s, h, :128, :] = grad[:, pl.ds(pl.multiple_of(h * DH + p * 128, 128), 128)]
                ref[s, h, 128:, :] = both.astype(BF16)


def qkv_back(idx, dqm, dkv_own, dkv_got, cosine, sine, weight, pieces, gain_one, gain_grad_two):
    res = pl.pallas_call(
        qkv_back_body,
        out_shape=(sds((4, 2, KVP, 128)),) * 2 + part_shapes(D),
        in_specs=[spec(pltpu.SMEM)] + [spec()] * 15,
        out_specs=(spec(),) * 7,
        scratch_shapes=[
            pltpu.VMEM((ROWS, D), BF16),
            pltpu.VMEM((ROWS, 128), BF16),
            pltpu.VMEM((128, D), BF16),
            pltpu.VMEM((2, D), F32),
        ],
        compiler_params=params(),
        cost_estimate=cost(2 * ROWS * D * QW, 1.3e7),
        name="qkv_back",
    )(
        idx, dqm, dkv_own, dkv_got, cosine, sine, *weight, *pieces,
        gain_one.reshape(1, D), gain_grad_two.reshape(1, D),
    )
    return res[0], res[1], res[2:]


TILES = 6
GAP = TILES * TILE


def load_down(idx, refs, dst, sem):
    copies = []
    for k, (s, ref) in enumerate(zip(weight_rows(idx, FF4 // 2), refs)):
        copies.append(pltpu.make_async_copy(ref, dst.at[s], sem.at[k]))
    return copies


def ffn_body(
    idx, n0, n1, n2a, n2b, n3, c0, c1, c2a, c2b, c3, gate_own, up_own, gate_par, up_par, w0, w1, w2,
    hid, dgate, dup, n_all, c_all, down, sem,
):
    i = pl.program_id(0)
    zh = idx[1]

    @pl.when(i == 0)
    def _():
        copies = load_down(idx, (w0, w1, w2), down, sem)
        for c in copies:
            c.start()
        for refs, dst in (((n0, n1, n2a, n2b, n3), n_all), ((c0, c1, c2a, c2b, c3), c_all)):
            for ref, row, (_, n) in zip(refs, PIECE_ROW, PIECES):
                dst[row : row + n, :] = ref[...]
        for c in copies:
            c.wait()

    own = n_all[:, pl.ds(pl.multiple_of(zh * DH, DH), DH)]
    par = n_all[:, pl.ds(pl.multiple_of((1 - zh) * DH, DH), DH)]
    gate = dot(own, gate_own[...]) + dot(par, gate_par[...])
    up = dot(own, up_own[...]) + dot(par, up_par[...])
    dh = dot_t(c_all[...], down[pl.ds(pl.multiple_of(i * TILE, TILE), TILE), :])
    sig = 1.0 / (1.0 + jnp.exp(-gate))
    act = gate * sig
    hid[...] = (act * up).astype(BF16)
    dgate[...] = (dh * up * sig * (1.0 + gate * (1.0 - sig))).astype(BF16)
    dup[...] = (dh * act).astype(BF16)


def whole(n, w):
    return pl.BlockSpec((n, w), lambda i: (0, 0))


def ffn(idx, normed, cots, gate, up, gate_up, down):
    column = lambda first: pl.BlockSpec((DH, TILE), lambda i: (0, i + first))
    hidden = pl.BlockSpec((ROWS, TILE), lambda i: (0, i))
    return pl.pallas_call(
        ffn_body,
        grid=(TILES,),
        out_shape=(sds((ROWS, FF4)),) * 3,
        in_specs=[spec(pltpu.SMEM)]
        + [whole(n, D) for _, n in PIECES] * 2
        + [column(0), column(0), column(0), column(TILES)]
        + [spec(pl.ANY)] * 3,
        out_specs=[hidden] * 3,
        scratch_shapes=[
            pltpu.VMEM((ROWS, D), BF16),
            pltpu.VMEM((ROWS, D), BF16),
            pltpu.VMEM((GAP, D), BF16),
            pltpu.SemaphoreType.DMA((3,)),
        ],
        compiler_params=params(),
        cost_estimate=cost(6 * ROWS * D * FF4, 3.4e7),
        name="ffn",
    )(idx, *normed, *cots, gate, up, gate_up, gate_up, *down)


def down_body(idx, hid, w0, w1, w2, o0, o1, o2, o3, down, sem):
    copies = load_down(idx, (w0, w1, w2), down, sem)
    for c in copies:
        c.start()
    for c in copies:
        c.wait()
    for n in range(D // 512):
        cols = slice(n * 512, (n + 1) * 512)
        res = dot(hid[...], down[:, cols]).astype(BF16)
        for d, ref in enumerate((o0, o1, o2, o3)):
            ref[:, cols] = res[d * BLK : (d + 1) * BLK]


def down_project(idx, hid, down):
    return pl.pallas_call(
        down_body,
        out_shape=(sds((BLK, D)),) * 4,
        in_specs=[spec(pltpu.SMEM), spec()] + [spec(pl.ANY)] * 3,
        out_specs=(spec(),) * 4,
        scratch_shapes=[pltpu.VMEM((FF4, D), BF16), pltpu.SemaphoreType.DMA((3,))],
        compiler_params=params(),
        cost_estimate=cost(2 * ROWS * D * FF4, 1.1e7),
        name="down_project",
    )(idx, hid, *down)


def ffn_back_body(idx, dgate, dup, gate_own, up_own, par, *refs):
    half = pl.num_programs(0) // 2

    @pl.when(pl.program_id(0) < half)
    def _():
        store_parts(dot_t(dgate[...], gate_own[...]) + dot_t(dup[...], up_own[...]), refs)

    @pl.when(pl.program_id(0) >= half)
    def _():
        store_parts(dot_t(dgate[...], par[:, :FF4]) + dot_t(dup[...], par[:, GAP:]), refs)


def ffn_back(idx, dgate, dup, gate, up, gate_up):
    half = DH // TILE
    rows = pl.BlockSpec((ROWS, FF4), lambda i, idx: (0, 0))
    own = pl.BlockSpec((TILE, FF4), lambda i, idx: (jnp.minimum(i, half - 1), 0))
    par = pl.BlockSpec((TILE, GAP + FF4), lambda i, idx: (jnp.maximum(i - half, 0), 0))
    place = lambda i, idx: (0, i ^ (idx[1] * half))
    return pl.pallas_call(
        ffn_back_body,
        grid_spec=pltpu.PrefetchScalarGridSpec(
            num_scalar_prefetch=1,
            grid=(D // TILE,),
            in_specs=[rows, rows, own, own, par],
            out_specs=[pl.BlockSpec((n, TILE), place) for _, n in PIECES],
        ),
        out_shape=part_shapes(D),
        compiler_params=params(),
        cost_estimate=cost(4 * ROWS * D * FF4, 1.8e7),
        name="ffn_back",
    )(idx, dgate, dup, gate, up, gate_up)


GU_ROWS = FF4 // 128 * 64
PIECE = 2 * GU_ROWS + FF4 // 2
QS = 4


def ffn_grads_body(*refs):
    na, nb, cots = refs[0:5], refs[5:10], refs[10:15]
    hid, dgate, dup, out, hid_t = refs[15:]

    @pl.when(pl.program_id(0) == 0)
    def _():
        hid_t[...] = hid[...].T

    stack = lambda parts: jnp.concatenate([r[...] for r in parts], 0)
    rows = jnp.concatenate([stack(na), stack(nb)], 1).T
    for k, ref in enumerate((dgate, dup)):
        g = dot(rows, ref[...]).astype(BF16)
        for h in range(2):
            for q in range(QS):
                r = g[(QS * h + q) * 64 : (QS * h + q + 1) * 64]
                for c in range(FF4 // 128):
                    first = k * GU_ROWS + c * 64
                    out[h, q, first : first + 64, :] = r[:, c * 128 : (c + 1) * 128]
    g = dot(hid_t[...], stack(cots)).astype(BF16)
    for h in range(2):
        for q in range(QS):
            out[h, q, 2 * GU_ROWS :, :] = g[
                h * (FF4 // 2) : (h + 1) * (FF4 // 2), q * 128 : (q + 1) * 128
            ]


def ffn_grads(normed, cots, hid, dgate, dup):
    return pl.pallas_call(
        ffn_grads_body,
        grid=(16 // QS,),
        out_shape=sds((2, 16, PIECE, 128)),
        in_specs=[pl.BlockSpec((n, 64 * QS), lambda i: (0, i)) for _, n in PIECES]
        + [pl.BlockSpec((n, 64 * QS), lambda i: (0, i + 16 // QS)) for _, n in PIECES]
        + [pl.BlockSpec((n, 128 * QS), lambda i: (0, i)) for _, n in PIECES]
        + [whole(ROWS, FF4)] * 3,
        out_specs=pl.BlockSpec((2, QS, PIECE, 128), lambda i: (0, i, 0, 0)),
        scratch_shapes=[pltpu.VMEM((FF4, ROWS), BF16)],
        compiler_params=params(),
        cost_estimate=cost(6 * ROWS * D * FF4, 3e7),
        name="ffn_grads",
    )(*normed, *normed, *cots, hid, dgate, dup)


def unpack_body(piece, gate, up, down):
    for q in range(QS):
        rows = slice(q * 64, (q + 1) * 64)
        for k, ref in enumerate((gate, up)):
            for c in range(FF4 // 128):
                first = k * GU_ROWS + c * 64
                ref[rows, c * 128 : (c + 1) * 128] = piece[q, first : first + 64, :].astype(F32)
        down[:, q * 128 : (q + 1) * 128] = piece[q, 2 * GU_ROWS :, :].astype(F32)


def unpack(pieces):
    return pl.pallas_call(
        unpack_body,
        grid=(16 // QS,),
        out_shape=(sds((DH, FF4), F32), sds((DH, FF4), F32), sds((FF4 // 2, D), F32)),
        in_specs=[pl.BlockSpec((QS, PIECE, 128), lambda i: (i, 0, 0))],
        out_specs=[
            pl.BlockSpec((64 * QS, FF4), lambda i: (i, 0)),
            pl.BlockSpec((64 * QS, FF4), lambda i: (i, 0)),
            pl.BlockSpec((FF4 // 2, 128 * QS), lambda i: (0, i)),
        ],
        compiler_params=params(),
        cost_estimate=cost(1e6, 2.6e7),
        name="unpack",
    )(pieces)


QP = 4 * 128
OP = 2 * (AW // 2)
QOP = QP + OP
KVP = 128 + 16
TAIL = QOP + KVP


def attn_grads_body(idx, *refs):
    na, nb, branch = refs[0:5], refs[5:10], refs[10:15]
    dqm, att, mine, theirs, att_t = refs[15:]
    core = idx[3]

    @pl.when(pl.program_id(0) == 0)
    def _():
        att_t[...] = att[...].T

    stack = lambda parts: jnp.concatenate([r[...] for r in parts], 0)

    def store(h, first, n, zero, one):
        mine[0, h, first : first + n, :] = jnp.where(core == 0, zero, one)
        theirs[0, h, first : first + n, :] = jnp.where(core == 0, one, zero)

    for h, cols in enumerate((na, nb)):
        g = dot(stack(cols).T, dqm[...]).astype(BF16)
        for c in range(4):
            lanes = slice(c * 128, (c + 1) * 128)
            store(h, c * 128, 128, g[:128, lanes], g[128:, lanes])
    g = dot(att_t[...], stack(branch)).astype(BF16)
    for h in range(2):
        r = g[h * (AW // 2) : (h + 1) * (AW // 2)]
        for c in range(2):
            lanes = lambda k: slice(k * 256 + c * 128, k * 256 + (c + 1) * 128)
            store(h, QP + c * (AW // 2), AW // 2, r[:, lanes(0)], r[:, lanes(1)])


def attn_grads(idx, normed, branch, dqm, att):
    turn = lambda s, idx: (s + idx[2]) & 3
    piece = pl.BlockSpec((1, 2, QOP, 128), lambda s, idx: (s, 0, 0, 0))
    fixed = pl.BlockSpec((ROWS, AW), lambda s, idx: (0, 0))
    return pl.pallas_call(
        attn_grads_body,
        grid_spec=pltpu.PrefetchScalarGridSpec(
            num_scalar_prefetch=1,
            grid=(4,),
            in_specs=[pl.BlockSpec((n, 256), lambda s, idx: (0, turn(s, idx))) for _, n in PIECES]
            + [pl.BlockSpec((n, 256), lambda s, idx: (0, turn(s, idx) + 4)) for _, n in PIECES]
            + [pl.BlockSpec((n, 512), lambda s, idx: (0, turn(s, idx))) for _, n in PIECES]
            + [fixed, fixed],
            out_specs=[piece, piece],
            scratch_shapes=[pltpu.VMEM((AW, ROWS), BF16)],
        ),
        out_shape=(sds((4, 2, QOP, 128)),) * 2,
        compiler_params=params(),
        cost_estimate=cost(4 * ROWS * D * AW, 1e7),
        name="attn_grads",
    )(idx, *normed, *normed, *branch, dqm, att)


def small_call(body, out_shape, *args, name):
    return pl.pallas_call(
        body,
        out_shape=out_shape,
        in_specs=[spec(pltpu.SMEM)] + [spec()] * (len(args) - 1),
        out_specs=jax.tree.map(lambda _: spec(), out_shape),
        compiler_params=params(),
        cost_estimate=cost(1e6, 4e6),
        name=name,
    )(*args)


def add(*values):
    return sum((v.astype(F32) for v in values[1:]), values[0].astype(F32)).astype(BF16)


def sum_core_body(idx, a, b, c, d, *outs):
    for s, out in enumerate(outs):
        out[:, :QOP, :] = add(a[s], b[s])
        out[:, QOP:, :] = add(c[s], d[s])


def sum_y_body(idx, a, b, c, d, own, other):
    zh = idx[1]
    own[...] = add(a[zh], b[zh], c[zh], d[zh])
    far = 1 - zh
    other[...] = add(a[far], b[far], c[far], d[far])


def sum_z_body(idx, a, b, c, d, out):
    out[...] = add(a[...], b[...], c[...], d[...])


def unpack_tail_body(idx, *refs):
    y, core = idx[2], idx[3]
    qkv, out, gains = refs[8:]
    for k in range(8):
        piece = refs[k]
        p = ((y - k % 4) & 3) * 2 + (core if k < 4 else 1 - core)
        rows = pl.ds(pl.multiple_of(p * 128, 128), 128)
        for c in range(4):
            qkv[rows, c * 128 : (c + 1) * 128] = piece[c * 128 : (c + 1) * 128, :].astype(F32)
        qkv[rows, AW:] = piece[QOP : QOP + 128, :].astype(F32).T
        g = piece[QOP + 128 :, :].astype(F32)
        for c in range(2):
            first = QP + c * (AW // 2)
            cols = pl.ds(pl.multiple_of(p * 256 + c * 128, 128), 128)
            out[:, cols] = piece[first : first + AW // 2, :].astype(F32)
            gains[:, cols] = g[2 * c : 2 * c + 2]


def sum_tail(idx, first, second, parts):
    got_a = lax.ppermute(first[1], "core", shift(2, 1))
    got_b = lax.ppermute(second[1], "core", shift(2, 1))
    part = sds((2, TAIL, 128))
    g = small_call(sum_core_body, (part,) * 4, idx, first[0], got_a, second[0], got_b, name="sum_core")
    g_core = g[0]
    got = [lax.ppermute(g[s], "y", shift(4, s)) for s in (2, 1, 3)]
    part = sds((TAIL, 128))
    own, other = small_call(sum_y_body, (part,) * 2, idx, g[0], *got, name="sum_y")
    p0, q1, q3 = relay([tie(p, own) for p in parts])
    cross = [(2 * a + b, 2 * (1 - a) + (1 - b)) for a in range(2) for b in range(2)]
    g = small_call(
        sum_z_body,
        part,
        idx,
        tie(own, q1, q3),
        lax.ppermute(own, "zl", shift(2, 1)),
        lax.ppermute(other, "zh", shift(2, 1)),
        lax.ppermute(other, ("zl", "zh"), cross),
        name="sum_z",
    )
    d_one = last_step(p0, q1, q3)
    mine = [tie(g, *d_one)] + [lax.ppermute(g, "y", shift(4, s)) for s in (1, 2, 3)]
    theirs = [lax.ppermute(v, "core", shift(2, 1)) for v in [g] + mine[1:]]
    shapes = (sds((DH, QW), F32), sds((AW // 2, D), F32), sds((2, D), F32))
    return g_core, own, d_one, small_call(unpack_tail_body, shapes, idx, *mine, *theirs, name="unpack_tail")


def inverse_rms(v):
    return lax.rsqrt(jnp.mean(v * v, axis=-1, keepdims=True) + EPSILON)


def total(terms):
    return sum((t[...].astype(F32) for t in terms[1:]), terms[0][...].astype(F32))


def norm_two_body(tok, a, b, c, gain, after, normed):
    v = total((tok, a, b, c))
    after[...] = v
    normed[...] = (v * inverse_rms(v) * gain[...]).astype(BF16)


def norm_back_body(add, v_ref, a, b, c, gain, out, low, gain_grad):
    v = v_ref[...].astype(F32)
    grad = total((a, b, c))
    r = inverse_rms(v)
    pulled = grad * gain[...]
    inner = jnp.mean(v * pulled, axis=-1, keepdims=True)
    res = add[...].astype(F32) + r * pulled - v * (r * r * r) * inner
    out[...] = res
    low[...] = res.astype(BF16)
    gain_grad[...] = jnp.sum(grad * v * r, axis=0, keepdims=True)


def row_call(body, out_shape, *args, name):
    return pl.pallas_call(
        body,
        out_shape=out_shape,
        in_specs=[spec()] * len(args),
        out_specs=tuple(spec() for _ in out_shape),
        compiler_params=params(),
        cost_estimate=cost(1e6, 5e6),
        name=name,
    )(*args)


def replica_layout(lengths, replica, replica_id):
    sizes = jnp.where(replica == replica_id, lengths, 0)
    starts = jnp.cumsum(sizes) - sizes
    row_ids = jnp.arange(CAP, dtype=jnp.int32)
    inside = (row_ids[:, None] >= starts[None, :]) & (row_ids[:, None] < (starts + sizes)[None, :])
    begin = jnp.sum(jnp.where(inside, starts[None, :], 0), axis=1)
    begin = begin + jnp.where(jnp.any(inside, axis=1), 0, jnp.sum(sizes))
    return begin, row_ids - begin


def on_device(
    tokens, cotangent, gain_one, qkv_weight, out_weight, gate_weight, up_weight, down_weight,
    gain_two, seq_lengths, seq_replica,
):
    x, zh, core = lax.axis_index("x"), lax.axis_index("zh"), lax.axis_index("core")
    y, zl = lax.axis_index("y"), lax.axis_index("zl")
    idx = jnp.stack([x, zh, y, core]).astype(jnp.int32)

    tok = tokens.astype(F32)
    s_one = inverse_rms(tok)
    begin, position = replica_layout(seq_lengths, seq_replica, (y * 2 + zl) * 2 + core)
    half_rows = lambda v: lax.dynamic_index_in_dim(v.reshape(4, 2, BLK), zh, 1, False).reshape(ROWS, 1)
    first = jnp.tile(half_rows(begin)[3 * BLK :, 0], 8).reshape(1, QALL)
    lane = jnp.arange(128, dtype=jnp.int32)
    frequency = ROTARY_BASE ** (-(lane % 32).astype(F32) * (2.0 / HD))
    angles = half_rows(position).astype(F32) * frequency[None, :]
    cosine = jnp.cos(angles)
    sine = jnp.where((lane % HD) < HD // 2, -1.0, 1.0)[None, :] * jnp.sin(angles)

    qkv_got = fetch_half(qkv_weight, core)
    normed_one = gather_x((tok * s_one * gain_one).astype(BF16), (cosine,))
    qkv_all = qkv_weight, qkv_got, lax.ppermute(tie(qkv_got, normed_one[2], normed_one[3]), "core", shift(2, 1))
    out_all = fetch_partner(out_weight, core, qkv_got)

    q, kv_own = qkv_forward(idx, normed_one, qkv_all, cosine, sine)
    cots = gather_x(tie(cotangent, normed_one[2], normed_one[3]), (kv_own,))
    rows = DH // 8
    mine = lambda w: lax.dynamic_slice_in_dim(w, (y * 2 + core) * rows, rows, 0)
    cross = [(2 * a + b, 2 * (1 - a) + (1 - b)) for a in range(2) for b in range(2)]
    gate_up = lax.ppermute(
        jnp.concatenate(
            [
                tie(mine(gate_weight), normed_one[2], normed_one[3]),
                jnp.zeros((rows, GAP - FF4), BF16),
                mine(up_weight),
            ],
            1,
        ),
        ("zl", "zh"),
        cross,
    )
    kv_par = lax.ppermute(kv_own, "zh", shift(2, 1))
    down_got = fetch_half(tie(down_weight, gate_up), core)
    att, qx = attend(idx, tie(q, cots[2], cots[3], out_all[1]), kv_own, kv_par, first)
    gate_up = lax.all_gather(tie(gate_up, qx), ("y", "core"), axis=0, tiled=True)
    parts = out_project(idx, att, out_all)
    after_attn, normed_two = row_call(
        norm_two_body,
        (sds((BLK, D), F32), sds((BLK, D))),
        tokens, *scatter_x(parts), gain_two.reshape(1, D), name="norm_two",
    )
    normed_two = gather_x(tie(normed_two, down_got))
    down_all = down_weight, down_got, lax.ppermute(tie(down_got, normed_two[1], normed_two[4]), "core", shift(2, 1))
    hid, dgate, dup = ffn(idx, normed_two, cots, gate_weight, up_weight, gate_up, down_all)
    own_grads = ffn_grads(normed_two, cots, hid, dgate, dup)
    grads = lax.psum_scatter(
        own_grads.reshape(32, PIECE, 128), ("zh", "zl", "y", "core"), scatter_dimension=0, tiled=True
    )
    after_grad, branch, gain_grad_two = row_call(
        norm_back_body,
        (sds((BLK, D), F32), sds((BLK, D)), sds((1, D), F32)),
        cotangent, after_attn,
        *scatter_x(ffn_back(idx, tie(dgate, own_grads), dup, gate_weight, up_weight, gate_up)),
        gain_two.reshape(1, D), name="norm_back_two",
    )
    branch = gather_x(branch)
    layer_parts = down_project(idx, tie(hid, after_grad), down_all)
    att = tie(att, *layer_parts)
    layer = [
        lax.ppermute(tie(layer_parts[k], branch[2], branch[3]), "x", shift(4, k)) for k in (1, 3)
    ]
    dqm, dkv_own, dkv_par = attend_back(
        idx, qx, kv_own, kv_par, first, att, cosine, sine, branch, out_all
    )
    dkv_got = lax.ppermute(dkv_par, "zh", shift(2, 1))
    tail = attn_grads(
        idx, normed_one, branch, dqm.reshape(ROWS, AW), tie(att, *layer).reshape(ROWS, AW)
    )
    dkv_got = tie(dkv_got, tail[0])
    *tail_kv, parts = qkv_back(
        idx, dqm.reshape(ROWS, AW), dkv_own, dkv_got, cosine, sine, qkv_all, normed_one, gain_one,
        gain_grad_two,
    )
    over_x = lambda v: sum((lax.ppermute(v, "x", shift(4, s)) for s in (1, 2, 3)), v)
    cores_summed, summed, d_one, (grad_qkv, grad_out, gains) = sum_tail(
        idx, (tail[0], tie(tail[1], dkv_got)), tail_kv, parts
    )
    layer.append(lax.ppermute(tie(layer_parts[2], summed), "x", shift(4, 2)))
    grads = lax.all_gather(tie(grads, cores_summed), ("zl", "y", "core"), axis=0, tiled=True)
    grad_gate, grad_up, grad_down = unpack(grads)
    _, input_grad, _ = row_call(
        norm_back_body,
        (sds((BLK, D), F32), sds((BLK, D)), sds((1, D), F32)),
        after_grad, tokens, *d_one, gain_one.reshape(1, D), name="norm_back_one",
    )
    layer_out = sum((v.astype(F32) for v in layer), after_attn + layer_parts[0].astype(F32))
    layer_out = layer_out.astype(BF16)
    gains = over_x(gains)
    return (
        layer_out, input_grad, gains[0], grad_qkv, grad_out, grad_gate, grad_up,
        grad_down, gains[1],
    )


def solution(mesh):
    grid = Mesh(mesh.devices.reshape(SIZES), AXES)
    rows = P(AXES, None)
    both = P(("x", "zh"), None)
    return jax.shard_map(
        on_device,
        mesh=grid,
        in_specs=(
            rows, rows, P(), P("zh", "x"), both, P("zh", "x"), P("zh", "x"), both, P(), P(), P(),
        ),
        out_specs=(
            rows, rows, P(), P("zh", "x"), both, P("zh", "x"), P("zh", "x"), both, P(),
        ),
        check_vma=False,
    )
```

```python
import jax
import jax.numpy as jnp
from jax import lax
from jax.experimental import pallas as pl
from jax.experimental.pallas import tpu as pltpu
from jax.sharding import Mesh
from jax.sharding import PartitionSpec as P

HEADS = 32
KV = 4
HD = 64
EPSILON = 1e-05
ROTARY_BASE = 10000.0
MASKED = -1e30

AXES = ("y", "zl", "core", "x", "zh")
SIZES = (4, 2, 2, 4, 2)
BLK = 160
HALF = BLK // 2
ROWS = 4 * BLK
CAP = 2 * ROWS
D = 2048
DH = D // 2
QW = 640
AW = 512
FF4 = 1408
TILE = 256
F32 = jnp.float32
BF16 = jnp.bfloat16
VLIM = 60 * 1024 * 1024


def spec(memory=pltpu.VMEM):
    return pl.BlockSpec(memory_space=memory)


def params(**kw):
    return pltpu.CompilerParams(vmem_limit_bytes=VLIM, **kw)


def cost(flops, nbytes):
    return pl.CostEstimate(flops=int(flops), bytes_accessed=int(nbytes), transcendentals=0)


def sds(shape, dtype=BF16):
    return jax.ShapeDtypeStruct(shape, dtype)


def dot(a, b):
    return jnp.dot(a, b, preferred_element_type=F32)


def dot_t(a, b):
    return lax.dot_general(a, b, (((1,), (1,)), ((), ())), preferred_element_type=F32)


def t_dot(a, b):
    return lax.dot_general(a, b, (((0,), (0,)), ((), ())), preferred_element_type=F32)


def tie(v, *deps):
    return lax.optimization_barrier((v,) + deps)[0]


def shift(n, s):
    return [(i, (i + s) % n) for i in range(n)]


def gather_x(v, wait=()):
    from_prev = lax.ppermute(v, "x", shift(4, 1))
    from_next = lax.ppermute(v, "x", shift(4, -1))
    send_a = tie(from_prev[:HALF], from_next, *wait)
    send_b = tie(from_next[HALF:], from_prev, *wait)
    opp_a = lax.ppermute(send_a, "x", shift(4, 1))
    opp_b = lax.ppermute(send_b, "x", shift(4, -1))
    return v, from_next, opp_a, opp_b, from_prev


def relay_body(p1, got_a, p3, got_b, q1, q3):
    q1[...] = (p1[...].astype(F32) + got_a[...].astype(F32)).astype(BF16)
    q3[...] = (p3[...].astype(F32) + got_b[...].astype(F32)).astype(BF16)


def relay(parts):
    p0, p1, p2a, p2b, p3 = parts
    got_a = lax.ppermute(p2a, "x", shift(4, 1))
    got_b = lax.ppermute(p2b, "x", shift(4, -1))
    half = lambda k: pl.BlockSpec((HALF, D), lambda i: (k, 0))
    q1, q3 = pl.pallas_call(
        relay_body,
        grid=(1,),
        out_shape=(sds((BLK, D)),) * 2,
        in_specs=[half(0), half(0), half(1), half(0)],
        out_specs=(half(0), half(1)),
        input_output_aliases={0: 0, 2: 1},
        compiler_params=params(),
        cost_estimate=cost(1e6, 2e6),
        name="relay",
    )(p1, got_a, p3, got_b)
    return p0, q1, q3


def scatter_x(parts):
    return last_step(*relay(parts))


def last_step(p0, q1, q3):
    return p0, lax.ppermute(q1, "x", shift(4, 1)), lax.ppermute(q3, "x", shift(4, -1))


PIECES = ((0, BLK), (1, BLK), (2, HALF), (2, HALF), (3, BLK))
PIECE_ROW = (0, BLK, 2 * BLK, 2 * BLK + HALF, 3 * BLK)


def part_shapes(width, dtype=BF16):
    return tuple(sds((n, width), dtype) for _, n in PIECES)


def low_lanes(shape):
    return lax.broadcasted_iota(jnp.int32, shape, 1) < HD


def swap_halves(v):
    lane = lax.broadcasted_iota(jnp.int32, v.shape, 1) % HD
    return jnp.where(lane < HD // 2, pltpu.roll(v, 128 - HD // 2, 1), pltpu.roll(v, HD // 2, 1))


def rows_at(block):
    return pl.ds(pl.multiple_of(block * BLK, 32), BLK)


def fetch_half(w, core):
    half = w.shape[0] // 2
    return lax.ppermute(lax.dynamic_slice_in_dim(w, core * half, half, 0), "zh", shift(2, 1))


def fetch_partner(w, core, *deps):
    got = fetch_half(tie(w, *deps), core)
    return w, got, lax.ppermute(got, "core", shift(2, 1))


def weight_rows(idx, rows):
    zh, core = idx[1], idx[3]
    far = (1 - zh) * rows
    half = rows // 2
    at = lambda first, n: pl.ds(pl.multiple_of(first, half), n)
    return at(zh * rows, rows), at(far + core * half, half), at(far + (1 - core) * half, half)


def qkv_body(idx, n0, n1, n2a, n2b, n3, w0, w1, w2, cosine, sine, q_ref, kv_ref, rows):
    x = idx[0]
    lo = low_lanes((BLK, 128))
    for ref, row, (_, n) in zip((n0, n1, n2a, n2b, n3), PIECE_ROW, PIECES):
        rows[row : row + n, :] = ref[...]
    s0, s1, s2 = weight_rows(idx, DH)
    acc = dot(rows[:, s0], w0[...]) + dot(rows[:, s1], w1[...]) + dot(rows[:, s2], w2[...])
    for d in range(4):
        at = rows_at((x + d) & 3)
        cs = cosine[at, :]
        sn = sine[at, :]
        for p in range(5):
            v = acc[d * BLK : (d + 1) * BLK, p * 128 : (p + 1) * 128]
            r = v * cs + swap_halves(v) * sn
            if p < 4:
                r = r * (HD**-0.5 * LOG2E)
                a = (x + d) & 3
                for k, w in enumerate((r, pltpu.roll(r, HD, 1))):
                    head = slice((2 * p + k) * BLK, (2 * p + k + 1) * BLK)
                    q_ref[a, head, :] = jnp.where(lo, w, 0.0).astype(BF16)
            else:
                kv_ref[at, :] = jnp.where(lo, r, v).astype(BF16)


def qkv_forward(idx, pieces, weight, cosine, sine):
    return pl.pallas_call(
        qkv_body,
        out_shape=(sds((4, QALL, 128)), sds((ROWS, 128))),
        in_specs=[spec(pltpu.SMEM)] + [spec()] * 10,
        out_specs=(spec(), spec()),
        scratch_shapes=[pltpu.VMEM((ROWS, D), BF16)],
        compiler_params=params(),
        cost_estimate=cost(2 * ROWS * D * QW, 7e6),
        name="qkv_forward",
    )(idx, *pieces, *weight, cosine, sine)


QALL = 8 * BLK
PAIR = 2 * BLK
LOG2E = 1.4426950408889634
LN2 = 0.6931471805599453


def split3(v):
    a = v.astype(BF16).astype(F32)
    b = (v - a).astype(BF16).astype(F32)
    return a, b, v - a - b


def with_lanes(v, parts):
    lane = lax.broadcasted_iota(jnp.int32, v.shape, 1)
    out = jnp.where(lane < HD, v, 0.0)
    for k, part in enumerate(parts):
        out = jnp.where(lane == HD + k, part, out)
    return out


def spread_keys(zh, kv_own, kv_par, kk, vv, fill):
    shape = (BLK, 128)
    lo = low_lanes(shape)
    rest = fill(lax.broadcasted_iota(jnp.int32, shape, 1) - HD)
    for j in range(4):
        for src, off in ((kv_own, zh), (kv_par, 1 - zh)):
            v = src[j * BLK : (j + 1) * BLK, :].astype(F32)
            at = rows_at(2 * j + off)
            kk[at, :] = jnp.where(lo, v, rest).astype(BF16)
            vv[at, :] = jnp.where(lo, pltpu.roll(v, HD, 1), rest).astype(BF16)


def masked(s, zh, j, kb, first):
    if j < 3 and kb < j:
        return s
    u = kb * PAIR + lax.broadcasted_iota(jnp.int32, (PAIR, QALL), 0)
    allowed = None
    if kb == j:
        t = (2 * j + zh) * BLK + lax.broadcasted_iota(jnp.int32, (1, QALL), 1) % BLK
        allowed = u <= t
    if j == 3:
        later = u >= first[...]
        allowed = later if allowed is None else allowed & later
    return jnp.where(allowed, s, MASKED)


def attend_body(idx, q, kv_own, kv_par, first, att, qx, kk, vv, vt, s_ref, e_ref):
    x, zh = idx[0], idx[1]
    spread_keys(zh, kv_own, kv_par, kk, vv, lambda lane: 1.0)
    vt[...] = vv[...].T
    lo = low_lanes((BLK, 128))
    for j in range(4):
        n = PAIR * (j + 1)
        qj = q[j]
        top = jnp.full((1, QALL), MASKED, F32)
        for kb in range(j + 1):
            rows = slice(kb * PAIR, (kb + 1) * PAIR)
            s = masked(dot_t(kk[rows, :], qj), zh, j, kb, first)
            s_ref[rows, :] = s
            top = jnp.maximum(top, jnp.max(s, axis=0, keepdims=True))
        for k in range(n // 64):
            rows = slice(k * 64, (k + 1) * 64)
            e_ref[rows, :] = jnp.exp2(s_ref[rows, :] - top).astype(BF16)
        o = dot(vt[:, :n], e_ref[:n, :])
        lse = split3(top + jnp.log(o[HD : HD + 1, :]) * LOG2E)
        row = lax.broadcasted_iota(jnp.int32, (128, QALL), 0)
        extra = jnp.zeros((128, QALL), F32)
        for k, part in enumerate(lse):
            extra = jnp.where(row == HD + k, part, extra)
        qx[j] = (qj.astype(F32) + extra.T).astype(BF16)
        o = o.T
        r = pltpu.roll(o, HD, 1)
        rel = (j - x) & 3
        for p in range(4):
            even, odd = slice(2 * p * BLK, (2 * p + 1) * BLK), slice((2 * p + 1) * BLK, (2 * p + 2) * BLK)
            num = jnp.where(lo, o[even], r[odd])
            den = jnp.where(lo, r[even], o[odd])
            att[rel, :, p * 128 : (p + 1) * 128] = (num / den).astype(BF16)


def attend(idx, q, kv_own, kv_par, first):
    return pl.pallas_call(
        attend_body,
        out_shape=(sds((4, BLK, AW)), sds((4, QALL, 128))),
        in_specs=[spec(pltpu.SMEM)] + [spec()] * 4,
        out_specs=(spec(), spec()),
        scratch_shapes=[
            pltpu.VMEM((CAP, 128), BF16),
            pltpu.VMEM((CAP, 128), BF16),
            pltpu.VMEM((128, CAP), BF16),
            pltpu.VMEM((CAP, QALL), F32),
            pltpu.VMEM((CAP, QALL), BF16),
        ],
        compiler_params=params(),
        cost_estimate=cost(1.2e10, 3e6),
        name="attend",
    )(idx, q, kv_own, kv_par, first)


def store_parts(res, refs):
    for ref, row, (_, n) in zip(refs, PIECE_ROW, PIECES):
        ref[...] = res[row : row + n].astype(BF16)


def out_body(idx, att, w0, w1, w2, o0, o1, o2a, o2b, o3):
    s0, s1, s2 = weight_rows(idx, AW // 2)
    for d, ref in ((2, None), (1, o1), (3, o3), (0, o0)):
        a = att.at[d]
        res = dot(a[:, s0], w0[...]) + dot(a[:, s1], w1[...]) + dot(a[:, s2], w2[...])
        res = res.astype(BF16)
        if d == 2:
            o2a[...] = res[:HALF]
            o2b[...] = res[HALF:]
        else:
            ref[...] = res


def out_project(idx, att, weight):
    return pl.pallas_call(
        out_body,
        out_shape=part_shapes(D),
        in_specs=[spec(pltpu.SMEM)] + [spec()] * 4,
        out_specs=(spec(),) * 5,
        compiler_params=params(),
        cost_estimate=cost(2 * ROWS * D * AW, 5.5e6),
        name="out_project",
    )(idx, att, *weight)


def stack_heads(v):
    return v, pltpu.roll(v, HD, 1)


def attend_back_body(
    idx, qx, kv_own, kv_par, first, att, cosine, sine, b0, b1, b2a, b2b, b3, w0, w1, w2,
    dq_ref, dkv_own, dkv_par, kk, vv, dout, do_all, dkk, dvv, e_ref, ds_ref, dq_acc,
):
    x, zh = idx[0], idx[1]
    spread_keys(zh, kv_own, kv_par, kk, vv, lambda lane: jnp.where(lane < 3, -1.0, 0.0))
    s0, s1, s2 = weight_rows(idx, AW // 2)
    for d in range(4):
        if d == 2:
            rows = jnp.concatenate([b2a[...], b2b[...]], 0)
        else:
            rows = (b0, b1, None, b3)[d][...]
        at = rows_at((x + d) & 3)
        for s, w in ((s0, w0), (s1, w1), (s2, w2)):
            dout[at, s] = dot_t(rows, w[...]).astype(BF16)
    lo = low_lanes((BLK, 128))
    for j in range(4):
        rel = (j - x) & 3
        here = slice(j * BLK, (j + 1) * BLK)
        for p in range(4):
            cols = slice(p * 128, (p + 1) * 128)
            do = dout[here, cols].astype(F32)
            prod = do * att[rel, :, cols].astype(F32)
            for k, (v, w) in enumerate(zip(stack_heads(do), stack_heads(prod))):
                delta = jnp.sum(jnp.where(lo, w, 0.0), axis=1, keepdims=True)
                head = slice((2 * p + k) * BLK, (2 * p + k + 1) * BLK)
                do_all[head, :] = with_lanes(v, split3(delta)).astype(BF16)
        for kb in range(j + 1):
            rows = slice(kb * PAIR, (kb + 1) * PAIR)
            e = jnp.exp2(masked(dot_t(kk[rows, :], qx[j]), zh, j, kb, first))
            e_ref[...] = e.astype(BF16)
            ds_ref[...] = (e * dot_t(vv[rows, :], do_all[...])).astype(BF16)
            dv = dot(e_ref[...], do_all[...])
            dk = dot(ds_ref[...], qx[j])
            dq = t_dot(ds_ref[...], kk[rows, :])
            if kb == j:
                dvv[rows, :], dkk[rows, :] = dv, dk
            else:
                dvv[rows, :] += dv
                dkk[rows, :] += dk
            if kb == 0:
                dq_acc[...] = dq
            else:
                dq_acc[...] += dq
        for p in range(4):
            even, odd = slice(2 * p * BLK, (2 * p + 1) * BLK), slice((2 * p + 1) * BLK, (2 * p + 2) * BLK)
            v = jnp.where(lo, dq_acc[even, :], pltpu.roll(dq_acc[odd, :], HD, 1)) * HD**-0.5
            v = v * cosine[here, :] - swap_halves(v) * sine[here, :]
            dq_ref[rel, :, p * 128 : (p + 1) * 128] = v.astype(BF16)
    for j in range(4):
        for dst, off in ((dkv_own, zh), (dkv_par, 1 - zh)):
            at = rows_at(2 * j + off)
            both = jnp.where(lo, dkk[at, :] * LN2, pltpu.roll(dvv[at, :], HD, 1))
            dst[j * BLK : (j + 1) * BLK, :] = both.astype(dst.dtype)


def attend_back(idx, qx, kv_own, kv_par, first, att, cosine, sine, branch, weight):
    return pl.pallas_call(
        attend_back_body,
        out_shape=(sds((4, BLK, AW)), sds((ROWS, 128), F32), sds((ROWS, 128))),
        in_specs=[spec(pltpu.SMEM)] + [spec()] * 15,
        out_specs=(spec(),) * 3,
        scratch_shapes=[
            pltpu.VMEM((CAP, 128), BF16),
            pltpu.VMEM((CAP, 128), BF16),
            pltpu.VMEM((ROWS, AW), BF16),
            pltpu.VMEM((QALL, 128), BF16),
            pltpu.VMEM((CAP, 128), F32),
            pltpu.VMEM((CAP, 128), F32),
            pltpu.VMEM((PAIR, QALL), BF16),
            pltpu.VMEM((PAIR, QALL), BF16),
            pltpu.VMEM((QALL, 128), F32),
        ],
        compiler_params=params(),
        cost_estimate=cost(3e10, 8e6),
        name="attend_back",
    )(idx, qx, kv_own, kv_par, first, att, cosine, sine, *branch, *weight)


def qkv_back_body(
    idx, dqm, dkv_own, dkv_got, cosine, sine, w0, w1, w2, n0, n1, n2a, n2b, n3, gain_one,
    gain_grad_two,
    mine, theirs, o0, o1, o2a, o2b, o3, n_all, dkv, grad, gains,
):
    x, y, core = idx[0], idx[2], idx[3]
    lo = low_lanes((BLK, 128))
    for ref, row, (_, n) in zip((n0, n1, n2a, n2b, n3), PIECE_ROW, PIECES):
        n_all[row : row + n, :] = ref[...]
    for d in range(4):
        at = rows_at((x + d) & 3)
        v = dkv_own[at, :] + dkv_got[at, :].astype(F32)
        v = jnp.where(lo, v * cosine[at, :] - swap_halves(v) * sine[at, :], v).astype(BF16)
        dkv[d * BLK : (d + 1) * BLK, :] = v
    rows = jnp.concatenate([dqm[...], dkv[...]], 1)
    for s, w in zip(weight_rows(idx, DH), (w0, w1, w2)):
        for c in range(w.shape[0] // 512):
            cols = pl.ds(pl.multiple_of(s.start + c * 512, 512), 512)
            res = dot_t(rows, w[c * 512 : (c + 1) * 512, :])
            part = (res * n_all[:, cols].astype(F32)).reshape(ROWS // 8, 8, 512)
            gains[0:1, cols] = jnp.sum(jnp.sum(part, axis=0), axis=0, keepdims=True) / gain_one[:, cols]
            store_parts(res, [r.at[:, cols] for r in (o0, o1, o2a, o2b, o3)])
    grad[...] = dot(dkv[...].T, n_all[...]).astype(BF16)
    gains[1:2, :] = gain_grad_two[...]
    for s in range(4):
        for k, ref in enumerate((mine, theirs)):
            p = ((y + s) & 3) * 2 + (core if k == 0 else 1 - core)
            both = gains[:, pl.ds(pl.multiple_of(p * 256, 256), 256)]
            both = jnp.concatenate([both[:, :128], both[:, 128:], jnp.zeros((12, 128), F32)], 0)
            for h in range(2):
                ref[s, h, :128, :] = grad[:, pl.ds(pl.multiple_of(h * DH + p * 128, 128), 128)]
                ref[s, h, 128:, :] = both.astype(BF16)


def qkv_back(idx, dqm, dkv_own, dkv_got, cosine, sine, weight, pieces, gain_one, gain_grad_two):
    res = pl.pallas_call(
        qkv_back_body,
        out_shape=(sds((4, 2, KVP, 128)),) * 2 + part_shapes(D),
        in_specs=[spec(pltpu.SMEM)] + [spec()] * 15,
        out_specs=(spec(),) * 7,
        scratch_shapes=[
            pltpu.VMEM((ROWS, D), BF16),
            pltpu.VMEM((ROWS, 128), BF16),
            pltpu.VMEM((128, D), BF16),
            pltpu.VMEM((2, D), F32),
        ],
        compiler_params=params(),
        cost_estimate=cost(2 * ROWS * D * QW, 1.3e7),
        name="qkv_back",
    )(
        idx, dqm, dkv_own, dkv_got, cosine, sine, *weight, *pieces,
        gain_one.reshape(1, D), gain_grad_two.reshape(1, D),
    )
    return res[0], res[1], res[2:]


TILES = 6
GAP = TILES * TILE


def load_down(idx, refs, dst, sem):
    copies = []
    for k, (s, ref) in enumerate(zip(weight_rows(idx, FF4 // 2), refs)):
        copies.append(pltpu.make_async_copy(ref, dst.at[s], sem.at[k]))
    return copies


def ffn_body(
    idx, n0, n1, n2a, n2b, n3, c0, c1, c2, c3, gate_own, up_own, gate_par, up_par, w0, w1, w2,
    hid, dgate, dup, n_all, c_all, down, sem,
):
    i = pl.program_id(0)
    zh = idx[1]

    @pl.when(i == 0)
    def _():
        copies = load_down(idx, (w0, w1, w2), down, sem)
        for c in copies:
            c.start()
        for ref, row, (_, n) in zip((n0, n1, n2a, n2b, n3), PIECE_ROW, PIECES):
            n_all[row : row + n, :] = ref[...]
        for d, ref in enumerate((c0, c1, c2, c3)):
            c_all[d * BLK : (d + 1) * BLK, :] = ref[...]
        for c in copies:
            c.wait()

    own = n_all[:, pl.ds(pl.multiple_of(zh * DH, DH), DH)]
    par = n_all[:, pl.ds(pl.multiple_of((1 - zh) * DH, DH), DH)]
    gate = dot(own, gate_own[...]) + dot(par, gate_par[...])
    up = dot(own, up_own[...]) + dot(par, up_par[...])
    dh = dot_t(c_all[...], down[pl.ds(pl.multiple_of(i * TILE, TILE), TILE), :])
    sig = 1.0 / (1.0 + jnp.exp(-gate))
    act = gate * sig
    hid[...] = (act * up).astype(BF16)
    dgate[...] = (dh * up * sig * (1.0 + gate * (1.0 - sig))).astype(BF16)
    dup[...] = (dh * act).astype(BF16)


def whole(n, w):
    return pl.BlockSpec((n, w), lambda i: (0, 0))


def ffn(idx, normed, cots, gate, up, gate_up, down):
    column = lambda first: pl.BlockSpec((DH, TILE), lambda i: (0, i + first))
    hidden = pl.BlockSpec((ROWS, TILE), lambda i: (0, i))
    return pl.pallas_call(
        ffn_body,
        grid=(TILES,),
        out_shape=(sds((ROWS, FF4)),) * 3,
        in_specs=[spec(pltpu.SMEM)]
        + [whole(n, D) for _, n in PIECES]
        + [whole(BLK, D)] * 4
        + [column(0), column(0), column(0), column(TILES)]
        + [spec(pl.ANY)] * 3,
        out_specs=[hidden] * 3,
        scratch_shapes=[
            pltpu.VMEM((ROWS, D), BF16),
            pltpu.VMEM((ROWS, D), BF16),
            pltpu.VMEM((GAP, D), BF16),
            pltpu.SemaphoreType.DMA((3,)),
        ],
        compiler_params=params(),
        cost_estimate=cost(6 * ROWS * D * FF4, 3.4e7),
        name="ffn",
    )(idx, *normed, *cots, gate, up, gate_up, gate_up, *down)


def down_body(idx, hid, w0, w1, w2, o0, o1, o2, o3, down, sem):
    copies = load_down(idx, (w0, w1, w2), down, sem)
    for c in copies:
        c.start()
    for c in copies:
        c.wait()
    for n in range(D // 512):
        cols = slice(n * 512, (n + 1) * 512)
        res = dot(hid[...], down[:, cols]).astype(BF16)
        for d, ref in enumerate((o0, o1, o2, o3)):
            ref[:, cols] = res[d * BLK : (d + 1) * BLK]


def down_project(idx, hid, down):
    return pl.pallas_call(
        down_body,
        out_shape=(sds((BLK, D)),) * 4,
        in_specs=[spec(pltpu.SMEM), spec()] + [spec(pl.ANY)] * 3,
        out_specs=(spec(),) * 4,
        scratch_shapes=[pltpu.VMEM((FF4, D), BF16), pltpu.SemaphoreType.DMA((3,))],
        compiler_params=params(),
        cost_estimate=cost(2 * ROWS * D * FF4, 1.1e7),
        name="down_project",
    )(idx, hid, *down)


def ffn_back_body(idx, dgate, dup, gate_own, up_own, par, *refs):
    half = pl.num_programs(0) // 2

    @pl.when(pl.program_id(0) < half)
    def _():
        store_parts(dot_t(dgate[...], gate_own[...]) + dot_t(dup[...], up_own[...]), refs)

    @pl.when(pl.program_id(0) >= half)
    def _():
        store_parts(dot_t(dgate[...], par[:, :FF4]) + dot_t(dup[...], par[:, GAP:]), refs)


def ffn_back(idx, dgate, dup, gate, up, gate_up):
    half = DH // TILE
    rows = pl.BlockSpec((ROWS, FF4), lambda i, idx: (0, 0))
    own = pl.BlockSpec((TILE, FF4), lambda i, idx: (jnp.minimum(i, half - 1), 0))
    par = pl.BlockSpec((TILE, GAP + FF4), lambda i, idx: (jnp.maximum(i - half, 0), 0))
    place = lambda i, idx: (0, i ^ (idx[1] * half))
    return pl.pallas_call(
        ffn_back_body,
        grid_spec=pltpu.PrefetchScalarGridSpec(
            num_scalar_prefetch=1,
            grid=(D // TILE,),
            in_specs=[rows, rows, own, own, par],
            out_specs=[pl.BlockSpec((n, TILE), place) for _, n in PIECES],
        ),
        out_shape=part_shapes(D),
        compiler_params=params(),
        cost_estimate=cost(4 * ROWS * D * FF4, 1.8e7),
        name="ffn_back",
    )(idx, dgate, dup, gate, up, gate_up)


GU_ROWS = FF4 // 128 * 64
PIECE = 2 * GU_ROWS + FF4 // 2
QS = 4


def gate_up_grads_body(*refs):
    na, nb = refs[0:5], refs[5:10]
    dgate, dup, _, out = refs[10:]
    stack = lambda parts: jnp.concatenate([r[...] for r in parts], 0)
    rows = jnp.concatenate([stack(na), stack(nb)], 1).T
    for k, ref in enumerate((dgate, dup)):
        g = dot(rows, ref[...]).astype(BF16)
        for h in range(2):
            for q in range(QS):
                r = g[(QS * h + q) * 64 : (QS * h + q + 1) * 64]
                for c in range(FF4 // 128):
                    first = k * GU_ROWS + c * 64
                    out[h, q, first : first + 64, :] = r[:, c * 128 : (c + 1) * 128]


def gate_up_grads(normed, dgate, dup, pieces):
    return pl.pallas_call(
        gate_up_grads_body,
        grid=(16 // QS,),
        out_shape=sds((2, 16, PIECE, 128)),
        in_specs=[pl.BlockSpec((n, 64 * QS), lambda i: (0, i)) for _, n in PIECES]
        + [pl.BlockSpec((n, 64 * QS), lambda i: (0, i + 16 // QS)) for _, n in PIECES]
        + [whole(ROWS, FF4)] * 2
        + [spec(pl.ANY)],
        out_specs=pl.BlockSpec((2, QS, 2 * GU_ROWS, 128), lambda i: (0, i, 0, 0)),
        input_output_aliases={12: 0},
        compiler_params=params(),
        cost_estimate=cost(4 * ROWS * D * FF4, 2e7),
        name="gate_up_grads",
    )(*normed, *normed, dgate, dup, pieces)


def down_grads_body(*refs):
    cots = refs[0:4]
    hid, out, hid_t = refs[4:]

    @pl.when(pl.program_id(0) == 0)
    def _():
        hid_t[...] = hid[...].T

    g = dot(hid_t[...], jnp.concatenate([r[...] for r in cots], 0)).astype(BF16)
    for h in range(2):
        for q in range(QS):
            out[h, q, :, :] = g[h * (FF4 // 2) : (h + 1) * (FF4 // 2), q * 128 : (q + 1) * 128]


def down_grads(cots, hid):
    return pl.pallas_call(
        down_grads_body,
        grid=(16 // QS,),
        out_shape=sds((2, 16, PIECE, 128)),
        in_specs=[pl.BlockSpec((BLK, 128 * QS), lambda i: (0, i))] * 4 + [whole(ROWS, FF4)],
        out_specs=pl.BlockSpec((2, QS, FF4 // 2, 128), lambda i: (0, i, 2, 0)),
        scratch_shapes=[pltpu.VMEM((FF4, ROWS), BF16)],
        compiler_params=params(),
        cost_estimate=cost(2 * ROWS * D * FF4, 1e7),
        name="down_grads",
    )(*cots, hid)


def unpack_body(piece, gate, up, down):
    for q in range(QS):
        rows = slice(q * 64, (q + 1) * 64)
        for k, ref in enumerate((gate, up)):
            for c in range(FF4 // 128):
                first = k * GU_ROWS + c * 64
                ref[rows, c * 128 : (c + 1) * 128] = piece[q, first : first + 64, :].astype(F32)
        down[:, q * 128 : (q + 1) * 128] = piece[q, 2 * GU_ROWS :, :].astype(F32)


def unpack(pieces):
    return pl.pallas_call(
        unpack_body,
        grid=(16 // QS,),
        out_shape=(sds((DH, FF4), F32), sds((DH, FF4), F32), sds((FF4 // 2, D), F32)),
        in_specs=[pl.BlockSpec((QS, PIECE, 128), lambda i: (i, 0, 0))],
        out_specs=[
            pl.BlockSpec((64 * QS, FF4), lambda i: (i, 0)),
            pl.BlockSpec((64 * QS, FF4), lambda i: (i, 0)),
            pl.BlockSpec((FF4 // 2, 128 * QS), lambda i: (0, i)),
        ],
        compiler_params=params(),
        cost_estimate=cost(1e6, 2.6e7),
        name="unpack",
    )(pieces)


QP = 4 * 128
OP = 2 * (AW // 2)
QOP = QP + OP
KVP = 128 + 16
TAIL = QOP + KVP


def attn_grads_body(idx, *refs):
    na, nb, branch = refs[0:5], refs[5:10], refs[10:15]
    dqm, att, mine, theirs, att_t = refs[15:]
    core = idx[3]

    @pl.when(pl.program_id(0) == 0)
    def _():
        att_t[...] = att[...].T

    stack = lambda parts: jnp.concatenate([r[...] for r in parts], 0)

    def store(h, first, n, zero, one):
        mine[0, h, first : first + n, :] = jnp.where(core == 0, zero, one)
        theirs[0, h, first : first + n, :] = jnp.where(core == 0, one, zero)

    for h, cols in enumerate((na, nb)):
        g = dot(stack(cols).T, dqm[...]).astype(BF16)
        for c in range(4):
            lanes = slice(c * 128, (c + 1) * 128)
            store(h, c * 128, 128, g[:128, lanes], g[128:, lanes])
    g = dot(att_t[...], stack(branch)).astype(BF16)
    for h in range(2):
        r = g[h * (AW // 2) : (h + 1) * (AW // 2)]
        for c in range(2):
            lanes = lambda k: slice(k * 256 + c * 128, k * 256 + (c + 1) * 128)
            store(h, QP + c * (AW // 2), AW // 2, r[:, lanes(0)], r[:, lanes(1)])


def attn_grads(idx, normed, branch, dqm, att):
    turn = lambda s, idx: (s + idx[2]) & 3
    piece = pl.BlockSpec((1, 2, QOP, 128), lambda s, idx: (s, 0, 0, 0))
    fixed = pl.BlockSpec((ROWS, AW), lambda s, idx: (0, 0))
    return pl.pallas_call(
        attn_grads_body,
        grid_spec=pltpu.PrefetchScalarGridSpec(
            num_scalar_prefetch=1,
            grid=(4,),
            in_specs=[pl.BlockSpec((n, 256), lambda s, idx: (0, turn(s, idx))) for _, n in PIECES]
            + [pl.BlockSpec((n, 256), lambda s, idx: (0, turn(s, idx) + 4)) for _, n in PIECES]
            + [pl.BlockSpec((n, 512), lambda s, idx: (0, turn(s, idx))) for _, n in PIECES]
            + [fixed, fixed],
            out_specs=[piece, piece],
            scratch_shapes=[pltpu.VMEM((AW, ROWS), BF16)],
        ),
        out_shape=(sds((4, 2, QOP, 128)),) * 2,
        compiler_params=params(),
        cost_estimate=cost(4 * ROWS * D * AW, 1e7),
        name="attn_grads",
    )(idx, *normed, *normed, *branch, dqm, att)


def small_call(body, out_shape, *args, name):
    return pl.pallas_call(
        body,
        out_shape=out_shape,
        in_specs=[spec(pltpu.SMEM)] + [spec()] * (len(args) - 1),
        out_specs=jax.tree.map(lambda _: spec(), out_shape),
        compiler_params=params(),
        cost_estimate=cost(1e6, 4e6),
        name=name,
    )(*args)


def add(*values):
    return sum((v.astype(F32) for v in values[1:]), values[0].astype(F32)).astype(BF16)


def sum_core_body(idx, a, b, c, d, *outs):
    for s, out in enumerate(outs):
        out[:, :QOP, :] = add(a[s], b[s])
        out[:, QOP:, :] = add(c[s], d[s])


def sum_y_body(idx, a, b, c, d, own, other):
    zh = idx[1]
    own[...] = add(a[zh], b[zh], c[zh], d[zh])
    far = 1 - zh
    other[...] = add(a[far], b[far], c[far], d[far])


def sum_z_body(idx, a, b, c, d, out):
    out[...] = add(a[...], b[...], c[...], d[...])


def unpack_tail_body(idx, *refs):
    y, core = idx[2], idx[3]
    qkv, out, gains = refs[8:]
    for k in range(8):
        piece = refs[k]
        p = ((y - k % 4) & 3) * 2 + (core if k < 4 else 1 - core)
        rows = pl.ds(pl.multiple_of(p * 128, 128), 128)
        for c in range(4):
            qkv[rows, c * 128 : (c + 1) * 128] = piece[c * 128 : (c + 1) * 128, :].astype(F32)
        qkv[rows, AW:] = piece[QOP : QOP + 128, :].astype(F32).T
        g = piece[QOP + 128 :, :].astype(F32)
        for c in range(2):
            first = QP + c * (AW // 2)
            cols = pl.ds(pl.multiple_of(p * 256 + c * 128, 128), 128)
            out[:, cols] = piece[first : first + AW // 2, :].astype(F32)
            gains[:, cols] = g[2 * c : 2 * c + 2]


def sum_tail(idx, first, second, parts):
    got_a = lax.ppermute(first[1], "core", shift(2, 1))
    got_b = lax.ppermute(second[1], "core", shift(2, 1))
    part = sds((2, TAIL, 128))
    g = small_call(sum_core_body, (part,) * 4, idx, first[0], got_a, second[0], got_b, name="sum_core")
    g_core = g[0]
    got = [lax.ppermute(g[s], "y", shift(4, s)) for s in (2, 1, 3)]
    part = sds((TAIL, 128))
    own, other = small_call(sum_y_body, (part,) * 2, idx, g[0], *got, name="sum_y")
    p0, q1, q3 = relay([tie(p, own) for p in parts])
    cross = [(2 * a + b, 2 * (1 - a) + (1 - b)) for a in range(2) for b in range(2)]
    g = small_call(
        sum_z_body,
        part,
        idx,
        tie(own, q1, q3),
        lax.ppermute(own, "zl", shift(2, 1)),
        lax.ppermute(other, "zh", shift(2, 1)),
        lax.ppermute(other, ("zl", "zh"), cross),
        name="sum_z",
    )
    d_one = last_step(p0, q1, q3)
    mine = [tie(g, *d_one)] + [lax.ppermute(g, "y", shift(4, s)) for s in (1, 2, 3)]
    theirs = [lax.ppermute(v, "core", shift(2, 1)) for v in [g] + mine[1:]]
    shapes = (sds((DH, QW), F32), sds((AW // 2, D), F32), sds((2, D), F32))
    return g_core, own, d_one, small_call(unpack_tail_body, shapes, idx, *mine, *theirs, name="unpack_tail")


def inverse_rms(v):
    return lax.rsqrt(jnp.mean(v * v, axis=-1, keepdims=True) + EPSILON)


def total(terms):
    return sum((t[...].astype(F32) for t in terms[1:]), terms[0][...].astype(F32))


def norm_two_body(tok, a, b, c, gain, after, normed):
    v = total((tok, a, b, c))
    after[...] = v
    normed[...] = (v * inverse_rms(v) * gain[...]).astype(BF16)


def norm_back_body(add, v_ref, a, b, c, gain, out, low, gain_grad):
    v = v_ref[...].astype(F32)
    grad = total((a, b, c))
    r = inverse_rms(v)
    pulled = grad * gain[...]
    inner = jnp.mean(v * pulled, axis=-1, keepdims=True)
    res = add[...].astype(F32) + r * pulled - v * (r * r * r) * inner
    out[...] = res
    low[...] = res.astype(BF16)
    part = jnp.sum(grad * v * r, axis=0, keepdims=True)

    @pl.when(pl.program_id(0) == 0)
    def _():
        gain_grad[...] = part

    @pl.when(pl.program_id(0) > 0)
    def _():
        gain_grad[...] += part


def row_call(body, out_shape, *args, name):
    block = lambda v: (
        pl.BlockSpec((HALF, D), lambda i: (i, 0))
        if v.shape[0] == BLK
        else pl.BlockSpec((1, D), lambda i: (0, 0))
    )
    return pl.pallas_call(
        body,
        grid=(2,),
        out_shape=out_shape,
        in_specs=[block(v) for v in args],
        out_specs=tuple(block(v) for v in out_shape),
        compiler_params=params(),
        cost_estimate=cost(1e6, 5e6),
        name=name,
    )(*args)


def replica_layout(lengths, replica, replica_id):
    sizes = jnp.where(replica == replica_id, lengths, 0)
    starts = jnp.cumsum(sizes) - sizes
    row_ids = jnp.arange(CAP, dtype=jnp.int32)
    inside = (row_ids[:, None] >= starts[None, :]) & (row_ids[:, None] < (starts + sizes)[None, :])
    begin = jnp.sum(jnp.where(inside, starts[None, :], 0), axis=1)
    begin = begin + jnp.where(jnp.any(inside, axis=1), 0, jnp.sum(sizes))
    return begin, row_ids - begin


def on_device(
    tokens, cotangent, gain_one, qkv_weight, out_weight, gate_weight, up_weight, down_weight,
    gain_two, seq_lengths, seq_replica,
):
    x, zh, core = lax.axis_index("x"), lax.axis_index("zh"), lax.axis_index("core")
    y, zl = lax.axis_index("y"), lax.axis_index("zl")
    idx = jnp.stack([x, zh, y, core]).astype(jnp.int32)

    tok = tokens.astype(F32)
    s_one = inverse_rms(tok)
    begin, position = replica_layout(seq_lengths, seq_replica, (y * 2 + zl) * 2 + core)
    half_rows = lambda v: lax.dynamic_index_in_dim(v.reshape(4, 2, BLK), zh, 1, False).reshape(ROWS, 1)
    first = jnp.tile(half_rows(begin)[3 * BLK :, 0], 8).reshape(1, QALL)
    lane = jnp.arange(128, dtype=jnp.int32)
    frequency = ROTARY_BASE ** (-(lane % 32).astype(F32) * (2.0 / HD))
    angles = half_rows(position).astype(F32) * frequency[None, :]
    cosine = jnp.cos(angles)
    sine = jnp.where((lane % HD) < HD // 2, -1.0, 1.0)[None, :] * jnp.sin(angles)

    qkv_got = fetch_half(qkv_weight, core)
    normed_one = gather_x((tok * s_one * gain_one).astype(BF16), (cosine,))
    out_got = fetch_half(out_weight, core)
    swap = lambda v, *deps: lax.ppermute(tie(v, *deps), "core", shift(2, 1))
    qkv_all = qkv_weight, qkv_got, swap(qkv_got, out_got, normed_one[2], normed_one[3])

    q, kv_own = qkv_forward(idx, normed_one, qkv_all, cosine, sine)
    cot = tie(cotangent, normed_one[2], normed_one[3])
    cots = [cotangent] + [lax.ppermute(cot, "x", shift(4, -k)) for k in (1, 2, 3)]
    kv_par = lax.ppermute(kv_own, "zh", shift(2, 1))
    out_all = out_weight, out_got, swap(out_got, kv_own)
    rows = DH // 8
    mine = lambda w: lax.dynamic_slice_in_dim(w, (y * 2 + core) * rows, rows, 0)
    cross = [(2 * a + b, 2 * (1 - a) + (1 - b)) for a in range(2) for b in range(2)]
    gate_up = lax.ppermute(
        jnp.concatenate(
            [
                mine(tie(gate_weight, kv_own)),
                jnp.zeros((rows, GAP - FF4), BF16),
                mine(tie(up_weight, kv_own)),
            ],
            1,
        ),
        ("zl", "zh"),
        cross,
    )
    att, qx = attend(idx, q, kv_own, kv_par, first)
    parts = out_project(idx, tie(att, *cots), out_all)
    down_got = fetch_half(tie(down_weight, parts[2]), core)
    gate_up = lax.all_gather(tie(gate_up, parts[2]), ("y", "core"), axis=0, tiled=True)
    after_attn, normed_two = row_call(
        norm_two_body,
        (sds((BLK, D), F32), sds((BLK, D))),
        tokens, *scatter_x(parts), gain_two.reshape(1, D), name="norm_two",
    )
    normed_two = gather_x(tie(normed_two, down_got))
    down_all = down_weight, down_got, lax.ppermute(tie(down_got, normed_two[1], normed_two[4]), "core", shift(2, 1))
    hid, dgate, dup = ffn(idx, normed_two, cots, gate_weight, up_weight, gate_up, down_all)
    d_parts = ffn_back(idx, dgate, dup, gate_weight, up_weight, gate_up)
    own_grads = down_grads(cots, tie(hid, d_parts[2]))
    d_own, q1, q3 = relay(d_parts)
    own_grads = gate_up_grads(normed_two, tie(dgate, q1, q3), dup, own_grads)
    d_two = last_step(d_own, q1, q3)
    grads = lax.psum_scatter(
        tie(own_grads, *d_two).reshape(32, PIECE, 128),
        ("zh", "zl", "y", "core"), scatter_dimension=0, tiled=True,
    )
    after_grad, branch, gain_grad_two = row_call(
        norm_back_body,
        (sds((BLK, D), F32), sds((BLK, D)), sds((1, D), F32)),
        cotangent, after_attn, *d_two, gain_two.reshape(1, D), name="norm_back_two",
    )
    branch = gather_x(branch)
    layer_parts = down_project(idx, tie(hid, after_grad), down_all)
    att = tie(att, *layer_parts)
    layer = [
        lax.ppermute(tie(layer_parts[k], branch[2], branch[3]), "x", shift(4, k)) for k in (1, 3)
    ]
    dqm, dkv_own, dkv_par = attend_back(
        idx, qx, kv_own, kv_par, first, att, cosine, sine, branch, out_all
    )
    dkv_got = lax.ppermute(dkv_par, "zh", shift(2, 1))
    tail = attn_grads(
        idx, normed_one, branch, dqm.reshape(ROWS, AW), tie(att, *layer).reshape(ROWS, AW)
    )
    dkv_got = tie(dkv_got, tail[0])
    *tail_kv, parts = qkv_back(
        idx, dqm.reshape(ROWS, AW), dkv_own, dkv_got, cosine, sine, qkv_all, normed_one, gain_one,
        gain_grad_two,
    )
    over_x = lambda v: sum((lax.ppermute(v, "x", shift(4, s)) for s in (1, 2, 3)), v)
    cores_summed, summed, d_one, (grad_qkv, grad_out, gains) = sum_tail(
        idx, (tail[0], tie(tail[1], dkv_got)), tail_kv, parts
    )
    layer.append(lax.ppermute(tie(layer_parts[2], summed), "x", shift(4, 2)))
    grads = lax.all_gather(tie(grads, summed), ("zl", "y", "core"), axis=0, tiled=True)
    grad_gate, grad_up, grad_down = unpack(grads)
    _, input_grad, _ = row_call(
        norm_back_body,
        (sds((BLK, D), F32), sds((BLK, D)), sds((1, D), F32)),
        after_grad, tokens, *d_one, gain_one.reshape(1, D), name="norm_back_one",
    )
    layer_out = sum((v.astype(F32) for v in layer), after_attn + layer_parts[0].astype(F32))
    layer_out = layer_out.astype(BF16)
    gains = over_x(gains)
    return (
        layer_out, input_grad, gains[0], grad_qkv, grad_out, grad_gate, grad_up,
        grad_down, gains[1],
    )


def solution(mesh):
    grid = Mesh(mesh.devices.reshape(SIZES), AXES)
    rows = P(AXES, None)
    both = P(("x", "zh"), None)
    return jax.shard_map(
        on_device,
        mesh=grid,
        in_specs=(
            rows, rows, P(), P("zh", "x"), both, P("zh", "x"), P("zh", "x"), both, P(), P(), P(),
        ),
        out_specs=(
            rows, rows, P(), P("zh", "x"), both, P("zh", "x"), P("zh", "x"), both, P(),
        ),
        check_vma=False,
    )
```

```python
import jax
import jax.numpy as jnp
from jax import lax
from jax.experimental import pallas as pl
from jax.experimental.pallas import tpu as pltpu
from jax.sharding import Mesh
from jax.sharding import PartitionSpec as P

HEADS = 32
KV = 4
HD = 64
EPSILON = 1e-05
ROTARY_BASE = 10000.0
MASKED = -1e30

AXES = ("y", "zl", "core", "x", "zh")
SIZES = (4, 2, 2, 4, 2)
BLK = 160
HALF = BLK // 2
ROWS = 4 * BLK
CAP = 2 * ROWS
D = 2048
DH = D // 2
QW = 640
AW = 512
FF4 = 1408
TILE = 256
F32 = jnp.float32
BF16 = jnp.bfloat16
VLIM = 60 * 1024 * 1024


def spec(memory=pltpu.VMEM):
    return pl.BlockSpec(memory_space=memory)


def params(**kw):
    return pltpu.CompilerParams(vmem_limit_bytes=VLIM, **kw)


def cost(flops, nbytes):
    return pl.CostEstimate(flops=int(flops), bytes_accessed=int(nbytes), transcendentals=0)


def sds(shape, dtype=BF16):
    return jax.ShapeDtypeStruct(shape, dtype)


def dot(a, b):
    return jnp.dot(a, b, preferred_element_type=F32)


def dot_t(a, b):
    return lax.dot_general(a, b, (((1,), (1,)), ((), ())), preferred_element_type=F32)


def t_dot(a, b):
    return lax.dot_general(a, b, (((0,), (0,)), ((), ())), preferred_element_type=F32)


def tie(v, *deps):
    return lax.optimization_barrier((v,) + deps)[0]


def shift(n, s):
    return [(i, (i + s) % n) for i in range(n)]


def gather_x(v, wait=()):
    from_prev = lax.ppermute(v, "x", shift(4, 1))
    from_next = lax.ppermute(v, "x", shift(4, -1))
    send_a = tie(from_prev[:HALF], from_next, *wait)
    send_b = tie(from_next[HALF:], from_prev, *wait)
    opp_a = lax.ppermute(send_a, "x", shift(4, 1))
    opp_b = lax.ppermute(send_b, "x", shift(4, -1))
    return v, from_next, opp_a, opp_b, from_prev


def relay_body(p1, got_a, p3, got_b, q1, q3):
    q1[...] = (p1[...].astype(F32) + got_a[...].astype(F32)).astype(BF16)
    q3[...] = (p3[...].astype(F32) + got_b[...].astype(F32)).astype(BF16)


def relay(parts):
    p0, p1, p2a, p2b, p3 = parts
    got_a = lax.ppermute(p2a, "x", shift(4, 1))
    got_b = lax.ppermute(p2b, "x", shift(4, -1))
    half = lambda k: pl.BlockSpec((HALF, D), lambda i: (k, 0))
    q1, q3 = pl.pallas_call(
        relay_body,
        grid=(1,),
        out_shape=(sds((BLK, D)),) * 2,
        in_specs=[half(0), half(0), half(1), half(0)],
        out_specs=(half(0), half(1)),
        input_output_aliases={0: 0, 2: 1},
        compiler_params=params(),
        cost_estimate=cost(1e6, 2e6),
        name="relay",
    )(p1, got_a, p3, got_b)
    return p0, q1, q3


def scatter_x(parts):
    return last_step(*relay(parts))


def last_step(p0, q1, q3):
    return p0, lax.ppermute(q1, "x", shift(4, 1)), lax.ppermute(q3, "x", shift(4, -1))


PIECES = ((0, BLK), (1, BLK), (2, HALF), (2, HALF), (3, BLK))
PIECE_ROW = (0, BLK, 2 * BLK, 2 * BLK + HALF, 3 * BLK)


def part_shapes(width, dtype=BF16):
    return tuple(sds((n, width), dtype) for _, n in PIECES)


def low_lanes(shape):
    return lax.broadcasted_iota(jnp.int32, shape, 1) < HD


def swap_halves(v):
    lane = lax.broadcasted_iota(jnp.int32, v.shape, 1) % HD
    return jnp.where(lane < HD // 2, pltpu.roll(v, 128 - HD // 2, 1), pltpu.roll(v, HD // 2, 1))


def rows_at(block):
    return pl.ds(pl.multiple_of(block * BLK, 32), BLK)


def fetch_half(w, core):
    half = w.shape[0] // 2
    return lax.ppermute(lax.dynamic_slice_in_dim(w, core * half, half, 0), "zh", shift(2, 1))


def fetch_partner(w, core, *deps):
    got = fetch_half(tie(w, *deps), core)
    return w, got, lax.ppermute(got, "core", shift(2, 1))


def weight_rows(idx, rows):
    zh, core = idx[1], idx[3]
    far = (1 - zh) * rows
    half = rows // 2
    at = lambda first, n: pl.ds(pl.multiple_of(first, half), n)
    return at(zh * rows, rows), at(far + core * half, half), at(far + (1 - core) * half, half)


def qkv_body(idx, n0, n1, n2a, n2b, n3, w0, w1, w2, cosine, sine, q_ref, kv_ref, rows):
    x = idx[0]
    lo = low_lanes((BLK, 128))
    for ref, row, (_, n) in zip((n0, n1, n2a, n2b, n3), PIECE_ROW, PIECES):
        rows[row : row + n, :] = ref[...]
    s0, s1, s2 = weight_rows(idx, DH)
    acc = dot(rows[:, s0], w0[...]) + dot(rows[:, s1], w1[...]) + dot(rows[:, s2], w2[...])
    for d in range(4):
        at = rows_at((x + d) & 3)
        cs = cosine[at, :]
        sn = sine[at, :]
        for p in range(5):
            v = acc[d * BLK : (d + 1) * BLK, p * 128 : (p + 1) * 128]
            r = v * cs + swap_halves(v) * sn
            if p < 4:
                r = r * (HD**-0.5 * LOG2E)
                a = (x + d) & 3
                for k, w in enumerate((r, pltpu.roll(r, HD, 1))):
                    head = slice((2 * p + k) * BLK, (2 * p + k + 1) * BLK)
                    q_ref[a, head, :] = jnp.where(lo, w, 0.0).astype(BF16)
            else:
                kv_ref[at, :] = jnp.where(lo, r, v).astype(BF16)


def qkv_forward(idx, pieces, weight, cosine, sine):
    return pl.pallas_call(
        qkv_body,
        out_shape=(sds((4, QALL, 128)), sds((ROWS, 128))),
        in_specs=[spec(pltpu.SMEM)] + [spec()] * 10,
        out_specs=(spec(), spec()),
        scratch_shapes=[pltpu.VMEM((ROWS, D), BF16)],
        compiler_params=params(),
        cost_estimate=cost(2 * ROWS * D * QW, 7e6),
        name="qkv_forward",
    )(idx, *pieces, *weight, cosine, sine)


QALL = 8 * BLK
PAIR = 2 * BLK
LOG2E = 1.4426950408889634
LN2 = 0.6931471805599453


def split3(v):
    a = v.astype(BF16).astype(F32)
    b = (v - a).astype(BF16).astype(F32)
    return a, b, v - a - b


def with_lanes(v, parts):
    lane = lax.broadcasted_iota(jnp.int32, v.shape, 1)
    out = jnp.where(lane < HD, v, 0.0)
    for k, part in enumerate(parts):
        out = jnp.where(lane == HD + k, part, out)
    return out


def spread_keys(zh, kv_own, kv_par, kk, vv, fill):
    shape = (BLK, 128)
    lo = low_lanes(shape)
    rest = fill(lax.broadcasted_iota(jnp.int32, shape, 1) - HD)
    for j in range(4):
        for src, off in ((kv_own, zh), (kv_par, 1 - zh)):
            v = src[j * BLK : (j + 1) * BLK, :].astype(F32)
            at = rows_at(2 * j + off)
            kk[at, :] = jnp.where(lo, v, rest).astype(BF16)
            vv[at, :] = jnp.where(lo, pltpu.roll(v, HD, 1), rest).astype(BF16)


def masked(s, zh, j, kb, first):
    if j < 3 and kb < j:
        return s
    u = kb * PAIR + lax.broadcasted_iota(jnp.int32, (PAIR, QALL), 0)
    allowed = None
    if kb == j:
        t = (2 * j + zh) * BLK + lax.broadcasted_iota(jnp.int32, (1, QALL), 1) % BLK
        allowed = u <= t
    if j == 3:
        later = u >= first[...]
        allowed = later if allowed is None else allowed & later
    return jnp.where(allowed, s, MASKED)


def attend_body(idx, q, kv_own, kv_par, first, att, qx, kk, vv, vt, s_ref, e_ref):
    x, zh = idx[0], idx[1]
    spread_keys(zh, kv_own, kv_par, kk, vv, lambda lane: 1.0)
    vt[...] = vv[...].T
    lo = low_lanes((BLK, 128))
    for j in range(4):
        n = PAIR * (j + 1)
        qj = q[j]
        top = jnp.full((1, QALL), MASKED, F32)
        for kb in range(j + 1):
            rows = slice(kb * PAIR, (kb + 1) * PAIR)
            s = masked(dot_t(kk[rows, :], qj), zh, j, kb, first)
            s_ref[rows, :] = s
            top = jnp.maximum(top, jnp.max(s, axis=0, keepdims=True))
        for k in range(n // 64):
            rows = slice(k * 64, (k + 1) * 64)
            e_ref[rows, :] = jnp.exp2(s_ref[rows, :] - top).astype(BF16)
        o = dot(vt[:, :n], e_ref[:n, :])
        lse = split3(top + jnp.log(o[HD : HD + 1, :]) * LOG2E)
        row = lax.broadcasted_iota(jnp.int32, (128, QALL), 0)
        extra = jnp.zeros((128, QALL), F32)
        for k, part in enumerate(lse):
            extra = jnp.where(row == HD + k, part, extra)
        qx[j] = (qj.astype(F32) + extra.T).astype(BF16)
        o = o.T
        r = pltpu.roll(o, HD, 1)
        rel = (j - x) & 3
        for p in range(4):
            even, odd = slice(2 * p * BLK, (2 * p + 1) * BLK), slice((2 * p + 1) * BLK, (2 * p + 2) * BLK)
            num = jnp.where(lo, o[even], r[odd])
            den = jnp.where(lo, r[even], o[odd])
            att[rel, :, p * 128 : (p + 1) * 128] = (num / den).astype(BF16)


def attend(idx, q, kv_own, kv_par, first):
    return pl.pallas_call(
        attend_body,
        out_shape=(sds((4, BLK, AW)), sds((4, QALL, 128))),
        in_specs=[spec(pltpu.SMEM)] + [spec()] * 4,
        out_specs=(spec(), spec()),
        scratch_shapes=[
            pltpu.VMEM((CAP, 128), BF16),
            pltpu.VMEM((CAP, 128), BF16),
            pltpu.VMEM((128, CAP), BF16),
            pltpu.VMEM((CAP, QALL), F32),
            pltpu.VMEM((CAP, QALL), BF16),
        ],
        compiler_params=params(),
        cost_estimate=cost(1.2e10, 3e6),
        name="attend",
    )(idx, q, kv_own, kv_par, first)


def store_parts(res, refs):
    for ref, row, (_, n) in zip(refs, PIECE_ROW, PIECES):
        ref[...] = res[row : row + n].astype(BF16)


def out_body(idx, att, w0, w1, w2, o0, o1, o2a, o2b, o3):
    s0, s1, s2 = weight_rows(idx, AW // 2)
    for d, ref in ((2, None), (1, o1), (3, o3), (0, o0)):
        a = att.at[d]
        res = dot(a[:, s0], w0[...]) + dot(a[:, s1], w1[...]) + dot(a[:, s2], w2[...])
        res = res.astype(BF16)
        if d == 2:
            o2a[...] = res[:HALF]
            o2b[...] = res[HALF:]
        else:
            ref[...] = res


def out_project(idx, att, weight):
    return pl.pallas_call(
        out_body,
        out_shape=part_shapes(D),
        in_specs=[spec(pltpu.SMEM)] + [spec()] * 4,
        out_specs=(spec(),) * 5,
        compiler_params=params(),
        cost_estimate=cost(2 * ROWS * D * AW, 5.5e6),
        name="out_project",
    )(idx, att, *weight)


def stack_heads(v):
    return v, pltpu.roll(v, HD, 1)


def attend_back_body(
    idx, qx, kv_own, kv_par, first, att, cosine, sine, b0, b1, b2a, b2b, b3, w0, w1, w2,
    dq_ref, dkv_own, dkv_par, kk, vv, dout, do_all, dkk, dvv, e_ref, ds_ref, dq_acc,
):
    x, zh = idx[0], idx[1]
    spread_keys(zh, kv_own, kv_par, kk, vv, lambda lane: jnp.where(lane < 3, -1.0, 0.0))
    s0, s1, s2 = weight_rows(idx, AW // 2)
    for d in range(4):
        if d == 2:
            rows = jnp.concatenate([b2a[...], b2b[...]], 0)
        else:
            rows = (b0, b1, None, b3)[d][...]
        at = rows_at((x + d) & 3)
        for s, w in ((s0, w0), (s1, w1), (s2, w2)):
            dout[at, s] = dot_t(rows, w[...]).astype(BF16)
    lo = low_lanes((BLK, 128))
    for j in range(4):
        rel = (j - x) & 3
        here = slice(j * BLK, (j + 1) * BLK)
        for p in range(4):
            cols = slice(p * 128, (p + 1) * 128)
            do = dout[here, cols].astype(F32)
            prod = do * att[rel, :, cols].astype(F32)
            for k, (v, w) in enumerate(zip(stack_heads(do), stack_heads(prod))):
                delta = jnp.sum(jnp.where(lo, w, 0.0), axis=1, keepdims=True)
                head = slice((2 * p + k) * BLK, (2 * p + k + 1) * BLK)
                do_all[head, :] = with_lanes(v, split3(delta)).astype(BF16)
        for kb in range(j + 1):
            rows = slice(kb * PAIR, (kb + 1) * PAIR)
            e = jnp.exp2(masked(dot_t(kk[rows, :], qx[j]), zh, j, kb, first))
            e_ref[...] = e.astype(BF16)
            ds_ref[...] = (e * dot_t(vv[rows, :], do_all[...])).astype(BF16)
            dv = dot(e_ref[...], do_all[...])
            dk = dot(ds_ref[...], qx[j])
            dq = t_dot(ds_ref[...], kk[rows, :])
            if kb == j:
                dvv[rows, :], dkk[rows, :] = dv, dk
            else:
                dvv[rows, :] += dv
                dkk[rows, :] += dk
            if kb == 0:
                dq_acc[...] = dq
            else:
                dq_acc[...] += dq
        for p in range(4):
            even, odd = slice(2 * p * BLK, (2 * p + 1) * BLK), slice((2 * p + 1) * BLK, (2 * p + 2) * BLK)
            v = jnp.where(lo, dq_acc[even, :], pltpu.roll(dq_acc[odd, :], HD, 1)) * HD**-0.5
            v = v * cosine[here, :] - swap_halves(v) * sine[here, :]
            dq_ref[rel, :, p * 128 : (p + 1) * 128] = v.astype(BF16)
    for j in range(4):
        for dst, off in ((dkv_own, zh), (dkv_par, 1 - zh)):
            at = rows_at(2 * j + off)
            both = jnp.where(lo, dkk[at, :] * LN2, pltpu.roll(dvv[at, :], HD, 1))
            dst[j * BLK : (j + 1) * BLK, :] = both.astype(dst.dtype)


def attend_back(idx, qx, kv_own, kv_par, first, att, cosine, sine, branch, weight):
    return pl.pallas_call(
        attend_back_body,
        out_shape=(sds((4, BLK, AW)), sds((ROWS, 128), F32), sds((ROWS, 128))),
        in_specs=[spec(pltpu.SMEM)] + [spec()] * 15,
        out_specs=(spec(),) * 3,
        scratch_shapes=[
            pltpu.VMEM((CAP, 128), BF16),
            pltpu.VMEM((CAP, 128), BF16),
            pltpu.VMEM((ROWS, AW), BF16),
            pltpu.VMEM((QALL, 128), BF16),
            pltpu.VMEM((CAP, 128), F32),
            pltpu.VMEM((CAP, 128), F32),
            pltpu.VMEM((PAIR, QALL), BF16),
            pltpu.VMEM((PAIR, QALL), BF16),
            pltpu.VMEM((QALL, 128), F32),
        ],
        compiler_params=params(),
        cost_estimate=cost(3e10, 8e6),
        name="attend_back",
    )(idx, qx, kv_own, kv_par, first, att, cosine, sine, *branch, *weight)


def qkv_back_body(
    idx, dqm, dkv_own, dkv_got, cosine, sine, w0, w1, w2, n0, n1, n2a, n2b, n3, gain_one,
    gain_grad_two,
    mine, theirs, o0, o1, o2a, o2b, o3, n_all, dkv, grad, gains,
):
    x, y, core = idx[0], idx[2], idx[3]
    lo = low_lanes((BLK, 128))
    for ref, row, (_, n) in zip((n0, n1, n2a, n2b, n3), PIECE_ROW, PIECES):
        n_all[row : row + n, :] = ref[...]
    for d in range(4):
        at = rows_at((x + d) & 3)
        v = dkv_own[at, :] + dkv_got[at, :].astype(F32)
        v = jnp.where(lo, v * cosine[at, :] - swap_halves(v) * sine[at, :], v).astype(BF16)
        dkv[d * BLK : (d + 1) * BLK, :] = v
    rows = jnp.concatenate([dqm[...], dkv[...]], 1)
    for s, w in zip(weight_rows(idx, DH), (w0, w1, w2)):
        for c in range(w.shape[0] // 512):
            cols = pl.ds(pl.multiple_of(s.start + c * 512, 512), 512)
            res = dot_t(rows, w[c * 512 : (c + 1) * 512, :])
            part = (res * n_all[:, cols].astype(F32)).reshape(ROWS // 8, 8, 512)
            gains[0:1, cols] = jnp.sum(jnp.sum(part, axis=0), axis=0, keepdims=True) / gain_one[:, cols]
            store_parts(res, [r.at[:, cols] for r in (o0, o1, o2a, o2b, o3)])
    grad[...] = dot(dkv[...].T, n_all[...]).astype(BF16)
    gains[1:2, :] = gain_grad_two[...]
    for s in range(4):
        for k, ref in enumerate((mine, theirs)):
            p = ((y + s) & 3) * 2 + (core if k == 0 else 1 - core)
            both = gains[:, pl.ds(pl.multiple_of(p * 256, 256), 256)]
            both = jnp.concatenate([both[:, :128], both[:, 128:], jnp.zeros((12, 128), F32)], 0)
            for h in range(2):
                ref[s, h, :128, :] = grad[:, pl.ds(pl.multiple_of(h * DH + p * 128, 128), 128)]
                ref[s, h, 128:, :] = both.astype(BF16)


def qkv_back(idx, dqm, dkv_own, dkv_got, cosine, sine, weight, pieces, gain_one, gain_grad_two):
    res = pl.pallas_call(
        qkv_back_body,
        out_shape=(sds((4, 2, KVP, 128)),) * 2 + part_shapes(D),
        in_specs=[spec(pltpu.SMEM)] + [spec()] * 15,
        out_specs=(spec(),) * 7,
        scratch_shapes=[
            pltpu.VMEM((ROWS, D), BF16),
            pltpu.VMEM((ROWS, 128), BF16),
            pltpu.VMEM((128, D), BF16),
            pltpu.VMEM((2, D), F32),
        ],
        compiler_params=params(),
        cost_estimate=cost(2 * ROWS * D * QW, 1.3e7),
        name="qkv_back",
    )(
        idx, dqm, dkv_own, dkv_got, cosine, sine, *weight, *pieces,
        gain_one.reshape(1, D), gain_grad_two.reshape(1, D),
    )
    return res[0], res[1], res[2:]


TILES = 6
GAP = TILES * TILE


def load_down(idx, refs, dst, sem):
    copies = []
    for k, (s, ref) in enumerate(zip(weight_rows(idx, FF4 // 2), refs)):
        copies.append(pltpu.make_async_copy(ref, dst.at[s], sem.at[k]))
    return copies


FFN_ORDER = (0, 1, 3, 2)
EARLY = 3 * BLK


def ffn_parts(refs):
    o0, o1, o2a, o2b, o3 = refs
    return (o0, 0, BLK), (o1, BLK, BLK), (o3, 2 * BLK, BLK), (o2a, EARLY, HALF), (o2b, EARLY + HALF, HALF)


def ffn_kernel(n_rows, n_cots, aliased):
    def body(idx, *refs):
        pieces, cots = refs[:n_rows], refs[n_rows : n_rows + n_cots]
        refs = refs[n_rows + n_cots :]
        gate_own, up_own, gate_par, up_par, w0, w1, w2 = refs[:7]
        hid, dgate, dup, n_all, c_all, down, sem = refs[7 + aliased :]
        i = pl.program_id(0)
        zh = idx[1]

        @pl.when(i == 0)
        def _():
            copies = load_down(idx, (w0, w1, w2), down, sem)
            for c in copies:
                c.start()
            for group, dst in ((pieces, n_all), (cots, c_all)):
                row = 0
                for ref in group:
                    dst[row : row + ref.shape[0], :] = ref[...]
                    row += ref.shape[0]
            for c in copies:
                c.wait()

        own = n_all[:, pl.ds(pl.multiple_of(zh * DH, DH), DH)]
        par = n_all[:, pl.ds(pl.multiple_of((1 - zh) * DH, DH), DH)]
        gate = dot(own, gate_own[...]) + dot(par, gate_par[...])
        up = dot(own, up_own[...]) + dot(par, up_par[...])
        dh = dot_t(c_all[...], down[pl.ds(pl.multiple_of(i * TILE, TILE), TILE), :])
        sig = 1.0 / (1.0 + jnp.exp(-gate))
        act = gate * sig
        hid[...] = (act * up).astype(BF16)
        dgate[...] = (dh * up * sig * (1.0 + gate * (1.0 - sig))).astype(BF16)
        dup[...] = (dh * act).astype(BF16)

    return body


def whole(n, w):
    return pl.BlockSpec((n, w), lambda i: (0, 0))


def ffn(idx, pieces, cots, gate, up, gate_up, down, earlier=()):
    rows = sum(v.shape[0] for v in pieces)
    column = lambda first: pl.BlockSpec((DH, TILE), lambda i: (0, i + first))
    place = EARLY // rows if earlier else 0
    hidden = pl.BlockSpec((rows, TILE), lambda i: (place, i))
    n = len(pieces) + len(cots)
    return pl.pallas_call(
        ffn_kernel(len(pieces), len(cots), len(earlier)),
        grid=(TILES,),
        out_shape=(sds((ROWS, FF4)),) * 3,
        in_specs=[spec(pltpu.SMEM)]
        + [whole(v.shape[0], D) for v in (*pieces, *cots)]
        + [column(0), column(0), column(0), column(TILES)]
        + [spec(pl.ANY)] * (3 + len(earlier)),
        out_specs=[hidden] * 3,
        scratch_shapes=[
            pltpu.VMEM((rows, D), BF16),
            pltpu.VMEM((rows, D), BF16),
            pltpu.VMEM((GAP, D), BF16),
            pltpu.SemaphoreType.DMA((3,)),
        ],
        input_output_aliases={n + 8 + k: k for k in range(len(earlier))},
        compiler_params=params(),
        cost_estimate=cost(6 * rows * D * FF4, 2.5e7),
        name="ffn_last" if earlier else "ffn",
    )(idx, *pieces, *cots, gate, up, gate_up, gate_up, *down, *earlier)


def down_body(idx, hid, w0, w1, w2, o0, o1, o2, o3, down, sem):
    copies = load_down(idx, (w0, w1, w2), down, sem)
    for c in copies:
        c.start()
    for c in copies:
        c.wait()
    for n in range(D // 512):
        cols = slice(n * 512, (n + 1) * 512)
        res = dot(hid[...], down[:, cols]).astype(BF16)
        for k, ref in enumerate((o0, o1, o3, o2)):
            ref[:, cols] = res[k * BLK : (k + 1) * BLK]


def down_project(idx, hid, down):
    return pl.pallas_call(
        down_body,
        out_shape=(sds((BLK, D)),) * 4,
        in_specs=[spec(pltpu.SMEM), spec()] + [spec(pl.ANY)] * 3,
        out_specs=(spec(),) * 4,
        scratch_shapes=[pltpu.VMEM((FF4, D), BF16), pltpu.SemaphoreType.DMA((3,))],
        compiler_params=params(),
        cost_estimate=cost(2 * ROWS * D * FF4, 1.1e7),
        name="down_project",
    )(idx, hid, *down)


def ffn_back_body(idx, dgate, dup, gate_own, up_own, par, *refs):
    half = pl.num_programs(0) // 2

    def store(res):
        for ref, row, n in ffn_parts(refs):
            ref[...] = res[row : row + n].astype(BF16)

    @pl.when(pl.program_id(0) < half)
    def _():
        store(dot_t(dgate[...], gate_own[...]) + dot_t(dup[...], up_own[...]))

    @pl.when(pl.program_id(0) >= half)
    def _():
        store(dot_t(dgate[...], par[:, :FF4]) + dot_t(dup[...], par[:, GAP:]))


def ffn_back(idx, dgate, dup, gate, up, gate_up):
    half = DH // TILE
    rows = pl.BlockSpec((ROWS, FF4), lambda i, idx: (0, 0))
    own = pl.BlockSpec((TILE, FF4), lambda i, idx: (jnp.minimum(i, half - 1), 0))
    par = pl.BlockSpec((TILE, GAP + FF4), lambda i, idx: (jnp.maximum(i - half, 0), 0))
    place = lambda i, idx: (0, i ^ (idx[1] * half))
    return pl.pallas_call(
        ffn_back_body,
        grid_spec=pltpu.PrefetchScalarGridSpec(
            num_scalar_prefetch=1,
            grid=(D // TILE,),
            in_specs=[rows, rows, own, own, par],
            out_specs=[pl.BlockSpec((n, TILE), place) for _, n in PIECES],
        ),
        out_shape=part_shapes(D),
        compiler_params=params(),
        cost_estimate=cost(4 * ROWS * D * FF4, 1.8e7),
        name="ffn_back",
    )(idx, dgate, dup, gate, up, gate_up)


GU_ROWS = FF4 // 128 * 64
PIECE = 2 * GU_ROWS + FF4 // 2
QS = 4


def gate_up_grads_body(*refs):
    na, nb = refs[0:5], refs[5:10]
    dgate, dup, _, out = refs[10:]
    stack = lambda parts: jnp.concatenate([r[...] for r in parts], 0)
    rows = jnp.concatenate([stack(na), stack(nb)], 1).T
    for k, ref in enumerate((dgate, dup)):
        g = dot(rows, ref[...]).astype(BF16)
        for h in range(2):
            for q in range(QS):
                r = g[(QS * h + q) * 64 : (QS * h + q + 1) * 64]
                for c in range(FF4 // 128):
                    first = k * GU_ROWS + c * 64
                    out[h, q, first : first + 64, :] = r[:, c * 128 : (c + 1) * 128]


def gate_up_grads(normed, dgate, dup, pieces):
    return pl.pallas_call(
        gate_up_grads_body,
        grid=(16 // QS,),
        out_shape=sds((2, 16, PIECE, 128)),
        in_specs=[pl.BlockSpec((v.shape[0], 64 * QS), lambda i: (0, i)) for v in normed]
        + [pl.BlockSpec((v.shape[0], 64 * QS), lambda i: (0, i + 16 // QS)) for v in normed]
        + [whole(ROWS, FF4)] * 2
        + [spec(pl.ANY)],
        out_specs=pl.BlockSpec((2, QS, 2 * GU_ROWS, 128), lambda i: (0, i, 0, 0)),
        input_output_aliases={12: 0},
        compiler_params=params(),
        cost_estimate=cost(4 * ROWS * D * FF4, 2e7),
        name="gate_up_grads",
    )(*normed, *normed, dgate, dup, pieces)


def down_grads_body(*refs):
    cots = refs[0:4]
    hid, out, hid_t = refs[4:]

    @pl.when(pl.program_id(0) == 0)
    def _():
        hid_t[...] = hid[...].T

    g = dot(hid_t[...], jnp.concatenate([r[...] for r in cots], 0)).astype(BF16)
    for h in range(2):
        for q in range(QS):
            out[h, q, :, :] = g[h * (FF4 // 2) : (h + 1) * (FF4 // 2), q * 128 : (q + 1) * 128]


def down_grads(cots, hid):
    return pl.pallas_call(
        down_grads_body,
        grid=(16 // QS,),
        out_shape=sds((2, 16, PIECE, 128)),
        in_specs=[pl.BlockSpec((BLK, 128 * QS), lambda i: (0, i))] * 4 + [whole(ROWS, FF4)],
        out_specs=pl.BlockSpec((2, QS, FF4 // 2, 128), lambda i: (0, i, 2, 0)),
        scratch_shapes=[pltpu.VMEM((FF4, ROWS), BF16)],
        compiler_params=params(),
        cost_estimate=cost(2 * ROWS * D * FF4, 1e7),
        name="down_grads",
    )(*cots, hid)


def unpack_body(piece, gate, up, down):
    for q in range(QS):
        rows = slice(q * 64, (q + 1) * 64)
        for k, ref in enumerate((gate, up)):
            for c in range(FF4 // 128):
                first = k * GU_ROWS + c * 64
                ref[rows, c * 128 : (c + 1) * 128] = piece[q, first : first + 64, :].astype(F32)
        down[:, q * 128 : (q + 1) * 128] = piece[q, 2 * GU_ROWS :, :].astype(F32)


def unpack(pieces):
    return pl.pallas_call(
        unpack_body,
        grid=(16 // QS,),
        out_shape=(sds((DH, FF4), F32), sds((DH, FF4), F32), sds((FF4 // 2, D), F32)),
        in_specs=[pl.BlockSpec((QS, PIECE, 128), lambda i: (i, 0, 0))],
        out_specs=[
            pl.BlockSpec((64 * QS, FF4), lambda i: (i, 0)),
            pl.BlockSpec((64 * QS, FF4), lambda i: (i, 0)),
            pl.BlockSpec((FF4 // 2, 128 * QS), lambda i: (0, i)),
        ],
        compiler_params=params(),
        cost_estimate=cost(1e6, 2.6e7),
        name="unpack",
    )(pieces)


QP = 4 * 128
OP = 2 * (AW // 2)
QOP = QP + OP
KVP = 128 + 16
TAIL = QOP + KVP


def attn_grads_body(idx, *refs):
    na, nb, branch = refs[0:5], refs[5:10], refs[10:15]
    dqm, att, mine, theirs, att_t = refs[15:]
    core = idx[3]

    @pl.when(pl.program_id(0) == 0)
    def _():
        att_t[...] = att[...].T

    stack = lambda parts: jnp.concatenate([r[...] for r in parts], 0)

    def store(h, first, n, zero, one):
        mine[0, h, first : first + n, :] = jnp.where(core == 0, zero, one)
        theirs[0, h, first : first + n, :] = jnp.where(core == 0, one, zero)

    for h, cols in enumerate((na, nb)):
        g = dot(stack(cols).T, dqm[...]).astype(BF16)
        for c in range(4):
            lanes = slice(c * 128, (c + 1) * 128)
            store(h, c * 128, 128, g[:128, lanes], g[128:, lanes])
    g = dot(att_t[...], stack(branch)).astype(BF16)
    for h in range(2):
        r = g[h * (AW // 2) : (h + 1) * (AW // 2)]
        for c in range(2):
            lanes = lambda k: slice(k * 256 + c * 128, k * 256 + (c + 1) * 128)
            store(h, QP + c * (AW // 2), AW // 2, r[:, lanes(0)], r[:, lanes(1)])


def attn_grads(idx, normed, branch, dqm, att):
    turn = lambda s, idx: (s + idx[2]) & 3
    piece = pl.BlockSpec((1, 2, QOP, 128), lambda s, idx: (s, 0, 0, 0))
    fixed = pl.BlockSpec((ROWS, AW), lambda s, idx: (0, 0))
    return pl.pallas_call(
        attn_grads_body,
        grid_spec=pltpu.PrefetchScalarGridSpec(
            num_scalar_prefetch=1,
            grid=(4,),
            in_specs=[pl.BlockSpec((n, 256), lambda s, idx: (0, turn(s, idx))) for _, n in PIECES]
            + [pl.BlockSpec((n, 256), lambda s, idx: (0, turn(s, idx) + 4)) for _, n in PIECES]
            + [pl.BlockSpec((n, 512), lambda s, idx: (0, turn(s, idx))) for _, n in PIECES]
            + [fixed, fixed],
            out_specs=[piece, piece],
            scratch_shapes=[pltpu.VMEM((AW, ROWS), BF16)],
        ),
        out_shape=(sds((4, 2, QOP, 128)),) * 2,
        compiler_params=params(),
        cost_estimate=cost(4 * ROWS * D * AW, 1e7),
        name="attn_grads",
    )(idx, *normed, *normed, *branch, dqm, att)


def small_call(body, out_shape, *args, name):
    return pl.pallas_call(
        body,
        out_shape=out_shape,
        in_specs=[spec(pltpu.SMEM)] + [spec()] * (len(args) - 1),
        out_specs=jax.tree.map(lambda _: spec(), out_shape),
        compiler_params=params(),
        cost_estimate=cost(1e6, 4e6),
        name=name,
    )(*args)


def add(*values):
    return sum((v.astype(F32) for v in values[1:]), values[0].astype(F32)).astype(BF16)


def sum_core_body(idx, a, b, c, d, *outs):
    for s, out in enumerate(outs):
        out[:, :QOP, :] = add(a[s], b[s])
        out[:, QOP:, :] = add(c[s], d[s])


def sum_y_body(idx, a, b, c, d, own, other):
    zh = idx[1]
    own[...] = add(a[zh], b[zh], c[zh], d[zh])
    far = 1 - zh
    other[...] = add(a[far], b[far], c[far], d[far])


def sum_z_body(idx, a, b, c, d, out):
    out[...] = add(a[...], b[...], c[...], d[...])


def unpack_tail_body(idx, *refs):
    y, core = idx[2], idx[3]
    qkv, out, gains = refs[8:]
    for k in range(8):
        piece = refs[k]
        p = ((y - k % 4) & 3) * 2 + (core if k < 4 else 1 - core)
        rows = pl.ds(pl.multiple_of(p * 128, 128), 128)
        for c in range(4):
            qkv[rows, c * 128 : (c + 1) * 128] = piece[c * 128 : (c + 1) * 128, :].astype(F32)
        qkv[rows, AW:] = piece[QOP : QOP + 128, :].astype(F32).T
        g = piece[QOP + 128 :, :].astype(F32)
        for c in range(2):
            first = QP + c * (AW // 2)
            cols = pl.ds(pl.multiple_of(p * 256 + c * 128, 128), 128)
            out[:, cols] = piece[first : first + AW // 2, :].astype(F32)
            gains[:, cols] = g[2 * c : 2 * c + 2]


def sum_tail(idx, first, second, parts):
    got_a = lax.ppermute(first[1], "core", shift(2, 1))
    got_b = lax.ppermute(second[1], "core", shift(2, 1))
    part = sds((2, TAIL, 128))
    g = small_call(sum_core_body, (part,) * 4, idx, first[0], got_a, second[0], got_b, name="sum_core")
    got = [lax.ppermute(g[s], "y", shift(4, s)) for s in (2, 1, 3)]
    part = sds((TAIL, 128))
    own, other = small_call(sum_y_body, (part,) * 2, idx, g[0], *got, name="sum_y")
    p0, q1, q3 = relay([tie(p, own) for p in parts])
    cross = [(2 * a + b, 2 * (1 - a) + (1 - b)) for a in range(2) for b in range(2)]
    g = small_call(
        sum_z_body,
        part,
        idx,
        tie(own, q1, q3),
        lax.ppermute(own, "zl", shift(2, 1)),
        lax.ppermute(other, "zh", shift(2, 1)),
        lax.ppermute(other, ("zl", "zh"), cross),
        name="sum_z",
    )
    d_one = last_step(p0, q1, q3)
    mine = [tie(g, *d_one)] + [lax.ppermute(g, "y", shift(4, s)) for s in (1, 2, 3)]
    theirs = [lax.ppermute(v, "core", shift(2, 1)) for v in [g] + mine[1:]]
    shapes = (sds((DH, QW), F32), sds((AW // 2, D), F32), sds((2, D), F32))
    return g, own, d_one, small_call(unpack_tail_body, shapes, idx, *mine, *theirs, name="unpack_tail")


def inverse_rms(v):
    return lax.rsqrt(jnp.mean(v * v, axis=-1, keepdims=True) + EPSILON)


def total(terms):
    return sum((t[...].astype(F32) for t in terms[1:]), terms[0][...].astype(F32))


def norm_two_body(tok, a, b, c, gain, after, normed):
    v = total((tok, a, b, c))
    after[...] = v
    normed[...] = (v * inverse_rms(v) * gain[...]).astype(BF16)


def norm_back_body(add, v_ref, a, b, c, gain, out, low, gain_grad):
    v = v_ref[...].astype(F32)
    grad = total((a, b, c))
    r = inverse_rms(v)
    pulled = grad * gain[...]
    inner = jnp.mean(v * pulled, axis=-1, keepdims=True)
    res = add[...].astype(F32) + r * pulled - v * (r * r * r) * inner
    out[...] = res
    low[...] = res.astype(BF16)
    part = jnp.sum(grad * v * r, axis=0, keepdims=True)

    @pl.when(pl.program_id(0) == 0)
    def _():
        gain_grad[...] = part

    @pl.when(pl.program_id(0) > 0)
    def _():
        gain_grad[...] += part


def row_call(body, out_shape, *args, name):
    block = lambda v: (
        pl.BlockSpec((HALF, D), lambda i: (i, 0))
        if v.shape[0] == BLK
        else pl.BlockSpec((1, D), lambda i: (0, 0))
    )
    return pl.pallas_call(
        body,
        grid=(2,),
        out_shape=out_shape,
        in_specs=[block(v) for v in args],
        out_specs=tuple(block(v) for v in out_shape),
        compiler_params=params(),
        cost_estimate=cost(1e6, 5e6),
        name=name,
    )(*args)


def replica_layout(lengths, replica, replica_id):
    sizes = jnp.where(replica == replica_id, lengths, 0)
    starts = jnp.cumsum(sizes) - sizes
    row_ids = jnp.arange(CAP, dtype=jnp.int32)
    inside = (row_ids[:, None] >= starts[None, :]) & (row_ids[:, None] < (starts + sizes)[None, :])
    begin = jnp.sum(jnp.where(inside, starts[None, :], 0), axis=1)
    begin = begin + jnp.where(jnp.any(inside, axis=1), 0, jnp.sum(sizes))
    return begin, row_ids - begin


def on_device(
    tokens, cotangent, gain_one, qkv_weight, out_weight, gate_weight, up_weight, down_weight,
    gain_two, seq_lengths, seq_replica,
):
    x, zh, core = lax.axis_index("x"), lax.axis_index("zh"), lax.axis_index("core")
    y, zl = lax.axis_index("y"), lax.axis_index("zl")
    idx = jnp.stack([x, zh, y, core]).astype(jnp.int32)

    tok = tokens.astype(F32)
    s_one = inverse_rms(tok)
    begin, position = replica_layout(seq_lengths, seq_replica, (y * 2 + zl) * 2 + core)
    half_rows = lambda v: lax.dynamic_index_in_dim(v.reshape(4, 2, BLK), zh, 1, False).reshape(ROWS, 1)
    first = jnp.tile(half_rows(begin)[3 * BLK :, 0], 8).reshape(1, QALL)
    lane = jnp.arange(128, dtype=jnp.int32)
    frequency = ROTARY_BASE ** (-(lane % 32).astype(F32) * (2.0 / HD))
    angles = half_rows(position).astype(F32) * frequency[None, :]
    cosine = jnp.cos(angles)
    sine = jnp.where((lane % HD) < HD // 2, -1.0, 1.0)[None, :] * jnp.sin(angles)

    qkv_got = fetch_half(qkv_weight, core)
    normed_one = gather_x((tok * s_one * gain_one).astype(BF16), (cosine,))
    out_got = fetch_half(out_weight, core)
    swap = lambda v, *deps: lax.ppermute(tie(v, *deps), "core", shift(2, 1))
    qkv_all = qkv_weight, qkv_got, swap(qkv_got, out_got, normed_one[2], normed_one[3])

    q, kv_own = qkv_forward(idx, normed_one, qkv_all, cosine, sine)
    cot = tie(cotangent, normed_one[2], normed_one[3])
    cots = [cotangent] + [lax.ppermute(cot, "x", shift(4, -k)) for k in (1, 2, 3)]
    kv_par = lax.ppermute(kv_own, "zh", shift(2, 1))
    out_all = out_weight, out_got, swap(out_got, kv_own)
    rows = DH // 8
    mine = lambda w: lax.dynamic_slice_in_dim(w, (y * 2 + core) * rows, rows, 0)
    cross = [(2 * a + b, 2 * (1 - a) + (1 - b)) for a in range(2) for b in range(2)]
    gate_up = lax.ppermute(
        jnp.concatenate(
            [
                mine(tie(gate_weight, kv_own)),
                jnp.zeros((rows, GAP - FF4), BF16),
                mine(tie(up_weight, kv_own)),
            ],
            1,
        ),
        ("zl", "zh"),
        cross,
    )
    att, qx = attend(idx, q, kv_own, kv_par, first)
    parts = out_project(idx, tie(att, *cots), out_all)
    down_got = fetch_half(tie(down_weight, parts[2]), core)
    gate_up = lax.all_gather(tie(gate_up, parts[2]), ("y", "core"), axis=0, tiled=True)
    after_attn, normed_two = row_call(
        norm_two_body,
        (sds((BLK, D), F32), sds((BLK, D))),
        tokens, *scatter_x(parts), gain_two.reshape(1, D), name="norm_two",
    )
    normed_two = gather_x(tie(normed_two, down_got))
    down_all = down_weight, down_got, lax.ppermute(tie(down_got, normed_two[0]), "core", shift(2, 1))
    normed_two = [normed_two[k] for k in (0, 1, 4, 2, 3)]
    cots = [cots[k] for k in FFN_ORDER]
    weights = gate_weight, up_weight, gate_up, down_all
    early = ffn(idx, normed_two[:3], cots[:3], *weights)
    hid, dgate, dup = ffn(idx, normed_two[3:], cots[3:], *weights, early)
    d_parts = ffn_back(idx, dgate, dup, gate_weight, up_weight, gate_up)
    own_grads = down_grads(cots, tie(hid, d_parts[2]))
    d_own, q1, q3 = relay(d_parts)
    own_grads = gate_up_grads(normed_two, tie(dgate, q1, q3), dup, own_grads)
    d_two = last_step(d_own, q1, q3)
    grads = lax.psum_scatter(
        tie(own_grads, *d_two).reshape(32, PIECE, 128),
        ("zh", "zl", "y", "core"), scatter_dimension=0, tiled=True,
    )
    after_grad, branch, gain_grad_two = row_call(
        norm_back_body,
        (sds((BLK, D), F32), sds((BLK, D)), sds((1, D), F32)),
        cotangent, after_attn, *d_two, gain_two.reshape(1, D), name="norm_back_two",
    )
    branch = gather_x(branch)
    layer_parts = down_project(idx, tie(hid, after_grad), down_all)
    att = tie(att, *layer_parts)
    layer = [
        lax.ppermute(tie(layer_parts[k], branch[2], branch[3]), "x", shift(4, k)) for k in (1, 3)
    ]
    dqm, dkv_own, dkv_par = attend_back(
        idx, qx, kv_own, kv_par, first, att, cosine, sine, branch, out_all
    )
    dkv_got = lax.ppermute(dkv_par, "zh", shift(2, 1))
    tail = attn_grads(
        idx, normed_one, branch, dqm.reshape(ROWS, AW), tie(att, *layer).reshape(ROWS, AW)
    )
    dkv_got = tie(dkv_got, tail[0])
    *tail_kv, parts = qkv_back(
        idx, dqm.reshape(ROWS, AW), dkv_own, dkv_got, cosine, sine, qkv_all, normed_one, gain_one,
        gain_grad_two,
    )
    over_x = lambda v: sum((lax.ppermute(v, "x", shift(4, s)) for s in (1, 2, 3)), v)
    z_summed, summed, d_one, (grad_qkv, grad_out, gains) = sum_tail(
        idx, (tail[0], tie(tail[1], dkv_got)), tail_kv, parts
    )
    layer.append(lax.ppermute(tie(layer_parts[2], summed), "x", shift(4, 2)))
    grads = lax.all_gather(tie(grads, z_summed), ("zl", "y", "core"), axis=0, tiled=True)
    grad_gate, grad_up, grad_down = unpack(grads)
    _, input_grad, _ = row_call(
        norm_back_body,
        (sds((BLK, D), F32), sds((BLK, D)), sds((1, D), F32)),
        after_grad, tokens, *d_one, gain_one.reshape(1, D), name="norm_back_one",
    )
    layer_out = sum((v.astype(F32) for v in layer), after_attn + layer_parts[0].astype(F32))
    layer_out = layer_out.astype(BF16)
    gains = over_x(gains)
    return (
        layer_out, input_grad, gains[0], grad_qkv, grad_out, grad_gate, grad_up,
        grad_down, gains[1],
    )


def solution(mesh):
    grid = Mesh(mesh.devices.reshape(SIZES), AXES)
    rows = P(AXES, None)
    both = P(("x", "zh"), None)
    return jax.shard_map(
        on_device,
        mesh=grid,
        in_specs=(
            rows, rows, P(), P("zh", "x"), both, P("zh", "x"), P("zh", "x"), both, P(), P(), P(),
        ),
        out_specs=(
            rows, rows, P(), P("zh", "x"), both, P("zh", "x"), P("zh", "x"), both, P(),
        ),
        check_vma=False,
    )
```

```python
import jax
import jax.numpy as jnp
from jax import lax
from jax.experimental import pallas as pl
from jax.experimental.pallas import tpu as pltpu
from jax.sharding import Mesh
from jax.sharding import PartitionSpec as P

HEADS = 32
KV = 4
HD = 64
EPSILON = 1e-05
ROTARY_BASE = 10000.0
MASKED = -1e30

AXES = ("y", "zl", "core", "x", "zh")
SIZES = (4, 2, 2, 4, 2)
BLK = 160
HALF = BLK // 2
ROWS = 4 * BLK
CAP = 2 * ROWS
D = 2048
DH = D // 2
QW = 640
AW = 512
FF4 = 1408
TILE = 256
F32 = jnp.float32
BF16 = jnp.bfloat16
VLIM = 60 * 1024 * 1024


def spec(memory=pltpu.VMEM):
    return pl.BlockSpec(memory_space=memory)


def params(**kw):
    return pltpu.CompilerParams(vmem_limit_bytes=VLIM, **kw)


def cost(flops, nbytes):
    return pl.CostEstimate(flops=int(flops), bytes_accessed=int(nbytes), transcendentals=0)


def sds(shape, dtype=BF16):
    return jax.ShapeDtypeStruct(shape, dtype)


def dot(a, b):
    return jnp.dot(a, b, preferred_element_type=F32)


def dot_t(a, b):
    return lax.dot_general(a, b, (((1,), (1,)), ((), ())), preferred_element_type=F32)


def t_dot(a, b):
    return lax.dot_general(a, b, (((0,), (0,)), ((), ())), preferred_element_type=F32)


def tie(v, *deps):
    return lax.optimization_barrier((v,) + deps)[0]


def shift(n, s):
    return [(i, (i + s) % n) for i in range(n)]


def gather_x(v, wait=()):
    from_prev = lax.ppermute(v, "x", shift(4, 1))
    from_next = lax.ppermute(v, "x", shift(4, -1))
    send_a = tie(from_prev[:HALF], from_next, *wait)
    send_b = tie(from_next[HALF:], from_prev, *wait)
    opp_a = lax.ppermute(send_a, "x", shift(4, 1))
    opp_b = lax.ppermute(send_b, "x", shift(4, -1))
    return v, from_next, opp_a, opp_b, from_prev


def relay_body(p1, got_a, p3, got_b, q1, q3):
    q1[...] = (p1[...].astype(F32) + got_a[...].astype(F32)).astype(BF16)
    q3[...] = (p3[...].astype(F32) + got_b[...].astype(F32)).astype(BF16)


def relay(parts):
    p0, p1, p2a, p2b, p3 = parts
    got_a = lax.ppermute(p2a, "x", shift(4, 1))
    got_b = lax.ppermute(p2b, "x", shift(4, -1))
    half = lambda k: pl.BlockSpec((HALF, D), lambda i: (k, 0))
    q1, q3 = pl.pallas_call(
        relay_body,
        grid=(1,),
        out_shape=(sds((BLK, D)),) * 2,
        in_specs=[half(0), half(0), half(1), half(0)],
        out_specs=(half(0), half(1)),
        input_output_aliases={0: 0, 2: 1},
        compiler_params=params(),
        cost_estimate=cost(1e6, 2e6),
        name="relay",
    )(p1, got_a, p3, got_b)
    return p0, q1, q3


def scatter_x(parts):
    return last_step(*relay(parts))


def last_step(p0, q1, q3):
    return p0, lax.ppermute(q1, "x", shift(4, 1)), lax.ppermute(q3, "x", shift(4, -1))


PIECES = ((0, BLK), (1, BLK), (2, HALF), (2, HALF), (3, BLK))
PIECE_ROW = (0, BLK, 2 * BLK, 2 * BLK + HALF, 3 * BLK)


def part_shapes(width, dtype=BF16):
    return tuple(sds((n, width), dtype) for _, n in PIECES)


def low_lanes(shape):
    return lax.broadcasted_iota(jnp.int32, shape, 1) < HD


def swap_halves(v):
    lane = lax.broadcasted_iota(jnp.int32, v.shape, 1) % HD
    return jnp.where(lane < HD // 2, pltpu.roll(v, 128 - HD // 2, 1), pltpu.roll(v, HD // 2, 1))


def rows_at(block):
    return pl.ds(pl.multiple_of(block * BLK, 32), BLK)


def fetch_half(w, core):
    half = w.shape[0] // 2
    return lax.ppermute(lax.dynamic_slice_in_dim(w, core * half, half, 0), "zh", shift(2, 1))


def own_and_partner(idx, rows):
    zh = idx[1]
    at = lambda k: pl.ds(pl.multiple_of(k * rows, rows), rows)
    return at(zh), at(1 - zh)


def weight_rows(idx, rows):
    zh, core = idx[1], idx[3]
    far = (1 - zh) * rows
    half = rows // 2
    at = lambda first, n: pl.ds(pl.multiple_of(first, half), n)
    return at(zh * rows, rows), at(far + core * half, half), at(far + (1 - core) * half, half)


def qkv_body(idx, n0, n1, n2a, n2b, n3, w0, w1, w2, cosine, sine, q_ref, kv_ref, rows):
    x = idx[0]
    lo = low_lanes((BLK, 128))
    for ref, row, (_, n) in zip((n0, n1, n2a, n2b, n3), PIECE_ROW, PIECES):
        rows[row : row + n, :] = ref[...]
    s0, s1, s2 = weight_rows(idx, DH)
    acc = dot(rows[:, s0], w0[...]) + dot(rows[:, s1], w1[...]) + dot(rows[:, s2], w2[...])
    for d in range(4):
        at = rows_at((x + d) & 3)
        cs = cosine[at, :]
        sn = sine[at, :]
        for p in range(5):
            v = acc[d * BLK : (d + 1) * BLK, p * 128 : (p + 1) * 128]
            r = v * cs + swap_halves(v) * sn
            if p < 4:
                r = r * (HD**-0.5 * LOG2E)
                a = (x + d) & 3
                for k, w in enumerate((r, pltpu.roll(r, HD, 1))):
                    head = slice((2 * p + k) * BLK, (2 * p + k + 1) * BLK)
                    q_ref[a, head, :] = jnp.where(lo, w, 0.0).astype(BF16)
            else:
                kv_ref[at, :] = jnp.where(lo, r, v).astype(BF16)


def qkv_forward(idx, pieces, weight, cosine, sine):
    return pl.pallas_call(
        qkv_body,
        out_shape=(sds((4, QALL, 128)), sds((ROWS, 128))),
        in_specs=[spec(pltpu.SMEM)] + [spec()] * 10,
        out_specs=(spec(), spec()),
        scratch_shapes=[pltpu.VMEM((ROWS, D), BF16)],
        compiler_params=params(),
        cost_estimate=cost(2 * ROWS * D * QW, 7e6),
        name="qkv_forward",
    )(idx, *pieces, *weight, cosine, sine)


QALL = 8 * BLK
PAIR = 2 * BLK
LOG2E = 1.4426950408889634
LN2 = 0.6931471805599453


def split3(v):
    a = v.astype(BF16).astype(F32)
    b = (v - a).astype(BF16).astype(F32)
    return a, b, v - a - b


def with_lanes(v, parts):
    lane = lax.broadcasted_iota(jnp.int32, v.shape, 1)
    out = jnp.where(lane < HD, v, 0.0)
    for k, part in enumerate(parts):
        out = jnp.where(lane == HD + k, part, out)
    return out


def spread_keys(zh, kv_own, kv_par, kk, vv, fill):
    shape = (BLK, 128)
    lo = low_lanes(shape)
    rest = fill(lax.broadcasted_iota(jnp.int32, shape, 1) - HD)
    for j in range(4):
        for src, off in ((kv_own, zh), (kv_par, 1 - zh)):
            v = src[j * BLK : (j + 1) * BLK, :].astype(F32)
            at = rows_at(2 * j + off)
            kk[at, :] = jnp.where(lo, v, rest).astype(BF16)
            vv[at, :] = jnp.where(lo, pltpu.roll(v, HD, 1), rest).astype(BF16)


def masked(s, zh, j, kb, first):
    if j < 3 and kb < j:
        return s
    u = kb * PAIR + lax.broadcasted_iota(jnp.int32, (PAIR, QALL), 0)
    allowed = None
    if kb == j:
        t = (2 * j + zh) * BLK + lax.broadcasted_iota(jnp.int32, (1, QALL), 1) % BLK
        allowed = u <= t
    if j == 3:
        later = u >= first[...]
        allowed = later if allowed is None else allowed & later
    return jnp.where(allowed, s, MASKED)


def attend_body(idx, q, kv_own, kv_par, first, att, qx, kk, vv, vt, s_ref, e_ref):
    x, zh = idx[0], idx[1]
    spread_keys(zh, kv_own, kv_par, kk, vv, lambda lane: 1.0)
    vt[...] = vv[...].T
    lo = low_lanes((BLK, 128))
    for j in range(4):
        n = PAIR * (j + 1)
        qj = q[j]
        top = jnp.full((1, QALL), MASKED, F32)
        for kb in range(j + 1):
            rows = slice(kb * PAIR, (kb + 1) * PAIR)
            s = masked(dot_t(kk[rows, :], qj), zh, j, kb, first)
            s_ref[rows, :] = s
            top = jnp.maximum(top, jnp.max(s, axis=0, keepdims=True))
        for k in range(n // 64):
            rows = slice(k * 64, (k + 1) * 64)
            e_ref[rows, :] = jnp.exp2(s_ref[rows, :] - top).astype(BF16)
        o = dot(vt[:, :n], e_ref[:n, :])
        lse = split3(top + jnp.log(o[HD : HD + 1, :]) * LOG2E)
        row = lax.broadcasted_iota(jnp.int32, (128, QALL), 0)
        extra = jnp.zeros((128, QALL), F32)
        for k, part in enumerate(lse):
            extra = jnp.where(row == HD + k, part, extra)
        qx[j] = (qj.astype(F32) + extra.T).astype(BF16)
        o = o.T
        r = pltpu.roll(o, HD, 1)
        rel = (j - x) & 3
        for p in range(4):
            even, odd = slice(2 * p * BLK, (2 * p + 1) * BLK), slice((2 * p + 1) * BLK, (2 * p + 2) * BLK)
            num = jnp.where(lo, o[even], r[odd])
            den = jnp.where(lo, r[even], o[odd])
            att[rel, :, p * 128 : (p + 1) * 128] = (num / den).astype(BF16)


def attend(idx, q, kv_own, kv_par, first):
    return pl.pallas_call(
        attend_body,
        out_shape=(sds((4, BLK, AW)), sds((4, QALL, 128))),
        in_specs=[spec(pltpu.SMEM)] + [spec()] * 4,
        out_specs=(spec(), spec()),
        scratch_shapes=[
            pltpu.VMEM((CAP, 128), BF16),
            pltpu.VMEM((CAP, 128), BF16),
            pltpu.VMEM((128, CAP), BF16),
            pltpu.VMEM((CAP, QALL), F32),
            pltpu.VMEM((CAP, QALL), BF16),
        ],
        compiler_params=params(),
        cost_estimate=cost(1.2e10, 3e6),
        name="attend",
    )(idx, q, kv_own, kv_par, first)


def store_parts(res, refs):
    for ref, row, (_, n) in zip(refs, PIECE_ROW, PIECES):
        ref[...] = res[row : row + n].astype(BF16)


def out_body(idx, att, w0, w1, o0, o1, o2a, o2b, o3):
    slots = own_and_partner(idx, AW // 2)
    for d, ref in ((2, None), (1, o1), (3, o3), (0, o0)):
        a = att.at[d]
        res = sum(dot(a[:, s], w[...]) for s, w in zip(slots, (w0, w1))).astype(BF16)
        if d == 2:
            o2a[...] = res[:HALF]
            o2b[...] = res[HALF:]
        else:
            ref[...] = res


def out_project(idx, att, weight):
    return pl.pallas_call(
        out_body,
        out_shape=part_shapes(D),
        in_specs=[spec(pltpu.SMEM)] + [spec()] * 3,
        out_specs=(spec(),) * 5,
        compiler_params=params(),
        cost_estimate=cost(2 * ROWS * D * AW, 5.5e6),
        name="out_project",
    )(idx, att, *weight)


def stack_heads(v):
    return v, pltpu.roll(v, HD, 1)


def attend_back_body(
    idx, qx, kv_own, kv_par, first, att, cosine, sine, b0, b1, b2a, b2b, b3, w0, w1,
    dq_ref, dkv_own, dkv_par, kk, vv, dout, do_all, dkk, dvv, e_ref, ds_ref, dq_acc,
):
    x, zh = idx[0], idx[1]
    spread_keys(zh, kv_own, kv_par, kk, vv, lambda lane: jnp.where(lane < 3, -1.0, 0.0))
    slots = own_and_partner(idx, AW // 2)
    for d in range(4):
        if d == 2:
            rows = jnp.concatenate([b2a[...], b2b[...]], 0)
        else:
            rows = (b0, b1, None, b3)[d][...]
        at = rows_at((x + d) & 3)
        for s, w in zip(slots, (w0, w1)):
            dout[at, s] = dot_t(rows, w[...]).astype(BF16)
    lo = low_lanes((BLK, 128))
    for j in range(4):
        rel = (j - x) & 3
        here = slice(j * BLK, (j + 1) * BLK)
        for p in range(4):
            cols = slice(p * 128, (p + 1) * 128)
            do = dout[here, cols].astype(F32)
            prod = do * att[rel, :, cols].astype(F32)
            for k, (v, w) in enumerate(zip(stack_heads(do), stack_heads(prod))):
                delta = jnp.sum(jnp.where(lo, w, 0.0), axis=1, keepdims=True)
                head = slice((2 * p + k) * BLK, (2 * p + k + 1) * BLK)
                do_all[head, :] = with_lanes(v, split3(delta)).astype(BF16)
        for kb in range(j + 1):
            rows = slice(kb * PAIR, (kb + 1) * PAIR)
            e = jnp.exp2(masked(dot_t(kk[rows, :], qx[j]), zh, j, kb, first))
            e_ref[...] = e.astype(BF16)
            ds_ref[...] = (e * dot_t(vv[rows, :], do_all[...])).astype(BF16)
            dv = dot(e_ref[...], do_all[...])
            dk = dot(ds_ref[...], qx[j])
            dq = t_dot(ds_ref[...], kk[rows, :])
            if kb == j:
                dvv[rows, :], dkk[rows, :] = dv, dk
            else:
                dvv[rows, :] += dv
                dkk[rows, :] += dk
            if kb == 0:
                dq_acc[...] = dq
            else:
                dq_acc[...] += dq
        for p in range(4):
            even, odd = slice(2 * p * BLK, (2 * p + 1) * BLK), slice((2 * p + 1) * BLK, (2 * p + 2) * BLK)
            v = jnp.where(lo, dq_acc[even, :], pltpu.roll(dq_acc[odd, :], HD, 1)) * HD**-0.5
            v = v * cosine[here, :] - swap_halves(v) * sine[here, :]
            dq_ref[rel, :, p * 128 : (p + 1) * 128] = v.astype(BF16)
    for j in range(4):
        for dst, off in ((dkv_own, zh), (dkv_par, 1 - zh)):
            at = rows_at(2 * j + off)
            both = jnp.where(lo, dkk[at, :] * LN2, pltpu.roll(dvv[at, :], HD, 1))
            dst[j * BLK : (j + 1) * BLK, :] = both.astype(dst.dtype)


def attend_back(idx, qx, kv_own, kv_par, first, att, cosine, sine, branch, weight):
    return pl.pallas_call(
        attend_back_body,
        out_shape=(sds((4, BLK, AW)), sds((ROWS, 128), F32), sds((ROWS, 128))),
        in_specs=[spec(pltpu.SMEM)] + [spec()] * 14,
        out_specs=(spec(),) * 3,
        scratch_shapes=[
            pltpu.VMEM((CAP, 128), BF16),
            pltpu.VMEM((CAP, 128), BF16),
            pltpu.VMEM((ROWS, AW), BF16),
            pltpu.VMEM((QALL, 128), BF16),
            pltpu.VMEM((CAP, 128), F32),
            pltpu.VMEM((CAP, 128), F32),
            pltpu.VMEM((PAIR, QALL), BF16),
            pltpu.VMEM((PAIR, QALL), BF16),
            pltpu.VMEM((QALL, 128), F32),
        ],
        compiler_params=params(),
        cost_estimate=cost(3e10, 8e6),
        name="attend_back",
    )(idx, qx, kv_own, kv_par, first, att, cosine, sine, *branch, *weight)


def qkv_back_body(
    idx, dqm, dkv_own, dkv_got, cosine, sine, w0, w1, w2, n0, n1, n2a, n2b, n3, gain_one,
    gain_grad_two,
    mine, theirs, o0, o1, o2a, o2b, o3, n_all, dkv, grad, gains,
):
    x, y, core = idx[0], idx[2], idx[3]
    lo = low_lanes((BLK, 128))
    for ref, row, (_, n) in zip((n0, n1, n2a, n2b, n3), PIECE_ROW, PIECES):
        n_all[row : row + n, :] = ref[...]
    for d in range(4):
        at = rows_at((x + d) & 3)
        v = dkv_own[at, :] + dkv_got[at, :].astype(F32)
        v = jnp.where(lo, v * cosine[at, :] - swap_halves(v) * sine[at, :], v).astype(BF16)
        dkv[d * BLK : (d + 1) * BLK, :] = v
    rows = jnp.concatenate([dqm[...], dkv[...]], 1)
    for s, w in zip(weight_rows(idx, DH), (w0, w1, w2)):
        for c in range(w.shape[0] // 512):
            cols = pl.ds(pl.multiple_of(s.start + c * 512, 512), 512)
            res = dot_t(rows, w[c * 512 : (c + 1) * 512, :])
            part = (res * n_all[:, cols].astype(F32)).reshape(ROWS // 8, 8, 512)
            gains[0:1, cols] = jnp.sum(jnp.sum(part, axis=0), axis=0, keepdims=True) / gain_one[:, cols]
            store_parts(res, [r.at[:, cols] for r in (o0, o1, o2a, o2b, o3)])
    grad[...] = dot(dkv[...].T, n_all[...]).astype(BF16)
    gains[1:2, :] = gain_grad_two[...]
    for s in range(4):
        for k, ref in enumerate((mine, theirs)):
            p = ((y + s) & 3) * 2 + (core if k == 0 else 1 - core)
            both = gains[:, pl.ds(pl.multiple_of(p * 256, 256), 256)]
            both = jnp.concatenate([both[:, :128], both[:, 128:], jnp.zeros((12, 128), F32)], 0)
            for h in range(2):
                ref[s, h, :128, :] = grad[:, pl.ds(pl.multiple_of(h * DH + p * 128, 128), 128)]
                ref[s, h, 128:, :] = both.astype(BF16)


def qkv_back(idx, dqm, dkv_own, dkv_got, cosine, sine, weight, pieces, gain_one, gain_grad_two):
    res = pl.pallas_call(
        qkv_back_body,
        out_shape=(sds((4, 2, KVP, 128)),) * 2 + part_shapes(D),
        in_specs=[spec(pltpu.SMEM)] + [spec()] * 15,
        out_specs=(spec(),) * 7,
        scratch_shapes=[
            pltpu.VMEM((ROWS, D), BF16),
            pltpu.VMEM((ROWS, 128), BF16),
            pltpu.VMEM((128, D), BF16),
            pltpu.VMEM((2, D), F32),
        ],
        compiler_params=params(),
        cost_estimate=cost(2 * ROWS * D * QW, 1.3e7),
        name="qkv_back",
    )(
        idx, dqm, dkv_own, dkv_got, cosine, sine, *weight, *pieces,
        gain_one.reshape(1, D), gain_grad_two.reshape(1, D),
    )
    return res[0], res[1], res[2:]


TILES = 6
GAP = TILES * TILE


def load_down(idx, refs, dst, sem):
    copies = []
    for k, (s, ref) in enumerate(zip(weight_rows(idx, FF4 // 2), refs)):
        copies.append(pltpu.make_async_copy(ref, dst.at[s], sem.at[k]))
    return copies


def ffn_body(
    idx, n0, n1, n2a, n2b, n3, c0, c1, c2, c3, gate_own, up_own, gate_par, up_par, w0, w1, w2,
    hid, dgate, dup, n_all, c_all, down, sem,
):
    i = pl.program_id(0)
    zh = idx[1]

    @pl.when(i == 0)
    def _():
        copies = load_down(idx, (w0, w1, w2), down, sem)
        for c in copies:
            c.start()
        for ref, row, (_, n) in zip((n0, n1, n2a, n2b, n3), PIECE_ROW, PIECES):
            n_all[row : row + n, :] = ref[...]
        for d, ref in enumerate((c0, c1, c2, c3)):
            c_all[d * BLK : (d + 1) * BLK, :] = ref[...]
        for c in copies:
            c.wait()

    own = n_all[:, pl.ds(pl.multiple_of(zh * DH, DH), DH)]
    par = n_all[:, pl.ds(pl.multiple_of((1 - zh) * DH, DH), DH)]
    gate = dot(own, gate_own[...]) + dot(par, gate_par[...])
    up = dot(own, up_own[...]) + dot(par, up_par[...])
    dh = dot_t(c_all[...], down[pl.ds(pl.multiple_of(i * TILE, TILE), TILE), :])
    sig = 1.0 / (1.0 + jnp.exp(-gate))
    act = gate * sig
    hid[...] = (act * up).astype(BF16)
    dgate[...] = (dh * up * sig * (1.0 + gate * (1.0 - sig))).astype(BF16)
    dup[...] = (dh * act).astype(BF16)


def whole(n, w):
    return pl.BlockSpec((n, w), lambda i: (0, 0))


def ffn(idx, normed, cots, gate, up, gate_up, down):
    column = lambda first: pl.BlockSpec((DH, TILE), lambda i: (0, i + first))
    hidden = pl.BlockSpec((ROWS, TILE), lambda i: (0, i))
    return pl.pallas_call(
        ffn_body,
        grid=(TILES,),
        out_shape=(sds((ROWS, FF4)),) * 3,
        in_specs=[spec(pltpu.SMEM)]
        + [whole(n, D) for _, n in PIECES]
        + [whole(BLK, D)] * 4
        + [column(0), column(0), column(0), column(TILES)]
        + [spec(pl.ANY)] * 3,
        out_specs=[hidden] * 3,
        scratch_shapes=[
            pltpu.VMEM((ROWS, D), BF16),
            pltpu.VMEM((ROWS, D), BF16),
            pltpu.VMEM((GAP, D), BF16),
            pltpu.SemaphoreType.DMA((3,)),
        ],
        compiler_params=params(),
        cost_estimate=cost(6 * ROWS * D * FF4, 3.4e7),
        name="ffn",
    )(idx, *normed, *cots, gate, up, gate_up, gate_up, *down)


def down_body(idx, hid, w0, w1, w2, o0, o1, o2, o3, down, sem):
    copies = load_down(idx, (w0, w1, w2), down, sem)
    for c in copies:
        c.start()
    for c in copies:
        c.wait()
    for n in range(D // 512):
        cols = slice(n * 512, (n + 1) * 512)
        res = dot(hid[...], down[:, cols]).astype(BF16)
        for d, ref in enumerate((o0, o1, o2, o3)):
            ref[:, cols] = res[d * BLK : (d + 1) * BLK]


def down_project(idx, hid, down):
    return pl.pallas_call(
        down_body,
        out_shape=(sds((BLK, D)),) * 4,
        in_specs=[spec(pltpu.SMEM), spec()] + [spec(pl.ANY)] * 3,
        out_specs=(spec(),) * 4,
        scratch_shapes=[pltpu.VMEM((FF4, D), BF16), pltpu.SemaphoreType.DMA((3,))],
        compiler_params=params(),
        cost_estimate=cost(2 * ROWS * D * FF4, 1.1e7),
        name="down_project",
    )(idx, hid, *down)


def ffn_back_body(idx, dgate, dup, gate_own, up_own, par, *refs):
    half = pl.num_programs(0) // 2

    @pl.when(pl.program_id(0) < half)
    def _():
        store_parts(dot_t(dgate[...], gate_own[...]) + dot_t(dup[...], up_own[...]), refs)

    @pl.when(pl.program_id(0) >= half)
    def _():
        store_parts(dot_t(dgate[...], par[:, :FF4]) + dot_t(dup[...], par[:, GAP:]), refs)


def ffn_back(idx, dgate, dup, gate, up, gate_up):
    half = DH // TILE
    rows = pl.BlockSpec((ROWS, FF4), lambda i, idx: (0, 0))
    own = pl.BlockSpec((TILE, FF4), lambda i, idx: (jnp.minimum(i, half - 1), 0))
    par = pl.BlockSpec((TILE, GAP + FF4), lambda i, idx: (jnp.maximum(i - half, 0), 0))
    place = lambda i, idx: (0, i ^ (idx[1] * half))
    return pl.pallas_call(
        ffn_back_body,
        grid_spec=pltpu.PrefetchScalarGridSpec(
            num_scalar_prefetch=1,
            grid=(D // TILE,),
            in_specs=[rows, rows, own, own, par],
            out_specs=[pl.BlockSpec((n, TILE), place) for _, n in PIECES],
        ),
        out_shape=part_shapes(D),
        compiler_params=params(),
        cost_estimate=cost(4 * ROWS * D * FF4, 1.8e7),
        name="ffn_back",
    )(idx, dgate, dup, gate, up, gate_up)


GU_ROWS = FF4 // 128 * 64
PIECE = 2 * GU_ROWS + FF4 // 2
QS = 4


def gate_up_grads_body(*refs):
    na, nb = refs[0:5], refs[5:10]
    dgate, dup, _, out = refs[10:]
    stack = lambda parts: jnp.concatenate([r[...] for r in parts], 0)
    rows = jnp.concatenate([stack(na), stack(nb)], 1).T
    for k, ref in enumerate((dgate, dup)):
        g = dot(rows, ref[...]).astype(BF16)
        for h in range(2):
            for q in range(QS):
                r = g[(QS * h + q) * 64 : (QS * h + q + 1) * 64]
                for c in range(FF4 // 128):
                    first = k * GU_ROWS + c * 64
                    out[h, q, first : first + 64, :] = r[:, c * 128 : (c + 1) * 128]


def gate_up_grads(normed, dgate, dup, pieces):
    return pl.pallas_call(
        gate_up_grads_body,
        grid=(16 // QS,),
        out_shape=sds((2, 16, PIECE, 128)),
        in_specs=[pl.BlockSpec((n, 64 * QS), lambda i: (0, i)) for _, n in PIECES]
        + [pl.BlockSpec((n, 64 * QS), lambda i: (0, i + 16 // QS)) for _, n in PIECES]
        + [whole(ROWS, FF4)] * 2
        + [spec(pl.ANY)],
        out_specs=pl.BlockSpec((2, QS, 2 * GU_ROWS, 128), lambda i: (0, i, 0, 0)),
        input_output_aliases={12: 0},
        compiler_params=params(),
        cost_estimate=cost(4 * ROWS * D * FF4, 2e7),
        name="gate_up_grads",
    )(*normed, *normed, dgate, dup, pieces)


def down_grads_body(*refs):
    cots = refs[0:4]
    hid, out, hid_t = refs[4:]

    @pl.when(pl.program_id(0) == 0)
    def _():
        hid_t[...] = hid[...].T

    g = dot(hid_t[...], jnp.concatenate([r[...] for r in cots], 0)).astype(BF16)
    for h in range(2):
        for q in range(QS):
            out[h, q, :, :] = g[h * (FF4 // 2) : (h + 1) * (FF4 // 2), q * 128 : (q + 1) * 128]


def down_grads(cots, hid):
    return pl.pallas_call(
        down_grads_body,
        grid=(16 // QS,),
        out_shape=sds((2, 16, PIECE, 128)),
        in_specs=[pl.BlockSpec((BLK, 128 * QS), lambda i: (0, i))] * 4 + [whole(ROWS, FF4)],
        out_specs=pl.BlockSpec((2, QS, FF4 // 2, 128), lambda i: (0, i, 2, 0)),
        scratch_shapes=[pltpu.VMEM((FF4, ROWS), BF16)],
        compiler_params=params(),
        cost_estimate=cost(2 * ROWS * D * FF4, 1e7),
        name="down_grads",
    )(*cots, hid)


def unpack_body(piece, gate, up, down):
    for q in range(QS):
        rows = slice(q * 64, (q + 1) * 64)
        for k, ref in enumerate((gate, up)):
            for c in range(FF4 // 128):
                first = k * GU_ROWS + c * 64
                ref[rows, c * 128 : (c + 1) * 128] = piece[q, first : first + 64, :].astype(F32)
        down[:, q * 128 : (q + 1) * 128] = piece[q, 2 * GU_ROWS :, :].astype(F32)


def unpack(pieces):
    return pl.pallas_call(
        unpack_body,
        grid=(16 // QS,),
        out_shape=(sds((DH, FF4), F32), sds((DH, FF4), F32), sds((FF4 // 2, D), F32)),
        in_specs=[pl.BlockSpec((QS, PIECE, 128), lambda i: (i, 0, 0))],
        out_specs=[
            pl.BlockSpec((64 * QS, FF4), lambda i: (i, 0)),
            pl.BlockSpec((64 * QS, FF4), lambda i: (i, 0)),
            pl.BlockSpec((FF4 // 2, 128 * QS), lambda i: (0, i)),
        ],
        compiler_params=params(),
        cost_estimate=cost(1e6, 2.6e7),
        name="unpack",
    )(pieces)


QP = 4 * 128
OP = 2 * (AW // 2)
QOP = QP + OP
KVP = 128 + 16
TAIL = QOP + KVP


def attn_grads_body(idx, *refs):
    na, nb, branch = refs[0:5], refs[5:10], refs[10:15]
    dqm, att, mine, theirs, att_t = refs[15:]
    core = idx[3]

    @pl.when(pl.program_id(0) == 0)
    def _():
        att_t[...] = att[...].T

    stack = lambda parts: jnp.concatenate([r[...] for r in parts], 0)

    def store(h, first, n, zero, one):
        mine[0, h, first : first + n, :] = jnp.where(core == 0, zero, one)
        theirs[0, h, first : first + n, :] = jnp.where(core == 0, one, zero)

    for h, cols in enumerate((na, nb)):
        g = dot(stack(cols).T, dqm[...]).astype(BF16)
        for c in range(4):
            lanes = slice(c * 128, (c + 1) * 128)
            store(h, c * 128, 128, g[:128, lanes], g[128:, lanes])
    g = dot(att_t[...], stack(branch)).astype(BF16)
    for h in range(2):
        r = g[h * (AW // 2) : (h + 1) * (AW // 2)]
        for c in range(2):
            lanes = lambda k: slice(k * 256 + c * 128, k * 256 + (c + 1) * 128)
            store(h, QP + c * (AW // 2), AW // 2, r[:, lanes(0)], r[:, lanes(1)])


def attn_grads(idx, normed, branch, dqm, att):
    turn = lambda s, idx: (s + idx[2]) & 3
    piece = pl.BlockSpec((1, 2, QOP, 128), lambda s, idx: (s, 0, 0, 0))
    fixed = pl.BlockSpec((ROWS, AW), lambda s, idx: (0, 0))
    return pl.pallas_call(
        attn_grads_body,
        grid_spec=pltpu.PrefetchScalarGridSpec(
            num_scalar_prefetch=1,
            grid=(4,),
            in_specs=[pl.BlockSpec((n, 256), lambda s, idx: (0, turn(s, idx))) for _, n in PIECES]
            + [pl.BlockSpec((n, 256), lambda s, idx: (0, turn(s, idx) + 4)) for _, n in PIECES]
            + [pl.BlockSpec((n, 512), lambda s, idx: (0, turn(s, idx))) for _, n in PIECES]
            + [fixed, fixed],
            out_specs=[piece, piece],
            scratch_shapes=[pltpu.VMEM((AW, ROWS), BF16)],
        ),
        out_shape=(sds((4, 2, QOP, 128)),) * 2,
        compiler_params=params(),
        cost_estimate=cost(4 * ROWS * D * AW, 1e7),
        name="attn_grads",
    )(idx, *normed, *normed, *branch, dqm, att)


def small_call(body, out_shape, *args, name):
    return pl.pallas_call(
        body,
        out_shape=out_shape,
        in_specs=[spec(pltpu.SMEM)] + [spec()] * (len(args) - 1),
        out_specs=jax.tree.map(lambda _: spec(), out_shape),
        compiler_params=params(),
        cost_estimate=cost(1e6, 4e6),
        name=name,
    )(*args)


def add(*values):
    return sum((v.astype(F32) for v in values[1:]), values[0].astype(F32)).astype(BF16)


def sum_core_body(idx, a, b, c, d, *outs):
    for s, out in enumerate(outs):
        out[:, :QOP, :] = add(a[s], b[s])
        out[:, QOP:, :] = add(c[s], d[s])


def sum_y_body(idx, a, b, c, d, own, other):
    zh = idx[1]
    own[...] = add(a[zh], b[zh], c[zh], d[zh])
    far = 1 - zh
    other[...] = add(a[far], b[far], c[far], d[far])


def sum_z_body(idx, a, b, c, d, out):
    out[...] = add(a[...], b[...], c[...], d[...])


def unpack_tail_body(idx, *refs):
    y, core = idx[2], idx[3]
    qkv, out, gains = refs[8:]
    for k in range(8):
        piece = refs[k]
        p = ((y - k % 4) & 3) * 2 + (core if k < 4 else 1 - core)
        rows = pl.ds(pl.multiple_of(p * 128, 128), 128)
        for c in range(4):
            qkv[rows, c * 128 : (c + 1) * 128] = piece[c * 128 : (c + 1) * 128, :].astype(F32)
        qkv[rows, AW:] = piece[QOP : QOP + 128, :].astype(F32).T
        g = piece[QOP + 128 :, :].astype(F32)
        for c in range(2):
            first = QP + c * (AW // 2)
            cols = pl.ds(pl.multiple_of(p * 256 + c * 128, 128), 128)
            out[:, cols] = piece[first : first + AW // 2, :].astype(F32)
            gains[:, cols] = g[2 * c : 2 * c + 2]


def sum_tail(idx, first, second, parts, finish):
    got_a = lax.ppermute(first[1], "core", shift(2, 1))
    got_b = lax.ppermute(second[1], "core", shift(2, 1))
    part = sds((2, TAIL, 128))
    g = small_call(sum_core_body, (part,) * 4, idx, first[0], got_a, second[0], got_b, name="sum_core")
    got = [lax.ppermute(g[s], "y", shift(4, s)) for s in (2, 1, 3)]
    part = sds((TAIL, 128))
    own, other = small_call(sum_y_body, (part,) * 2, idx, g[0], *got, name="sum_y")
    p0, q1, q3 = relay([tie(p, own) for p in parts])
    cross = [(2 * a + b, 2 * (1 - a) + (1 - b)) for a in range(2) for b in range(2)]
    g = small_call(
        sum_z_body,
        part,
        idx,
        tie(own, q1, q3),
        lax.ppermute(own, "zl", shift(2, 1)),
        lax.ppermute(other, "zh", shift(2, 1)),
        lax.ppermute(other, ("zl", "zh"), cross),
        name="sum_z",
    )
    d_one = last_step(p0, q1, q3)
    input_grad = finish(d_one)
    mine = [tie(g, input_grad)] + [lax.ppermute(g, "y", shift(4, s)) for s in (1, 2, 3)]
    theirs = [lax.ppermute(v, "core", shift(2, 1)) for v in [g] + mine[1:]]
    shapes = (sds((DH, QW), F32), sds((AW // 2, D), F32), sds((2, D), F32))
    return own, input_grad, small_call(unpack_tail_body, shapes, idx, *mine, *theirs, name="unpack_tail")


def inverse_rms(v):
    return lax.rsqrt(jnp.mean(v * v, axis=-1, keepdims=True) + EPSILON)


def total(terms):
    return sum((t[...].astype(F32) for t in terms[1:]), terms[0][...].astype(F32))


def norm_two_body(tok, a, b, c, gain, after, normed):
    v = total((tok, a, b, c))
    after[...] = v
    normed[...] = (v * inverse_rms(v) * gain[...]).astype(BF16)


def norm_back_body(add, v_ref, a, b, c, gain, out, low, gain_grad):
    v = v_ref[...].astype(F32)
    grad = total((a, b, c))
    r = inverse_rms(v)
    pulled = grad * gain[...]
    inner = jnp.mean(v * pulled, axis=-1, keepdims=True)
    res = add[...].astype(F32) + r * pulled - v * (r * r * r) * inner
    out[...] = res
    low[...] = res.astype(BF16)
    part = jnp.sum(grad * v * r, axis=0, keepdims=True)

    @pl.when(pl.program_id(0) == 0)
    def _():
        gain_grad[...] = part

    @pl.when(pl.program_id(0) > 0)
    def _():
        gain_grad[...] += part


def row_call(body, out_shape, *args, name):
    block = lambda v: (
        pl.BlockSpec((HALF, D), lambda i: (i, 0))
        if v.shape[0] == BLK
        else pl.BlockSpec((1, D), lambda i: (0, 0))
    )
    return pl.pallas_call(
        body,
        grid=(2,),
        out_shape=out_shape,
        in_specs=[block(v) for v in args],
        out_specs=tuple(block(v) for v in out_shape),
        compiler_params=params(),
        cost_estimate=cost(1e6, 5e6),
        name=name,
    )(*args)


def replica_layout(lengths, replica, replica_id):
    sizes = jnp.where(replica == replica_id, lengths, 0)
    starts = jnp.cumsum(sizes) - sizes
    row_ids = jnp.arange(CAP, dtype=jnp.int32)
    inside = (row_ids[:, None] >= starts[None, :]) & (row_ids[:, None] < (starts + sizes)[None, :])
    begin = jnp.sum(jnp.where(inside, starts[None, :], 0), axis=1)
    begin = begin + jnp.where(jnp.any(inside, axis=1), 0, jnp.sum(sizes))
    return begin, row_ids - begin


def on_device(
    tokens, cotangent, gain_one, qkv_weight, out_weight, gate_weight, up_weight, down_weight,
    gain_two, seq_lengths, seq_replica,
):
    x, zh, core = lax.axis_index("x"), lax.axis_index("zh"), lax.axis_index("core")
    y, zl = lax.axis_index("y"), lax.axis_index("zl")
    idx = jnp.stack([x, zh, y, core]).astype(jnp.int32)

    tok = tokens.astype(F32)
    s_one = inverse_rms(tok)
    begin, position = replica_layout(seq_lengths, seq_replica, (y * 2 + zl) * 2 + core)
    half_rows = lambda v: lax.dynamic_index_in_dim(v.reshape(4, 2, BLK), zh, 1, False).reshape(ROWS, 1)
    first = jnp.tile(half_rows(begin)[3 * BLK :, 0], 8).reshape(1, QALL)
    lane = jnp.arange(128, dtype=jnp.int32)
    frequency = ROTARY_BASE ** (-(lane % 32).astype(F32) * (2.0 / HD))
    angles = half_rows(position).astype(F32) * frequency[None, :]
    cosine = jnp.cos(angles)
    sine = jnp.where((lane % HD) < HD // 2, -1.0, 1.0)[None, :] * jnp.sin(angles)

    qkv_got = fetch_half(qkv_weight, core)
    normed_one = gather_x((tok * s_one * gain_one).astype(BF16), (cosine,))
    eighth = lambda w: lax.dynamic_slice_in_dim(w, (y * 2 + core) * (w.shape[0] // 8), w.shape[0] // 8, 0)
    spread = lambda v: lax.all_gather(v, ("y", "core"), axis=0, tiled=True)
    fetch = lambda w: lax.ppermute(eighth(w), "zh", shift(2, 1))
    out_got = fetch(out_weight)
    out_all = out_weight, spread(tie(out_got, normed_one[1], normed_one[4]))
    swap = lambda v, *deps: lax.ppermute(tie(v, *deps), "core", shift(2, 1))
    qkv_all = qkv_weight, qkv_got, swap(qkv_got, out_got, normed_one[2], normed_one[3])

    q, kv_own = qkv_forward(idx, normed_one, qkv_all, cosine, sine)
    cot = tie(cotangent, normed_one[2], normed_one[3])
    cots = [cotangent] + [lax.ppermute(cot, "x", shift(4, -k)) for k in (1, 2, 3)]
    kv_par = lax.ppermute(kv_own, "zh", shift(2, 1))
    down_got = fetch_half(tie(down_weight, kv_par), core)
    rows = DH // 8
    cross = [(2 * a + b, 2 * (1 - a) + (1 - b)) for a in range(2) for b in range(2)]
    gate_up = lax.ppermute(
        jnp.concatenate(
            [
                eighth(tie(gate_weight, kv_own)),
                jnp.zeros((rows, GAP - FF4), BF16),
                eighth(tie(up_weight, kv_own)),
            ],
            1,
        ),
        ("zl", "zh"),
        cross,
    )
    att, qx = attend(idx, q, kv_own, kv_par, first)
    parts = out_project(idx, tie(att, *cots), out_all)
    gate_up = spread(tie(gate_up, parts[2]))
    p0, q1, q3 = relay(parts)
    after_attn, normed_two = row_call(
        norm_two_body,
        (sds((BLK, D), F32), sds((BLK, D))),
        tokens, *last_step(p0, q1, q3), gain_two.reshape(1, D), name="norm_two",
    )
    normed_two = gather_x(tie(normed_two, down_got))
    down_all = down_weight, down_got, swap(down_got, normed_two[1], normed_two[4])
    hid, dgate, dup = ffn(idx, normed_two, cots, gate_weight, up_weight, gate_up, down_all)
    d_parts = ffn_back(idx, dgate, dup, gate_weight, up_weight, gate_up)
    own_grads = down_grads(cots, tie(hid, d_parts[2]))
    d_own, q1, q3 = relay(d_parts)
    own_grads = gate_up_grads(normed_two, tie(dgate, q1, q3), dup, own_grads)
    d_two = last_step(d_own, q1, q3)
    grads = lax.psum_scatter(
        tie(own_grads, *d_two).reshape(32, PIECE, 128),
        ("zh", "zl", "y", "core"), scatter_dimension=0, tiled=True,
    )
    after_grad, branch, gain_grad_two = row_call(
        norm_back_body,
        (sds((BLK, D), F32), sds((BLK, D)), sds((1, D), F32)),
        cotangent, after_attn, *d_two, gain_two.reshape(1, D), name="norm_back_two",
    )
    branch = gather_x(branch)
    layer_parts = down_project(idx, tie(hid, after_grad), down_all)
    att = tie(att, *layer_parts)
    layer = [
        lax.ppermute(tie(layer_parts[k], branch[2], branch[3]), "x", shift(4, k)) for k in (1, 3)
    ]
    dqm, dkv_own, dkv_par = attend_back(
        idx, qx, kv_own, kv_par, first, att, cosine, sine, branch, out_all
    )
    dkv_got = lax.ppermute(dkv_par, "zh", shift(2, 1))
    tail = attn_grads(
        idx, normed_one, branch, dqm.reshape(ROWS, AW), tie(att, *layer).reshape(ROWS, AW)
    )
    dkv_got = tie(dkv_got, tail[0])
    *tail_kv, parts = qkv_back(
        idx, dqm.reshape(ROWS, AW), dkv_own, dkv_got, cosine, sine, qkv_all, normed_one, gain_one,
        gain_grad_two,
    )
    over_x = lambda v: sum((lax.ppermute(v, "x", shift(4, s)) for s in (1, 2, 3)), v)
    finish = lambda d_one: row_call(
        norm_back_body,
        (sds((BLK, D), F32), sds((BLK, D)), sds((1, D), F32)),
        after_grad, tokens, *d_one, gain_one.reshape(1, D), name="norm_back_one",
    )[1]
    summed, input_grad, (grad_qkv, grad_out, gains) = sum_tail(
        idx, (tail[0], tie(tail[1], dkv_got)), tail_kv, parts, finish
    )
    layer.append(lax.ppermute(tie(layer_parts[2], summed), "x", shift(4, 2)))
    grads = lax.all_gather(tie(grads, summed), ("zl", "y", "core"), axis=0, tiled=True)
    grad_gate, grad_up, grad_down = unpack(grads)
    layer_out = sum((v.astype(F32) for v in layer), after_attn + layer_parts[0].astype(F32))
    layer_out = layer_out.astype(BF16)
    gains = over_x(gains)
    return (
        layer_out, input_grad, gains[0], grad_qkv, grad_out, grad_gate, grad_up,
        grad_down, gains[1],
    )


def solution(mesh):
    grid = Mesh(mesh.devices.reshape(SIZES), AXES)
    rows = P(AXES, None)
    both = P(("x", "zh"), None)
    return jax.shard_map(
        on_device,
        mesh=grid,
        in_specs=(
            rows, rows, P(), P("zh", "x"), both, P("zh", "x"), P("zh", "x"), both, P(), P(), P(),
        ),
        out_specs=(
            rows, rows, P(), P("zh", "x"), both, P("zh", "x"), P("zh", "x"), both, P(),
        ),
        check_vma=False,
    )
```

```python
import jax
import jax.numpy as jnp
from jax import lax
from jax.experimental import pallas as pl
from jax.experimental.pallas import tpu as pltpu
from jax.sharding import Mesh
from jax.sharding import PartitionSpec as P

HEADS = 32
KV = 4
HD = 64
EPSILON = 1e-05
ROTARY_BASE = 10000.0
MASKED = -1e30

AXES = ("y", "zl", "core", "x", "zh")
SIZES = (4, 2, 2, 4, 2)
BLK = 160
HALF = BLK // 2
ROWS = 4 * BLK
CAP = 2 * ROWS
D = 2048
DH = D // 2
QW = 640
AW = 512
FF4 = 1408
TILE = 256
F32 = jnp.float32
BF16 = jnp.bfloat16
VLIM = 60 * 1024 * 1024


def spec(memory=pltpu.VMEM):
    return pl.BlockSpec(memory_space=memory)


def params(**kw):
    return pltpu.CompilerParams(vmem_limit_bytes=VLIM, **kw)


def cost(flops, nbytes):
    return pl.CostEstimate(flops=int(flops), bytes_accessed=int(nbytes), transcendentals=0)


def sds(shape, dtype=BF16):
    return jax.ShapeDtypeStruct(shape, dtype)


def dot(a, b):
    return jnp.dot(a, b, preferred_element_type=F32)


def dot_t(a, b):
    return lax.dot_general(a, b, (((1,), (1,)), ((), ())), preferred_element_type=F32)


def t_dot(a, b):
    return lax.dot_general(a, b, (((0,), (0,)), ((), ())), preferred_element_type=F32)


def tie(v, *deps):
    return lax.optimization_barrier((v,) + deps)[0]


def shift(n, s):
    return [(i, (i + s) % n) for i in range(n)]


def gather_x(v, wait=()):
    from_prev = lax.ppermute(v, "x", shift(4, 1))
    from_next = lax.ppermute(v, "x", shift(4, -1))
    send_a = tie(from_prev[:HALF], from_next, *wait)
    send_b = tie(from_next[HALF:], from_prev, *wait)
    opp_a = lax.ppermute(send_a, "x", shift(4, 1))
    opp_b = lax.ppermute(send_b, "x", shift(4, -1))
    return v, from_next, opp_a, opp_b, from_prev


def relay_body(p1, got_a, p3, got_b, q1, q3):
    q1[...] = (p1[...].astype(F32) + got_a[...].astype(F32)).astype(BF16)
    q3[...] = (p3[...].astype(F32) + got_b[...].astype(F32)).astype(BF16)


def relay(parts):
    p0, p1, p2a, p2b, p3 = parts
    got_a = lax.ppermute(p2a, "x", shift(4, 1))
    got_b = lax.ppermute(p2b, "x", shift(4, -1))
    half = lambda k: pl.BlockSpec((HALF, D), lambda i: (k, 0))
    q1, q3 = pl.pallas_call(
        relay_body,
        grid=(1,),
        out_shape=(sds((BLK, D)),) * 2,
        in_specs=[half(0), half(0), half(1), half(0)],
        out_specs=(half(0), half(1)),
        input_output_aliases={0: 0, 2: 1},
        compiler_params=params(),
        cost_estimate=cost(1e6, 2e6),
        name="relay",
    )(p1, got_a, p3, got_b)
    return p0, q1, q3


def scatter_x(parts):
    return last_step(*relay(parts))


def last_step(p0, q1, q3):
    return p0, lax.ppermute(q1, "x", shift(4, 1)), lax.ppermute(q3, "x", shift(4, -1))


PIECES = ((0, BLK), (1, BLK), (2, HALF), (2, HALF), (3, BLK))
PIECE_ROW = (0, BLK, 2 * BLK, 2 * BLK + HALF, 3 * BLK)


def part_shapes(width, dtype=BF16):
    return tuple(sds((n, width), dtype) for _, n in PIECES)


def low_lanes(shape):
    return lax.broadcasted_iota(jnp.int32, shape, 1) < HD


def swap_halves(v):
    lane = lax.broadcasted_iota(jnp.int32, v.shape, 1) % HD
    return jnp.where(lane < HD // 2, pltpu.roll(v, 128 - HD // 2, 1), pltpu.roll(v, HD // 2, 1))


def rows_at(block):
    return pl.ds(pl.multiple_of(block * BLK, 32), BLK)


def fetch_half(w, core):
    half = w.shape[0] // 2
    return lax.ppermute(lax.dynamic_slice_in_dim(w, core * half, half, 0), "zh", shift(2, 1))


OUT_ROWS = AW // 2 // 8
DOWN_ROWS = 96


def out_rows_spec():
    return pl.BlockSpec((8, OUT_ROWS, D), lambda i: (0, 0, 0))


def own_and_partner(idx, rows):
    zh = idx[1]
    at = lambda k: pl.ds(pl.multiple_of(k * rows, rows), rows)
    return at(zh), at(1 - zh)


def weight_rows(idx, rows):
    zh, core = idx[1], idx[3]
    far = (1 - zh) * rows
    half = rows // 2
    at = lambda first, n: pl.ds(pl.multiple_of(first, half), n)
    return at(zh * rows, rows), at(far + core * half, half), at(far + (1 - core) * half, half)


def qkv_body(idx, n0, n1, n2a, n2b, n3, w0, w1, w2, cosine, sine, q_ref, kv_ref, rows):
    x = idx[0]
    lo = low_lanes((BLK, 128))
    for ref, row, (_, n) in zip((n0, n1, n2a, n2b, n3), PIECE_ROW, PIECES):
        rows[row : row + n, :] = ref[...]
    s0, s1, s2 = weight_rows(idx, DH)
    acc = dot(rows[:, s0], w0[...]) + dot(rows[:, s1], w1[...]) + dot(rows[:, s2], w2[...])
    for d in range(4):
        at = rows_at((x + d) & 3)
        cs = cosine[at, :]
        sn = sine[at, :]
        for p in range(5):
            v = acc[d * BLK : (d + 1) * BLK, p * 128 : (p + 1) * 128]
            r = v * cs + swap_halves(v) * sn
            if p < 4:
                r = r * (HD**-0.5 * LOG2E)
                a = (x + d) & 3
                for k, w in enumerate((r, pltpu.roll(r, HD, 1))):
                    head = slice((2 * p + k) * BLK, (2 * p + k + 1) * BLK)
                    q_ref[a, head, :] = jnp.where(lo, w, 0.0).astype(BF16)
            else:
                kv_ref[at, :] = jnp.where(lo, r, v).astype(BF16)


def qkv_forward(idx, pieces, weight, cosine, sine):
    return pl.pallas_call(
        qkv_body,
        out_shape=(sds((4, QALL, 128)), sds((ROWS, 128))),
        in_specs=[spec(pltpu.SMEM)] + [spec()] * 10,
        out_specs=(spec(), spec()),
        scratch_shapes=[pltpu.VMEM((ROWS, D), BF16)],
        compiler_params=params(),
        cost_estimate=cost(2 * ROWS * D * QW, 7e6),
        name="qkv_forward",
    )(idx, *pieces, *weight, cosine, sine)


QALL = 8 * BLK
PAIR = 2 * BLK
LOG2E = 1.4426950408889634
LN2 = 0.6931471805599453


def split3(v):
    a = v.astype(BF16).astype(F32)
    b = (v - a).astype(BF16).astype(F32)
    return a, b, v - a - b


def with_lanes(v, parts):
    lane = lax.broadcasted_iota(jnp.int32, v.shape, 1)
    out = jnp.where(lane < HD, v, 0.0)
    for k, part in enumerate(parts):
        out = jnp.where(lane == HD + k, part, out)
    return out


def spread_keys(zh, kv_own, kv_par, kk, vv, fill):
    shape = (BLK, 128)
    lo = low_lanes(shape)
    rest = fill(lax.broadcasted_iota(jnp.int32, shape, 1) - HD)
    for j in range(4):
        for src, off in ((kv_own, zh), (kv_par, 1 - zh)):
            v = src[j * BLK : (j + 1) * BLK, :].astype(F32)
            at = rows_at(2 * j + off)
            kk[at, :] = jnp.where(lo, v, rest).astype(BF16)
            vv[at, :] = jnp.where(lo, pltpu.roll(v, HD, 1), rest).astype(BF16)


def masked(s, zh, j, kb, first):
    if j < 3 and kb < j:
        return s
    u = kb * PAIR + lax.broadcasted_iota(jnp.int32, (PAIR, QALL), 0)
    allowed = None
    if kb == j:
        t = (2 * j + zh) * BLK + lax.broadcasted_iota(jnp.int32, (1, QALL), 1) % BLK
        allowed = u <= t
    if j == 3:
        later = u >= first[...]
        allowed = later if allowed is None else allowed & later
    return jnp.where(allowed, s, MASKED)


def attend_body(idx, q, kv_own, kv_par, first, att, qx, kk, vv, vt, s_ref, e_ref):
    x, zh = idx[0], idx[1]
    spread_keys(zh, kv_own, kv_par, kk, vv, lambda lane: 1.0)
    vt[...] = vv[...].T
    lo = low_lanes((BLK, 128))
    for j in range(4):
        n = PAIR * (j + 1)
        qj = q[j]
        top = jnp.full((1, QALL), MASKED, F32)
        for kb in range(j + 1):
            rows = slice(kb * PAIR, (kb + 1) * PAIR)
            s = masked(dot_t(kk[rows, :], qj), zh, j, kb, first)
            s_ref[rows, :] = s
            top = jnp.maximum(top, jnp.max(s, axis=0, keepdims=True))
        for k in range(n // 64):
            rows = slice(k * 64, (k + 1) * 64)
            e_ref[rows, :] = jnp.exp2(s_ref[rows, :] - top).astype(BF16)
        o = dot(vt[:, :n], e_ref[:n, :])
        lse = split3(top + jnp.log(o[HD : HD + 1, :]) * LOG2E)
        row = lax.broadcasted_iota(jnp.int32, (128, QALL), 0)
        extra = jnp.zeros((128, QALL), F32)
        for k, part in enumerate(lse):
            extra = jnp.where(row == HD + k, part, extra)
        qx[j] = (qj.astype(F32) + extra.T).astype(BF16)
        o = o.T
        r = pltpu.roll(o, HD, 1)
        rel = (j - x) & 3
        for p in range(4):
            even, odd = slice(2 * p * BLK, (2 * p + 1) * BLK), slice((2 * p + 1) * BLK, (2 * p + 2) * BLK)
            num = jnp.where(lo, o[even], r[odd])
            den = jnp.where(lo, r[even], o[odd])
            att[rel, :, p * 128 : (p + 1) * 128] = (num / den).astype(BF16)


def attend(idx, q, kv_own, kv_par, first):
    return pl.pallas_call(
        attend_body,
        out_shape=(sds((4, BLK, AW)), sds((4, QALL, 128))),
        in_specs=[spec(pltpu.SMEM)] + [spec()] * 4,
        out_specs=(spec(), spec()),
        scratch_shapes=[
            pltpu.VMEM((CAP, 128), BF16),
            pltpu.VMEM((CAP, 128), BF16),
            pltpu.VMEM((128, CAP), BF16),
            pltpu.VMEM((CAP, QALL), F32),
            pltpu.VMEM((CAP, QALL), BF16),
        ],
        compiler_params=params(),
        cost_estimate=cost(1.2e10, 3e6),
        name="attend",
    )(idx, q, kv_own, kv_par, first)


def store_parts(res, refs):
    for ref, row, (_, n) in zip(refs, PIECE_ROW, PIECES):
        ref[...] = res[row : row + n].astype(BF16)


def out_body(idx, att, w0, w1, o0, o1, o2a, o2b, o3):
    slots = own_and_partner(idx, AW // 2)
    weights = w0[...], w1[...].reshape(AW // 2, D)
    for d, ref in ((2, None), (1, o1), (3, o3), (0, o0)):
        a = att.at[d]
        res = sum(dot(a[:, s], w) for s, w in zip(slots, weights)).astype(BF16)
        if d == 2:
            o2a[...] = res[:HALF]
            o2b[...] = res[HALF:]
        else:
            ref[...] = res


def out_project(idx, att, weight):
    return pl.pallas_call(
        out_body,
        grid=(1,),
        out_shape=part_shapes(D),
        in_specs=[spec(pltpu.SMEM), spec(), spec(), out_rows_spec()],
        out_specs=(spec(),) * 5,
        compiler_params=params(),
        cost_estimate=cost(2 * ROWS * D * AW, 5.5e6),
        name="out_project",
    )(idx, att, *weight)


def stack_heads(v):
    return v, pltpu.roll(v, HD, 1)


def attend_back_body(
    idx, qx, kv_own, kv_par, first, att, cosine, sine, b0, b1, b2a, b2b, b3, w0, w1,
    dq_ref, dkv_own, dkv_par, kk, vv, dout, do_all, dkk, dvv, e_ref, ds_ref, dq_acc,
):
    x, zh = idx[0], idx[1]
    spread_keys(zh, kv_own, kv_par, kk, vv, lambda lane: jnp.where(lane < 3, -1.0, 0.0))
    slots = own_and_partner(idx, AW // 2)
    weights = w0[...], w1[...].reshape(AW // 2, D)
    for d in range(4):
        if d == 2:
            rows = jnp.concatenate([b2a[...], b2b[...]], 0)
        else:
            rows = (b0, b1, None, b3)[d][...]
        at = rows_at((x + d) & 3)
        for s, w in zip(slots, weights):
            dout[at, s] = dot_t(rows, w).astype(BF16)
    lo = low_lanes((BLK, 128))
    for j in range(4):
        rel = (j - x) & 3
        here = slice(j * BLK, (j + 1) * BLK)
        for p in range(4):
            cols = slice(p * 128, (p + 1) * 128)
            do = dout[here, cols].astype(F32)
            prod = do * att[rel, :, cols].astype(F32)
            for k, (v, w) in enumerate(zip(stack_heads(do), stack_heads(prod))):
                delta = jnp.sum(jnp.where(lo, w, 0.0), axis=1, keepdims=True)
                head = slice((2 * p + k) * BLK, (2 * p + k + 1) * BLK)
                do_all[head, :] = with_lanes(v, split3(delta)).astype(BF16)
        for kb in range(j + 1):
            rows = slice(kb * PAIR, (kb + 1) * PAIR)
            e = jnp.exp2(masked(dot_t(kk[rows, :], qx[j]), zh, j, kb, first))
            e_ref[...] = e.astype(BF16)
            ds_ref[...] = (e * dot_t(vv[rows, :], do_all[...])).astype(BF16)
            dv = dot(e_ref[...], do_all[...])
            dk = dot(ds_ref[...], qx[j])
            dq = t_dot(ds_ref[...], kk[rows, :])
            if kb == j:
                dvv[rows, :], dkk[rows, :] = dv, dk
            else:
                dvv[rows, :] += dv
                dkk[rows, :] += dk
            if kb == 0:
                dq_acc[...] = dq
            else:
                dq_acc[...] += dq
        for p in range(4):
            even, odd = slice(2 * p * BLK, (2 * p + 1) * BLK), slice((2 * p + 1) * BLK, (2 * p + 2) * BLK)
            v = jnp.where(lo, dq_acc[even, :], pltpu.roll(dq_acc[odd, :], HD, 1)) * HD**-0.5
            v = v * cosine[here, :] - swap_halves(v) * sine[here, :]
            dq_ref[rel, :, p * 128 : (p + 1) * 128] = v.astype(BF16)
    for j in range(4):
        for dst, off in ((dkv_own, zh), (dkv_par, 1 - zh)):
            at = rows_at(2 * j + off)
            both = jnp.where(lo, dkk[at, :] * LN2, pltpu.roll(dvv[at, :], HD, 1))
            dst[j * BLK : (j + 1) * BLK, :] = both.astype(dst.dtype)


def attend_back(idx, qx, kv_own, kv_par, first, att, cosine, sine, branch, weight):
    return pl.pallas_call(
        attend_back_body,
        grid=(1,),
        out_shape=(sds((4, BLK, AW)), sds((ROWS, 128), F32), sds((ROWS, 128))),
        in_specs=[spec(pltpu.SMEM)] + [spec()] * 13 + [out_rows_spec()],
        out_specs=(spec(),) * 3,
        scratch_shapes=[
            pltpu.VMEM((CAP, 128), BF16),
            pltpu.VMEM((CAP, 128), BF16),
            pltpu.VMEM((ROWS, AW), BF16),
            pltpu.VMEM((QALL, 128), BF16),
            pltpu.VMEM((CAP, 128), F32),
            pltpu.VMEM((CAP, 128), F32),
            pltpu.VMEM((PAIR, QALL), BF16),
            pltpu.VMEM((PAIR, QALL), BF16),
            pltpu.VMEM((QALL, 128), F32),
        ],
        compiler_params=params(),
        cost_estimate=cost(3e10, 8e6),
        name="attend_back",
    )(idx, qx, kv_own, kv_par, first, att, cosine, sine, *branch, *weight)


def qkv_back_body(
    idx, dqm, dkv_own, dkv_got, cosine, sine, w0, w1, w2, n0, n1, n2a, n2b, n3, gain_one,
    gain_grad_two,
    mine, theirs, o0, o1, o2a, o2b, o3, n_all, dkv, grad, gains,
):
    x, y, core = idx[0], idx[2], idx[3]
    lo = low_lanes((BLK, 128))
    for ref, row, (_, n) in zip((n0, n1, n2a, n2b, n3), PIECE_ROW, PIECES):
        n_all[row : row + n, :] = ref[...]
    for d in range(4):
        at = rows_at((x + d) & 3)
        v = dkv_own[at, :] + dkv_got[at, :].astype(F32)
        v = jnp.where(lo, v * cosine[at, :] - swap_halves(v) * sine[at, :], v).astype(BF16)
        dkv[d * BLK : (d + 1) * BLK, :] = v
    rows = jnp.concatenate([dqm[...], dkv[...]], 1)
    for s, w in zip(weight_rows(idx, DH), (w0, w1, w2)):
        for c in range(w.shape[0] // 512):
            cols = pl.ds(pl.multiple_of(s.start + c * 512, 512), 512)
            res = dot_t(rows, w[c * 512 : (c + 1) * 512, :])
            part = (res * n_all[:, cols].astype(F32)).reshape(ROWS // 8, 8, 512)
            gains[0:1, cols] = jnp.sum(jnp.sum(part, axis=0), axis=0, keepdims=True) / gain_one[:, cols]
            store_parts(res, [r.at[:, cols] for r in (o0, o1, o2a, o2b, o3)])
    grad[...] = dot(dkv[...].T, n_all[...]).astype(BF16)
    gains[1:2, :] = gain_grad_two[...]
    for s in range(4):
        for k, ref in enumerate((mine, theirs)):
            p = ((y + s) & 3) * 2 + (core if k == 0 else 1 - core)
            both = gains[:, pl.ds(pl.multiple_of(p * 256, 256), 256)]
            both = jnp.concatenate([both[:, :128], both[:, 128:], jnp.zeros((12, 128), F32)], 0)
            for h in range(2):
                ref[s, h, :128, :] = grad[:, pl.ds(pl.multiple_of(h * DH + p * 128, 128), 128)]
                ref[s, h, 128:, :] = both.astype(BF16)


def qkv_back(idx, dqm, dkv_own, dkv_got, cosine, sine, weight, pieces, gain_one, gain_grad_two):
    res = pl.pallas_call(
        qkv_back_body,
        out_shape=(sds((4, 2, KVP, 128)),) * 2 + part_shapes(D),
        in_specs=[spec(pltpu.SMEM)] + [spec()] * 15,
        out_specs=(spec(),) * 7,
        scratch_shapes=[
            pltpu.VMEM((ROWS, D), BF16),
            pltpu.VMEM((ROWS, 128), BF16),
            pltpu.VMEM((128, D), BF16),
            pltpu.VMEM((2, D), F32),
        ],
        compiler_params=params(),
        cost_estimate=cost(2 * ROWS * D * QW, 1.3e7),
        name="qkv_back",
    )(
        idx, dqm, dkv_own, dkv_got, cosine, sine, *weight, *pieces,
        gain_one.reshape(1, D), gain_grad_two.reshape(1, D),
    )
    return res[0], res[1], res[2:]


TILES = 6
GAP = TILES * TILE


def load_down(idx, own, far, dst, sem):
    half = FF4 // 2
    zh = idx[1]
    at = lambda first, n: pl.ds(pl.multiple_of(first, 32), n)
    copies = [pltpu.make_async_copy(own, dst.at[at(zh * half, half)], sem.at[8])]
    for k in range(8):
        first = min(k * DOWN_ROWS, half - DOWN_ROWS)
        skip = k * DOWN_ROWS - first
        n = DOWN_ROWS - skip
        source = far.at[k, OUT_ROWS + skip : OUT_ROWS + DOWN_ROWS]
        copies.append(pltpu.make_async_copy(source, dst.at[at((1 - zh) * half + first + skip, n)], sem.at[k]))
    return copies


def ffn_body(
    idx, n0, n1, n2a, n2b, n3, c0, c1, c2, c3, gate_own, up_own, gate_par, up_par, w0, w1,
    hid, dgate, dup, n_all, c_all, down, sem,
):
    i = pl.program_id(0)
    zh = idx[1]

    @pl.when(i == 0)
    def _():
        copies = load_down(idx, w0, w1, down, sem)
        for c in copies:
            c.start()
        for ref, row, (_, n) in zip((n0, n1, n2a, n2b, n3), PIECE_ROW, PIECES):
            n_all[row : row + n, :] = ref[...]
        for d, ref in enumerate((c0, c1, c2, c3)):
            c_all[d * BLK : (d + 1) * BLK, :] = ref[...]
        for c in copies:
            c.wait()

    own = n_all[:, pl.ds(pl.multiple_of(zh * DH, DH), DH)]
    par = n_all[:, pl.ds(pl.multiple_of((1 - zh) * DH, DH), DH)]
    gate = dot(own, gate_own[...]) + dot(par, gate_par[...])
    up = dot(own, up_own[...]) + dot(par, up_par[...])
    dh = dot_t(c_all[...], down[pl.ds(pl.multiple_of(i * TILE, TILE), TILE), :])
    sig = 1.0 / (1.0 + jnp.exp(-gate))
    act = gate * sig
    hid[...] = (act * up).astype(BF16)
    dgate[...] = (dh * up * sig * (1.0 + gate * (1.0 - sig))).astype(BF16)
    dup[...] = (dh * act).astype(BF16)


def whole(n, w):
    return pl.BlockSpec((n, w), lambda i: (0, 0))


def ffn(idx, normed, cots, gate, up, gate_up, down):
    column = lambda first: pl.BlockSpec((DH, TILE), lambda i: (0, i + first))
    hidden = pl.BlockSpec((ROWS, TILE), lambda i: (0, i))
    return pl.pallas_call(
        ffn_body,
        grid=(TILES,),
        out_shape=(sds((ROWS, FF4)),) * 3,
        in_specs=[spec(pltpu.SMEM)]
        + [whole(n, D) for _, n in PIECES]
        + [whole(BLK, D)] * 4
        + [column(0), column(0), column(0), column(TILES)]
        + [spec(pl.ANY)] * 2,
        out_specs=[hidden] * 3,
        scratch_shapes=[
            pltpu.VMEM((ROWS, D), BF16),
            pltpu.VMEM((ROWS, D), BF16),
            pltpu.VMEM((GAP, D), BF16),
            pltpu.SemaphoreType.DMA((9,)),
        ],
        compiler_params=params(),
        cost_estimate=cost(6 * ROWS * D * FF4, 3.4e7),
        name="ffn",
    )(idx, *normed, *cots, gate, up, gate_up, gate_up, *down)


def down_body(idx, hid, w0, w1, o0, o1, o2, o3, down, sem):
    copies = load_down(idx, w0, w1, down, sem)
    for c in copies:
        c.start()
    for c in copies:
        c.wait()
    for n in range(D // 512):
        cols = slice(n * 512, (n + 1) * 512)
        res = dot(hid[...], down[:, cols]).astype(BF16)
        for d, ref in enumerate((o0, o1, o2, o3)):
            ref[:, cols] = res[d * BLK : (d + 1) * BLK]


def down_project(idx, hid, down):
    return pl.pallas_call(
        down_body,
        out_shape=(sds((BLK, D)),) * 4,
        in_specs=[spec(pltpu.SMEM), spec()] + [spec(pl.ANY)] * 2,
        out_specs=(spec(),) * 4,
        scratch_shapes=[pltpu.VMEM((FF4, D), BF16), pltpu.SemaphoreType.DMA((9,))],
        compiler_params=params(),
        cost_estimate=cost(2 * ROWS * D * FF4, 1.1e7),
        name="down_project",
    )(idx, hid, *down)


def ffn_back_body(idx, dgate, dup, gate_own, up_own, par, *refs):
    half = pl.num_programs(0) // 2

    @pl.when(pl.program_id(0) < half)
    def _():
        store_parts(dot_t(dgate[...], gate_own[...]) + dot_t(dup[...], up_own[...]), refs)

    @pl.when(pl.program_id(0) >= half)
    def _():
        store_parts(dot_t(dgate[...], par[:, :FF4]) + dot_t(dup[...], par[:, GAP:]), refs)


def ffn_back(idx, dgate, dup, gate, up, gate_up):
    half = DH // TILE
    rows = pl.BlockSpec((ROWS, FF4), lambda i, idx: (0, 0))
    own = pl.BlockSpec((TILE, FF4), lambda i, idx: (jnp.minimum(i, half - 1), 0))
    par = pl.BlockSpec((TILE, GAP + FF4), lambda i, idx: (jnp.maximum(i - half, 0), 0))
    place = lambda i, idx: (0, i ^ (idx[1] * half))
    return pl.pallas_call(
        ffn_back_body,
        grid_spec=pltpu.PrefetchScalarGridSpec(
            num_scalar_prefetch=1,
            grid=(D // TILE,),
            in_specs=[rows, rows, own, own, par],
            out_specs=[pl.BlockSpec((n, TILE), place) for _, n in PIECES],
        ),
        out_shape=part_shapes(D),
        compiler_params=params(),
        cost_estimate=cost(4 * ROWS * D * FF4, 1.8e7),
        name="ffn_back",
    )(idx, dgate, dup, gate, up, gate_up)


GU_ROWS = FF4 // 128 * 64
PIECE = 2 * GU_ROWS + FF4 // 2
QS = 4


def gate_up_grads_body(*refs):
    na, nb = refs[0:5], refs[5:10]
    dgate, dup, _, out = refs[10:]
    stack = lambda parts: jnp.concatenate([r[...] for r in parts], 0)
    rows = jnp.concatenate([stack(na), stack(nb)], 1).T
    for k, ref in enumerate((dgate, dup)):
        g = dot(rows, ref[...]).astype(BF16)
        for h in range(2):
            for q in range(QS):
                r = g[(QS * h + q) * 64 : (QS * h + q + 1) * 64]
                for c in range(FF4 // 128):
                    first = k * GU_ROWS + c * 64
                    out[h, q, first : first + 64, :] = r[:, c * 128 : (c + 1) * 128]


def gate_up_grads(normed, dgate, dup, pieces):
    return pl.pallas_call(
        gate_up_grads_body,
        grid=(16 // QS,),
        out_shape=sds((2, 16, PIECE, 128)),
        in_specs=[pl.BlockSpec((n, 64 * QS), lambda i: (0, i)) for _, n in PIECES]
        + [pl.BlockSpec((n, 64 * QS), lambda i: (0, i + 16 // QS)) for _, n in PIECES]
        + [whole(ROWS, FF4)] * 2
        + [spec(pl.ANY)],
        out_specs=pl.BlockSpec((2, QS, 2 * GU_ROWS, 128), lambda i: (0, i, 0, 0)),
        input_output_aliases={12: 0},
        compiler_params=params(),
        cost_estimate=cost(4 * ROWS * D * FF4, 2e7),
        name="gate_up_grads",
    )(*normed, *normed, dgate, dup, pieces)


def down_grads_body(*refs):
    cots = refs[0:4]
    hid, out, hid_t = refs[4:]

    @pl.when(pl.program_id(0) == 0)
    def _():
        hid_t[...] = hid[...].T

    g = dot(hid_t[...], jnp.concatenate([r[...] for r in cots], 0)).astype(BF16)
    for h in range(2):
        for q in range(QS):
            out[h, q, :, :] = g[h * (FF4 // 2) : (h + 1) * (FF4 // 2), q * 128 : (q + 1) * 128]


def down_grads(cots, hid):
    return pl.pallas_call(
        down_grads_body,
        grid=(16 // QS,),
        out_shape=sds((2, 16, PIECE, 128)),
        in_specs=[pl.BlockSpec((BLK, 128 * QS), lambda i: (0, i))] * 4 + [whole(ROWS, FF4)],
        out_specs=pl.BlockSpec((2, QS, FF4 // 2, 128), lambda i: (0, i, 2, 0)),
        scratch_shapes=[pltpu.VMEM((FF4, ROWS), BF16)],
        compiler_params=params(),
        cost_estimate=cost(2 * ROWS * D * FF4, 1e7),
        name="down_grads",
    )(*cots, hid)


def unpack_body(piece, gate, up, down):
    for q in range(QS):
        rows = slice(q * 64, (q + 1) * 64)
        for k, ref in enumerate((gate, up)):
            for c in range(FF4 // 128):
                first = k * GU_ROWS + c * 64
                ref[rows, c * 128 : (c + 1) * 128] = piece[q, first : first + 64, :].astype(F32)
        down[:, q * 128 : (q + 1) * 128] = piece[q, 2 * GU_ROWS :, :].astype(F32)


def unpack(pieces):
    return pl.pallas_call(
        unpack_body,
        grid=(16 // QS,),
        out_shape=(sds((DH, FF4), F32), sds((DH, FF4), F32), sds((FF4 // 2, D), F32)),
        in_specs=[pl.BlockSpec((QS, PIECE, 128), lambda i: (i, 0, 0))],
        out_specs=[
            pl.BlockSpec((64 * QS, FF4), lambda i: (i, 0)),
            pl.BlockSpec((64 * QS, FF4), lambda i: (i, 0)),
            pl.BlockSpec((FF4 // 2, 128 * QS), lambda i: (0, i)),
        ],
        compiler_params=params(),
        cost_estimate=cost(1e6, 2.6e7),
        name="unpack",
    )(pieces)


QP = 4 * 128
OP = 2 * (AW // 2)
QOP = QP + OP
KVP = 128 + 16
TAIL = QOP + KVP


def attn_grads_body(idx, *refs):
    na, nb, branch = refs[0:5], refs[5:10], refs[10:15]
    dqm, att, mine, theirs, att_t = refs[15:]
    core = idx[3]

    @pl.when(pl.program_id(0) == 0)
    def _():
        att_t[...] = att[...].T

    stack = lambda parts: jnp.concatenate([r[...] for r in parts], 0)

    def store(h, first, n, zero, one):
        mine[0, h, first : first + n, :] = jnp.where(core == 0, zero, one)
        theirs[0, h, first : first + n, :] = jnp.where(core == 0, one, zero)

    for h, cols in enumerate((na, nb)):
        g = dot(stack(cols).T, dqm[...]).astype(BF16)
        for c in range(4):
            lanes = slice(c * 128, (c + 1) * 128)
            store(h, c * 128, 128, g[:128, lanes], g[128:, lanes])
    g = dot(att_t[...], stack(branch)).astype(BF16)
    for h in range(2):
        r = g[h * (AW // 2) : (h + 1) * (AW // 2)]
        for c in range(2):
            lanes = lambda k: slice(k * 256 + c * 128, k * 256 + (c + 1) * 128)
            store(h, QP + c * (AW // 2), AW // 2, r[:, lanes(0)], r[:, lanes(1)])


def attn_grads(idx, normed, branch, dqm, att):
    turn = lambda s, idx: (s + idx[2]) & 3
    piece = pl.BlockSpec((1, 2, QOP, 128), lambda s, idx: (s, 0, 0, 0))
    fixed = pl.BlockSpec((ROWS, AW), lambda s, idx: (0, 0))
    return pl.pallas_call(
        attn_grads_body,
        grid_spec=pltpu.PrefetchScalarGridSpec(
            num_scalar_prefetch=1,
            grid=(4,),
            in_specs=[pl.BlockSpec((n, 256), lambda s, idx: (0, turn(s, idx))) for _, n in PIECES]
            + [pl.BlockSpec((n, 256), lambda s, idx: (0, turn(s, idx) + 4)) for _, n in PIECES]
            + [pl.BlockSpec((n, 512), lambda s, idx: (0, turn(s, idx))) for _, n in PIECES]
            + [fixed, fixed],
            out_specs=[piece, piece],
            scratch_shapes=[pltpu.VMEM((AW, ROWS), BF16)],
        ),
        out_shape=(sds((4, 2, QOP, 128)),) * 2,
        compiler_params=params(),
        cost_estimate=cost(4 * ROWS * D * AW, 1e7),
        name="attn_grads",
    )(idx, *normed, *normed, *branch, dqm, att)


def small_call(body, out_shape, *args, name):
    return pl.pallas_call(
        body,
        out_shape=out_shape,
        in_specs=[spec(pltpu.SMEM)] + [spec()] * (len(args) - 1),
        out_specs=jax.tree.map(lambda _: spec(), out_shape),
        compiler_params=params(),
        cost_estimate=cost(1e6, 4e6),
        name=name,
    )(*args)


def add(*values):
    return sum((v.astype(F32) for v in values[1:]), values[0].astype(F32)).astype(BF16)


def sum_core_body(idx, a, b, c, d, *outs):
    for s, out in enumerate(outs):
        out[:, :QOP, :] = add(a[s], b[s])
        out[:, QOP:, :] = add(c[s], d[s])


def sum_y_body(idx, a, b, c, d, own, other):
    zh = idx[1]
    own[...] = add(a[zh], b[zh], c[zh], d[zh])
    far = 1 - zh
    other[...] = add(a[far], b[far], c[far], d[far])


def sum_z_body(idx, a, b, c, d, out):
    out[...] = add(a[...], b[...], c[...], d[...])


def unpack_tail_body(idx, *refs):
    y, core = idx[2], idx[3]
    qkv, out, gains = refs[8:]
    for k in range(8):
        piece = refs[k]
        p = ((y - k % 4) & 3) * 2 + (core if k < 4 else 1 - core)
        rows = pl.ds(pl.multiple_of(p * 128, 128), 128)
        for c in range(4):
            qkv[rows, c * 128 : (c + 1) * 128] = piece[c * 128 : (c + 1) * 128, :].astype(F32)
        qkv[rows, AW:] = piece[QOP : QOP + 128, :].astype(F32).T
        g = piece[QOP + 128 :, :].astype(F32)
        for c in range(2):
            first = QP + c * (AW // 2)
            cols = pl.ds(pl.multiple_of(p * 256 + c * 128, 128), 128)
            out[:, cols] = piece[first : first + AW // 2, :].astype(F32)
            gains[:, cols] = g[2 * c : 2 * c + 2]


def sum_tail(idx, first, second, parts, finish):
    got_a = lax.ppermute(first[1], "core", shift(2, 1))
    got_b = lax.ppermute(second[1], "core", shift(2, 1))
    part = sds((2, TAIL, 128))
    g = small_call(sum_core_body, (part,) * 4, idx, first[0], got_a, second[0], got_b, name="sum_core")
    got = [lax.ppermute(g[s], "y", shift(4, s)) for s in (2, 1, 3)]
    part = sds((TAIL, 128))
    own, other = small_call(sum_y_body, (part,) * 2, idx, g[0], *got, name="sum_y")
    p0, q1, q3 = relay([tie(p, own) for p in parts])
    cross = [(2 * a + b, 2 * (1 - a) + (1 - b)) for a in range(2) for b in range(2)]
    g = small_call(
        sum_z_body,
        part,
        idx,
        tie(own, q1, q3),
        lax.ppermute(own, "zl", shift(2, 1)),
        lax.ppermute(other, "zh", shift(2, 1)),
        lax.ppermute(other, ("zl", "zh"), cross),
        name="sum_z",
    )
    d_one = last_step(p0, q1, q3)
    input_grad = finish(d_one)
    mine = [tie(g, input_grad)] + [lax.ppermute(g, "y", shift(4, s)) for s in (1, 2, 3)]
    theirs = [lax.ppermute(v, "core", shift(2, 1)) for v in [g] + mine[1:]]
    shapes = (sds((DH, QW), F32), sds((AW // 2, D), F32), sds((2, D), F32))
    return own, input_grad, small_call(unpack_tail_body, shapes, idx, *mine, *theirs, name="unpack_tail")


def inverse_rms(v):
    return lax.rsqrt(jnp.mean(v * v, axis=-1, keepdims=True) + EPSILON)


def total(terms):
    return sum((t[...].astype(F32) for t in terms[1:]), terms[0][...].astype(F32))


def norm_two_body(tok, a, b, c, gain, after, normed):
    v = total((tok, a, b, c))
    after[...] = v
    normed[...] = (v * inverse_rms(v) * gain[...]).astype(BF16)


def norm_back_body(add, v_ref, a, b, c, gain, out, low, gain_grad):
    v = v_ref[...].astype(F32)
    grad = total((a, b, c))
    r = inverse_rms(v)
    pulled = grad * gain[...]
    inner = jnp.mean(v * pulled, axis=-1, keepdims=True)
    res = add[...].astype(F32) + r * pulled - v * (r * r * r) * inner
    out[...] = res
    low[...] = res.astype(BF16)
    part = jnp.sum(grad * v * r, axis=0, keepdims=True)

    @pl.when(pl.program_id(0) == 0)
    def _():
        gain_grad[...] = part

    @pl.when(pl.program_id(0) > 0)
    def _():
        gain_grad[...] += part


def row_call(body, out_shape, *args, name):
    block = lambda v: (
        pl.BlockSpec((HALF, D), lambda i: (i, 0))
        if v.shape[0] == BLK
        else pl.BlockSpec((1, D), lambda i: (0, 0))
    )
    return pl.pallas_call(
        body,
        grid=(2,),
        out_shape=out_shape,
        in_specs=[block(v) for v in args],
        out_specs=tuple(block(v) for v in out_shape),
        compiler_params=params(),
        cost_estimate=cost(1e6, 5e6),
        name=name,
    )(*args)


def replica_layout(lengths, replica, replica_id):
    sizes = jnp.where(replica == replica_id, lengths, 0)
    starts = jnp.cumsum(sizes) - sizes
    row_ids = jnp.arange(CAP, dtype=jnp.int32)
    inside = (row_ids[:, None] >= starts[None, :]) & (row_ids[:, None] < (starts + sizes)[None, :])
    begin = jnp.sum(jnp.where(inside, starts[None, :], 0), axis=1)
    begin = begin + jnp.where(jnp.any(inside, axis=1), 0, jnp.sum(sizes))
    return begin, row_ids - begin


def on_device(
    tokens, cotangent, gain_one, qkv_weight, out_weight, gate_weight, up_weight, down_weight,
    gain_two, seq_lengths, seq_replica,
):
    x, zh, core = lax.axis_index("x"), lax.axis_index("zh"), lax.axis_index("core")
    y, zl = lax.axis_index("y"), lax.axis_index("zl")
    idx = jnp.stack([x, zh, y, core]).astype(jnp.int32)

    tok = tokens.astype(F32)
    s_one = inverse_rms(tok)
    begin, position = replica_layout(seq_lengths, seq_replica, (y * 2 + zl) * 2 + core)
    half_rows = lambda v: lax.dynamic_index_in_dim(v.reshape(4, 2, BLK), zh, 1, False).reshape(ROWS, 1)
    first = jnp.tile(half_rows(begin)[3 * BLK :, 0], 8).reshape(1, QALL)
    lane = jnp.arange(128, dtype=jnp.int32)
    frequency = ROTARY_BASE ** (-(lane % 32).astype(F32) * (2.0 / HD))
    angles = half_rows(position).astype(F32) * frequency[None, :]
    cosine = jnp.cos(angles)
    sine = jnp.where((lane % HD) < HD // 2, -1.0, 1.0)[None, :] * jnp.sin(angles)

    qkv_got = fetch_half(qkv_weight, core)
    normed_one = gather_x((tok * s_one * gain_one).astype(BF16), (cosine,))
    slot = y * 2 + core
    eighth = lambda w: lax.dynamic_slice_in_dim(w, slot * (w.shape[0] // 8), w.shape[0] // 8, 0)
    spread = lambda v: lax.all_gather(v, ("y", "core"), axis=0, tiled=True)
    first_row = jnp.minimum(slot * DOWN_ROWS, FF4 // 2 - DOWN_ROWS)
    some = jnp.concatenate(
        [eighth(out_weight), lax.dynamic_slice_in_dim(down_weight, first_row, DOWN_ROWS, 0)], 0
    )
    some = lax.ppermute(some, "zh", shift(2, 1))
    far_rows = spread(tie(some, qkv_got, normed_one[2], normed_one[3])).reshape(8, OUT_ROWS + DOWN_ROWS, D)
    out_all, down_all = (out_weight, far_rows), (down_weight, far_rows)
    swap = lambda v, *deps: lax.ppermute(tie(v, *deps), "core", shift(2, 1))
    qkv_all = qkv_weight, qkv_got, swap(qkv_got, some, normed_one[2], normed_one[3])

    q, kv_own = qkv_forward(idx, normed_one, qkv_all, cosine, sine)
    cot = tie(cotangent, normed_one[2], normed_one[3])
    cots = [cotangent] + [lax.ppermute(cot, "x", shift(4, -k)) for k in (1, 2, 3)]
    kv_par = lax.ppermute(kv_own, "zh", shift(2, 1))
    rows = DH // 8
    cross = [(2 * a + b, 2 * (1 - a) + (1 - b)) for a in range(2) for b in range(2)]
    gate_up = lax.ppermute(
        jnp.concatenate(
            [
                eighth(tie(gate_weight, kv_own)),
                jnp.zeros((rows, GAP - FF4), BF16),
                eighth(tie(up_weight, kv_own)),
            ],
            1,
        ),
        ("zl", "zh"),
        cross,
    )
    att, qx = attend(idx, q, kv_own, kv_par, first)
    parts = out_project(idx, tie(att, *cots), out_all)
    gate_up = spread(tie(gate_up, parts[2]))
    p0, q1, q3 = relay(parts)
    after_attn, normed_two = row_call(
        norm_two_body,
        (sds((BLK, D), F32), sds((BLK, D))),
        tokens, *last_step(p0, q1, q3), gain_two.reshape(1, D), name="norm_two",
    )
    normed_two = gather_x(normed_two)
    hid, dgate, dup = ffn(idx, normed_two, cots, gate_weight, up_weight, gate_up, down_all)
    d_parts = ffn_back(idx, dgate, dup, gate_weight, up_weight, gate_up)
    own_grads = down_grads(cots, tie(hid, d_parts[2]))
    d_own, q1, q3 = relay(d_parts)
    own_grads = gate_up_grads(normed_two, tie(dgate, q1, q3), dup, own_grads)
    d_two = last_step(d_own, q1, q3)
    grads = lax.psum_scatter(
        tie(own_grads, *d_two).reshape(32, PIECE, 128),
        ("zh", "zl", "y", "core"), scatter_dimension=0, tiled=True,
    )
    after_grad, branch, gain_grad_two = row_call(
        norm_back_body,
        (sds((BLK, D), F32), sds((BLK, D)), sds((1, D), F32)),
        cotangent, after_attn, *d_two, gain_two.reshape(1, D), name="norm_back_two",
    )
    branch = gather_x(branch)
    layer_parts = down_project(idx, tie(hid, after_grad), down_all)
    att = tie(att, *layer_parts)
    layer = [
        lax.ppermute(tie(layer_parts[k], branch[2], branch[3]), "x", shift(4, k)) for k in (1, 3)
    ]
    dqm, dkv_own, dkv_par = attend_back(
        idx, qx, kv_own, kv_par, first, att, cosine, sine, branch, out_all
    )
    dkv_got = lax.ppermute(dkv_par, "zh", shift(2, 1))
    tail = attn_grads(
        idx, normed_one, branch, dqm.reshape(ROWS, AW), tie(att, *layer).reshape(ROWS, AW)
    )
    dkv_got = tie(dkv_got, tail[0])
    *tail_kv, parts = qkv_back(
        idx, dqm.reshape(ROWS, AW), dkv_own, dkv_got, cosine, sine, qkv_all, normed_one, gain_one,
        gain_grad_two,
    )
    over_x = lambda v: sum((tie(lax.ppermute(v, "x", shift(4, s)), grad_gate) for s in (1, 2, 3)), v)
    finish = lambda d_one: row_call(
        norm_back_body,
        (sds((BLK, D), F32), sds((BLK, D)), sds((1, D), F32)),
        after_grad, tokens, *d_one, gain_one.reshape(1, D), name="norm_back_one",
    )[1]
    summed, input_grad, (grad_qkv, grad_out, gains) = sum_tail(
        idx, (tail[0], tie(tail[1], dkv_got)), tail_kv, parts, finish
    )
    layer.append(lax.ppermute(tie(layer_parts[2], summed), "x", shift(4, 2)))
    grads = lax.all_gather(tie(grads, summed), ("zl", "y", "core"), axis=0, tiled=True)
    grad_gate, grad_up, grad_down = unpack(grads)
    layer_out = sum((v.astype(F32) for v in layer), after_attn + layer_parts[0].astype(F32))
    layer_out = layer_out.astype(BF16)
    gains = over_x(gains)
    return (
        layer_out, input_grad, gains[0], grad_qkv, grad_out, grad_gate, grad_up,
        grad_down, gains[1],
    )


def solution(mesh):
    grid = Mesh(mesh.devices.reshape(SIZES), AXES)
    rows = P(AXES, None)
    both = P(("x", "zh"), None)
    return jax.shard_map(
        on_device,
        mesh=grid,
        in_specs=(
            rows, rows, P(), P("zh", "x"), both, P("zh", "x"), P("zh", "x"), both, P(), P(), P(),
        ),
        out_specs=(
            rows, rows, P(), P("zh", "x"), both, P("zh", "x"), P("zh", "x"), both, P(),
        ),
        check_vma=False,
    )
```

```python
import jax
import jax.numpy as jnp
from jax import lax
from jax.experimental import pallas as pl
from jax.experimental.pallas import tpu as pltpu
from jax.sharding import Mesh
from jax.sharding import PartitionSpec as P

HEADS = 32
KV = 4
HD = 64
EPSILON = 1e-05
ROTARY_BASE = 10000.0
MASKED = -1e30

AXES = ("y", "zl", "core", "x", "zh")
SIZES = (4, 2, 2, 4, 2)
BLK = 160
HALF = BLK // 2
ROWS = 4 * BLK
CAP = 2 * ROWS
D = 2048
DH = D // 2
QW = 640
AW = 512
FF4 = 1408
TILE = 256
F32 = jnp.float32
BF16 = jnp.bfloat16
VLIM = 60 * 1024 * 1024


def spec(memory=pltpu.VMEM):
    return pl.BlockSpec(memory_space=memory)


def params(**kw):
    return pltpu.CompilerParams(vmem_limit_bytes=VLIM, **kw)


def cost(flops, nbytes):
    return pl.CostEstimate(flops=int(flops), bytes_accessed=int(nbytes), transcendentals=0)


def sds(shape, dtype=BF16):
    return jax.ShapeDtypeStruct(shape, dtype)


def dot(a, b):
    return jnp.dot(a, b, preferred_element_type=F32)


def dot_t(a, b):
    return lax.dot_general(a, b, (((1,), (1,)), ((), ())), preferred_element_type=F32)


def t_dot(a, b):
    return lax.dot_general(a, b, (((0,), (0,)), ((), ())), preferred_element_type=F32)


def tie(v, *deps):
    return lax.optimization_barrier((v,) + deps)[0]


def shift(n, s):
    return [(i, (i + s) % n) for i in range(n)]


def gather_x(v, wait=()):
    from_prev = lax.ppermute(v, "x", shift(4, 1))
    from_next = lax.ppermute(v, "x", shift(4, -1))
    send_a = tie(from_prev[:HALF], from_next, *wait)
    send_b = tie(from_next[HALF:], from_prev, *wait)
    opp_a = lax.ppermute(send_a, "x", shift(4, 1))
    opp_b = lax.ppermute(send_b, "x", shift(4, -1))
    return v, from_next, opp_a, opp_b, from_prev


def relay_body(p1, got_a, p3, got_b, q1, q3):
    q1[...] = (p1[...].astype(F32) + got_a[...].astype(F32)).astype(BF16)
    q3[...] = (p3[...].astype(F32) + got_b[...].astype(F32)).astype(BF16)


def relay(parts):
    p0, p1, p2a, p2b, p3 = parts
    got_a = lax.ppermute(p2a, "x", shift(4, 1))
    got_b = lax.ppermute(p2b, "x", shift(4, -1))
    half = lambda k: pl.BlockSpec((HALF, D), lambda i: (k, 0))
    q1, q3 = pl.pallas_call(
        relay_body,
        grid=(1,),
        out_shape=(sds((BLK, D)),) * 2,
        in_specs=[half(0), half(0), half(1), half(0)],
        out_specs=(half(0), half(1)),
        input_output_aliases={0: 0, 2: 1},
        compiler_params=params(),
        cost_estimate=cost(1e6, 2e6),
        name="relay",
    )(p1, got_a, p3, got_b)
    return p0, q1, q3


def scatter_x(parts):
    return last_step(*relay(parts))


def last_step(p0, q1, q3):
    return p0, lax.ppermute(q1, "x", shift(4, 1)), lax.ppermute(q3, "x", shift(4, -1))


PIECES = ((0, BLK), (1, BLK), (2, HALF), (2, HALF), (3, BLK))
PIECE_ROW = (0, BLK, 2 * BLK, 2 * BLK + HALF, 3 * BLK)


def part_shapes(width, dtype=BF16):
    return tuple(sds((n, width), dtype) for _, n in PIECES)


def low_lanes(shape):
    return lax.broadcasted_iota(jnp.int32, shape, 1) < HD


def swap_halves(v):
    lane = lax.broadcasted_iota(jnp.int32, v.shape, 1) % HD
    return jnp.where(lane < HD // 2, pltpu.roll(v, 128 - HD // 2, 1), pltpu.roll(v, HD // 2, 1))


def rows_at(block):
    return pl.ds(pl.multiple_of(block * BLK, 32), BLK)


def fetch_half(w, core):
    half = w.shape[0] // 2
    return lax.ppermute(lax.dynamic_slice_in_dim(w, core * half, half, 0), "zh", shift(2, 1))


OUT_ROWS = AW // 2 // 8
DOWN_ROWS = 96


def out_rows_spec():
    return pl.BlockSpec((8, OUT_ROWS, D), lambda i: (0, 0, 0))


def own_and_partner(idx, rows):
    zh = idx[1]
    at = lambda k: pl.ds(pl.multiple_of(k * rows, rows), rows)
    return at(zh), at(1 - zh)


def weight_rows(idx, rows):
    zh, core = idx[1], idx[3]
    far = (1 - zh) * rows
    half = rows // 2
    at = lambda first, n: pl.ds(pl.multiple_of(first, half), n)
    return at(zh * rows, rows), at(far + core * half, half), at(far + (1 - core) * half, half)


def qkv_body(idx, n0, n1, n2a, n2b, n3, w0, w1, w2, cosine, sine, q_ref, kv_ref, rows):
    x = idx[0]
    lo = low_lanes((BLK, 128))
    for ref, row, (_, n) in zip((n0, n1, n2a, n2b, n3), PIECE_ROW, PIECES):
        rows[row : row + n, :] = ref[...]
    s0, s1, s2 = weight_rows(idx, DH)
    acc = dot(rows[:, s0], w0[...]) + dot(rows[:, s1], w1[...]) + dot(rows[:, s2], w2[...])
    for d in range(4):
        at = rows_at((x + d) & 3)
        cs = cosine[at, :]
        sn = sine[at, :]
        for p in range(5):
            v = acc[d * BLK : (d + 1) * BLK, p * 128 : (p + 1) * 128]
            r = v * cs + swap_halves(v) * sn
            if p < 4:
                r = r * (HD**-0.5 * LOG2E)
                a = (x + d) & 3
                for k, w in enumerate((r, pltpu.roll(r, HD, 1))):
                    head = slice((2 * p + k) * BLK, (2 * p + k + 1) * BLK)
                    q_ref[a, head, :] = jnp.where(lo, w, 0.0).astype(BF16)
            else:
                kv_ref[at, :] = jnp.where(lo, r, v).astype(BF16)


def qkv_forward(idx, pieces, weight, cosine, sine):
    return pl.pallas_call(
        qkv_body,
        out_shape=(sds((4, QALL, 128)), sds((ROWS, 128))),
        in_specs=[spec(pltpu.SMEM)] + [spec()] * 10,
        out_specs=(spec(), spec()),
        scratch_shapes=[pltpu.VMEM((ROWS, D), BF16)],
        compiler_params=params(),
        cost_estimate=cost(2 * ROWS * D * QW, 7e6),
        name="qkv_forward",
    )(idx, *pieces, *weight, cosine, sine)


QALL = 8 * BLK
PAIR = 2 * BLK
LOG2E = 1.4426950408889634
LN2 = 0.6931471805599453


def split3(v):
    a = v.astype(BF16).astype(F32)
    b = (v - a).astype(BF16).astype(F32)
    return a, b, v - a - b


def with_lanes(v, parts):
    lane = lax.broadcasted_iota(jnp.int32, v.shape, 1)
    out = jnp.where(lane < HD, v, 0.0)
    for k, part in enumerate(parts):
        out = jnp.where(lane == HD + k, part, out)
    return out


def spread_keys(zh, kv_own, kv_par, kk, vv, fill):
    shape = (BLK, 128)
    lo = low_lanes(shape)
    rest = fill(lax.broadcasted_iota(jnp.int32, shape, 1) - HD)
    for j in range(4):
        for src, off in ((kv_own, zh), (kv_par, 1 - zh)):
            v = src[j * BLK : (j + 1) * BLK, :].astype(F32)
            at = rows_at(2 * j + off)
            kk[at, :] = jnp.where(lo, v, rest).astype(BF16)
            vv[at, :] = jnp.where(lo, pltpu.roll(v, HD, 1), rest).astype(BF16)


def masked(s, zh, j, kb, first):
    if j < 3 and kb < j:
        return s
    u = kb * PAIR + lax.broadcasted_iota(jnp.int32, (PAIR, QALL), 0)
    allowed = None
    if kb == j:
        t = (2 * j + zh) * BLK + lax.broadcasted_iota(jnp.int32, (1, QALL), 1) % BLK
        allowed = u <= t
    if j == 3:
        later = u >= first[...]
        allowed = later if allowed is None else allowed & later
    return jnp.where(allowed, s, MASKED)


def attend_body(idx, q, kv_own, kv_par, first, att, qx, kk, vv, vt, s_ref, e_ref):
    x, zh = idx[0], idx[1]
    spread_keys(zh, kv_own, kv_par, kk, vv, lambda lane: 1.0)
    vt[...] = vv[...].T
    lo = low_lanes((BLK, 128))
    for j in range(4):
        n = PAIR * (j + 1)
        qj = q[j]
        top = jnp.full((1, QALL), MASKED, F32)
        for kb in range(j + 1):
            rows = slice(kb * PAIR, (kb + 1) * PAIR)
            s = masked(dot_t(kk[rows, :], qj), zh, j, kb, first)
            s_ref[rows, :] = s
            top = jnp.maximum(top, jnp.max(s, axis=0, keepdims=True))
        for k in range(n // 64):
            rows = slice(k * 64, (k + 1) * 64)
            e_ref[rows, :] = jnp.exp2(s_ref[rows, :] - top).astype(BF16)
        o = dot(vt[:, :n], e_ref[:n, :])
        lse = split3(top + jnp.log(o[HD : HD + 1, :]) * LOG2E)
        row = lax.broadcasted_iota(jnp.int32, (128, QALL), 0)
        extra = jnp.zeros((128, QALL), F32)
        for k, part in enumerate(lse):
            extra = jnp.where(row == HD + k, part, extra)
        qx[j] = (qj.astype(F32) + extra.T).astype(BF16)
        o = o.T
        r = pltpu.roll(o, HD, 1)
        rel = (j - x) & 3
        for p in range(4):
            even, odd = slice(2 * p * BLK, (2 * p + 1) * BLK), slice((2 * p + 1) * BLK, (2 * p + 2) * BLK)
            num = jnp.where(lo, o[even], r[odd])
            den = jnp.where(lo, r[even], o[odd])
            att[rel, :, p * 128 : (p + 1) * 128] = (num / den).astype(BF16)


def attend(idx, q, kv_own, kv_par, first):
    return pl.pallas_call(
        attend_body,
        out_shape=(sds((4, BLK, AW)), sds((4, QALL, 128))),
        in_specs=[spec(pltpu.SMEM)] + [spec()] * 4,
        out_specs=(spec(), spec()),
        scratch_shapes=[
            pltpu.VMEM((CAP, 128), BF16),
            pltpu.VMEM((CAP, 128), BF16),
            pltpu.VMEM((128, CAP), BF16),
            pltpu.VMEM((CAP, QALL), F32),
            pltpu.VMEM((CAP, QALL), BF16),
        ],
        compiler_params=params(),
        cost_estimate=cost(1.2e10, 3e6),
        name="attend",
    )(idx, q, kv_own, kv_par, first)


def store_parts(res, refs):
    for ref, row, (_, n) in zip(refs, PIECE_ROW, PIECES):
        ref[...] = res[row : row + n].astype(BF16)


def out_body(idx, att, w0, w1, o0, o1, o2a, o2b, o3):
    slots = own_and_partner(idx, AW // 2)
    weights = w0[...], w1[...].reshape(AW // 2, D)
    for d, ref in ((2, None), (1, o1), (3, o3), (0, o0)):
        a = att.at[d]
        res = sum(dot(a[:, s], w) for s, w in zip(slots, weights)).astype(BF16)
        if d == 2:
            o2a[...] = res[:HALF]
            o2b[...] = res[HALF:]
        else:
            ref[...] = res


def out_project(idx, att, weight):
    return pl.pallas_call(
        out_body,
        grid=(1,),
        out_shape=part_shapes(D),
        in_specs=[spec(pltpu.SMEM), spec(), spec(), out_rows_spec()],
        out_specs=(spec(),) * 5,
        compiler_params=params(),
        cost_estimate=cost(2 * ROWS * D * AW, 5.5e6),
        name="out_project",
    )(idx, att, *weight)


def stack_heads(v):
    return v, pltpu.roll(v, HD, 1)


def attend_back_body(
    idx, qx, kv_own, kv_par, first, att, cosine, sine, b0, b1, b2a, b2b, b3, w0, w1,
    dq_ref, dkv_own, dkv_par, kk, vv, dout, do_all, dkk, dvv, e_ref, ds_ref, dq_acc,
):
    x, zh = idx[0], idx[1]
    spread_keys(zh, kv_own, kv_par, kk, vv, lambda lane: jnp.where(lane < 3, -1.0, 0.0))
    slots = own_and_partner(idx, AW // 2)
    weights = w0[...], w1[...].reshape(AW // 2, D)
    for d in range(4):
        if d == 2:
            rows = jnp.concatenate([b2a[...], b2b[...]], 0)
        else:
            rows = (b0, b1, None, b3)[d][...]
        at = rows_at((x + d) & 3)
        for s, w in zip(slots, weights):
            dout[at, s] = dot_t(rows, w).astype(BF16)
    lo = low_lanes((BLK, 128))
    for j in range(4):
        rel = (j - x) & 3
        here = slice(j * BLK, (j + 1) * BLK)
        for p in range(4):
            cols = slice(p * 128, (p + 1) * 128)
            do = dout[here, cols].astype(F32)
            prod = do * att[rel, :, cols].astype(F32)
            for k, (v, w) in enumerate(zip(stack_heads(do), stack_heads(prod))):
                delta = jnp.sum(jnp.where(lo, w, 0.0), axis=1, keepdims=True)
                head = slice((2 * p + k) * BLK, (2 * p + k + 1) * BLK)
                do_all[head, :] = with_lanes(v, split3(delta)).astype(BF16)
        for kb in range(j + 1):
            rows = slice(kb * PAIR, (kb + 1) * PAIR)
            e = jnp.exp2(masked(dot_t(kk[rows, :], qx[j]), zh, j, kb, first))
            e_ref[...] = e.astype(BF16)
            ds_ref[...] = (e * dot_t(vv[rows, :], do_all[...])).astype(BF16)
            dv = dot(e_ref[...], do_all[...])
            dk = dot(ds_ref[...], qx[j])
            dq = t_dot(ds_ref[...], kk[rows, :])
            if kb == j:
                dvv[rows, :], dkk[rows, :] = dv, dk
            else:
                dvv[rows, :] += dv
                dkk[rows, :] += dk
            if kb == 0:
                dq_acc[...] = dq
            else:
                dq_acc[...] += dq
        for p in range(4):
            even, odd = slice(2 * p * BLK, (2 * p + 1) * BLK), slice((2 * p + 1) * BLK, (2 * p + 2) * BLK)
            v = jnp.where(lo, dq_acc[even, :], pltpu.roll(dq_acc[odd, :], HD, 1)) * HD**-0.5
            v = v * cosine[here, :] - swap_halves(v) * sine[here, :]
            dq_ref[rel, :, p * 128 : (p + 1) * 128] = v.astype(BF16)
    for j in range(4):
        for dst, off in ((dkv_own, zh), (dkv_par, 1 - zh)):
            at = rows_at(2 * j + off)
            both = jnp.where(lo, dkk[at, :] * LN2, pltpu.roll(dvv[at, :], HD, 1))
            dst[j * BLK : (j + 1) * BLK, :] = both.astype(dst.dtype)


def attend_back(idx, qx, kv_own, kv_par, first, att, cosine, sine, branch, weight):
    return pl.pallas_call(
        attend_back_body,
        grid=(1,),
        out_shape=(sds((4, BLK, AW)), sds((ROWS, 128), F32), sds((ROWS, 128))),
        in_specs=[spec(pltpu.SMEM)] + [spec()] * 13 + [out_rows_spec()],
        out_specs=(spec(),) * 3,
        scratch_shapes=[
            pltpu.VMEM((CAP, 128), BF16),
            pltpu.VMEM((CAP, 128), BF16),
            pltpu.VMEM((ROWS, AW), BF16),
            pltpu.VMEM((QALL, 128), BF16),
            pltpu.VMEM((CAP, 128), F32),
            pltpu.VMEM((CAP, 128), F32),
            pltpu.VMEM((PAIR, QALL), BF16),
            pltpu.VMEM((PAIR, QALL), BF16),
            pltpu.VMEM((QALL, 128), F32),
        ],
        compiler_params=params(),
        cost_estimate=cost(3e10, 8e6),
        name="attend_back",
    )(idx, qx, kv_own, kv_par, first, att, cosine, sine, *branch, *weight)


def qkv_back_body(
    idx, dqm, dkv_own, dkv_got, cosine, sine, w0, w1, w2, n0, n1, n2a, n2b, n3, gain_one,
    gain_grad_two,
    mine, theirs, o0, o1, o2a, o2b, o3, n_all, dkv, grad, gains,
):
    x, y, core = idx[0], idx[2], idx[3]
    lo = low_lanes((BLK, 128))
    for ref, row, (_, n) in zip((n0, n1, n2a, n2b, n3), PIECE_ROW, PIECES):
        n_all[row : row + n, :] = ref[...]
    for d in range(4):
        at = rows_at((x + d) & 3)
        v = dkv_own[at, :] + dkv_got[at, :].astype(F32)
        v = jnp.where(lo, v * cosine[at, :] - swap_halves(v) * sine[at, :], v).astype(BF16)
        dkv[d * BLK : (d + 1) * BLK, :] = v
    rows = jnp.concatenate([dqm[...], dkv[...]], 1)
    for s, w in zip(weight_rows(idx, DH), (w0, w1, w2)):
        for c in range(w.shape[0] // 512):
            cols = pl.ds(pl.multiple_of(s.start + c * 512, 512), 512)
            res = dot_t(rows, w[c * 512 : (c + 1) * 512, :])
            part = (res * n_all[:, cols].astype(F32)).reshape(ROWS // 8, 8, 512)
            gains[0:1, cols] = jnp.sum(jnp.sum(part, axis=0), axis=0, keepdims=True) / gain_one[:, cols]
            store_parts(res, [r.at[:, cols] for r in (o0, o1, o2a, o2b, o3)])
    grad[...] = dot(dkv[...].T, n_all[...]).astype(BF16)
    gains[1:2, :] = gain_grad_two[...]
    for s in range(4):
        for k, ref in enumerate((mine, theirs)):
            p = ((y + s) & 3) * 2 + (core if k == 0 else 1 - core)
            both = gains[:, pl.ds(pl.multiple_of(p * 256, 256), 256)]
            both = jnp.concatenate([both[:, :128], both[:, 128:], jnp.zeros((12, 128), F32)], 0)
            for h in range(2):
                ref[s, h, :128, :] = grad[:, pl.ds(pl.multiple_of(h * DH + p * 128, 128), 128)]
                ref[s, h, 128:, :] = both.astype(BF16)


def qkv_back(idx, dqm, dkv_own, dkv_got, cosine, sine, weight, pieces, gain_one, gain_grad_two):
    res = pl.pallas_call(
        qkv_back_body,
        out_shape=(sds((4, 2, KVP, 128)),) * 2 + part_shapes(D),
        in_specs=[spec(pltpu.SMEM)] + [spec()] * 15,
        out_specs=(spec(),) * 7,
        scratch_shapes=[
            pltpu.VMEM((ROWS, D), BF16),
            pltpu.VMEM((ROWS, 128), BF16),
            pltpu.VMEM((128, D), BF16),
            pltpu.VMEM((2, D), F32),
        ],
        compiler_params=params(),
        cost_estimate=cost(2 * ROWS * D * QW, 1.3e7),
        name="qkv_back",
    )(
        idx, dqm, dkv_own, dkv_got, cosine, sine, *weight, *pieces,
        gain_one.reshape(1, D), gain_grad_two.reshape(1, D),
    )
    return res[0], res[1], res[2:]


TILES = 6
GAP = TILES * TILE


def load_down(idx, own, far, dst, sem):
    half = FF4 // 2
    zh = idx[1]
    at = lambda first, n: pl.ds(pl.multiple_of(first, 32), n)
    copies = [pltpu.make_async_copy(own, dst.at[at(zh * half, half)], sem.at[8])]
    for k in range(8):
        first = min(k * DOWN_ROWS, half - DOWN_ROWS)
        skip = k * DOWN_ROWS - first
        n = DOWN_ROWS - skip
        source = far.at[k, OUT_ROWS + skip : OUT_ROWS + DOWN_ROWS]
        copies.append(pltpu.make_async_copy(source, dst.at[at((1 - zh) * half + first + skip, n)], sem.at[k]))
    return copies


def ffn_body(
    idx, n0, n1, n2a, n2b, n3, c0, c1, c2, c3, gate_own, up_own, gate_par, up_par, w0, w1,
    hid, dgate, dup, n_all, c_all, down, sem,
):
    i = pl.program_id(0)
    zh = idx[1]

    @pl.when(i == 0)
    def _():
        copies = load_down(idx, w0, w1, down, sem)
        for c in copies:
            c.start()
        for ref, row, (_, n) in zip((n0, n1, n2a, n2b, n3), PIECE_ROW, PIECES):
            n_all[row : row + n, :] = ref[...]
        for d, ref in enumerate((c0, c1, c2, c3)):
            c_all[d * BLK : (d + 1) * BLK, :] = ref[...]
        for c in copies:
            c.wait()

    own = n_all[:, pl.ds(pl.multiple_of(zh * DH, DH), DH)]
    par = n_all[:, pl.ds(pl.multiple_of((1 - zh) * DH, DH), DH)]
    gate = dot(own, gate_own[...]) + dot(par, gate_par[...])
    up = dot(own, up_own[...]) + dot(par, up_par[...])
    dh = dot_t(c_all[...], down[pl.ds(pl.multiple_of(i * TILE, TILE), TILE), :])
    sig = 1.0 / (1.0 + jnp.exp(-gate))
    act = gate * sig
    hid[...] = (act * up).astype(BF16)
    dgate[...] = (dh * up * sig * (1.0 + gate * (1.0 - sig))).astype(BF16)
    dup[...] = (dh * act).astype(BF16)


def whole(n, w):
    return pl.BlockSpec((n, w), lambda i: (0, 0))


def ffn(idx, normed, cots, gate, up, gate_up, down):
    column = lambda first: pl.BlockSpec((DH, TILE), lambda i: (0, i + first))
    hidden = pl.BlockSpec((ROWS, TILE), lambda i: (0, i))
    return pl.pallas_call(
        ffn_body,
        grid=(TILES,),
        out_shape=(sds((ROWS, FF4)),) * 3,
        in_specs=[spec(pltpu.SMEM)]
        + [whole(n, D) for _, n in PIECES]
        + [whole(BLK, D)] * 4
        + [column(0), column(0), column(0), column(TILES)]
        + [spec(pl.ANY)] * 2,
        out_specs=[hidden] * 3,
        scratch_shapes=[
            pltpu.VMEM((ROWS, D), BF16),
            pltpu.VMEM((ROWS, D), BF16),
            pltpu.VMEM((GAP, D), BF16),
            pltpu.SemaphoreType.DMA((9,)),
        ],
        compiler_params=params(),
        cost_estimate=cost(6 * ROWS * D * FF4, 3.4e7),
        name="ffn",
    )(idx, *normed, *cots, gate, up, gate_up, gate_up, *down)


def down_body(idx, hid, w0, w1, o0, o1, o2, o3, down, sem):
    copies = load_down(idx, w0, w1, down, sem)
    for c in copies:
        c.start()
    for c in copies:
        c.wait()
    for n in range(D // 512):
        cols = slice(n * 512, (n + 1) * 512)
        res = dot(hid[...], down[:, cols]).astype(BF16)
        for d, ref in enumerate((o0, o1, o2, o3)):
            ref[:, cols] = res[d * BLK : (d + 1) * BLK]


def down_project(idx, hid, down):
    return pl.pallas_call(
        down_body,
        out_shape=(sds((BLK, D)),) * 4,
        in_specs=[spec(pltpu.SMEM), spec()] + [spec(pl.ANY)] * 2,
        out_specs=(spec(),) * 4,
        scratch_shapes=[pltpu.VMEM((FF4, D), BF16), pltpu.SemaphoreType.DMA((9,))],
        compiler_params=params(),
        cost_estimate=cost(2 * ROWS * D * FF4, 1.1e7),
        name="down_project",
    )(idx, hid, *down)


def ffn_back_body(idx, dgate, dup, gate_own, up_own, par, *refs):
    half = pl.num_programs(0) // 2

    @pl.when(pl.program_id(0) < half)
    def _():
        store_parts(dot_t(dgate[...], gate_own[...]) + dot_t(dup[...], up_own[...]), refs)

    @pl.when(pl.program_id(0) >= half)
    def _():
        store_parts(dot_t(dgate[...], par[:, :FF4]) + dot_t(dup[...], par[:, GAP:]), refs)


def ffn_back(idx, dgate, dup, gate, up, gate_up):
    half = DH // TILE
    rows = pl.BlockSpec((ROWS, FF4), lambda i, idx: (0, 0))
    own = pl.BlockSpec((TILE, FF4), lambda i, idx: (jnp.minimum(i, half - 1), 0))
    par = pl.BlockSpec((TILE, GAP + FF4), lambda i, idx: (jnp.maximum(i - half, 0), 0))
    place = lambda i, idx: (0, i ^ (idx[1] * half))
    return pl.pallas_call(
        ffn_back_body,
        grid_spec=pltpu.PrefetchScalarGridSpec(
            num_scalar_prefetch=1,
            grid=(D // TILE,),
            in_specs=[rows, rows, own, own, par],
            out_specs=[pl.BlockSpec((n, TILE), place) for _, n in PIECES],
        ),
        out_shape=part_shapes(D),
        compiler_params=params(),
        cost_estimate=cost(4 * ROWS * D * FF4, 1.8e7),
        name="ffn_back",
    )(idx, dgate, dup, gate, up, gate_up)


GU_ROWS = FF4 // 128 * 64
PIECE = 2 * GU_ROWS + FF4 // 2
QS = 4


def gate_up_grads_body(*refs):
    na, nb = refs[0:5], refs[5:10]
    dgate, dup, _, out = refs[10:]
    stack = lambda parts: jnp.concatenate([r[...] for r in parts], 0)
    rows = jnp.concatenate([stack(na), stack(nb)], 1).T
    for k, ref in enumerate((dgate, dup)):
        g = dot(rows, ref[...]).astype(BF16)
        for h in range(2):
            for q in range(QS):
                r = g[(QS * h + q) * 64 : (QS * h + q + 1) * 64]
                for c in range(FF4 // 128):
                    first = k * GU_ROWS + c * 64
                    out[h, q, first : first + 64, :] = r[:, c * 128 : (c + 1) * 128]


def gate_up_grads(normed, dgate, dup, pieces):
    return pl.pallas_call(
        gate_up_grads_body,
        grid=(16 // QS,),
        out_shape=sds((2, 16, PIECE, 128)),
        in_specs=[pl.BlockSpec((n, 64 * QS), lambda i: (0, i)) for _, n in PIECES]
        + [pl.BlockSpec((n, 64 * QS), lambda i: (0, i + 16 // QS)) for _, n in PIECES]
        + [whole(ROWS, FF4)] * 2
        + [spec(pl.ANY)],
        out_specs=pl.BlockSpec((2, QS, 2 * GU_ROWS, 128), lambda i: (0, i, 0, 0)),
        input_output_aliases={12: 0},
        compiler_params=params(),
        cost_estimate=cost(4 * ROWS * D * FF4, 2e7),
        name="gate_up_grads",
    )(*normed, *normed, dgate, dup, pieces)


def down_grads_body(*refs):
    cots = refs[0:4]
    hid, out, hid_t = refs[4:]

    @pl.when(pl.program_id(0) == 0)
    def _():
        hid_t[...] = hid[...].T

    g = dot(hid_t[...], jnp.concatenate([r[...] for r in cots], 0)).astype(BF16)
    for h in range(2):
        for q in range(QS):
            out[h, q, :, :] = g[h * (FF4 // 2) : (h + 1) * (FF4 // 2), q * 128 : (q + 1) * 128]


def down_grads(cots, hid):
    return pl.pallas_call(
        down_grads_body,
        grid=(16 // QS,),
        out_shape=sds((2, 16, PIECE, 128)),
        in_specs=[pl.BlockSpec((BLK, 128 * QS), lambda i: (0, i))] * 4 + [whole(ROWS, FF4)],
        out_specs=pl.BlockSpec((2, QS, FF4 // 2, 128), lambda i: (0, i, 2, 0)),
        scratch_shapes=[pltpu.VMEM((FF4, ROWS), BF16)],
        compiler_params=params(),
        cost_estimate=cost(2 * ROWS * D * FF4, 1e7),
        name="down_grads",
    )(*cots, hid)


def unpack_body(piece, gate, up, down):
    for q in range(QS):
        rows = slice(q * 64, (q + 1) * 64)
        for k, ref in enumerate((gate, up)):
            for c in range(FF4 // 128):
                first = k * GU_ROWS + c * 64
                ref[rows, c * 128 : (c + 1) * 128] = piece[q, first : first + 64, :].astype(F32)
        down[:, q * 128 : (q + 1) * 128] = piece[q, 2 * GU_ROWS :, :].astype(F32)


def unpack(pieces):
    return pl.pallas_call(
        unpack_body,
        grid=(16 // QS,),
        out_shape=(sds((DH, FF4), F32), sds((DH, FF4), F32), sds((FF4 // 2, D), F32)),
        in_specs=[pl.BlockSpec((QS, PIECE, 128), lambda i: (i, 0, 0))],
        out_specs=[
            pl.BlockSpec((64 * QS, FF4), lambda i: (i, 0)),
            pl.BlockSpec((64 * QS, FF4), lambda i: (i, 0)),
            pl.BlockSpec((FF4 // 2, 128 * QS), lambda i: (0, i)),
        ],
        compiler_params=params(),
        cost_estimate=cost(1e6, 2.6e7),
        name="unpack",
    )(pieces)


QP = 4 * 128
OP = 2 * (AW // 2)
QOP = QP + OP
KVP = 128 + 16
TAIL = QOP + KVP


def attn_grads_body(idx, *refs):
    na, nb, branch = refs[0:5], refs[5:10], refs[10:15]
    dqm, att, mine, theirs, att_t = refs[15:]
    core = idx[3]

    @pl.when(pl.program_id(0) == 0)
    def _():
        att_t[...] = att[...].T

    stack = lambda parts: jnp.concatenate([r[...] for r in parts], 0)

    def store(h, first, n, zero, one):
        mine[0, h, first : first + n, :] = jnp.where(core == 0, zero, one)
        theirs[0, h, first : first + n, :] = jnp.where(core == 0, one, zero)

    for h, cols in enumerate((na, nb)):
        g = dot(stack(cols).T, dqm[...]).astype(BF16)
        for c in range(4):
            lanes = slice(c * 128, (c + 1) * 128)
            store(h, c * 128, 128, g[:128, lanes], g[128:, lanes])
    g = dot(att_t[...], stack(branch)).astype(BF16)
    for h in range(2):
        r = g[h * (AW // 2) : (h + 1) * (AW // 2)]
        for c in range(2):
            lanes = lambda k: slice(k * 256 + c * 128, k * 256 + (c + 1) * 128)
            store(h, QP + c * (AW // 2), AW // 2, r[:, lanes(0)], r[:, lanes(1)])


def attn_grads(idx, normed, branch, dqm, att):
    turn = lambda s, idx: (s + idx[2]) & 3
    piece = pl.BlockSpec((1, 2, QOP, 128), lambda s, idx: (s, 0, 0, 0))
    fixed = pl.BlockSpec((ROWS, AW), lambda s, idx: (0, 0))
    return pl.pallas_call(
        attn_grads_body,
        grid_spec=pltpu.PrefetchScalarGridSpec(
            num_scalar_prefetch=1,
            grid=(4,),
            in_specs=[pl.BlockSpec((n, 256), lambda s, idx: (0, turn(s, idx))) for _, n in PIECES]
            + [pl.BlockSpec((n, 256), lambda s, idx: (0, turn(s, idx) + 4)) for _, n in PIECES]
            + [pl.BlockSpec((n, 512), lambda s, idx: (0, turn(s, idx))) for _, n in PIECES]
            + [fixed, fixed],
            out_specs=[piece, piece],
            scratch_shapes=[pltpu.VMEM((AW, ROWS), BF16)],
        ),
        out_shape=(sds((4, 2, QOP, 128)),) * 2,
        compiler_params=params(),
        cost_estimate=cost(4 * ROWS * D * AW, 1e7),
        name="attn_grads",
    )(idx, *normed, *normed, *branch, dqm, att)


def small_call(body, out_shape, *args, name):
    return pl.pallas_call(
        body,
        out_shape=out_shape,
        in_specs=[spec(pltpu.SMEM)] + [spec()] * (len(args) - 1),
        out_specs=jax.tree.map(lambda _: spec(), out_shape),
        compiler_params=params(),
        cost_estimate=cost(1e6, 4e6),
        name=name,
    )(*args)


def add(*values):
    return sum((v.astype(F32) for v in values[1:]), values[0].astype(F32)).astype(BF16)


def sum_core_body(idx, a, b, c, d, *outs):
    for s, out in enumerate(outs):
        out[:, :QOP, :] = add(a[s], b[s])
        out[:, QOP:, :] = add(c[s], d[s])


def sum_y_body(idx, a, b, c, d, own, other):
    zh = idx[1]
    own[...] = add(a[zh], b[zh], c[zh], d[zh])
    far = 1 - zh
    other[...] = add(a[far], b[far], c[far], d[far])


def sum_z_body(idx, a, b, c, d, out):
    out[...] = add(a[...], b[...], c[...], d[...])


def unpack_tail_body(idx, *refs):
    y, core = idx[2], idx[3]
    qkv, out, gains = refs[8:]
    for k in range(8):
        piece = refs[k]
        p = ((y - k % 4) & 3) * 2 + (core if k < 4 else 1 - core)
        rows = pl.ds(pl.multiple_of(p * 128, 128), 128)
        for c in range(4):
            qkv[rows, c * 128 : (c + 1) * 128] = piece[c * 128 : (c + 1) * 128, :].astype(F32)
        qkv[rows, AW:] = piece[QOP : QOP + 128, :].astype(F32).T
        g = piece[QOP + 128 :, :].astype(F32)
        for c in range(2):
            first = QP + c * (AW // 2)
            cols = pl.ds(pl.multiple_of(p * 256 + c * 128, 128), 128)
            out[:, cols] = piece[first : first + AW // 2, :].astype(F32)
            gains[:, cols] = g[2 * c : 2 * c + 2]


def sum_tail(idx, first, second, parts, finish):
    got_a = lax.ppermute(first[1], "core", shift(2, 1))
    got_b = lax.ppermute(second[1], "core", shift(2, 1))
    part = sds((2, TAIL, 128))
    g = small_call(sum_core_body, (part,) * 4, idx, first[0], got_a, second[0], got_b, name="sum_core")
    got = [lax.ppermute(g[s], "y", shift(4, s)) for s in (2, 1, 3)]
    part = sds((TAIL, 128))
    own, other = small_call(sum_y_body, (part,) * 2, idx, g[0], *got, name="sum_y")
    p0, q1, q3 = relay([tie(p, own) for p in parts])
    cross = [(2 * a + b, 2 * (1 - a) + (1 - b)) for a in range(2) for b in range(2)]
    g = small_call(
        sum_z_body,
        part,
        idx,
        tie(own, q1, q3),
        lax.ppermute(own, "zl", shift(2, 1)),
        lax.ppermute(other, "zh", shift(2, 1)),
        lax.ppermute(other, ("zl", "zh"), cross),
        name="sum_z",
    )
    d_one = last_step(p0, q1, q3)
    outputs = own, *finish(d_one, own)
    mine = [g] + [lax.ppermute(g, "y", shift(4, s)) for s in (1, 2, 3)]
    mine[1:] = [tie(v, *outputs[1:]) for v in mine[1:]]
    theirs = [lax.ppermute(v, "core", shift(2, 1)) for v in mine]
    shapes = (sds((DH, QW), F32), sds((AW // 2, D), F32), sds((2, D), F32))
    return outputs, small_call(unpack_tail_body, shapes, idx, *mine, *theirs, name="unpack_tail")


def inverse_rms(v):
    return lax.rsqrt(jnp.mean(v * v, axis=-1, keepdims=True) + EPSILON)


def total(terms):
    return sum((t[...].astype(F32) for t in terms[1:]), terms[0][...].astype(F32))


def norm_two_body(tok, a, b, c, gain, after, normed):
    v = total((tok, a, b, c))
    after[...] = v
    normed[...] = (v * inverse_rms(v) * gain[...]).astype(BF16)


def norm_back_body(add, v_ref, a, b, c, gain, out, low, gain_grad):
    v = v_ref[...].astype(F32)
    grad = total((a, b, c))
    r = inverse_rms(v)
    pulled = grad * gain[...]
    inner = jnp.mean(v * pulled, axis=-1, keepdims=True)
    res = add[...].astype(F32) + r * pulled - v * (r * r * r) * inner
    out[...] = res
    low[...] = res.astype(BF16)
    part = jnp.sum(grad * v * r, axis=0, keepdims=True)

    @pl.when(pl.program_id(0) == 0)
    def _():
        gain_grad[...] = part

    @pl.when(pl.program_id(0) > 0)
    def _():
        gain_grad[...] += part


def row_call(body, out_shape, *args, name):
    block = lambda v: (
        pl.BlockSpec((HALF, D), lambda i: (i, 0))
        if v.shape[0] == BLK
        else pl.BlockSpec((1, D), lambda i: (0, 0))
    )
    return pl.pallas_call(
        body,
        grid=(2,),
        out_shape=out_shape,
        in_specs=[block(v) for v in args],
        out_specs=tuple(block(v) for v in out_shape),
        compiler_params=params(),
        cost_estimate=cost(1e6, 5e6),
        name=name,
    )(*args)


def replica_layout(lengths, replica, replica_id):
    sizes = jnp.where(replica == replica_id, lengths, 0)
    starts = jnp.cumsum(sizes) - sizes
    row_ids = jnp.arange(CAP, dtype=jnp.int32)
    inside = (row_ids[:, None] >= starts[None, :]) & (row_ids[:, None] < (starts + sizes)[None, :])
    begin = jnp.sum(jnp.where(inside, starts[None, :], 0), axis=1)
    begin = begin + jnp.where(jnp.any(inside, axis=1), 0, jnp.sum(sizes))
    return begin, row_ids - begin


def on_device(
    tokens, cotangent, gain_one, qkv_weight, out_weight, gate_weight, up_weight, down_weight,
    gain_two, seq_lengths, seq_replica,
):
    x, zh, core = lax.axis_index("x"), lax.axis_index("zh"), lax.axis_index("core")
    y, zl = lax.axis_index("y"), lax.axis_index("zl")
    idx = jnp.stack([x, zh, y, core]).astype(jnp.int32)

    tok = tokens.astype(F32)
    s_one = inverse_rms(tok)
    begin, position = replica_layout(seq_lengths, seq_replica, (y * 2 + zl) * 2 + core)
    half_rows = lambda v: lax.dynamic_index_in_dim(v.reshape(4, 2, BLK), zh, 1, False).reshape(ROWS, 1)
    first = jnp.tile(half_rows(begin)[3 * BLK :, 0], 8).reshape(1, QALL)
    lane = jnp.arange(128, dtype=jnp.int32)
    frequency = ROTARY_BASE ** (-(lane % 32).astype(F32) * (2.0 / HD))
    angles = half_rows(position).astype(F32) * frequency[None, :]
    cosine = jnp.cos(angles)
    sine = jnp.where((lane % HD) < HD // 2, -1.0, 1.0)[None, :] * jnp.sin(angles)

    qkv_got = fetch_half(qkv_weight, core)
    normed_one = gather_x((tok * s_one * gain_one).astype(BF16), (cosine,))
    slot = y * 2 + core
    eighth = lambda w: lax.dynamic_slice_in_dim(w, slot * (w.shape[0] // 8), w.shape[0] // 8, 0)
    spread = lambda v: lax.all_gather(v, ("y", "core"), axis=0, tiled=True)
    first_row = jnp.minimum(slot * DOWN_ROWS, FF4 // 2 - DOWN_ROWS)
    some = jnp.concatenate(
        [eighth(out_weight), lax.dynamic_slice_in_dim(down_weight, first_row, DOWN_ROWS, 0)], 0
    )
    some = lax.ppermute(some, "zh", shift(2, 1))
    far_rows = spread(tie(some, qkv_got, normed_one[2], normed_one[3])).reshape(8, OUT_ROWS + DOWN_ROWS, D)
    out_all, down_all = (out_weight, far_rows), (down_weight, far_rows)
    swap = lambda v, *deps: lax.ppermute(tie(v, *deps), "core", shift(2, 1))
    qkv_all = qkv_weight, qkv_got, swap(qkv_got, some, normed_one[2], normed_one[3])

    q, kv_own = qkv_forward(idx, normed_one, qkv_all, cosine, sine)
    cot = tie(cotangent, normed_one[2], normed_one[3])
    cots = [cotangent] + [lax.ppermute(cot, "x", shift(4, -k)) for k in (1, 2, 3)]
    kv_par = lax.ppermute(kv_own, "zh", shift(2, 1))
    rows = DH // 8
    cross = [(2 * a + b, 2 * (1 - a) + (1 - b)) for a in range(2) for b in range(2)]
    gate_up = lax.ppermute(
        jnp.concatenate(
            [
                eighth(tie(gate_weight, kv_own)),
                jnp.zeros((rows, GAP - FF4), BF16),
                eighth(tie(up_weight, kv_own)),
            ],
            1,
        ),
        ("zl", "zh"),
        cross,
    )
    att, qx = attend(idx, q, kv_own, kv_par, first)
    parts = out_project(idx, tie(att, *cots), out_all)
    gate_up = spread(tie(gate_up, parts[2]))
    p0, q1, q3 = relay(parts)
    after_attn, normed_two = row_call(
        norm_two_body,
        (sds((BLK, D), F32), sds((BLK, D))),
        tokens, *last_step(p0, q1, q3), gain_two.reshape(1, D), name="norm_two",
    )
    normed_two = gather_x(normed_two)
    hid, dgate, dup = ffn(idx, normed_two, cots, gate_weight, up_weight, gate_up, down_all)
    d_parts = ffn_back(idx, dgate, dup, gate_weight, up_weight, gate_up)
    own_grads = down_grads(cots, tie(hid, d_parts[2]))
    d_own, q1, q3 = relay(d_parts)
    own_grads = gate_up_grads(normed_two, tie(dgate, q1, q3), dup, own_grads)
    d_two = last_step(d_own, q1, q3)
    grads = lax.psum_scatter(
        tie(own_grads, *d_two).reshape(32, PIECE, 128),
        ("zh", "zl", "y", "core"), scatter_dimension=0, tiled=True,
    )
    after_grad, branch, gain_grad_two = row_call(
        norm_back_body,
        (sds((BLK, D), F32), sds((BLK, D)), sds((1, D), F32)),
        cotangent, after_attn, *d_two, gain_two.reshape(1, D), name="norm_back_two",
    )
    branch = gather_x(branch)
    layer_parts = down_project(idx, tie(hid, after_grad), down_all)
    att = tie(att, *layer_parts)
    layer = [
        lax.ppermute(tie(layer_parts[k], branch[2], branch[3]), "x", shift(4, k)) for k in (1, 3)
    ]
    dqm, dkv_own, dkv_par = attend_back(
        idx, qx, kv_own, kv_par, first, att, cosine, sine, branch, out_all
    )
    dkv_got = lax.ppermute(dkv_par, "zh", shift(2, 1))
    tail = attn_grads(
        idx, normed_one, branch, dqm.reshape(ROWS, AW), tie(att, *layer).reshape(ROWS, AW)
    )
    dkv_got = tie(dkv_got, tail[0])
    *tail_kv, parts = qkv_back(
        idx, dqm.reshape(ROWS, AW), dkv_own, dkv_got, cosine, sine, qkv_all, normed_one, gain_one,
        gain_grad_two,
    )
    over_x = lambda v: sum((tie(lax.ppermute(v, "x", shift(4, s)), grad_gate) for s in (1, 2, 3)), v)
    def finish(d_one, own):
        last = lax.ppermute(tie(layer_parts[2], own), "x", shift(4, 2))
        terms = [layer_parts[0], *layer, last]
        layer_out = sum((v.astype(F32) for v in terms), after_attn).astype(BF16)
        _, input_grad, _ = row_call(
            norm_back_body,
            (sds((BLK, D), F32), sds((BLK, D)), sds((1, D), F32)),
            after_grad, tokens, *d_one, gain_one.reshape(1, D), name="norm_back_one",
        )
        return input_grad, layer_out

    (own_sum, input_grad, layer_out), (grad_qkv, grad_out, gains) = sum_tail(
        idx, (tail[0], tie(tail[1], dkv_got)), tail_kv, parts, finish
    )
    grads = lax.all_gather(tie(grads, own_sum), ("zl", "y", "core"), axis=0, tiled=True)
    grad_gate, grad_up, grad_down = unpack(grads)
    gains = over_x(gains)
    return (
        layer_out, input_grad, gains[0], grad_qkv, grad_out, grad_gate, grad_up,
        grad_down, gains[1],
    )


def solution(mesh):
    grid = Mesh(mesh.devices.reshape(SIZES), AXES)
    rows = P(AXES, None)
    both = P(("x", "zh"), None)
    return jax.shard_map(
        on_device,
        mesh=grid,
        in_specs=(
            rows, rows, P(), P("zh", "x"), both, P("zh", "x"), P("zh", "x"), both, P(), P(), P(),
        ),
        out_specs=(
            rows, rows, P(), P("zh", "x"), both, P("zh", "x"), P("zh", "x"), both, P(),
        ),
        check_vma=False,
    )
```

```python
import jax
import jax.numpy as jnp
from jax import lax
from jax.experimental import pallas as pl
from jax.experimental.pallas import tpu as pltpu
from jax.sharding import Mesh
from jax.sharding import PartitionSpec as P

HEADS = 32
KV = 4
HD = 64
EPSILON = 1e-05
ROTARY_BASE = 10000.0
MASKED = -1e30

AXES = ("y", "zl", "core", "x", "zh")
SIZES = (4, 2, 2, 4, 2)
BLK = 160
HALF = BLK // 2
ROWS = 4 * BLK
CAP = 2 * ROWS
D = 2048
DH = D // 2
QW = 640
AW = 512
FF4 = 1408
TILE = 256
F32 = jnp.float32
BF16 = jnp.bfloat16
VLIM = 60 * 1024 * 1024


def spec(memory=pltpu.VMEM):
    return pl.BlockSpec(memory_space=memory)


def params(**kw):
    return pltpu.CompilerParams(vmem_limit_bytes=VLIM, **kw)


def cost(flops, nbytes):
    return pl.CostEstimate(flops=int(flops), bytes_accessed=int(nbytes), transcendentals=0)


def sds(shape, dtype=BF16):
    return jax.ShapeDtypeStruct(shape, dtype)


def dot(a, b):
    return jnp.dot(a, b, preferred_element_type=F32)


def dot_t(a, b):
    return lax.dot_general(a, b, (((1,), (1,)), ((), ())), preferred_element_type=F32)


def t_dot(a, b):
    return lax.dot_general(a, b, (((0,), (0,)), ((), ())), preferred_element_type=F32)


def tie(v, *deps):
    return lax.optimization_barrier((v,) + deps)[0]


def shift(n, s):
    return [(i, (i + s) % n) for i in range(n)]


def gather_x(v, wait=()):
    from_prev = lax.ppermute(v, "x", shift(4, 1))
    from_next = lax.ppermute(v, "x", shift(4, -1))
    send_a = tie(from_prev[:HALF], from_next, *wait)
    send_b = tie(from_next[HALF:], from_prev, *wait)
    opp_a = lax.ppermute(send_a, "x", shift(4, 1))
    opp_b = lax.ppermute(send_b, "x", shift(4, -1))
    return v, from_next, opp_a, opp_b, from_prev


def relay_body(p1, got_a, p3, got_b, q1, q3):
    q1[...] = (p1[...].astype(F32) + got_a[...].astype(F32)).astype(BF16)
    q3[...] = (p3[...].astype(F32) + got_b[...].astype(F32)).astype(BF16)


def relay(parts):
    p0, p1, p2a, p2b, p3 = parts
    got_a = lax.ppermute(p2a, "x", shift(4, 1))
    got_b = lax.ppermute(p2b, "x", shift(4, -1))
    half = lambda k: pl.BlockSpec((HALF, D), lambda i: (k, 0))
    q1, q3 = pl.pallas_call(
        relay_body,
        grid=(1,),
        out_shape=(sds((BLK, D)),) * 2,
        in_specs=[half(0), half(0), half(1), half(0)],
        out_specs=(half(0), half(1)),
        input_output_aliases={0: 0, 2: 1},
        compiler_params=params(),
        cost_estimate=cost(1e6, 2e6),
        name="relay",
    )(p1, got_a, p3, got_b)
    return p0, q1, q3


def scatter_x(parts):
    return last_step(*relay(parts))


def last_step(p0, q1, q3):
    return p0, lax.ppermute(q1, "x", shift(4, 1)), lax.ppermute(q3, "x", shift(4, -1))


PIECES = ((0, BLK), (1, BLK), (2, HALF), (2, HALF), (3, BLK))
PIECE_ROW = (0, BLK, 2 * BLK, 2 * BLK + HALF, 3 * BLK)


def part_shapes(width, dtype=BF16):
    return tuple(sds((n, width), dtype) for _, n in PIECES)


def low_lanes(shape):
    return lax.broadcasted_iota(jnp.int32, shape, 1) < HD


def swap_halves(v):
    lane = lax.broadcasted_iota(jnp.int32, v.shape, 1) % HD
    return jnp.where(lane < HD // 2, pltpu.roll(v, 128 - HD // 2, 1), pltpu.roll(v, HD // 2, 1))


def rows_at(block):
    return pl.ds(pl.multiple_of(block * BLK, 32), BLK)


def fetch_half(w, core):
    half = w.shape[0] // 2
    return lax.ppermute(lax.dynamic_slice_in_dim(w, core * half, half, 0), "zh", shift(2, 1))


OUT_ROWS = AW // 2 // 8
DOWN_ROWS = 96


def out_rows_spec():
    return pl.BlockSpec((8, OUT_ROWS, D), lambda i: (0, 0, 0))


def own_and_partner(idx, rows):
    zh = idx[1]
    at = lambda k: pl.ds(pl.multiple_of(k * rows, rows), rows)
    return at(zh), at(1 - zh)


def weight_rows(idx, rows):
    zh, core = idx[1], idx[3]
    far = (1 - zh) * rows
    half = rows // 2
    at = lambda first, n: pl.ds(pl.multiple_of(first, half), n)
    return at(zh * rows, rows), at(far + core * half, half), at(far + (1 - core) * half, half)


def qkv_body(idx, n0, n1, n2a, n2b, n3, w0, w1, w2, cosine, sine, q_ref, kv_ref, rows):
    x = idx[0]
    lo = low_lanes((BLK, 128))
    for ref, row, (_, n) in zip((n0, n1, n2a, n2b, n3), PIECE_ROW, PIECES):
        rows[row : row + n, :] = ref[...]
    s0, s1, s2 = weight_rows(idx, DH)
    acc = dot(rows[:, s0], w0[...]) + dot(rows[:, s1], w1[...]) + dot(rows[:, s2], w2[...])
    for d in range(4):
        at = rows_at((x + d) & 3)
        cs = cosine[at, :]
        sn = sine[at, :]
        for p in range(5):
            v = acc[d * BLK : (d + 1) * BLK, p * 128 : (p + 1) * 128]
            r = v * cs + swap_halves(v) * sn
            if p < 4:
                r = r * (HD**-0.5 * LOG2E)
                a = (x + d) & 3
                for k, w in enumerate((r, pltpu.roll(r, HD, 1))):
                    head = slice((2 * p + k) * BLK, (2 * p + k + 1) * BLK)
                    q_ref[a, head, :] = jnp.where(lo, w, 0.0).astype(BF16)
            else:
                kv_ref[at, :] = jnp.where(lo, r, v).astype(BF16)


def qkv_forward(idx, pieces, weight, cosine, sine):
    return pl.pallas_call(
        qkv_body,
        out_shape=(sds((4, QALL, 128)), sds((ROWS, 128))),
        in_specs=[spec(pltpu.SMEM)] + [spec()] * 10,
        out_specs=(spec(), spec()),
        scratch_shapes=[pltpu.VMEM((ROWS, D), BF16)],
        compiler_params=params(),
        cost_estimate=cost(2 * ROWS * D * QW, 7e6),
        name="qkv_forward",
    )(idx, *pieces, *weight, cosine, sine)


QALL = 8 * BLK
PAIR = 2 * BLK
LOG2E = 1.4426950408889634
LN2 = 0.6931471805599453


def split3(v):
    a = v.astype(BF16).astype(F32)
    b = (v - a).astype(BF16).astype(F32)
    return a, b, v - a - b


def with_lanes(v, parts):
    lane = lax.broadcasted_iota(jnp.int32, v.shape, 1)
    out = jnp.where(lane < HD, v, 0.0)
    for k, part in enumerate(parts):
        out = jnp.where(lane == HD + k, part, out)
    return out


def spread_keys(zh, kv_own, kv_par, kk, vv, fill):
    shape = (BLK, 128)
    lo = low_lanes(shape)
    rest = fill(lax.broadcasted_iota(jnp.int32, shape, 1) - HD)
    for j in range(4):
        for src, off in ((kv_own, zh), (kv_par, 1 - zh)):
            v = src[j * BLK : (j + 1) * BLK, :].astype(F32)
            at = rows_at(2 * j + off)
            kk[at, :] = jnp.where(lo, v, rest).astype(BF16)
            vv[at, :] = jnp.where(lo, pltpu.roll(v, HD, 1), rest).astype(BF16)


def masked(s, zh, j, kb, first):
    if j < 3 and kb < j:
        return s
    u = kb * PAIR + lax.broadcasted_iota(jnp.int32, (PAIR, QALL), 0)
    allowed = None
    if kb == j:
        t = (2 * j + zh) * BLK + lax.broadcasted_iota(jnp.int32, (1, QALL), 1) % BLK
        allowed = u <= t
    if j == 3:
        later = u >= first[...]
        allowed = later if allowed is None else allowed & later
    return jnp.where(allowed, s, MASKED)


def attend_body(idx, q, kv_own, kv_par, first, att, qx, kk, vv, vt, s_ref, e_ref):
    x, zh = idx[0], idx[1]
    spread_keys(zh, kv_own, kv_par, kk, vv, lambda lane: 1.0)
    vt[...] = vv[...].T
    lo = low_lanes((BLK, 128))
    for j in range(4):
        n = PAIR * (j + 1)
        qj = q[j]
        top = jnp.full((1, QALL), MASKED, F32)
        for kb in range(j + 1):
            rows = slice(kb * PAIR, (kb + 1) * PAIR)
            s = masked(dot_t(kk[rows, :], qj), zh, j, kb, first)
            s_ref[rows, :] = s
            top = jnp.maximum(top, jnp.max(s, axis=0, keepdims=True))
        for k in range(n // 64):
            rows = slice(k * 64, (k + 1) * 64)
            e_ref[rows, :] = jnp.exp2(s_ref[rows, :] - top).astype(BF16)
        o = dot(vt[:, :n], e_ref[:n, :])
        lse = split3(top + jnp.log(o[HD : HD + 1, :]) * LOG2E)
        row = lax.broadcasted_iota(jnp.int32, (128, QALL), 0)
        extra = jnp.zeros((128, QALL), F32)
        for k, part in enumerate(lse):
            extra = jnp.where(row == HD + k, part, extra)
        qx[j] = (qj.astype(F32) + extra.T).astype(BF16)
        o = o.T
        r = pltpu.roll(o, HD, 1)
        rel = (j - x) & 3
        for p in range(4):
            even, odd = slice(2 * p * BLK, (2 * p + 1) * BLK), slice((2 * p + 1) * BLK, (2 * p + 2) * BLK)
            num = jnp.where(lo, o[even], r[odd])
            den = jnp.where(lo, r[even], o[odd])
            att[rel, :, p * 128 : (p + 1) * 128] = (num / den).astype(BF16)


def attend(idx, q, kv_own, kv_par, first):
    return pl.pallas_call(
        attend_body,
        out_shape=(sds((4, BLK, AW)), sds((4, QALL, 128))),
        in_specs=[spec(pltpu.SMEM)] + [spec()] * 4,
        out_specs=(spec(), spec()),
        scratch_shapes=[
            pltpu.VMEM((CAP, 128), BF16),
            pltpu.VMEM((CAP, 128), BF16),
            pltpu.VMEM((128, CAP), BF16),
            pltpu.VMEM((CAP, QALL), F32),
            pltpu.VMEM((CAP, QALL), BF16),
        ],
        compiler_params=params(),
        cost_estimate=cost(1.2e10, 3e6),
        name="attend",
    )(idx, q, kv_own, kv_par, first)


def store_parts(res, refs):
    for ref, row, (_, n) in zip(refs, PIECE_ROW, PIECES):
        ref[...] = res[row : row + n].astype(BF16)


def out_body(idx, att, w0, w1, o0, o1, o2a, o2b, o3):
    slots = own_and_partner(idx, AW // 2)
    weights = w0[...], w1[...].reshape(AW // 2, D)
    for d, ref in ((2, None), (1, o1), (3, o3), (0, o0)):
        a = att.at[d]
        res = sum(dot(a[:, s], w) for s, w in zip(slots, weights)).astype(BF16)
        if d == 2:
            o2a[...] = res[:HALF]
            o2b[...] = res[HALF:]
        else:
            ref[...] = res


def out_project(idx, att, weight):
    return pl.pallas_call(
        out_body,
        grid=(1,),
        out_shape=part_shapes(D),
        in_specs=[spec(pltpu.SMEM), spec(), spec(), out_rows_spec()],
        out_specs=(spec(),) * 5,
        compiler_params=params(),
        cost_estimate=cost(2 * ROWS * D * AW, 5.5e6),
        name="out_project",
    )(idx, att, *weight)


def stack_heads(v):
    return v, pltpu.roll(v, HD, 1)


def attend_back_body(
    idx, qx, kv_own, kv_par, first, att, cosine, sine, b0, b1, b2a, b2b, b3, w0, w1,
    dq_ref, dkv_own, dkv_par, kk, vv, dout, do_all, dkk, dvv, e_ref, ds_ref, dq_acc,
):
    x, zh = idx[0], idx[1]
    spread_keys(zh, kv_own, kv_par, kk, vv, lambda lane: jnp.where(lane < 3, -1.0, 0.0))
    slots = own_and_partner(idx, AW // 2)
    weights = w0[...], w1[...].reshape(AW // 2, D)
    for d in range(4):
        if d == 2:
            rows = jnp.concatenate([b2a[...], b2b[...]], 0)
        else:
            rows = (b0, b1, None, b3)[d][...]
        at = rows_at((x + d) & 3)
        for s, w in zip(slots, weights):
            dout[at, s] = dot_t(rows, w).astype(BF16)
    lo = low_lanes((BLK, 128))
    for j in range(4):
        rel = (j - x) & 3
        here = slice(j * BLK, (j + 1) * BLK)
        for p in range(4):
            cols = slice(p * 128, (p + 1) * 128)
            do = dout[here, cols].astype(F32)
            prod = do * att[rel, :, cols].astype(F32)
            for k, (v, w) in enumerate(zip(stack_heads(do), stack_heads(prod))):
                delta = jnp.sum(jnp.where(lo, w, 0.0), axis=1, keepdims=True)
                head = slice((2 * p + k) * BLK, (2 * p + k + 1) * BLK)
                do_all[head, :] = with_lanes(v, split3(delta)).astype(BF16)
        for kb in range(j + 1):
            rows = slice(kb * PAIR, (kb + 1) * PAIR)
            e = jnp.exp2(masked(dot_t(kk[rows, :], qx[j]), zh, j, kb, first))
            e_ref[...] = e.astype(BF16)
            ds_ref[...] = (e * dot_t(vv[rows, :], do_all[...])).astype(BF16)
            dv = dot(e_ref[...], do_all[...])
            dk = dot(ds_ref[...], qx[j])
            dq = t_dot(ds_ref[...], kk[rows, :])
            if kb == j:
                dvv[rows, :], dkk[rows, :] = dv, dk
            else:
                dvv[rows, :] += dv
                dkk[rows, :] += dk
            if kb == 0:
                dq_acc[...] = dq
            else:
                dq_acc[...] += dq
        for p in range(4):
            even, odd = slice(2 * p * BLK, (2 * p + 1) * BLK), slice((2 * p + 1) * BLK, (2 * p + 2) * BLK)
            v = jnp.where(lo, dq_acc[even, :], pltpu.roll(dq_acc[odd, :], HD, 1)) * HD**-0.5
            v = v * cosine[here, :] - swap_halves(v) * sine[here, :]
            dq_ref[rel, :, p * 128 : (p + 1) * 128] = v.astype(BF16)
    for j in range(4):
        for dst, off in ((dkv_own, zh), (dkv_par, 1 - zh)):
            at = rows_at(2 * j + off)
            both = jnp.where(lo, dkk[at, :] * LN2, pltpu.roll(dvv[at, :], HD, 1))
            dst[j * BLK : (j + 1) * BLK, :] = both.astype(dst.dtype)


def attend_back(idx, qx, kv_own, kv_par, first, att, cosine, sine, branch, weight):
    return pl.pallas_call(
        attend_back_body,
        grid=(1,),
        out_shape=(sds((4, BLK, AW)), sds((ROWS, 128), F32), sds((ROWS, 128))),
        in_specs=[spec(pltpu.SMEM)] + [spec()] * 13 + [out_rows_spec()],
        out_specs=(spec(),) * 3,
        scratch_shapes=[
            pltpu.VMEM((CAP, 128), BF16),
            pltpu.VMEM((CAP, 128), BF16),
            pltpu.VMEM((ROWS, AW), BF16),
            pltpu.VMEM((QALL, 128), BF16),
            pltpu.VMEM((CAP, 128), F32),
            pltpu.VMEM((CAP, 128), F32),
            pltpu.VMEM((PAIR, QALL), BF16),
            pltpu.VMEM((PAIR, QALL), BF16),
            pltpu.VMEM((QALL, 128), F32),
        ],
        compiler_params=params(),
        cost_estimate=cost(3e10, 8e6),
        name="attend_back",
    )(idx, qx, kv_own, kv_par, first, att, cosine, sine, *branch, *weight)


def qkv_back_body(
    idx, dqm, dkv_own, dkv_got, cosine, sine, w0, w1, w2, n0, n1, n2a, n2b, n3, gain_one,
    gain_grad_two,
    mine, theirs, o0, o1, o2a, o2b, o3, n_all, dkv, grad, gains,
):
    x, y, core = idx[0], idx[2], idx[3]
    lo = low_lanes((BLK, 128))
    for ref, row, (_, n) in zip((n0, n1, n2a, n2b, n3), PIECE_ROW, PIECES):
        n_all[row : row + n, :] = ref[...]
    for d in range(4):
        at = rows_at((x + d) & 3)
        v = dkv_own[at, :] + dkv_got[at, :].astype(F32)
        v = jnp.where(lo, v * cosine[at, :] - swap_halves(v) * sine[at, :], v).astype(BF16)
        dkv[d * BLK : (d + 1) * BLK, :] = v
    rows = jnp.concatenate([dqm[...], dkv[...]], 1)
    for s, w in zip(weight_rows(idx, DH), (w0, w1, w2)):
        for c in range(w.shape[0] // 512):
            cols = pl.ds(pl.multiple_of(s.start + c * 512, 512), 512)
            res = dot_t(rows, w[c * 512 : (c + 1) * 512, :])
            part = (res * n_all[:, cols].astype(F32)).reshape(ROWS // 8, 8, 512)
            gains[0:1, cols] = jnp.sum(jnp.sum(part, axis=0), axis=0, keepdims=True) / gain_one[:, cols]
            store_parts(res, [r.at[:, cols] for r in (o0, o1, o2a, o2b, o3)])
    grad[...] = dot(dkv[...].T, n_all[...]).astype(BF16)
    gains[1:2, :] = gain_grad_two[...]
    for s in range(4):
        for k, ref in enumerate((mine, theirs)):
            p = ((y + s) & 3) * 2 + (core if k == 0 else 1 - core)
            both = gains[:, pl.ds(pl.multiple_of(p * 256, 256), 256)]
            both = jnp.concatenate([both[:, :128], both[:, 128:], jnp.zeros((12, 128), F32)], 0)
            for h in range(2):
                ref[s, h, :128, :] = grad[:, pl.ds(pl.multiple_of(h * DH + p * 128, 128), 128)]
                ref[s, h, 128:, :] = both.astype(BF16)


def qkv_back(idx, dqm, dkv_own, dkv_got, cosine, sine, weight, pieces, gain_one, gain_grad_two):
    res = pl.pallas_call(
        qkv_back_body,
        out_shape=(sds((4, 2, KVP, 128)),) * 2 + part_shapes(D),
        in_specs=[spec(pltpu.SMEM)] + [spec()] * 15,
        out_specs=(spec(),) * 7,
        scratch_shapes=[
            pltpu.VMEM((ROWS, D), BF16),
            pltpu.VMEM((ROWS, 128), BF16),
            pltpu.VMEM((128, D), BF16),
            pltpu.VMEM((2, D), F32),
        ],
        compiler_params=params(),
        cost_estimate=cost(2 * ROWS * D * QW, 1.3e7),
        name="qkv_back",
    )(
        idx, dqm, dkv_own, dkv_got, cosine, sine, *weight, *pieces,
        gain_one.reshape(1, D), gain_grad_two.reshape(1, D),
    )
    return res[0], res[1], res[2:]


TILES = 6
GAP = TILES * TILE


def load_down(idx, own, far, dst, sem):
    half = FF4 // 2
    zh = idx[1]
    at = lambda first, n: pl.ds(pl.multiple_of(first, 32), n)
    copies = [pltpu.make_async_copy(own, dst.at[at(zh * half, half)], sem.at[8])]
    for k in range(8):
        first = min(k * DOWN_ROWS, half - DOWN_ROWS)
        skip = k * DOWN_ROWS - first
        n = DOWN_ROWS - skip
        source = far.at[k, OUT_ROWS + skip : OUT_ROWS + DOWN_ROWS]
        copies.append(pltpu.make_async_copy(source, dst.at[at((1 - zh) * half + first + skip, n)], sem.at[k]))
    return copies


def ffn_body(
    idx, n0, n1, n2a, n2b, n3, c0, c1, c2, c3, gate_own, up_own, gate_par, up_par, w0, w1,
    hid, dgate, dup, n_all, c_all, down, sem,
):
    i = pl.program_id(0)
    zh = idx[1]

    @pl.when(i == 0)
    def _():
        copies = load_down(idx, w0, w1, down, sem)
        for c in copies:
            c.start()
        for ref, row, (_, n) in zip((n0, n1, n2a, n2b, n3), PIECE_ROW, PIECES):
            n_all[row : row + n, :] = ref[...]
        for d, ref in enumerate((c0, c1, c2, c3)):
            c_all[d * BLK : (d + 1) * BLK, :] = ref[...]
        for c in copies:
            c.wait()

    own = n_all[:, pl.ds(pl.multiple_of(zh * DH, DH), DH)]
    par = n_all[:, pl.ds(pl.multiple_of((1 - zh) * DH, DH), DH)]
    gate = dot(own, gate_own[...]) + dot(par, gate_par[...])
    up = dot(own, up_own[...]) + dot(par, up_par[...])
    dh = dot_t(c_all[...], down[pl.ds(pl.multiple_of(i * TILE, TILE), TILE), :])
    sig = 1.0 / (1.0 + jnp.exp(-gate))
    act = gate * sig
    hid[...] = (act * up).astype(BF16)
    dgate[...] = (dh * up * sig * (1.0 + gate * (1.0 - sig))).astype(BF16)
    dup[...] = (dh * act).astype(BF16)


def whole(n, w):
    return pl.BlockSpec((n, w), lambda i: (0, 0))


def ffn(idx, normed, cots, gate, up, gate_up, down):
    column = lambda first: pl.BlockSpec((DH, TILE), lambda i: (0, i + first))
    hidden = pl.BlockSpec((ROWS, TILE), lambda i: (0, i))
    return pl.pallas_call(
        ffn_body,
        grid=(TILES,),
        out_shape=(sds((ROWS, FF4)),) * 3,
        in_specs=[spec(pltpu.SMEM)]
        + [whole(n, D) for _, n in PIECES]
        + [whole(BLK, D)] * 4
        + [column(0), column(0), column(0), column(TILES)]
        + [spec(pl.ANY)] * 2,
        out_specs=[hidden] * 3,
        scratch_shapes=[
            pltpu.VMEM((ROWS, D), BF16),
            pltpu.VMEM((ROWS, D), BF16),
            pltpu.VMEM((GAP, D), BF16),
            pltpu.SemaphoreType.DMA((9,)),
        ],
        compiler_params=params(),
        cost_estimate=cost(6 * ROWS * D * FF4, 3.4e7),
        name="ffn",
    )(idx, *normed, *cots, gate, up, gate_up, gate_up, *down)


def down_body(idx, hid, w0, w1, o0, o1, o2, o3, down, sem):
    copies = load_down(idx, w0, w1, down, sem)
    for c in copies:
        c.start()
    for c in copies:
        c.wait()
    for n in range(D // 512):
        cols = slice(n * 512, (n + 1) * 512)
        res = dot(hid[...], down[:, cols]).astype(BF16)
        for d, ref in enumerate((o0, o1, o2, o3)):
            ref[:, cols] = res[d * BLK : (d + 1) * BLK]


def down_project(idx, hid, down):
    return pl.pallas_call(
        down_body,
        out_shape=(sds((BLK, D)),) * 4,
        in_specs=[spec(pltpu.SMEM), spec()] + [spec(pl.ANY)] * 2,
        out_specs=(spec(),) * 4,
        scratch_shapes=[pltpu.VMEM((FF4, D), BF16), pltpu.SemaphoreType.DMA((9,))],
        compiler_params=params(),
        cost_estimate=cost(2 * ROWS * D * FF4, 1.1e7),
        name="down_project",
    )(idx, hid, *down)


def ffn_back_body(idx, dgate, dup, gate_own, up_own, par, *refs):
    half = pl.num_programs(0) // 2

    @pl.when(pl.program_id(0) < half)
    def _():
        store_parts(dot_t(dgate[...], gate_own[...]) + dot_t(dup[...], up_own[...]), refs)

    @pl.when(pl.program_id(0) >= half)
    def _():
        store_parts(dot_t(dgate[...], par[:, :FF4]) + dot_t(dup[...], par[:, GAP:]), refs)


def ffn_back(idx, dgate, dup, gate, up, gate_up):
    half = DH // TILE
    rows = pl.BlockSpec((ROWS, FF4), lambda i, idx: (0, 0))
    own = pl.BlockSpec((TILE, FF4), lambda i, idx: (jnp.minimum(i, half - 1), 0))
    par = pl.BlockSpec((TILE, GAP + FF4), lambda i, idx: (jnp.maximum(i - half, 0), 0))
    place = lambda i, idx: (0, i ^ (idx[1] * half))
    return pl.pallas_call(
        ffn_back_body,
        grid_spec=pltpu.PrefetchScalarGridSpec(
            num_scalar_prefetch=1,
            grid=(D // TILE,),
            in_specs=[rows, rows, own, own, par],
            out_specs=[pl.BlockSpec((n, TILE), place) for _, n in PIECES],
        ),
        out_shape=part_shapes(D),
        compiler_params=params(),
        cost_estimate=cost(4 * ROWS * D * FF4, 1.8e7),
        name="ffn_back",
    )(idx, dgate, dup, gate, up, gate_up)


GU_ROWS = FF4 // 128 * 64
PIECE = 2 * GU_ROWS + FF4 // 2
QS = 4


def gate_up_grads_body(*refs):
    na, nb = refs[0:5], refs[5:10]
    dgate, dup, _, out = refs[10:]
    stack = lambda parts: jnp.concatenate([r[...] for r in parts], 0)
    rows = jnp.concatenate([stack(na), stack(nb)], 1).T
    for k, ref in enumerate((dgate, dup)):
        g = dot(rows, ref[...]).astype(BF16)
        for h in range(2):
            for q in range(QS):
                r = g[(QS * h + q) * 64 : (QS * h + q + 1) * 64]
                for c in range(FF4 // 128):
                    first = k * GU_ROWS + c * 64
                    out[h, q, first : first + 64, :] = r[:, c * 128 : (c + 1) * 128]


def gate_up_grads(normed, dgate, dup, pieces):
    return pl.pallas_call(
        gate_up_grads_body,
        grid=(16 // QS,),
        out_shape=sds((2, 16, PIECE, 128)),
        in_specs=[pl.BlockSpec((n, 64 * QS), lambda i: (0, i)) for _, n in PIECES]
        + [pl.BlockSpec((n, 64 * QS), lambda i: (0, i + 16 // QS)) for _, n in PIECES]
        + [whole(ROWS, FF4)] * 2
        + [spec(pl.ANY)],
        out_specs=pl.BlockSpec((2, QS, 2 * GU_ROWS, 128), lambda i: (0, i, 0, 0)),
        input_output_aliases={12: 0},
        compiler_params=params(),
        cost_estimate=cost(4 * ROWS * D * FF4, 2e7),
        name="gate_up_grads",
    )(*normed, *normed, dgate, dup, pieces)


def down_grads_body(*refs):
    cots = refs[0:4]
    hid, out, hid_t = refs[4:]

    @pl.when(pl.program_id(0) == 0)
    def _():
        hid_t[...] = hid[...].T

    g = dot(hid_t[...], jnp.concatenate([r[...] for r in cots], 0)).astype(BF16)
    for h in range(2):
        for q in range(QS):
            out[h, q, :, :] = g[h * (FF4 // 2) : (h + 1) * (FF4 // 2), q * 128 : (q + 1) * 128]


def down_grads(cots, hid):
    return pl.pallas_call(
        down_grads_body,
        grid=(16 // QS,),
        out_shape=sds((2, 16, PIECE, 128)),
        in_specs=[pl.BlockSpec((BLK, 128 * QS), lambda i: (0, i))] * 4 + [whole(ROWS, FF4)],
        out_specs=pl.BlockSpec((2, QS, FF4 // 2, 128), lambda i: (0, i, 2, 0)),
        scratch_shapes=[pltpu.VMEM((FF4, ROWS), BF16)],
        compiler_params=params(),
        cost_estimate=cost(2 * ROWS * D * FF4, 1e7),
        name="down_grads",
    )(*cots, hid)


def unpack_body(piece, gate, up, down):
    for q in range(QS):
        rows = slice(q * 64, (q + 1) * 64)
        for k, ref in enumerate((gate, up)):
            for c in range(FF4 // 128):
                first = k * GU_ROWS + c * 64
                ref[rows, c * 128 : (c + 1) * 128] = piece[q, first : first + 64, :].astype(F32)
        down[:, q * 128 : (q + 1) * 128] = piece[q, 2 * GU_ROWS :, :].astype(F32)


def unpack(pieces):
    return pl.pallas_call(
        unpack_body,
        grid=(16 // QS,),
        out_shape=(sds((DH, FF4), F32), sds((DH, FF4), F32), sds((FF4 // 2, D), F32)),
        in_specs=[pl.BlockSpec((QS, PIECE, 128), lambda i: (i, 0, 0))],
        out_specs=[
            pl.BlockSpec((64 * QS, FF4), lambda i: (i, 0)),
            pl.BlockSpec((64 * QS, FF4), lambda i: (i, 0)),
            pl.BlockSpec((FF4 // 2, 128 * QS), lambda i: (0, i)),
        ],
        compiler_params=params(),
        cost_estimate=cost(1e6, 2.6e7),
        name="unpack",
    )(pieces)


QP = 4 * 128
OP = 2 * (AW // 2)
QOP = QP + OP
KVP = 128 + 16
TAIL = QOP + KVP


def attn_grads_body(idx, *refs):
    na, nb, branch = refs[0:5], refs[5:10], refs[10:15]
    dqm, att, mine, theirs, att_t = refs[15:]
    core = idx[3]

    @pl.when(pl.program_id(0) == 0)
    def _():
        att_t[...] = att[...].T

    stack = lambda parts: jnp.concatenate([r[...] for r in parts], 0)

    def store(h, first, n, zero, one):
        mine[0, h, first : first + n, :] = jnp.where(core == 0, zero, one)
        theirs[0, h, first : first + n, :] = jnp.where(core == 0, one, zero)

    for h, cols in enumerate((na, nb)):
        g = dot(stack(cols).T, dqm[...]).astype(BF16)
        for c in range(4):
            lanes = slice(c * 128, (c + 1) * 128)
            store(h, c * 128, 128, g[:128, lanes], g[128:, lanes])
    g = dot(att_t[...], stack(branch)).astype(BF16)
    for h in range(2):
        r = g[h * (AW // 2) : (h + 1) * (AW // 2)]
        for c in range(2):
            lanes = lambda k: slice(k * 256 + c * 128, k * 256 + (c + 1) * 128)
            store(h, QP + c * (AW // 2), AW // 2, r[:, lanes(0)], r[:, lanes(1)])


def attn_grads(idx, normed, branch, dqm, att):
    turn = lambda s, idx: (s + idx[2]) & 3
    piece = pl.BlockSpec((1, 2, QOP, 128), lambda s, idx: (s, 0, 0, 0))
    fixed = pl.BlockSpec((ROWS, AW), lambda s, idx: (0, 0))
    return pl.pallas_call(
        attn_grads_body,
        grid_spec=pltpu.PrefetchScalarGridSpec(
            num_scalar_prefetch=1,
            grid=(4,),
            in_specs=[pl.BlockSpec((n, 256), lambda s, idx: (0, turn(s, idx))) for _, n in PIECES]
            + [pl.BlockSpec((n, 256), lambda s, idx: (0, turn(s, idx) + 4)) for _, n in PIECES]
            + [pl.BlockSpec((n, 512), lambda s, idx: (0, turn(s, idx))) for _, n in PIECES]
            + [fixed, fixed],
            out_specs=[piece, piece],
            scratch_shapes=[pltpu.VMEM((AW, ROWS), BF16)],
        ),
        out_shape=(sds((4, 2, QOP, 128)),) * 2,
        compiler_params=params(),
        cost_estimate=cost(4 * ROWS * D * AW, 1e7),
        name="attn_grads",
    )(idx, *normed, *normed, *branch, dqm, att)


def small_call(body, out_shape, *args, name):
    return pl.pallas_call(
        body,
        out_shape=out_shape,
        in_specs=[spec(pltpu.SMEM)] + [spec()] * (len(args) - 1),
        out_specs=jax.tree.map(lambda _: spec(), out_shape),
        compiler_params=params(),
        cost_estimate=cost(1e6, 4e6),
        name=name,
    )(*args)


def add(*values):
    return sum((v.astype(F32) for v in values[1:]), values[0].astype(F32)).astype(BF16)


def sum_core_body(idx, a, b, c, d, *outs):
    for s, out in enumerate(outs):
        out[:, :QOP, :] = add(a[s], b[s])
        out[:, QOP:, :] = add(c[s], d[s])


def sum_y_body(idx, a, b, c, d, own, other):
    zh = idx[1]
    own[...] = add(a[zh], b[zh], c[zh], d[zh])
    far = 1 - zh
    other[...] = add(a[far], b[far], c[far], d[far])


def sum_z_body(idx, a, b, c, d, out):
    out[...] = add(a[...], b[...], c[...], d[...])


def unpack_tail_body(idx, *refs):
    y, core = idx[2], idx[3]
    qkv, out, gains = refs[8:]
    for k in range(8):
        piece = refs[k]
        p = ((y - k % 4) & 3) * 2 + (core if k < 4 else 1 - core)
        rows = pl.ds(pl.multiple_of(p * 128, 128), 128)
        for c in range(4):
            qkv[rows, c * 128 : (c + 1) * 128] = piece[c * 128 : (c + 1) * 128, :].astype(F32)
        qkv[rows, AW:] = piece[QOP : QOP + 128, :].astype(F32).T
        g = piece[QOP + 128 :, :].astype(F32)
        for c in range(2):
            first = QP + c * (AW // 2)
            cols = pl.ds(pl.multiple_of(p * 256 + c * 128, 128), 128)
            out[:, cols] = piece[first : first + AW // 2, :].astype(F32)
            gains[:, cols] = g[2 * c : 2 * c + 2]


def sum_tail(idx, first, second, parts, finish):
    got_a = lax.ppermute(first[1], "core", shift(2, 1))
    got_b = lax.ppermute(second[1], "core", shift(2, 1))
    part = sds((2, TAIL, 128))
    g = small_call(sum_core_body, (part,) * 4, idx, first[0], got_a, second[0], got_b, name="sum_core")
    got = [lax.ppermute(g[s], "y", shift(4, s)) for s in (2, 1, 3)]
    part = sds((TAIL, 128))
    own, other = small_call(sum_y_body, (part,) * 2, idx, g[0], *got, name="sum_y")
    cross = [(2 * a + b, 2 * (1 - a) + (1 - b)) for a in range(2) for b in range(2)]
    g = small_call(
        sum_z_body,
        part,
        idx,
        own,
        lax.ppermute(own, "zl", shift(2, 1)),
        lax.ppermute(other, "zh", shift(2, 1)),
        lax.ppermute(other, ("zl", "zh"), cross),
        name="sum_z",
    )
    input_grad = finish(last_step(*relay([tie(p, g) for p in parts])))
    mine = [g] + [lax.ppermute(g, "y", shift(4, s)) for s in (1, 2, 3)]
    theirs = [lax.ppermute(v, "core", shift(2, 1)) for v in mine]
    shapes = (sds((DH, QW), F32), sds((AW // 2, D), F32), sds((2, D), F32))
    return own, input_grad, small_call(unpack_tail_body, shapes, idx, *mine, *theirs, name="unpack_tail")


def inverse_rms(v):
    return lax.rsqrt(jnp.mean(v * v, axis=-1, keepdims=True) + EPSILON)


def total(terms):
    return sum((t[...].astype(F32) for t in terms[1:]), terms[0][...].astype(F32))


def norm_two_body(tok, a, b, c, gain, after, normed):
    v = total((tok, a, b, c))
    after[...] = v
    normed[...] = (v * inverse_rms(v) * gain[...]).astype(BF16)


def norm_back_body(add, v_ref, a, b, c, gain, out, low, gain_grad):
    v = v_ref[...].astype(F32)
    grad = total((a, b, c))
    r = inverse_rms(v)
    pulled = grad * gain[...]
    inner = jnp.mean(v * pulled, axis=-1, keepdims=True)
    res = add[...].astype(F32) + r * pulled - v * (r * r * r) * inner
    out[...] = res
    low[...] = res.astype(BF16)
    part = jnp.sum(grad * v * r, axis=0, keepdims=True)

    @pl.when(pl.program_id(0) == 0)
    def _():
        gain_grad[...] = part

    @pl.when(pl.program_id(0) > 0)
    def _():
        gain_grad[...] += part


def row_call(body, out_shape, *args, name):
    block = lambda v: (
        pl.BlockSpec((HALF, D), lambda i: (i, 0))
        if v.shape[0] == BLK
        else pl.BlockSpec((1, D), lambda i: (0, 0))
    )
    return pl.pallas_call(
        body,
        grid=(2,),
        out_shape=out_shape,
        in_specs=[block(v) for v in args],
        out_specs=tuple(block(v) for v in out_shape),
        compiler_params=params(),
        cost_estimate=cost(1e6, 5e6),
        name=name,
    )(*args)


def replica_layout(lengths, replica, replica_id):
    sizes = jnp.where(replica == replica_id, lengths, 0)
    starts = jnp.cumsum(sizes) - sizes
    row_ids = jnp.arange(CAP, dtype=jnp.int32)
    inside = (row_ids[:, None] >= starts[None, :]) & (row_ids[:, None] < (starts + sizes)[None, :])
    begin = jnp.sum(jnp.where(inside, starts[None, :], 0), axis=1)
    begin = begin + jnp.where(jnp.any(inside, axis=1), 0, jnp.sum(sizes))
    return begin, row_ids - begin


def on_device(
    tokens, cotangent, gain_one, qkv_weight, out_weight, gate_weight, up_weight, down_weight,
    gain_two, seq_lengths, seq_replica,
):
    x, zh, core = lax.axis_index("x"), lax.axis_index("zh"), lax.axis_index("core")
    y, zl = lax.axis_index("y"), lax.axis_index("zl")
    idx = jnp.stack([x, zh, y, core]).astype(jnp.int32)

    tok = tokens.astype(F32)
    s_one = inverse_rms(tok)
    begin, position = replica_layout(seq_lengths, seq_replica, (y * 2 + zl) * 2 + core)
    half_rows = lambda v: lax.dynamic_index_in_dim(v.reshape(4, 2, BLK), zh, 1, False).reshape(ROWS, 1)
    first = jnp.tile(half_rows(begin)[3 * BLK :, 0], 8).reshape(1, QALL)
    lane = jnp.arange(128, dtype=jnp.int32)
    frequency = ROTARY_BASE ** (-(lane % 32).astype(F32) * (2.0 / HD))
    angles = half_rows(position).astype(F32) * frequency[None, :]
    cosine = jnp.cos(angles)
    sine = jnp.where((lane % HD) < HD // 2, -1.0, 1.0)[None, :] * jnp.sin(angles)

    qkv_got = fetch_half(qkv_weight, core)
    normed_one = gather_x((tok * s_one * gain_one).astype(BF16), (cosine,))
    slot = y * 2 + core
    eighth = lambda w: lax.dynamic_slice_in_dim(w, slot * (w.shape[0] // 8), w.shape[0] // 8, 0)
    spread = lambda v: lax.all_gather(v, ("y", "core"), axis=0, tiled=True)
    first_row = jnp.minimum(slot * DOWN_ROWS, FF4 // 2 - DOWN_ROWS)
    some = jnp.concatenate(
        [eighth(out_weight), lax.dynamic_slice_in_dim(down_weight, first_row, DOWN_ROWS, 0)], 0
    )
    some = lax.ppermute(some, "zh", shift(2, 1))
    far_rows = spread(tie(some, qkv_got, normed_one[2], normed_one[3])).reshape(8, OUT_ROWS + DOWN_ROWS, D)
    out_all, down_all = (out_weight, far_rows), (down_weight, far_rows)
    swap = lambda v, *deps: lax.ppermute(tie(v, *deps), "core", shift(2, 1))
    qkv_all = qkv_weight, qkv_got, swap(qkv_got, some, normed_one[2], normed_one[3])

    q, kv_own = qkv_forward(idx, normed_one, qkv_all, cosine, sine)
    cot = tie(cotangent, normed_one[2], normed_one[3])
    cots = [cotangent] + [lax.ppermute(cot, "x", shift(4, -k)) for k in (1, 2, 3)]
    kv_par = lax.ppermute(kv_own, "zh", shift(2, 1))
    rows = DH // 8
    cross = [(2 * a + b, 2 * (1 - a) + (1 - b)) for a in range(2) for b in range(2)]
    gate_up = lax.ppermute(
        jnp.concatenate(
            [
                eighth(tie(gate_weight, kv_own)),
                jnp.zeros((rows, GAP - FF4), BF16),
                eighth(tie(up_weight, kv_own)),
            ],
            1,
        ),
        ("zl", "zh"),
        cross,
    )
    att, qx = attend(idx, q, kv_own, kv_par, first)
    parts = out_project(idx, tie(att, *cots), out_all)
    gate_up = spread(tie(gate_up, parts[2]))
    p0, q1, q3 = relay(parts)
    after_attn, normed_two = row_call(
        norm_two_body,
        (sds((BLK, D), F32), sds((BLK, D))),
        tokens, *last_step(p0, q1, q3), gain_two.reshape(1, D), name="norm_two",
    )
    normed_two = gather_x(normed_two)
    hid, dgate, dup = ffn(idx, normed_two, cots, gate_weight, up_weight, gate_up, down_all)
    d_parts = ffn_back(idx, dgate, dup, gate_weight, up_weight, gate_up)
    own_grads = down_grads(cots, tie(hid, d_parts[2]))
    d_own, q1, q3 = relay(d_parts)
    own_grads = gate_up_grads(normed_two, tie(dgate, q1, q3), dup, own_grads)
    d_two = last_step(d_own, q1, q3)
    grads = lax.psum_scatter(
        tie(own_grads, *d_two).reshape(32, PIECE, 128),
        ("zh", "zl", "y", "core"), scatter_dimension=0, tiled=True,
    )
    after_grad, branch, gain_grad_two = row_call(
        norm_back_body,
        (sds((BLK, D), F32), sds((BLK, D)), sds((1, D), F32)),
        cotangent, after_attn, *d_two, gain_two.reshape(1, D), name="norm_back_two",
    )
    branch = gather_x(branch)
    layer_parts = down_project(idx, tie(hid, after_grad), down_all)
    att = tie(att, *layer_parts)
    layer = [
        lax.ppermute(tie(layer_parts[k], branch[2], branch[3]), "x", shift(4, k)) for k in (1, 3)
    ]
    dqm, dkv_own, dkv_par = attend_back(
        idx, qx, kv_own, kv_par, first, att, cosine, sine, branch, out_all
    )
    dkv_got = lax.ppermute(dkv_par, "zh", shift(2, 1))
    tail = attn_grads(
        idx, normed_one, branch, dqm.reshape(ROWS, AW), tie(att, *layer).reshape(ROWS, AW)
    )
    dkv_got = tie(dkv_got, tail[0])
    *tail_kv, parts = qkv_back(
        idx, dqm.reshape(ROWS, AW), dkv_own, dkv_got, cosine, sine, qkv_all, normed_one, gain_one,
        gain_grad_two,
    )
    over_x = lambda v: sum((tie(lax.ppermute(v, "x", shift(4, s)), grad_gate) for s in (1, 2, 3)), v)
    finish = lambda d_one: row_call(
        norm_back_body,
        (sds((BLK, D), F32), sds((BLK, D)), sds((1, D), F32)),
        after_grad, tokens, *d_one, gain_one.reshape(1, D), name="norm_back_one",
    )[1]
    summed, input_grad, (grad_qkv, grad_out, gains) = sum_tail(
        idx, (tail[0], tie(tail[1], dkv_got)), tail_kv, parts, finish
    )
    layer.append(lax.ppermute(tie(layer_parts[2], summed), "x", shift(4, 2)))
    grads = lax.all_gather(tie(grads, summed), ("zl", "y", "core"), axis=0, tiled=True)
    grad_gate, grad_up, grad_down = unpack(grads)
    layer_out = sum((v.astype(F32) for v in layer), after_attn + layer_parts[0].astype(F32))
    layer_out = layer_out.astype(BF16)
    gains = over_x(gains)
    return (
        layer_out, input_grad, gains[0], grad_qkv, grad_out, grad_gate, grad_up,
        grad_down, gains[1],
    )


def solution(mesh):
    grid = Mesh(mesh.devices.reshape(SIZES), AXES)
    rows = P(AXES, None)
    both = P(("x", "zh"), None)
    return jax.shard_map(
        on_device,
        mesh=grid,
        in_specs=(
            rows, rows, P(), P("zh", "x"), both, P("zh", "x"), P("zh", "x"), both, P(), P(), P(),
        ),
        out_specs=(
            rows, rows, P(), P("zh", "x"), both, P("zh", "x"), P("zh", "x"), both, P(),
        ),
        check_vma=False,
    )
```

```python
import jax
import jax.numpy as jnp
from jax import lax
from jax.experimental import pallas as pl
from jax.experimental.pallas import tpu as pltpu
from jax.sharding import Mesh
from jax.sharding import PartitionSpec as P

HEADS = 32
KV = 4
HD = 64
EPSILON = 1e-05
ROTARY_BASE = 10000.0
MASKED = -1e30

AXES = ("y", "zl", "core", "x", "zh")
SIZES = (4, 2, 2, 4, 2)
BLK = 160
HALF = BLK // 2
ROWS = 4 * BLK
CAP = 2 * ROWS
D = 2048
DH = D // 2
QW = 640
AW = 512
FF4 = 1408
TILE = 256
F32 = jnp.float32
BF16 = jnp.bfloat16
VLIM = 60 * 1024 * 1024


def spec(memory=pltpu.VMEM):
    return pl.BlockSpec(memory_space=memory)


def params(**kw):
    return pltpu.CompilerParams(vmem_limit_bytes=VLIM, **kw)


def cost(flops, nbytes):
    return pl.CostEstimate(flops=int(flops), bytes_accessed=int(nbytes), transcendentals=0)


def sds(shape, dtype=BF16):
    return jax.ShapeDtypeStruct(shape, dtype)


def dot(a, b):
    return jnp.dot(a, b, preferred_element_type=F32)


def dot_t(a, b):
    return lax.dot_general(a, b, (((1,), (1,)), ((), ())), preferred_element_type=F32)


def t_dot(a, b):
    return lax.dot_general(a, b, (((0,), (0,)), ((), ())), preferred_element_type=F32)


def tie(v, *deps):
    return lax.optimization_barrier((v,) + deps)[0]


def shift(n, s):
    return [(i, (i + s) % n) for i in range(n)]


def gather_x(v, wait=()):
    from_prev = lax.ppermute(v, "x", shift(4, 1))
    from_next = lax.ppermute(v, "x", shift(4, -1))
    send_a = tie(from_prev[:HALF], from_next, *wait)
    send_b = tie(from_next[HALF:], from_prev, *wait)
    opp_a = lax.ppermute(send_a, "x", shift(4, 1))
    opp_b = lax.ppermute(send_b, "x", shift(4, -1))
    return v, from_next, opp_a, opp_b, from_prev


def relay_body(p1, got_a, p3, got_b, q1, q3):
    q1[...] = (p1[...].astype(F32) + got_a[...].astype(F32)).astype(BF16)
    q3[...] = (p3[...].astype(F32) + got_b[...].astype(F32)).astype(BF16)


def relay(parts):
    p0, p1, p2a, p2b, p3 = parts
    got_a = lax.ppermute(p2a, "x", shift(4, 1))
    got_b = lax.ppermute(p2b, "x", shift(4, -1))
    half = lambda k: pl.BlockSpec((HALF, D), lambda i: (k, 0))
    q1, q3 = pl.pallas_call(
        relay_body,
        grid=(1,),
        out_shape=(sds((BLK, D)),) * 2,
        in_specs=[half(0), half(0), half(1), half(0)],
        out_specs=(half(0), half(1)),
        input_output_aliases={0: 0, 2: 1},
        compiler_params=params(),
        cost_estimate=cost(1e6, 2e6),
        name="relay",
    )(p1, got_a, p3, got_b)
    return p0, q1, q3


def scatter_x(parts):
    return last_step(*relay(parts))


def last_step(p0, q1, q3):
    return p0, lax.ppermute(q1, "x", shift(4, 1)), lax.ppermute(q3, "x", shift(4, -1))


PIECES = ((0, BLK), (1, BLK), (2, HALF), (2, HALF), (3, BLK))
PIECE_ROW = (0, BLK, 2 * BLK, 2 * BLK + HALF, 3 * BLK)


def part_shapes(width, dtype=BF16):
    return tuple(sds((n, width), dtype) for _, n in PIECES)


def low_lanes(shape):
    return lax.broadcasted_iota(jnp.int32, shape, 1) < HD


def swap_halves(v):
    lane = lax.broadcasted_iota(jnp.int32, v.shape, 1) % HD
    return jnp.where(lane < HD // 2, pltpu.roll(v, 128 - HD // 2, 1), pltpu.roll(v, HD // 2, 1))


def rows_at(block):
    return pl.ds(pl.multiple_of(block * BLK, 32), BLK)


def fetch_half(w, core):
    half = w.shape[0] // 2
    return lax.ppermute(lax.dynamic_slice_in_dim(w, core * half, half, 0), "zh", shift(2, 1))


OUT_ROWS = AW // 2 // 8
DOWN_ROWS = 96


def out_rows_spec():
    return pl.BlockSpec((8, OUT_ROWS, D), lambda i: (0, 0, 0))


def own_and_partner(idx, rows):
    zh = idx[1]
    at = lambda k: pl.ds(pl.multiple_of(k * rows, rows), rows)
    return at(zh), at(1 - zh)


def weight_rows(idx, rows):
    zh, core = idx[1], idx[3]
    far = (1 - zh) * rows
    half = rows // 2
    at = lambda first, n: pl.ds(pl.multiple_of(first, half), n)
    return at(zh * rows, rows), at(far + core * half, half), at(far + (1 - core) * half, half)


def qkv_body(idx, n0, n1, n2a, n2b, n3, w0, w1, w2, cosine, sine, q_ref, kv_ref, rows):
    x = idx[0]
    lo = low_lanes((BLK, 128))
    for ref, row, (_, n) in zip((n0, n1, n2a, n2b, n3), PIECE_ROW, PIECES):
        rows[row : row + n, :] = ref[...]
    s0, s1, s2 = weight_rows(idx, DH)
    acc = dot(rows[:, s0], w0[...]) + dot(rows[:, s1], w1[...]) + dot(rows[:, s2], w2[...])
    for d in range(4):
        at = rows_at((x + d) & 3)
        cs = cosine[at, :]
        sn = sine[at, :]
        for p in range(5):
            v = acc[d * BLK : (d + 1) * BLK, p * 128 : (p + 1) * 128]
            r = v * cs + swap_halves(v) * sn
            if p < 4:
                r = r * (HD**-0.5 * LOG2E)
                a = (x + d) & 3
                for k, w in enumerate((r, pltpu.roll(r, HD, 1))):
                    head = slice((2 * p + k) * BLK, (2 * p + k + 1) * BLK)
                    q_ref[a, head, :] = jnp.where(lo, w, 0.0).astype(BF16)
            else:
                kv_ref[at, :] = jnp.where(lo, r, v).astype(BF16)


def qkv_forward(idx, pieces, weight, cosine, sine):
    return pl.pallas_call(
        qkv_body,
        out_shape=(sds((4, QALL, 128)), sds((ROWS, 128))),
        in_specs=[spec(pltpu.SMEM)] + [spec()] * 10,
        out_specs=(spec(), spec()),
        scratch_shapes=[pltpu.VMEM((ROWS, D), BF16)],
        compiler_params=params(),
        cost_estimate=cost(2 * ROWS * D * QW, 7e6),
        name="qkv_forward",
    )(idx, *pieces, *weight, cosine, sine)


QALL = 8 * BLK
PAIR = 2 * BLK
LOG2E = 1.4426950408889634
LN2 = 0.6931471805599453


def split3(v):
    a = v.astype(BF16).astype(F32)
    b = (v - a).astype(BF16).astype(F32)
    return a, b, v - a - b


def with_lanes(v, parts):
    lane = lax.broadcasted_iota(jnp.int32, v.shape, 1)
    out = jnp.where(lane < HD, v, 0.0)
    for k, part in enumerate(parts):
        out = jnp.where(lane == HD + k, part, out)
    return out


def spread_keys(zh, kv_own, kv_par, kk, vv, fill):
    shape = (BLK, 128)
    lo = low_lanes(shape)
    rest = fill(lax.broadcasted_iota(jnp.int32, shape, 1) - HD)
    for j in range(4):
        for src, off in ((kv_own, zh), (kv_par, 1 - zh)):
            v = src[j * BLK : (j + 1) * BLK, :].astype(F32)
            at = rows_at(2 * j + off)
            kk[at, :] = jnp.where(lo, v, rest).astype(BF16)
            vv[at, :] = jnp.where(lo, pltpu.roll(v, HD, 1), rest).astype(BF16)


def masked(s, zh, j, kb, first):
    if j < 3 and kb < j:
        return s
    u = kb * PAIR + lax.broadcasted_iota(jnp.int32, (PAIR, QALL), 0)
    allowed = None
    if kb == j:
        t = (2 * j + zh) * BLK + lax.broadcasted_iota(jnp.int32, (1, QALL), 1) % BLK
        allowed = u <= t
    if j == 3:
        later = u >= first[...]
        allowed = later if allowed is None else allowed & later
    return jnp.where(allowed, s, MASKED)


def attend_body(idx, q, kv_own, kv_par, first, att, qx, kk, vv, vt, s_ref, e_ref):
    x, zh = idx[0], idx[1]
    spread_keys(zh, kv_own, kv_par, kk, vv, lambda lane: 1.0)
    vt[...] = vv[...].T
    lo = low_lanes((BLK, 128))
    for j in range(4):
        n = PAIR * (j + 1)
        qj = q[j]
        top = jnp.full((1, QALL), MASKED, F32)
        for kb in range(j + 1):
            rows = slice(kb * PAIR, (kb + 1) * PAIR)
            s = masked(dot_t(kk[rows, :], qj), zh, j, kb, first)
            s_ref[rows, :] = s
            top = jnp.maximum(top, jnp.max(s, axis=0, keepdims=True))
        for k in range(n // 64):
            rows = slice(k * 64, (k + 1) * 64)
            e_ref[rows, :] = jnp.exp2(s_ref[rows, :] - top).astype(BF16)
        o = dot(vt[:, :n], e_ref[:n, :])
        lse = split3(top + jnp.log(o[HD : HD + 1, :]) * LOG2E)
        row = lax.broadcasted_iota(jnp.int32, (128, QALL), 0)
        extra = jnp.zeros((128, QALL), F32)
        for k, part in enumerate(lse):
            extra = jnp.where(row == HD + k, part, extra)
        qx[j] = (qj.astype(F32) + extra.T).astype(BF16)
        o = o.T
        r = pltpu.roll(o, HD, 1)
        rel = (j - x) & 3
        for p in range(4):
            even, odd = slice(2 * p * BLK, (2 * p + 1) * BLK), slice((2 * p + 1) * BLK, (2 * p + 2) * BLK)
            num = jnp.where(lo, o[even], r[odd])
            den = jnp.where(lo, r[even], o[odd])
            att[rel, :, p * 128 : (p + 1) * 128] = (num / den).astype(BF16)


def attend(idx, q, kv_own, kv_par, first):
    return pl.pallas_call(
        attend_body,
        out_shape=(sds((4, BLK, AW)), sds((4, QALL, 128))),
        in_specs=[spec(pltpu.SMEM)] + [spec()] * 4,
        out_specs=(spec(), spec()),
        scratch_shapes=[
            pltpu.VMEM((CAP, 128), BF16),
            pltpu.VMEM((CAP, 128), BF16),
            pltpu.VMEM((128, CAP), BF16),
            pltpu.VMEM((CAP, QALL), F32),
            pltpu.VMEM((CAP, QALL), BF16),
        ],
        compiler_params=params(),
        cost_estimate=cost(1.2e10, 3e6),
        name="attend",
    )(idx, q, kv_own, kv_par, first)


def store_parts(res, refs):
    for ref, row, (_, n) in zip(refs, PIECE_ROW, PIECES):
        ref[...] = res[row : row + n].astype(BF16)


def out_body(idx, att, w0, w1, o0, o1, o2a, o2b, o3):
    slots = own_and_partner(idx, AW // 2)
    weights = w0[...], w1[...].reshape(AW // 2, D)
    for d, ref in ((2, None), (1, o1), (3, o3), (0, o0)):
        a = att.at[d]
        res = sum(dot(a[:, s], w) for s, w in zip(slots, weights)).astype(BF16)
        if d == 2:
            o2a[...] = res[:HALF]
            o2b[...] = res[HALF:]
        else:
            ref[...] = res


def out_project(idx, att, weight):
    return pl.pallas_call(
        out_body,
        grid=(1,),
        out_shape=part_shapes(D),
        in_specs=[spec(pltpu.SMEM), spec(), spec(), out_rows_spec()],
        out_specs=(spec(),) * 5,
        compiler_params=params(),
        cost_estimate=cost(2 * ROWS * D * AW, 5.5e6),
        name="out_project",
    )(idx, att, *weight)


def stack_heads(v):
    return v, pltpu.roll(v, HD, 1)


def attend_back_body(
    idx, qx, kv_own, kv_par, first, att, cosine, sine, b0, b1, b2a, b2b, b3, w0, w1,
    dq_ref, dkv_own, dkv_par, kk, vv, dout, do_all, dkk, dvv, e_ref, ds_ref, dq_acc,
):
    x, zh = idx[0], idx[1]
    spread_keys(zh, kv_own, kv_par, kk, vv, lambda lane: jnp.where(lane < 3, -1.0, 0.0))
    slots = own_and_partner(idx, AW // 2)
    weights = w0[...], w1[...].reshape(AW // 2, D)
    for d in range(4):
        if d == 2:
            rows = jnp.concatenate([b2a[...], b2b[...]], 0)
        else:
            rows = (b0, b1, None, b3)[d][...]
        at = rows_at((x + d) & 3)
        for s, w in zip(slots, weights):
            dout[at, s] = dot_t(rows, w).astype(BF16)
    lo = low_lanes((BLK, 128))
    for j in range(4):
        rel = (j - x) & 3
        here = slice(j * BLK, (j + 1) * BLK)
        for p in range(4):
            cols = slice(p * 128, (p + 1) * 128)
            do = dout[here, cols].astype(F32)
            prod = do * att[rel, :, cols].astype(F32)
            for k, (v, w) in enumerate(zip(stack_heads(do), stack_heads(prod))):
                delta = jnp.sum(jnp.where(lo, w, 0.0), axis=1, keepdims=True)
                head = slice((2 * p + k) * BLK, (2 * p + k + 1) * BLK)
                do_all[head, :] = with_lanes(v, split3(delta)).astype(BF16)
        for kb in range(j + 1):
            rows = slice(kb * PAIR, (kb + 1) * PAIR)
            e = jnp.exp2(masked(dot_t(kk[rows, :], qx[j]), zh, j, kb, first))
            e_ref[...] = e.astype(BF16)
            ds_ref[...] = (e * dot_t(vv[rows, :], do_all[...])).astype(BF16)
            dv = dot(e_ref[...], do_all[...])
            dk = dot(ds_ref[...], qx[j])
            dq = t_dot(ds_ref[...], kk[rows, :])
            if kb == j:
                dvv[rows, :], dkk[rows, :] = dv, dk
            else:
                dvv[rows, :] += dv
                dkk[rows, :] += dk
            if kb == 0:
                dq_acc[...] = dq
            else:
                dq_acc[...] += dq
        for p in range(4):
            even, odd = slice(2 * p * BLK, (2 * p + 1) * BLK), slice((2 * p + 1) * BLK, (2 * p + 2) * BLK)
            v = jnp.where(lo, dq_acc[even, :], pltpu.roll(dq_acc[odd, :], HD, 1)) * HD**-0.5
            v = v * cosine[here, :] - swap_halves(v) * sine[here, :]
            dq_ref[rel, :, p * 128 : (p + 1) * 128] = v.astype(BF16)
    for j in range(4):
        for dst, off in ((dkv_own, zh), (dkv_par, 1 - zh)):
            at = rows_at(2 * j + off)
            both = jnp.where(lo, dkk[at, :] * LN2, pltpu.roll(dvv[at, :], HD, 1))
            dst[j * BLK : (j + 1) * BLK, :] = both.astype(dst.dtype)


def attend_back(idx, qx, kv_own, kv_par, first, att, cosine, sine, branch, weight):
    return pl.pallas_call(
        attend_back_body,
        grid=(1,),
        out_shape=(sds((4, BLK, AW)), sds((ROWS, 128), F32), sds((ROWS, 128))),
        in_specs=[spec(pltpu.SMEM)] + [spec()] * 13 + [out_rows_spec()],
        out_specs=(spec(),) * 3,
        scratch_shapes=[
            pltpu.VMEM((CAP, 128), BF16),
            pltpu.VMEM((CAP, 128), BF16),
            pltpu.VMEM((ROWS, AW), BF16),
            pltpu.VMEM((QALL, 128), BF16),
            pltpu.VMEM((CAP, 128), F32),
            pltpu.VMEM((CAP, 128), F32),
            pltpu.VMEM((PAIR, QALL), BF16),
            pltpu.VMEM((PAIR, QALL), BF16),
            pltpu.VMEM((QALL, 128), F32),
        ],
        compiler_params=params(),
        cost_estimate=cost(3e10, 8e6),
        name="attend_back",
    )(idx, qx, kv_own, kv_par, first, att, cosine, sine, *branch, *weight)


def qkv_back_body(
    idx, dqm, dkv_own, dkv_got, cosine, sine, w0, w1, w2, n0, n1, n2a, n2b, n3, gain_one,
    gain_grad_two,
    mine, theirs, o0, o1, o2a, o2b, o3, n_all, dkv, grad, gains,
):
    x, y, core = idx[0], idx[2], idx[3]
    lo = low_lanes((BLK, 128))
    for ref, row, (_, n) in zip((n0, n1, n2a, n2b, n3), PIECE_ROW, PIECES):
        n_all[row : row + n, :] = ref[...]
    for d in range(4):
        at = rows_at((x + d) & 3)
        v = dkv_own[at, :] + dkv_got[at, :].astype(F32)
        v = jnp.where(lo, v * cosine[at, :] - swap_halves(v) * sine[at, :], v).astype(BF16)
        dkv[d * BLK : (d + 1) * BLK, :] = v
    rows = jnp.concatenate([dqm[...], dkv[...]], 1)
    for s, w in zip(weight_rows(idx, DH), (w0, w1, w2)):
        for c in range(w.shape[0] // 512):
            cols = pl.ds(pl.multiple_of(s.start + c * 512, 512), 512)
            res = dot_t(rows, w[c * 512 : (c + 1) * 512, :])
            part = (res * n_all[:, cols].astype(F32)).reshape(ROWS // 8, 8, 512)
            gains[0:1, cols] = jnp.sum(jnp.sum(part, axis=0), axis=0, keepdims=True) / gain_one[:, cols]
            store_parts(res, [r.at[:, cols] for r in (o0, o1, o2a, o2b, o3)])
    grad[...] = dot(dkv[...].T, n_all[...]).astype(BF16)
    gains[1:2, :] = gain_grad_two[...]
    for s in range(4):
        for k, ref in enumerate((mine, theirs)):
            p = ((y + s) & 3) * 2 + (core if k == 0 else 1 - core)
            both = gains[:, pl.ds(pl.multiple_of(p * 256, 256), 256)]
            both = jnp.concatenate([both[:, :128], both[:, 128:], jnp.zeros((12, 128), F32)], 0)
            for h in range(2):
                ref[s, h, :128, :] = grad[:, pl.ds(pl.multiple_of(h * DH + p * 128, 128), 128)]
                ref[s, h, 128:, :] = both.astype(BF16)


def qkv_back(idx, dqm, dkv_own, dkv_got, cosine, sine, weight, pieces, gain_one, gain_grad_two):
    res = pl.pallas_call(
        qkv_back_body,
        out_shape=(sds((4, 2, KVP, 128)),) * 2 + part_shapes(D),
        in_specs=[spec(pltpu.SMEM)] + [spec()] * 15,
        out_specs=(spec(),) * 7,
        scratch_shapes=[
            pltpu.VMEM((ROWS, D), BF16),
            pltpu.VMEM((ROWS, 128), BF16),
            pltpu.VMEM((128, D), BF16),
            pltpu.VMEM((2, D), F32),
        ],
        compiler_params=params(),
        cost_estimate=cost(2 * ROWS * D * QW, 1.3e7),
        name="qkv_back",
    )(
        idx, dqm, dkv_own, dkv_got, cosine, sine, *weight, *pieces,
        gain_one.reshape(1, D), gain_grad_two.reshape(1, D),
    )
    return res[0], res[1], res[2:]


TILES = 6
GAP = TILES * TILE


def load_down(idx, own, far, dst, sem):
    half = FF4 // 2
    zh = idx[1]
    at = lambda first, n: pl.ds(pl.multiple_of(first, 32), n)
    copies = [pltpu.make_async_copy(own, dst.at[at(zh * half, half)], sem.at[8])]
    for k in range(8):
        first = min(k * DOWN_ROWS, half - DOWN_ROWS)
        skip = k * DOWN_ROWS - first
        n = DOWN_ROWS - skip
        source = far.at[k, OUT_ROWS + skip : OUT_ROWS + DOWN_ROWS]
        copies.append(pltpu.make_async_copy(source, dst.at[at((1 - zh) * half + first + skip, n)], sem.at[k]))
    return copies


def ffn_body(
    idx, n0, n1, n2a, n2b, n3, c0, c1, c2, c3, gate_own, up_own, gate_par, up_par, w0, w1,
    hid, dgate, dup, n_all, c_all, down, sem,
):
    i = pl.program_id(0)
    zh = idx[1]

    @pl.when(i == 0)
    def _():
        copies = load_down(idx, w0, w1, down, sem)
        for c in copies:
            c.start()
        for ref, row, (_, n) in zip((n0, n1, n2a, n2b, n3), PIECE_ROW, PIECES):
            n_all[row : row + n, :] = ref[...]
        for d, ref in enumerate((c0, c1, c2, c3)):
            c_all[d * BLK : (d + 1) * BLK, :] = ref[...]
        for c in copies:
            c.wait()

    own = n_all[:, pl.ds(pl.multiple_of(zh * DH, DH), DH)]
    par = n_all[:, pl.ds(pl.multiple_of((1 - zh) * DH, DH), DH)]
    gate = dot(own, gate_own[...]) + dot(par, gate_par[...])
    up = dot(own, up_own[...]) + dot(par, up_par[...])
    dh = dot_t(c_all[...], down[pl.ds(pl.multiple_of(i * TILE, TILE), TILE), :])
    sig = 1.0 / (1.0 + jnp.exp(-gate))
    act = gate * sig
    hid[...] = (act * up).astype(BF16)
    dgate[...] = (dh * up * sig * (1.0 + gate * (1.0 - sig))).astype(BF16)
    dup[...] = (dh * act).astype(BF16)


def whole(n, w):
    return pl.BlockSpec((n, w), lambda i: (0, 0))


def ffn(idx, normed, cots, gate, up, gate_up, down):
    column = lambda first: pl.BlockSpec((DH, TILE), lambda i: (0, i + first))
    hidden = pl.BlockSpec((ROWS, TILE), lambda i: (0, i))
    return pl.pallas_call(
        ffn_body,
        grid=(TILES,),
        out_shape=(sds((ROWS, FF4)),) * 3,
        in_specs=[spec(pltpu.SMEM)]
        + [whole(n, D) for _, n in PIECES]
        + [whole(BLK, D)] * 4
        + [column(0), column(0), column(0), column(TILES)]
        + [spec(pl.ANY)] * 2,
        out_specs=[hidden] * 3,
        scratch_shapes=[
            pltpu.VMEM((ROWS, D), BF16),
            pltpu.VMEM((ROWS, D), BF16),
            pltpu.VMEM((GAP, D), BF16),
            pltpu.SemaphoreType.DMA((9,)),
        ],
        compiler_params=params(),
        cost_estimate=cost(6 * ROWS * D * FF4, 3.4e7),
        name="ffn",
    )(idx, *normed, *cots, gate, up, gate_up, gate_up, *down)


def down_body(idx, hid, w0, w1, o0, o1, o2, o3, down, sem):
    copies = load_down(idx, w0, w1, down, sem)
    for c in copies:
        c.start()
    for c in copies:
        c.wait()
    for n in range(D // 512):
        cols = slice(n * 512, (n + 1) * 512)
        res = dot(hid[...], down[:, cols]).astype(BF16)
        for d, ref in enumerate((o0, o1, o2, o3)):
            ref[:, cols] = res[d * BLK : (d + 1) * BLK]


def down_project(idx, hid, down):
    return pl.pallas_call(
        down_body,
        out_shape=(sds((BLK, D)),) * 4,
        in_specs=[spec(pltpu.SMEM), spec()] + [spec(pl.ANY)] * 2,
        out_specs=(spec(),) * 4,
        scratch_shapes=[pltpu.VMEM((FF4, D), BF16), pltpu.SemaphoreType.DMA((9,))],
        compiler_params=params(),
        cost_estimate=cost(2 * ROWS * D * FF4, 1.1e7),
        name="down_project",
    )(idx, hid, *down)


def ffn_back_body(idx, dgate, dup, gate_own, up_own, par, *refs):
    half = pl.num_programs(0) // 2

    @pl.when(pl.program_id(0) < half)
    def _():
        store_parts(dot_t(dgate[...], gate_own[...]) + dot_t(dup[...], up_own[...]), refs)

    @pl.when(pl.program_id(0) >= half)
    def _():
        store_parts(dot_t(dgate[...], par[:, :FF4]) + dot_t(dup[...], par[:, GAP:]), refs)


def ffn_back(idx, dgate, dup, gate, up, gate_up):
    half = DH // TILE
    rows = pl.BlockSpec((ROWS, FF4), lambda i, idx: (0, 0))
    own = pl.BlockSpec((TILE, FF4), lambda i, idx: (jnp.minimum(i, half - 1), 0))
    par = pl.BlockSpec((TILE, GAP + FF4), lambda i, idx: (jnp.maximum(i - half, 0), 0))
    place = lambda i, idx: (0, i ^ (idx[1] * half))
    return pl.pallas_call(
        ffn_back_body,
        grid_spec=pltpu.PrefetchScalarGridSpec(
            num_scalar_prefetch=1,
            grid=(D // TILE,),
            in_specs=[rows, rows, own, own, par],
            out_specs=[pl.BlockSpec((n, TILE), place) for _, n in PIECES],
        ),
        out_shape=part_shapes(D),
        compiler_params=params(),
        cost_estimate=cost(4 * ROWS * D * FF4, 1.8e7),
        name="ffn_back",
    )(idx, dgate, dup, gate, up, gate_up)


GU_ROWS = FF4 // 128 * 64
PIECE = 2 * GU_ROWS + FF4 // 2
QS = 4


def gate_up_grads_body(*refs):
    na, nb = refs[0:5], refs[5:10]
    dgate, dup, _, out = refs[10:]
    stack = lambda parts: jnp.concatenate([r[...] for r in parts], 0)
    rows = jnp.concatenate([stack(na), stack(nb)], 1).T
    for k, ref in enumerate((dgate, dup)):
        g = dot(rows, ref[...]).astype(BF16)
        for h in range(2):
            for q in range(QS):
                r = g[(QS * h + q) * 64 : (QS * h + q + 1) * 64]
                for c in range(FF4 // 128):
                    first = k * GU_ROWS + c * 64
                    out[h, q, first : first + 64, :] = r[:, c * 128 : (c + 1) * 128]


def gate_up_grads(normed, dgate, dup, pieces):
    return pl.pallas_call(
        gate_up_grads_body,
        grid=(16 // QS,),
        out_shape=sds((2, 16, PIECE, 128)),
        in_specs=[pl.BlockSpec((n, 64 * QS), lambda i: (0, i)) for _, n in PIECES]
        + [pl.BlockSpec((n, 64 * QS), lambda i: (0, i + 16 // QS)) for _, n in PIECES]
        + [whole(ROWS, FF4)] * 2
        + [spec(pl.ANY)],
        out_specs=pl.BlockSpec((2, QS, 2 * GU_ROWS, 128), lambda i: (0, i, 0, 0)),
        input_output_aliases={12: 0},
        compiler_params=params(),
        cost_estimate=cost(4 * ROWS * D * FF4, 2e7),
        name="gate_up_grads",
    )(*normed, *normed, dgate, dup, pieces)


def down_grads_body(*refs):
    cots = refs[0:4]
    hid, out, hid_t = refs[4:]

    @pl.when(pl.program_id(0) == 0)
    def _():
        hid_t[...] = hid[...].T

    g = dot(hid_t[...], jnp.concatenate([r[...] for r in cots], 0)).astype(BF16)
    for h in range(2):
        for q in range(QS):
            out[h, q, :, :] = g[h * (FF4 // 2) : (h + 1) * (FF4 // 2), q * 128 : (q + 1) * 128]


def down_grads(cots, hid):
    return pl.pallas_call(
        down_grads_body,
        grid=(16 // QS,),
        out_shape=sds((2, 16, PIECE, 128)),
        in_specs=[pl.BlockSpec((BLK, 128 * QS), lambda i: (0, i))] * 4 + [whole(ROWS, FF4)],
        out_specs=pl.BlockSpec((2, QS, FF4 // 2, 128), lambda i: (0, i, 2, 0)),
        scratch_shapes=[pltpu.VMEM((FF4, ROWS), BF16)],
        compiler_params=params(),
        cost_estimate=cost(2 * ROWS * D * FF4, 1e7),
        name="down_grads",
    )(*cots, hid)


def unpack_body(piece, gate, up, down):
    for q in range(QS):
        rows = slice(q * 64, (q + 1) * 64)
        for k, ref in enumerate((gate, up)):
            for c in range(FF4 // 128):
                first = k * GU_ROWS + c * 64
                ref[rows, c * 128 : (c + 1) * 128] = piece[q, first : first + 64, :].astype(F32)
        down[:, q * 128 : (q + 1) * 128] = piece[q, 2 * GU_ROWS :, :].astype(F32)


def unpack(pieces):
    return pl.pallas_call(
        unpack_body,
        grid=(16 // QS,),
        out_shape=(sds((DH, FF4), F32), sds((DH, FF4), F32), sds((FF4 // 2, D), F32)),
        in_specs=[pl.BlockSpec((QS, PIECE, 128), lambda i: (i, 0, 0))],
        out_specs=[
            pl.BlockSpec((64 * QS, FF4), lambda i: (i, 0)),
            pl.BlockSpec((64 * QS, FF4), lambda i: (i, 0)),
            pl.BlockSpec((FF4 // 2, 128 * QS), lambda i: (0, i)),
        ],
        compiler_params=params(),
        cost_estimate=cost(1e6, 2.6e7),
        name="unpack",
    )(pieces)


QP = 4 * 128
OP = 2 * (AW // 2)
QOP = QP + OP
KVP = 128 + 16
TAIL = QOP + KVP


def attn_grads_body(idx, *refs):
    na, nb, branch = refs[0:5], refs[5:10], refs[10:15]
    dqm, att, mine, theirs, att_t = refs[15:]
    core = idx[3]

    @pl.when(pl.program_id(0) == 0)
    def _():
        att_t[...] = att[...].T

    stack = lambda parts: jnp.concatenate([r[...] for r in parts], 0)

    def store(h, first, n, zero, one):
        mine[0, h, first : first + n, :] = jnp.where(core == 0, zero, one)
        theirs[0, h, first : first + n, :] = jnp.where(core == 0, one, zero)

    for h, cols in enumerate((na, nb)):
        g = dot(stack(cols).T, dqm[...]).astype(BF16)
        for c in range(4):
            lanes = slice(c * 128, (c + 1) * 128)
            store(h, c * 128, 128, g[:128, lanes], g[128:, lanes])
    g = dot(att_t[...], stack(branch)).astype(BF16)
    for h in range(2):
        r = g[h * (AW // 2) : (h + 1) * (AW // 2)]
        for c in range(2):
            lanes = lambda k: slice(k * 256 + c * 128, k * 256 + (c + 1) * 128)
            store(h, QP + c * (AW // 2), AW // 2, r[:, lanes(0)], r[:, lanes(1)])


def attn_grads(idx, normed, branch, dqm, att):
    turn = lambda s, idx: (s + idx[2]) & 3
    piece = pl.BlockSpec((1, 2, QOP, 128), lambda s, idx: (s, 0, 0, 0))
    fixed = pl.BlockSpec((ROWS, AW), lambda s, idx: (0, 0))
    return pl.pallas_call(
        attn_grads_body,
        grid_spec=pltpu.PrefetchScalarGridSpec(
            num_scalar_prefetch=1,
            grid=(4,),
            in_specs=[pl.BlockSpec((n, 256), lambda s, idx: (0, turn(s, idx))) for _, n in PIECES]
            + [pl.BlockSpec((n, 256), lambda s, idx: (0, turn(s, idx) + 4)) for _, n in PIECES]
            + [pl.BlockSpec((n, 512), lambda s, idx: (0, turn(s, idx))) for _, n in PIECES]
            + [fixed, fixed],
            out_specs=[piece, piece],
            scratch_shapes=[pltpu.VMEM((AW, ROWS), BF16)],
        ),
        out_shape=(sds((4, 2, QOP, 128)),) * 2,
        compiler_params=params(),
        cost_estimate=cost(4 * ROWS * D * AW, 1e7),
        name="attn_grads",
    )(idx, *normed, *normed, *branch, dqm, att)


def small_call(body, out_shape, *args, name):
    return pl.pallas_call(
        body,
        out_shape=out_shape,
        in_specs=[spec(pltpu.SMEM)] + [spec()] * (len(args) - 1),
        out_specs=jax.tree.map(lambda _: spec(), out_shape),
        compiler_params=params(),
        cost_estimate=cost(1e6, 4e6),
        name=name,
    )(*args)


def add(*values):
    return sum((v.astype(F32) for v in values[1:]), values[0].astype(F32)).astype(BF16)


def sum_core_body(idx, a, b, c, d, *outs):
    for s, out in enumerate(outs):
        out[:, :QOP, :] = add(a[s], b[s])
        out[:, QOP:, :] = add(c[s], d[s])


def sum_y_body(idx, a, b, c, d, own, other):
    zh = idx[1]
    own[...] = add(a[zh], b[zh], c[zh], d[zh])
    far = 1 - zh
    other[...] = add(a[far], b[far], c[far], d[far])


def sum_z_body(idx, a, b, c, d, out):
    out[...] = add(a[...], b[...], c[...], d[...])


def unpack_tail_body(idx, *refs):
    y, core = idx[2], idx[3]
    qkv, out, gains = refs[8:]
    for k in range(8):
        piece = refs[k]
        p = ((y - k % 4) & 3) * 2 + (core if k < 4 else 1 - core)
        rows = pl.ds(pl.multiple_of(p * 128, 128), 128)
        for c in range(4):
            qkv[rows, c * 128 : (c + 1) * 128] = piece[c * 128 : (c + 1) * 128, :].astype(F32)
        qkv[rows, AW:] = piece[QOP : QOP + 128, :].astype(F32).T
        g = piece[QOP + 128 :, :].astype(F32)
        for c in range(2):
            first = QP + c * (AW // 2)
            cols = pl.ds(pl.multiple_of(p * 256 + c * 128, 128), 128)
            out[:, cols] = piece[first : first + AW // 2, :].astype(F32)
            gains[:, cols] = g[2 * c : 2 * c + 2]


def sum_tail(idx, first, second, parts, finish):
    got_a = lax.ppermute(first[1], "core", shift(2, 1))
    got_b = lax.ppermute(second[1], "core", shift(2, 1))
    part = sds((2, TAIL, 128))
    g = small_call(sum_core_body, (part,) * 4, idx, first[0], got_a, second[0], got_b, name="sum_core")
    got = [lax.ppermute(g[s], "y", shift(4, s)) for s in (2, 1, 3)]
    part = sds((TAIL, 128))
    own, other = small_call(sum_y_body, (part,) * 2, idx, g[0], *got, name="sum_y")
    p0, q1, q3 = relay([tie(p, own) for p in parts])
    cross = [(2 * a + b, 2 * (1 - a) + (1 - b)) for a in range(2) for b in range(2)]
    g = small_call(
        sum_z_body,
        part,
        idx,
        tie(own, q1, q3),
        lax.ppermute(own, "zl", shift(2, 1)),
        lax.ppermute(other, "zh", shift(2, 1)),
        lax.ppermute(other, ("zl", "zh"), cross),
        name="sum_z",
    )
    d_one = last_step(p0, q1, q3)
    input_grad = finish(d_one)
    mine = [g] + [lax.ppermute(g, "y", shift(4, s)) for s in (1, 2, 3)]
    mine[3] = tie(mine[3], input_grad)
    theirs = [lax.ppermute(v, "core", shift(2, 1)) for v in mine]
    shapes = (sds((DH, QW), F32), sds((AW // 2, D), F32), sds((2, D), F32))
    return own, input_grad, small_call(unpack_tail_body, shapes, idx, *mine, *theirs, name="unpack_tail")


def inverse_rms(v):
    return lax.rsqrt(jnp.mean(v * v, axis=-1, keepdims=True) + EPSILON)


def total(terms):
    return sum((t[...].astype(F32) for t in terms[1:]), terms[0][...].astype(F32))


def norm_two_body(tok, a, b, c, gain, after, normed):
    v = total((tok, a, b, c))
    after[...] = v
    normed[...] = (v * inverse_rms(v) * gain[...]).astype(BF16)


def norm_back_body(add, v_ref, a, b, c, gain, out, low, gain_grad):
    v = v_ref[...].astype(F32)
    grad = total((a, b, c))
    r = inverse_rms(v)
    pulled = grad * gain[...]
    inner = jnp.mean(v * pulled, axis=-1, keepdims=True)
    res = add[...].astype(F32) + r * pulled - v * (r * r * r) * inner
    out[...] = res
    low[...] = res.astype(BF16)
    part = jnp.sum(grad * v * r, axis=0, keepdims=True)

    @pl.when(pl.program_id(0) == 0)
    def _():
        gain_grad[...] = part

    @pl.when(pl.program_id(0) > 0)
    def _():
        gain_grad[...] += part


def row_call(body, out_shape, *args, name):
    block = lambda v: (
        pl.BlockSpec((HALF, D), lambda i: (i, 0))
        if v.shape[0] == BLK
        else pl.BlockSpec((1, D), lambda i: (0, 0))
    )
    return pl.pallas_call(
        body,
        grid=(2,),
        out_shape=out_shape,
        in_specs=[block(v) for v in args],
        out_specs=tuple(block(v) for v in out_shape),
        compiler_params=params(),
        cost_estimate=cost(1e6, 5e6),
        name=name,
    )(*args)


def replica_layout(lengths, replica, replica_id):
    sizes = jnp.where(replica == replica_id, lengths, 0)
    starts = jnp.cumsum(sizes) - sizes
    row_ids = jnp.arange(CAP, dtype=jnp.int32)
    inside = (row_ids[:, None] >= starts[None, :]) & (row_ids[:, None] < (starts + sizes)[None, :])
    begin = jnp.sum(jnp.where(inside, starts[None, :], 0), axis=1)
    begin = begin + jnp.where(jnp.any(inside, axis=1), 0, jnp.sum(sizes))
    return begin, row_ids - begin


def on_device(
    tokens, cotangent, gain_one, qkv_weight, out_weight, gate_weight, up_weight, down_weight,
    gain_two, seq_lengths, seq_replica,
):
    x, zh, core = lax.axis_index("x"), lax.axis_index("zh"), lax.axis_index("core")
    y, zl = lax.axis_index("y"), lax.axis_index("zl")
    idx = jnp.stack([x, zh, y, core]).astype(jnp.int32)

    tok = tokens.astype(F32)
    s_one = inverse_rms(tok)
    begin, position = replica_layout(seq_lengths, seq_replica, (y * 2 + zl) * 2 + core)
    half_rows = lambda v: lax.dynamic_index_in_dim(v.reshape(4, 2, BLK), zh, 1, False).reshape(ROWS, 1)
    first = jnp.tile(half_rows(begin)[3 * BLK :, 0], 8).reshape(1, QALL)
    lane = jnp.arange(128, dtype=jnp.int32)
    frequency = ROTARY_BASE ** (-(lane % 32).astype(F32) * (2.0 / HD))
    angles = half_rows(position).astype(F32) * frequency[None, :]
    cosine = jnp.cos(angles)
    sine = jnp.where((lane % HD) < HD // 2, -1.0, 1.0)[None, :] * jnp.sin(angles)

    qkv_got = fetch_half(qkv_weight, core)
    normed_one = gather_x((tok * s_one * gain_one).astype(BF16), (cosine,))
    slot = y * 2 + core
    eighth = lambda w: lax.dynamic_slice_in_dim(w, slot * (w.shape[0] // 8), w.shape[0] // 8, 0)
    spread = lambda v: lax.all_gather(v, ("y", "core"), axis=0, tiled=True)
    first_row = jnp.minimum(slot * DOWN_ROWS, FF4 // 2 - DOWN_ROWS)
    some = jnp.concatenate(
        [eighth(out_weight), lax.dynamic_slice_in_dim(down_weight, first_row, DOWN_ROWS, 0)], 0
    )
    some = lax.ppermute(some, "zh", shift(2, 1))
    far_rows = spread(tie(some, qkv_got, normed_one[2], normed_one[3])).reshape(8, OUT_ROWS + DOWN_ROWS, D)
    out_all, down_all = (out_weight, far_rows), (down_weight, far_rows)
    swap = lambda v, *deps: lax.ppermute(tie(v, *deps), "core", shift(2, 1))
    qkv_all = qkv_weight, qkv_got, swap(qkv_got, some, normed_one[2], normed_one[3])

    q, kv_own = qkv_forward(idx, normed_one, qkv_all, cosine, sine)
    cot = tie(cotangent, normed_one[2], normed_one[3])
    cots = [cotangent] + [lax.ppermute(cot, "x", shift(4, -k)) for k in (1, 2, 3)]
    kv_par = lax.ppermute(kv_own, "zh", shift(2, 1))
    rows = DH // 8
    cross = [(2 * a + b, 2 * (1 - a) + (1 - b)) for a in range(2) for b in range(2)]
    gate_up = lax.ppermute(
        jnp.concatenate(
            [
                eighth(tie(gate_weight, kv_own)),
                jnp.zeros((rows, GAP - FF4), BF16),
                eighth(tie(up_weight, kv_own)),
            ],
            1,
        ),
        ("zl", "zh"),
        cross,
    )
    att, qx = attend(idx, q, kv_own, kv_par, first)
    parts = out_project(idx, tie(att, *cots), out_all)
    gate_up = spread(tie(gate_up, parts[2]))
    p0, q1, q3 = relay(parts)
    after_attn, normed_two = row_call(
        norm_two_body,
        (sds((BLK, D), F32), sds((BLK, D))),
        tokens, *last_step(p0, q1, q3), gain_two.reshape(1, D), name="norm_two",
    )
    normed_two = gather_x(normed_two)
    hid, dgate, dup = ffn(idx, normed_two, cots, gate_weight, up_weight, gate_up, down_all)
    d_parts = ffn_back(idx, dgate, dup, gate_weight, up_weight, gate_up)
    own_grads = down_grads(cots, tie(hid, d_parts[2]))
    d_own, q1, q3 = relay(d_parts)
    own_grads = gate_up_grads(normed_two, tie(dgate, q1, q3), dup, own_grads)
    d_two = last_step(d_own, q1, q3)
    grads = lax.psum_scatter(
        tie(own_grads, *d_two).reshape(32, PIECE, 128),
        ("zh", "zl", "y", "core"), scatter_dimension=0, tiled=True,
    )
    after_grad, branch, gain_grad_two = row_call(
        norm_back_body,
        (sds((BLK, D), F32), sds((BLK, D)), sds((1, D), F32)),
        cotangent, after_attn, *d_two, gain_two.reshape(1, D), name="norm_back_two",
    )
    branch = gather_x(branch)
    layer_parts = down_project(idx, tie(hid, after_grad), down_all)
    att = tie(att, *layer_parts)
    layer = [
        lax.ppermute(tie(layer_parts[k], branch[2], branch[3]), "x", shift(4, k)) for k in (1, 3)
    ]
    dqm, dkv_own, dkv_par = attend_back(
        idx, qx, kv_own, kv_par, first, att, cosine, sine, branch, out_all
    )
    dkv_got = lax.ppermute(dkv_par, "zh", shift(2, 1))
    tail = attn_grads(
        idx, normed_one, branch, dqm.reshape(ROWS, AW), tie(att, *layer).reshape(ROWS, AW)
    )
    dkv_got = tie(dkv_got, tail[0])
    *tail_kv, parts = qkv_back(
        idx, dqm.reshape(ROWS, AW), dkv_own, dkv_got, cosine, sine, qkv_all, normed_one, gain_one,
        gain_grad_two,
    )
    over_x = lambda v: sum((tie(lax.ppermute(v, "x", shift(4, s)), grad_gate) for s in (1, 2, 3)), v)
    finish = lambda d_one: row_call(
        norm_back_body,
        (sds((BLK, D), F32), sds((BLK, D)), sds((1, D), F32)),
        after_grad, tokens, *d_one, gain_one.reshape(1, D), name="norm_back_one",
    )[1]
    summed, input_grad, (grad_qkv, grad_out, gains) = sum_tail(
        idx, (tail[0], tie(tail[1], dkv_got)), tail_kv, parts, finish
    )
    layer.append(lax.ppermute(tie(layer_parts[2], summed), "x", shift(4, 2)))
    grads = lax.all_gather(tie(grads, summed), ("zl", "y", "core"), axis=0, tiled=True)
    grad_gate, grad_up, grad_down = unpack(grads)
    layer_out = sum((v.astype(F32) for v in layer), after_attn + layer_parts[0].astype(F32))
    layer_out = layer_out.astype(BF16)
    gains = over_x(gains)
    return (
        layer_out, input_grad, gains[0], grad_qkv, grad_out, grad_gate, grad_up,
        grad_down, gains[1],
    )


def solution(mesh):
    grid = Mesh(mesh.devices.reshape(SIZES), AXES)
    rows = P(AXES, None)
    both = P(("x", "zh"), None)
    return jax.shard_map(
        on_device,
        mesh=grid,
        in_specs=(
            rows, rows, P(), P("zh", "x"), both, P("zh", "x"), P("zh", "x"), both, P(), P(), P(),
        ),
        out_specs=(
            rows, rows, P(), P("zh", "x"), both, P("zh", "x"), P("zh", "x"), both, P(),
        ),
        check_vma=False,
    )
```
